32 devices in a mesh: dp: 2 (over x), ctx: 4 (over y, core), tp: 4 (over z).
Axes of the slice: x: 2, y: 2, z: 4, core: 2. Of those that a mesh axis runs over, the one named last changes fastest.
Arguments:
- query_rows: bfloat16 [2, 1536, 4096], P('dp', 'ctx', 'tp'), may hold values from -2.5 to 2.5
- key_rows: bfloat16 [2, 1536, 512], P('dp', 'ctx', 'tp'), may hold values from -2.5 to 2.5
- value_rows: bfloat16 [2, 1536, 512], P('dp', 'ctx', 'tp'), may hold values from -6 to 6
- out_grad: bfloat16 [2, 1536, 4096], P('dp', 'ctx', 'tp'), may hold values from -6 to 6
- assistant: int32 [2, 12], P('dp'), may hold values from 0 to 1, as said below
- turn_first: int32 [2, 12], P('dp'), may hold values from 0 to 11, as said below
Outputs:
- query_grad: bfloat16 [2, 1536, 4096], P('dp', 'ctx', 'tp')
- key_grad: bfloat16 [2, 1536, 512], P('dp', 'ctx', 'tp')
- value_grad: bfloat16 [2, 1536, 512], P('dp', 'ctx', 'tp')
The draws below stay inside these ranges and needn't reach their ends.
Inputs may be any that keep to these rules, and one draw needn't show every extreme that they name: Among the 3 blocks at positions d * 3 to d * 3 + 2 at most 2 are assistant blocks, and in every sequence some such group holds exactly 2. Turns are runs of whole blocks: turn_first never falls, equals the block's own index where a turn begins, and q - 4 <= turn_first[q] <= q; in every sequence some block has q - turn_first[q] = 4.
All inputs are finite; a program needn't handle non-finite values.
Results may differ from the reference program's by a relative error of at most 0.005.
Values may be sent and summed in bfloat16 or wider, within the bound.
No kernel may reach another device: no remote copies, remote signals or barrier semaphores. Data moves between devices by JAX's collectives and lax.ppermute only.
A program may use at most 64 MiB of HBM per device.

```python
import math
import jax
import jax.numpy as jnp
from jax import lax

BLK = 128
QH = 8
HD = 128
KVH = 4
BATCH = 2
SEQ = 1536
NB_DEV = 3
NBLK = 12
REACH = 4
A_MAX = 2


def draw_assistant(key, part):
    groups = NBLK // NB_DEV

    def one_sequence(seq_key):
        count_key, forced_key, order_key = jax.random.split(seq_key, 3)
        counts = jax.random.randint(count_key, (groups,), 0, A_MAX + 1)
        forced = jax.random.randint(forced_key, (), 0, groups)
        counts = jnp.where(jnp.arange(groups) == forced, A_MAX, counts)
        ranking = jax.vmap(lambda inner_key: jax.random.permutation(inner_key, NB_DEV))(jax.random.split(order_key, groups))
        return (ranking < counts[:, None]).astype(jnp.int32).reshape(NBLK)
    return jax.vmap(one_sequence)(jax.random.split(jax.random.fold_in(key, 11), BATCH))


def draw_turn_first(key, part):

    def one_sequence(seq_key):
        lengths = jax.random.randint(seq_key, (NBLK,), 1, REACH + 2)
        lengths = lengths.at[0].set(REACH + 1)
        starts = jnp.cumsum(lengths) - lengths
        block_ids = jnp.arange(NBLK, dtype=jnp.int32)
        is_start = jnp.any(starts[None, :] == block_ids[:, None], axis=1)
        return lax.cummax(jnp.where(is_start, block_ids, 0), axis=0).astype(jnp.int32)
    return jax.vmap(one_sequence)(jax.random.split(jax.random.fold_in(key, 23), BATCH))


def level_of(stream_key, shape, shards, smallest, high):
    def one(position, blocks):
        draws = jax.random.uniform(jax.random.fold_in(jax.random.fold_in(stream_key, 6), position), (blocks,), jnp.float32, smallest / len(shards), high / len(shards))
        return jnp.repeat(jnp.exp(draws), shape[position] // blocks).reshape((-1,) + (1,) * (len(shape) - position - 1))

    loudness = one(*shards[0])
    for cut in shards[1:]:
        loudness = loudness * one(*cut)
    return loudness


def centred(key, extent, spread, limit, cuts=(), kind=jnp.bfloat16):
    array = spread * jax.random.normal(key, extent, jnp.float32)
    if cuts:
        array = array * level_of(key, extent, cuts, -0.22, 0.18)
    return jnp.clip(array, -limit, limit).astype(kind)


def setup_inputs(seed: int = 0) -> dict:
    key_of = jax.random.split(jax.random.key(seed), 7)
    return {
        "query_rows": centred(key_of[0], (BATCH, SEQ, KVH * QH * HD), 1.0, 2.5, ((0, 2), (1, 4), (2, 4))),
        "key_rows": centred(key_of[1], (BATCH, SEQ, KVH * HD), 1.0, 2.5, ((0, 2), (1, 4), (2, 4))),
        "value_rows": centred(key_of[2], (BATCH, SEQ, KVH * HD), 1.0, 6.0, ((0, 2), (1, 4), (2, 4))),
        "out_grad": centred(key_of[3], (BATCH, SEQ, KVH * QH * HD), 1.0, 6.0, ((0, 2), (1, 4), (2, 4))),
        "assistant": draw_assistant(jax.random.fold_in(key_of[6], 71), 0),
        "turn_first": draw_turn_first(jax.random.fold_in(key_of[6], 71), 0),
    }


def reference(query_rows, key_rows, value_rows, out_grad, assistant, turn_first):
    scale_factor = 1.0 / math.sqrt(HD)
    key_span = (REACH + 1) * BLK
    pad_rows = REACH * BLK
    highest = lax.Precision.HIGHEST

    def one_sequence(seq_args):
        query_seq, key_seq, value_seq, grad_seq, assist_mark, turn_start = seq_args
        query_blocks = query_seq.reshape(NBLK, BLK, KVH, QH, HD)
        grad_blocks = grad_seq.reshape(NBLK, BLK, KVH, QH, HD)
        key_padded = jnp.concatenate([jnp.zeros((pad_rows, KVH * HD), key_seq.dtype), key_seq], 0).reshape(-1, KVH, HD)
        value_padded = jnp.concatenate([jnp.zeros((pad_rows, KVH * HD), value_seq.dtype), value_seq], 0).reshape(-1, KVH, HD)

        def live_block(block_index):
            query_block = lax.dynamic_index_in_dim(query_blocks, block_index, 0, keepdims=False).astype(jnp.float32)
            grad_block = lax.dynamic_index_in_dim(grad_blocks, block_index, 0, keepdims=False).astype(jnp.float32)
            key_window = lax.dynamic_slice_in_dim(key_padded, block_index * BLK, key_span, 0).astype(jnp.float32)
            value_window = lax.dynamic_slice_in_dim(value_padded, block_index * BLK, key_span, 0).astype(jnp.float32)
            scores = jnp.einsum('bghd,kgd->ghbk', query_block, key_window, precision=highest)
            key_pos = (block_index - REACH) * BLK + jnp.arange(key_span, dtype=jnp.int32)
            query_pos = block_index * BLK + jnp.arange(BLK, dtype=jnp.int32)
            turn_begin = lax.dynamic_index_in_dim(turn_start, block_index, 0, keepdims=False) * BLK
            allowed = (key_pos[None, :] >= turn_begin) & (key_pos[None, :] <= query_pos[:, None])
            weights = jnp.where(allowed, jnp.exp(scores * scale_factor), 0.0)
            attention = weights / lax.optimization_barrier(jnp.sum(weights, axis=3, keepdims=True))
            prob_grad = jnp.einsum('bghd,kgd->ghbk', grad_block, value_window, precision=highest)
            row_delta = lax.optimization_barrier(jnp.sum(attention * prob_grad, axis=3, keepdims=True))
            score_grad = (attention * (prob_grad - row_delta)).astype(jnp.bfloat16).astype(jnp.float32)
            attention_low = attention.astype(jnp.bfloat16).astype(jnp.float32)
            query_grad = (scale_factor * jnp.einsum('ghbk,kgd->bghd', score_grad, key_window, precision=highest)).astype(jnp.bfloat16)
            key_part = scale_factor * jnp.einsum('ghbk,bghd->kgd', score_grad, query_block, precision=highest)
            value_part = jnp.einsum('ghbk,bghd->kgd', attention_low, grad_block, precision=highest)
            return (query_grad, key_part, value_part)

        def dead_block(block_index):
            return (jnp.zeros((BLK, KVH, QH, HD), jnp.bfloat16), jnp.zeros((key_span, KVH, HD), jnp.float32), jnp.zeros((key_span, KVH, HD), jnp.float32))

        def block_step(carried, block_index):
            key_acc, value_acc = carried
            is_live = lax.dynamic_index_in_dim(assist_mark, block_index, 0, keepdims=False) == 1
            query_grad, key_part, value_part = lax.cond(is_live, live_block, dead_block, block_index)
            offset = block_index * BLK
            key_acc = lax.dynamic_update_slice_in_dim(key_acc, lax.dynamic_slice_in_dim(key_acc, offset, key_span, 0) + key_part, offset, 0)
            value_acc = lax.dynamic_update_slice_in_dim(value_acc, lax.dynamic_slice_in_dim(value_acc, offset, key_span, 0) + value_part, offset, 0)
            return ((key_acc, value_acc), query_grad)
        start_acc = jnp.zeros(((NBLK + REACH) * BLK, KVH, HD), jnp.float32)
        (key_acc, value_acc), query_all = lax.scan(block_step, (start_acc, start_acc), jnp.arange(NBLK, dtype=jnp.int32))
        query_seq_grad = query_all.reshape(SEQ, KVH * QH * HD)
        key_seq_grad = key_acc[pad_rows:].reshape(SEQ, KVH * HD).astype(jnp.bfloat16)
        value_seq_grad = value_acc[pad_rows:].reshape(SEQ, KVH * HD).astype(jnp.bfloat16)
        return (query_seq_grad, key_seq_grad, value_seq_grad)
    query_grad, key_grad, value_grad = lax.map(one_sequence, (query_rows, key_rows, value_rows, out_grad, assistant, turn_first))
    return (query_grad, key_grad, value_grad)
```

```python
import math

import jax
import jax.numpy as jnp
from jax import lax
from jax.experimental import pallas as pl
from jax.experimental.pallas import tpu as pltpu
from jax.sharding import PartitionSpec as P

BLK = 128
SUB = 8
CHUNK = 256
F32 = jnp.float32
BF16 = jnp.bfloat16
MIB = 1 << 20


def shifted(block, axis, distance):
    devices = range(lax.axis_size(axis))
    route = [(i - distance, i) for i in devices if i - distance in devices]
    return lax.ppermute(block, axis, route)


def vmem(array):
    return pltpu.with_memory_space_constraint(array, pltpu.VMEM)


def nt_dot(left, right):
    return lax.dot_general(left, right, (((1,), (1,)), ((), ())), preferred_element_type=F32)


def nn_dot(left, right):
    return lax.dot_general(left, right, (((1,), (0,)), ((), ())), preferred_element_type=F32)


def fold(tile):
    return jnp.sum(tile.reshape(tile.shape[0] // SUB, SUB, tile.shape[1]), axis=0)


def slots_of(assistant, turn_first, base, block_count, slot_count):
    found = jnp.int32(0)
    blocks = [jnp.int32(0)] * slot_count
    starts = [jnp.int32(0)] * slot_count
    for i in range(block_count):
        mark = assistant[0, base + i]
        start = turn_first[0, base + i] - base
        for s in range(slot_count):
            here = (mark == 1) & (found == s)
            blocks[s] = jnp.where(here, i, blocks[s])
            starts[s] = jnp.where(here, start, starts[s])
        found = found + jnp.where(mark == 1, 1, 0)
    return [(blocks[s], found > s, starts[s]) for s in range(slot_count)]


def pack_kernel(key_ref, value_ref, near_ref, far_ref, sem):
    far_rows = far_ref.shape[1]
    first = near_ref.shape[1] - far_rows
    copies = []
    for i, source in enumerate((key_ref, value_ref)):
        copies.append(pltpu.make_async_copy(source.at[0], near_ref.at[i], sem.at[2 * i]))
        copies.append(
            pltpu.make_async_copy(
                source.at[0, pl.ds(first, far_rows)], far_ref.at[i], sem.at[2 * i + 1]
            )
        )
    for copy in copies:
        copy.start()
    for copy in copies:
        copy.wait()


def score_pass(key_tile, value_tile, query_ref, grad_ref, slot, keep, weight_ref, prob_ref, rows,
               sum_ref, dot_ref, scale):
    columns = query_ref.shape[1]
    for c in range(0, columns, CHUNK):
        span = slice(c, c + CHUNK)
        scores = nt_dot(key_tile, query_ref[slot, span, :])
        prob_grad = nt_dot(value_tile, grad_ref[slot, span, :])
        weights = jnp.exp2(scores * scale)
        if keep is not None:
            weights = jnp.where(jnp.concatenate([keep] * (CHUNK // BLK), axis=1), weights, 0.0)
        weight_ref[slot, rows, span] = weights
        prob_ref[slot, rows, span] = prob_grad
        sum_ref[slot, :, span] += fold(weights)
        dot_ref[slot, :, span] += fold(weights * prob_grad)


def grad_pass(weight_ref, prob_ref, query_ref, grad_ref, slot, rows, inverse_ref, delta_ref, low_ref,
              score_ref, score_rows, key_acc, value_acc, acc_rows):
    columns = query_ref.shape[1]
    for c in range(0, columns, CHUNK):
        span = slice(c, c + CHUNK)
        shape = (BLK // SUB, SUB, CHUNK)
        attention = weight_ref[slot, rows, span].reshape(shape) * inverse_ref[slot, :, span][None]
        lifted = prob_ref[slot, rows, span].reshape(shape) - delta_ref[slot, :, span][None]
        score_grad = (attention * lifted).reshape(BLK, CHUNK)
        low_ref[:, span] = attention.reshape(BLK, CHUNK).astype(BF16)
        score_ref[slot, score_rows, span] = score_grad.astype(BF16)
    value_acc[acc_rows, :] += nn_dot(low_ref[...], grad_ref[slot])
    key_acc[acc_rows, :] += nn_dot(score_ref[slot, score_rows, :], query_ref[slot])


def block_rows(index):
    return pl.ds(pl.multiple_of(index * BLK, BLK), BLK)


def local_kernel(sizes, assistant, turn_first, query_hbm, grad_hbm, kv_ref, query_ref, grad_ref,
                 weight_ref, prob_ref, sum_ref, dot_ref, sem):
    block_count, slot_count, head_count, width, scale = sizes
    base = lax.axis_index("ctx") * block_count
    slots = slots_of(assistant, turn_first, base, block_count, slot_count)

    def copies(s, block):
        for i, (source, target) in enumerate(((query_hbm, query_ref), (grad_hbm, grad_ref))):
            for h in range(head_count):
                yield pltpu.make_async_copy(
                    source.at[0, block_rows(block), pl.ds(h * width, width)],
                    target.at[s, pl.ds(h * BLK, BLK)],
                    sem.at[s, i, h],
                )

    for s, (block, live, start) in enumerate(slots):
        @pl.when(live)
        def _():
            for copy in copies(s, block):
                copy.start()
    sum_ref[...] = jnp.zeros_like(sum_ref)
    dot_ref[...] = jnp.zeros_like(dot_ref)
    ahead = lax.broadcasted_iota(jnp.int32, (BLK, BLK), 1) - lax.broadcasted_iota(
        jnp.int32, (BLK, BLK), 0
    )
    for s, (block, live, start) in enumerate(slots):
        @pl.when(live)
        def _():
            for copy in copies(s, block):
                copy.wait()

            def step(k, carry):
                rows = block_rows(k)
                keep = ahead >= (k - block) * BLK
                score_pass(kv_ref[0, rows, :], kv_ref[1, rows, :], query_ref, grad_ref, s, keep,
                           weight_ref, prob_ref, rows, sum_ref, dot_ref, scale * math.log2(math.e))
                return carry

            lax.fori_loop(jnp.maximum(start, 0), block + 1, step, 0)


def remote_kernel(sizes, assistant, turn_first, query_ref, grad_ref, sum_in, dot_in, near_ref, far_ref,
                  near_out, far_out, score_ref, inverse_ref, delta_ref,
                  window, weight_ref, prob_ref, sum_ref, dot_ref, low_ref, key_acc, value_acc):
    block_count, slot_count, head_count, width, scale = sizes
    base = lax.axis_index("ctx") * block_count
    slots = slots_of(assistant, turn_first, base, block_count, slot_count)
    far_rows = far_ref.shape[1]
    reach = window.shape[1] // BLK
    window[:, :far_rows, :] = far_ref[...]
    window[:, far_rows:, :] = near_ref[...]
    key_acc[...] = jnp.zeros_like(key_acc)
    value_acc[...] = jnp.zeros_like(value_acc)
    sum_ref[...] = sum_in[...]
    dot_ref[...] = dot_in[...]
    for s, (block, live, start) in enumerate(slots):
        @pl.when(live)
        def _():
            first = jnp.minimum(start + reach, reach)

            def score_step(k, carry):
                rows = block_rows(k)
                score_pass(window[0, rows, :], window[1, rows, :], query_ref, grad_ref, s, None,
                           weight_ref, prob_ref, rows, sum_ref, dot_ref, scale * math.log2(math.e))
                return carry

            lax.fori_loop(first, reach, score_step, 0)
            inverse = 1.0 / jnp.sum(sum_ref[s], axis=0, keepdims=True)
            delta = jnp.sum(dot_ref[s], axis=0, keepdims=True) * inverse
            inverse_ref[s] = jnp.broadcast_to(inverse, inverse_ref.shape[1:])
            delta_ref[s] = jnp.broadcast_to(delta, delta_ref.shape[1:])

            def grad_step(k, carry):
                rows = block_rows(k)
                grad_pass(weight_ref, prob_ref, query_ref, grad_ref, s, rows, inverse_ref, delta_ref,
                          low_ref, score_ref, rows, key_acc, value_acc, rows)
                return carry

            lax.fori_loop(first, reach, grad_step, 0)
    key_low = (key_acc[...] * scale).astype(BF16)
    value_low = value_acc[...].astype(BF16)
    far_out[0] = key_low[:far_rows]
    far_out[1] = value_low[:far_rows]
    near_out[0] = key_low[far_rows:]
    near_out[1] = value_low[far_rows:]


def finish_kernel(sizes, assistant, turn_first, query_ref, grad_ref, weight_ref, prob_ref, score_in,
                  inverse_ref, delta_ref, kv_ref, near_ref, far_ref, query_out, key_acc, value_acc,
                  score_ref, low_ref, query_acc):
    block_count, slot_count, head_count, width, scale = sizes
    base = lax.axis_index("ctx") * block_count
    slots = slots_of(assistant, turn_first, base, block_count, slot_count)
    far_blocks = far_ref.shape[1] // BLK
    reach = block_count + far_blocks
    key_acc[...] = jnp.zeros_like(key_acc)
    value_acc[...] = jnp.zeros_like(value_acc)
    query_out[...] = jnp.zeros_like(query_out)
    for s, (block, live, start) in enumerate(slots):
        @pl.when(live)
        def _():
            query_acc[...] = jnp.zeros_like(query_acc)

            def add_query(key_tile, score_source, rows):
                turned = key_tile.T
                for c in range(0, query_acc.shape[1], CHUNK):
                    span = slice(c, c + CHUNK)
                    query_acc[:, span] += nn_dot(turned, score_source[s, rows, span])

            def far_step(k, carry):
                add_query(far_ref[0, block_rows(k), :], score_in, block_rows(k))
                return carry

            def near_step(k, carry):
                add_query(near_ref[0, block_rows(k - far_blocks), :], score_in, block_rows(k))
                return carry

            def local_step(k, carry):
                rows = block_rows(k)
                grad_pass(weight_ref, prob_ref, query_ref, grad_ref, s, rows, inverse_ref, delta_ref,
                          low_ref, score_ref, rows, key_acc, value_acc, rows)
                add_query(kv_ref[0, rows, :], score_ref, rows)
                return carry

            first = jnp.minimum(start + reach, reach)
            lax.fori_loop(first, far_blocks, far_step, 0)
            lax.fori_loop(jnp.maximum(first, far_blocks), reach, near_step, 0)
            lax.fori_loop(jnp.maximum(start, 0), block + 1, local_step, 0)
            for h in range(head_count):
                turned = (query_acc[:, h * BLK:(h + 1) * BLK] * scale).T
                query_out[0, block_rows(block), h * width:(h + 1) * width] = turned.astype(BF16)
    key_acc[...] = key_acc[...] * scale


def total_kernel(key_acc, value_acc, near_ref, far_ref, key_out, value_out):
    far_rows = far_ref.shape[1]
    split = near_ref.shape[1] - far_rows
    for i, (acc, out) in enumerate(((key_acc, key_out), (value_acc, value_out))):
        total = acc[...] + near_ref[i].astype(F32)
        out[0, :split] = total[:split].astype(BF16)
        out[0, split:] = (total[split:] + far_ref[i].astype(F32)).astype(BF16)


def per_device(query_rows, key_rows, value_rows, out_grad, assistant, turn_first):
    token_count = query_rows.shape[1]
    width = key_rows.shape[2]
    head_count = query_rows.shape[2] // width
    block_count = token_count // BLK
    far_rows = block_count // 2 * BLK
    reach_rows = token_count + far_rows
    slot_count = (block_count + 1) // 2
    columns = head_count * BLK
    sizes = (block_count, slot_count, head_count, width, 1.0 / math.sqrt(width))
    any_spec = pl.BlockSpec(memory_space=pl.ANY)
    smem_spec = pl.BlockSpec(memory_space=pltpu.SMEM)
    vmem_spec = pl.BlockSpec(memory_space=pltpu.VMEM)

    def call(kernel, inputs, in_specs, outputs, out_specs, scratch, limit, macs):
        return pl.pallas_call(
            kernel,
            out_shape=outputs,
            in_specs=in_specs,
            out_specs=out_specs,
            scratch_shapes=scratch,
            compiler_params=pltpu.CompilerParams(vmem_limit_bytes=limit * MIB),
            cost_estimate=pl.CostEstimate(flops=2 * macs, bytes_accessed=2 * MIB, transcendentals=0),
        )(*inputs)

    pair = columns * BLK * width
    near, far = call(
        pack_kernel,
        (key_rows, value_rows),
        [any_spec] * 2,
        (
            pltpu.VMEM((2, token_count, width), BF16),
            pltpu.VMEM((2, far_rows, width), BF16),
        ),
        [vmem_spec] * 2,
        [pltpu.SemaphoreType.DMA((4,))],
        8,
        BLK,
    )
    near_in = shifted(near, "ctx", 1)
    far_in = shifted(far, "ctx", 2)
    slot_rows = (slot_count, columns, width)
    stat_rows = (slot_count, SUB, columns)
    query_slots, grad_slots, weights, prob_grad, sums, dots = call(
        lambda *refs: local_kernel(sizes, *refs),
        (assistant, turn_first, query_rows, out_grad, vmem(near)),
        [smem_spec] * 2 + [any_spec] * 2 + [vmem_spec],
        (
            pltpu.VMEM(slot_rows, BF16),
            pltpu.VMEM(slot_rows, BF16),
            pltpu.VMEM((slot_count, token_count, columns), F32),
            pltpu.VMEM((slot_count, token_count, columns), F32),
            pltpu.VMEM(stat_rows, F32),
            pltpu.VMEM(stat_rows, F32),
        ),
        [vmem_spec] * 6,
        [pltpu.SemaphoreType.DMA((slot_count, 2, head_count))],
        16,
        10 * pair,
    )
    near_grad, far_grad, score_grad, inverse, delta = call(
        lambda *refs: remote_kernel(sizes, *refs),
        (assistant, turn_first)
        + tuple(vmem(a) for a in (query_slots, grad_slots, sums, dots, near_in, far_in)),
        [smem_spec] * 2 + [vmem_spec] * 6,
        (
            pltpu.VMEM((2, token_count, width), BF16),
            pltpu.VMEM((2, far_rows, width), BF16),
            pltpu.VMEM((slot_count, reach_rows, columns), BF16),
            pltpu.VMEM(stat_rows, F32),
            pltpu.VMEM(stat_rows, F32),
        ),
        [vmem_spec] * 5,
        [
            pltpu.VMEM((2, reach_rows, width), BF16),
            pltpu.VMEM((slot_count, reach_rows, columns), F32),
            pltpu.VMEM((slot_count, reach_rows, columns), F32),
            pltpu.VMEM(stat_rows, F32),
            pltpu.VMEM(stat_rows, F32),
            pltpu.VMEM((BLK, columns), BF16),
            pltpu.VMEM((reach_rows, width), F32),
            pltpu.VMEM((reach_rows, width), F32),
        ],
        20,
        20 * pair,
    )
    near_back = shifted(near_grad, "ctx", -1)
    far_back = shifted(far_grad, "ctx", -2)
    query_grad, key_acc, value_acc = call(
        lambda *refs: finish_kernel(sizes, *refs),
        (assistant, turn_first)
        + tuple(
            vmem(a)
            for a in (query_slots, grad_slots, weights, prob_grad, score_grad, inverse, delta, near,
                      near_in, far_in)
        ),
        [smem_spec] * 2 + [vmem_spec] * 10,
        (
            jax.ShapeDtypeStruct(query_rows.shape, BF16),
            pltpu.VMEM((token_count, width), F32),
            pltpu.VMEM((token_count, width), F32),
        ),
        [vmem_spec] * 3,
        [
            pltpu.VMEM((slot_count, token_count, columns), BF16),
            pltpu.VMEM((BLK, columns), BF16),
            pltpu.VMEM((BLK, columns), F32),
        ],
        16,
        25 * pair,
    )
    key_grad, value_grad = call(
        total_kernel,
        tuple(vmem(a) for a in (key_acc, value_acc, near_back, far_back)),
        [vmem_spec] * 4,
        (
            jax.ShapeDtypeStruct(key_rows.shape, BF16),
            jax.ShapeDtypeStruct(value_rows.shape, BF16),
        ),
        [vmem_spec] * 2,
        [],
        8,
        BLK,
    )
    return (query_grad, key_grad, value_grad)


def solution(mesh):
    return jax.shard_map(
        per_device,
        mesh=mesh,
        in_specs=(
            P("dp", "ctx", "tp"),
            P("dp", "ctx", "tp"),
            P("dp", "ctx", "tp"),
            P("dp", "ctx", "tp"),
            P("dp", None),
            P("dp", None),
        ),
        out_specs=(P("dp", "ctx", "tp"), P("dp", "ctx", "tp"), P("dp", "ctx", "tp")),
        check_vma=False,
    )
```

```python
import math

import jax
import jax.numpy as jnp
from jax import lax
from jax.experimental import pallas as pl
from jax.experimental.pallas import tpu as pltpu
from jax.sharding import PartitionSpec as P

BLK = 128
SUB = 8
CHUNK = 256
F32 = jnp.float32
BF16 = jnp.bfloat16
MIB = 1 << 20


def shifted(block, axis, distance):
    devices = range(lax.axis_size(axis))
    route = [(i - distance, i) for i in devices if i - distance in devices]
    return lax.ppermute(block, axis, route)


def vmem(array):
    return pltpu.with_memory_space_constraint(array, pltpu.VMEM)


def smem(array):
    return pltpu.with_memory_space_constraint(array, pltpu.SMEM)


def hbm(array):
    return pltpu.with_memory_space_constraint(array, pltpu.HBM)


def nt_dot(left, right):
    return lax.dot_general(left, right, (((1,), (1,)), ((), ())), preferred_element_type=F32)


def nn_dot(left, right):
    return lax.dot_general(left, right, (((1,), (0,)), ((), ())), preferred_element_type=F32)


def fold(tile):
    return jnp.sum(tile.reshape(tile.shape[0] // SUB, SUB, tile.shape[1]), axis=0)


def slots_of(assistant, turn_first, base, block_count, slot_count):
    found = jnp.int32(0)
    blocks = [jnp.int32(0)] * slot_count
    starts = [jnp.int32(0)] * slot_count
    for i in range(block_count):
        mark = assistant[0, base + i]
        start = turn_first[0, base + i] - base
        for s in range(slot_count):
            here = (mark == 1) & (found == s)
            blocks[s] = jnp.where(here, i, blocks[s])
            starts[s] = jnp.where(here, start, starts[s])
        found = found + jnp.where(mark == 1, 1, 0)
    return [(blocks[s], found > s, starts[s]) for s in range(slot_count)]


def pack_kernel(key_ref, value_ref, assistant_ref, turn_ref, near_ref, far_ref, assistant, turn_first,
                sem):
    far_rows = far_ref.shape[1]
    first = near_ref.shape[1] - far_rows
    copies = [
        pltpu.make_async_copy(assistant_ref, assistant, sem.at[4]),
        pltpu.make_async_copy(turn_ref, turn_first, sem.at[5]),
    ]
    for i, source in enumerate((key_ref, value_ref)):
        copies.append(pltpu.make_async_copy(source.at[0], near_ref.at[i], sem.at[2 * i]))
        copies.append(
            pltpu.make_async_copy(
                source.at[0, pl.ds(first, far_rows)], far_ref.at[i], sem.at[2 * i + 1]
            )
        )
    for copy in copies:
        copy.start()
    for copy in copies:
        copy.wait()


def score_pass(key_tile, value_tile, query_ref, grad_ref, slot, keep, weight_ref, prob_ref, rows,
               sum_ref, dot_ref, scale):
    columns = query_ref.shape[1]
    for c in range(0, columns, CHUNK):
        span = slice(c, c + CHUNK)
        scores = nt_dot(key_tile, query_ref[slot, span, :])
        prob_grad = nt_dot(value_tile, grad_ref[slot, span, :])
        weights = jnp.exp2(scores * scale)
        if keep is not None:
            weights = jnp.where(jnp.concatenate([keep] * (CHUNK // BLK), axis=1), weights, 0.0)
        weight_ref[slot, rows, span] = weights
        prob_ref[slot, rows, span] = prob_grad
        sum_ref[slot, :, span] += fold(weights)
        dot_ref[slot, :, span] += fold(weights * prob_grad)


def grad_pass(weight_ref, prob_ref, query_ref, grad_ref, slot, rows, inverse_ref, delta_ref, low_ref,
              score_ref, score_rows, key_acc, value_acc, acc_rows):
    columns = query_ref.shape[1]
    for c in range(0, columns, CHUNK):
        span = slice(c, c + CHUNK)
        shape = (BLK // SUB, SUB, CHUNK)
        attention = weight_ref[slot, rows, span].reshape(shape) * inverse_ref[slot, :, span][None]
        lifted = prob_ref[slot, rows, span].reshape(shape) - delta_ref[slot, :, span][None]
        score_grad = (attention * lifted).reshape(BLK, CHUNK)
        low_ref[:, span] = attention.reshape(BLK, CHUNK).astype(BF16)
        score_ref[slot, score_rows, span] = score_grad.astype(BF16)
    value_acc[acc_rows, :] += nn_dot(low_ref[...], grad_ref[slot])
    key_acc[acc_rows, :] += nn_dot(score_ref[slot, score_rows, :], query_ref[slot])


def block_rows(index):
    return pl.ds(pl.multiple_of(index * BLK, BLK), BLK)


def local_kernel(sizes, assistant, turn_first, query_hbm, grad_hbm, kv_ref, query_ref, grad_ref,
                 weight_ref, prob_ref, sum_ref, dot_ref, sem):
    block_count, slot_count, head_count, width, scale = sizes
    base = lax.axis_index("ctx") * block_count
    slots = slots_of(assistant, turn_first, base, block_count, slot_count)

    def copies(s, block):
        for i, (source, target) in enumerate(((query_hbm, query_ref), (grad_hbm, grad_ref))):
            for h in range(head_count):
                yield pltpu.make_async_copy(
                    source.at[0, block_rows(block), pl.ds(h * width, width)],
                    target.at[s, pl.ds(h * BLK, BLK)],
                    sem.at[s, i, h],
                )

    for s, (block, live, start) in enumerate(slots):
        @pl.when(live)
        def _():
            for copy in copies(s, block):
                copy.start()
    sum_ref[...] = jnp.zeros_like(sum_ref)
    dot_ref[...] = jnp.zeros_like(dot_ref)
    ahead = lax.broadcasted_iota(jnp.int32, (BLK, BLK), 1) - lax.broadcasted_iota(
        jnp.int32, (BLK, BLK), 0
    )
    for s, (block, live, start) in enumerate(slots):
        @pl.when(live)
        def _():
            for copy in copies(s, block):
                copy.wait()

            def step(k, carry):
                rows = block_rows(k)
                keep = ahead >= (k - block) * BLK
                score_pass(kv_ref[0, rows, :], kv_ref[1, rows, :], query_ref, grad_ref, s, keep,
                           weight_ref, prob_ref, rows, sum_ref, dot_ref, scale * math.log2(math.e))
                return carry

            lax.fori_loop(jnp.maximum(start, 0), block + 1, step, 0)


def remote_kernel(sizes, assistant, turn_first, query_ref, grad_ref, sum_in, dot_in, near_ref, far_ref,
                  near_out, far_out, score_ref, inverse_ref, delta_ref,
                  window, weight_ref, prob_ref, sum_ref, dot_ref, low_ref, key_acc, value_acc):
    block_count, slot_count, head_count, width, scale = sizes
    base = lax.axis_index("ctx") * block_count
    slots = slots_of(assistant, turn_first, base, block_count, slot_count)
    far_rows = far_ref.shape[1]
    reach = window.shape[1] // BLK
    window[:, :far_rows, :] = far_ref[...]
    window[:, far_rows:, :] = near_ref[...]
    key_acc[...] = jnp.zeros_like(key_acc)
    value_acc[...] = jnp.zeros_like(value_acc)
    sum_ref[...] = sum_in[...]
    dot_ref[...] = dot_in[...]
    for s, (block, live, start) in enumerate(slots):
        @pl.when(live)
        def _():
            first = jnp.minimum(start + reach, reach)

            def score_step(k, carry):
                rows = block_rows(k)
                score_pass(window[0, rows, :], window[1, rows, :], query_ref, grad_ref, s, None,
                           weight_ref, prob_ref, rows, sum_ref, dot_ref, scale * math.log2(math.e))
                return carry

            lax.fori_loop(first, reach, score_step, 0)
            inverse = 1.0 / jnp.sum(sum_ref[s], axis=0, keepdims=True)
            delta = jnp.sum(dot_ref[s], axis=0, keepdims=True) * inverse
            inverse_ref[s] = jnp.broadcast_to(inverse, inverse_ref.shape[1:])
            delta_ref[s] = jnp.broadcast_to(delta, delta_ref.shape[1:])

            def grad_step(k, carry):
                rows = block_rows(k)
                grad_pass(weight_ref, prob_ref, query_ref, grad_ref, s, rows, inverse_ref, delta_ref,
                          low_ref, score_ref, rows, key_acc, value_acc, rows)
                return carry

            lax.fori_loop(first, reach, grad_step, 0)
    key_low = (key_acc[...] * scale).astype(BF16)
    value_low = value_acc[...].astype(BF16)
    far_out[0] = key_low[:far_rows]
    far_out[1] = value_low[:far_rows]
    near_out[0] = key_low[far_rows:]
    near_out[1] = value_low[far_rows:]


def finish_kernel(sizes, assistant, turn_first, query_ref, grad_ref, weight_ref, prob_ref, score_in,
                  inverse_ref, delta_ref, kv_ref, near_ref, far_ref, query_out, key_acc, value_acc,
                  score_ref, low_ref, query_acc):
    block_count, slot_count, head_count, width, scale = sizes
    base = lax.axis_index("ctx") * block_count
    slots = slots_of(assistant, turn_first, base, block_count, slot_count)
    far_blocks = far_ref.shape[1] // BLK
    reach = block_count + far_blocks
    key_acc[...] = jnp.zeros_like(key_acc)
    value_acc[...] = jnp.zeros_like(value_acc)
    query_out[...] = jnp.zeros_like(query_out)
    for s, (block, live, start) in enumerate(slots):
        @pl.when(live)
        def _():
            query_acc[...] = jnp.zeros_like(query_acc)

            def add_query(key_tile, score_source, rows):
                turned = key_tile.T
                for c in range(0, query_acc.shape[1], CHUNK):
                    span = slice(c, c + CHUNK)
                    query_acc[:, span] += nn_dot(turned, score_source[s, rows, span])

            def far_step(k, carry):
                add_query(far_ref[0, block_rows(k), :], score_in, block_rows(k))
                return carry

            def near_step(k, carry):
                add_query(near_ref[0, block_rows(k - far_blocks), :], score_in, block_rows(k))
                return carry

            def local_step(k, carry):
                rows = block_rows(k)
                grad_pass(weight_ref, prob_ref, query_ref, grad_ref, s, rows, inverse_ref, delta_ref,
                          low_ref, score_ref, rows, key_acc, value_acc, rows)
                add_query(kv_ref[0, rows, :], score_ref, rows)
                return carry

            first = jnp.minimum(start + reach, reach)
            lax.fori_loop(first, far_blocks, far_step, 0)
            lax.fori_loop(jnp.maximum(first, far_blocks), reach, near_step, 0)
            lax.fori_loop(jnp.maximum(start, 0), block + 1, local_step, 0)
            for h in range(head_count):
                turned = (query_acc[:, h * BLK:(h + 1) * BLK] * scale).T
                query_out[0, block_rows(block), h * width:(h + 1) * width] = turned.astype(BF16)
    key_acc[...] = key_acc[...] * scale


def total_kernel(key_acc, value_acc, near_ref, far_ref, key_out, value_out):
    far_rows = far_ref.shape[1]
    split = near_ref.shape[1] - far_rows
    for i, (acc, out) in enumerate(((key_acc, key_out), (value_acc, value_out))):
        total = acc[...] + near_ref[i].astype(F32)
        out[0, :split] = total[:split].astype(BF16)
        out[0, split:] = (total[split:] + far_ref[i].astype(F32)).astype(BF16)


def per_device(query_rows, key_rows, value_rows, out_grad, assistant, turn_first):
    token_count = query_rows.shape[1]
    width = key_rows.shape[2]
    head_count = query_rows.shape[2] // width
    block_count = token_count // BLK
    far_rows = block_count // 2 * BLK
    reach_rows = token_count + far_rows
    slot_count = (block_count + 1) // 2
    columns = head_count * BLK
    sizes = (block_count, slot_count, head_count, width, 1.0 / math.sqrt(width))
    any_spec = pl.BlockSpec(memory_space=pl.ANY)
    smem_spec = pl.BlockSpec(memory_space=pltpu.SMEM)
    vmem_spec = pl.BlockSpec(memory_space=pltpu.VMEM)

    def call(kernel, inputs, in_specs, outputs, out_specs, scratch, limit, macs):
        return pl.pallas_call(
            kernel,
            out_shape=outputs,
            in_specs=in_specs,
            out_specs=out_specs,
            scratch_shapes=scratch,
            compiler_params=pltpu.CompilerParams(vmem_limit_bytes=limit * MIB),
            cost_estimate=pl.CostEstimate(flops=2 * macs, bytes_accessed=2 * MIB, transcendentals=0),
        )(*inputs)

    pair = columns * BLK * width
    near, far, assistant, turn_first = call(
        pack_kernel,
        tuple(hbm(a) for a in (key_rows, value_rows, assistant, turn_first)),
        [any_spec] * 4,
        (
            pltpu.VMEM((2, token_count, width), BF16),
            pltpu.VMEM((2, far_rows, width), BF16),
            pltpu.SMEM(assistant.shape, jnp.int32),
            pltpu.SMEM(turn_first.shape, jnp.int32),
        ),
        [vmem_spec] * 2 + [smem_spec] * 2,
        [pltpu.SemaphoreType.DMA((6,))],
        8,
        BLK,
    )
    assistant, turn_first = smem(assistant), smem(turn_first)
    near_in = shifted(near, "ctx", 1)
    far_in = shifted(far, "ctx", 2)
    slot_rows = (slot_count, columns, width)
    stat_rows = (slot_count, SUB, columns)
    query_slots, grad_slots, weights, prob_grad, sums, dots = call(
        lambda *refs: local_kernel(sizes, *refs),
        (assistant, turn_first, hbm(query_rows), hbm(out_grad), vmem(near)),
        [smem_spec] * 2 + [any_spec] * 2 + [vmem_spec],
        (
            pltpu.VMEM(slot_rows, BF16),
            pltpu.VMEM(slot_rows, BF16),
            pltpu.VMEM((slot_count, token_count, columns), F32),
            pltpu.VMEM((slot_count, token_count, columns), F32),
            pltpu.VMEM(stat_rows, F32),
            pltpu.VMEM(stat_rows, F32),
        ),
        [vmem_spec] * 6,
        [pltpu.SemaphoreType.DMA((slot_count, 2, head_count))],
        16,
        10 * pair,
    )
    near_grad, far_grad, score_grad, inverse, delta = call(
        lambda *refs: remote_kernel(sizes, *refs),
        (assistant, turn_first)
        + tuple(vmem(a) for a in (query_slots, grad_slots, sums, dots, near_in, far_in)),
        [smem_spec] * 2 + [vmem_spec] * 6,
        (
            pltpu.VMEM((2, token_count, width), BF16),
            pltpu.VMEM((2, far_rows, width), BF16),
            pltpu.VMEM((slot_count, reach_rows, columns), BF16),
            pltpu.VMEM(stat_rows, F32),
            pltpu.VMEM(stat_rows, F32),
        ),
        [vmem_spec] * 5,
        [
            pltpu.VMEM((2, reach_rows, width), BF16),
            pltpu.VMEM((slot_count, reach_rows, columns), F32),
            pltpu.VMEM((slot_count, reach_rows, columns), F32),
            pltpu.VMEM(stat_rows, F32),
            pltpu.VMEM(stat_rows, F32),
            pltpu.VMEM((BLK, columns), BF16),
            pltpu.VMEM((reach_rows, width), F32),
            pltpu.VMEM((reach_rows, width), F32),
        ],
        20,
        20 * pair,
    )
    near_back = shifted(near_grad, "ctx", -1)
    far_back = shifted(far_grad, "ctx", -2)
    query_grad, key_acc, value_acc = call(
        lambda *refs: finish_kernel(sizes, *refs),
        (assistant, turn_first)
        + tuple(
            vmem(a)
            for a in (query_slots, grad_slots, weights, prob_grad, score_grad, inverse, delta, near,
                      near_in, far_in)
        ),
        [smem_spec] * 2 + [vmem_spec] * 10,
        (
            jax.ShapeDtypeStruct(query_rows.shape, BF16),
            pltpu.VMEM((token_count, width), F32),
            pltpu.VMEM((token_count, width), F32),
        ),
        [vmem_spec] * 3,
        [
            pltpu.VMEM((slot_count, token_count, columns), BF16),
            pltpu.VMEM((BLK, columns), BF16),
            pltpu.VMEM((BLK, columns), F32),
        ],
        16,
        25 * pair,
    )
    key_grad, value_grad = call(
        total_kernel,
        tuple(vmem(a) for a in (key_acc, value_acc, near_back, far_back)),
        [vmem_spec] * 4,
        (
            jax.ShapeDtypeStruct(key_rows.shape, BF16),
            jax.ShapeDtypeStruct(value_rows.shape, BF16),
        ),
        [vmem_spec] * 2,
        [],
        8,
        BLK,
    )
    return (query_grad, key_grad, value_grad)


def solution(mesh):
    return jax.shard_map(
        per_device,
        mesh=mesh,
        in_specs=(
            P("dp", "ctx", "tp"),
            P("dp", "ctx", "tp"),
            P("dp", "ctx", "tp"),
            P("dp", "ctx", "tp"),
            P("dp", None),
            P("dp", None),
        ),
        out_specs=(P("dp", "ctx", "tp"), P("dp", "ctx", "tp"), P("dp", "ctx", "tp")),
        check_vma=False,
    )
```

```python
import math

import jax
import jax.numpy as jnp
from jax import lax
from jax.experimental import pallas as pl
from jax.experimental.pallas import tpu as pltpu
from jax.sharding import PartitionSpec as P

BLK = 128
SUB = 8
CHUNK = 256
F32 = jnp.float32
BF16 = jnp.bfloat16
MIB = 1 << 20


def shifted(block, axis, distance):
    devices = range(lax.axis_size(axis))
    route = [(i - distance, i) for i in devices if i - distance in devices]
    return lax.ppermute(block, axis, route)


def vmem(array):
    return pltpu.with_memory_space_constraint(array, pltpu.VMEM)


def smem(array):
    return pltpu.with_memory_space_constraint(array, pltpu.SMEM)


def hbm(array):
    return pltpu.with_memory_space_constraint(array, pltpu.HBM)


def nt_dot(left, right):
    return lax.dot_general(left, right, (((1,), (1,)), ((), ())), preferred_element_type=F32)


def nn_dot(left, right):
    return lax.dot_general(left, right, (((1,), (0,)), ((), ())), preferred_element_type=F32)


def fold(tile):
    return jnp.sum(tile.reshape(tile.shape[0] // SUB, SUB, tile.shape[1]), axis=0)


def slots_of(assistant, turn_first, base, block_count, slot_count):
    found = jnp.int32(0)
    blocks = [jnp.int32(0)] * slot_count
    starts = [jnp.int32(0)] * slot_count
    for i in range(block_count):
        mark = assistant[0, base + i]
        start = turn_first[0, base + i] - base
        for s in range(slot_count):
            here = (mark == 1) & (found == s)
            blocks[s] = jnp.where(here, i, blocks[s])
            starts[s] = jnp.where(here, start, starts[s])
        found = found + jnp.where(mark == 1, 1, 0)
    return [(blocks[s], found > s, starts[s]) for s in range(slot_count)]


def pack_kernel(key_ref, value_ref, assistant_ref, turn_ref, near_ref, far_ref, assistant, turn_first,
                sem):
    far_rows = far_ref.shape[1]
    first = near_ref.shape[1] - far_rows
    copies = [
        pltpu.make_async_copy(assistant_ref, assistant, sem.at[4]),
        pltpu.make_async_copy(turn_ref, turn_first, sem.at[5]),
    ]
    for i, source in enumerate((key_ref, value_ref)):
        copies.append(pltpu.make_async_copy(source.at[0], near_ref.at[i], sem.at[2 * i]))
        copies.append(
            pltpu.make_async_copy(
                source.at[0, pl.ds(first, far_rows)], far_ref.at[i], sem.at[2 * i + 1]
            )
        )
    for copy in copies:
        copy.start()
    for copy in copies:
        copy.wait()


def score_pass(key_tile, value_tile, query_ref, grad_ref, slot, keep, weight_ref, prob_ref, rows,
               sum_ref, dot_ref, scale):
    columns = query_ref.shape[1]
    for c in range(0, columns, CHUNK):
        span = slice(c, c + CHUNK)
        scores = nt_dot(key_tile, query_ref[slot, span, :])
        prob_grad = nt_dot(value_tile, grad_ref[slot, span, :])
        weights = jnp.exp2(scores * scale)
        if keep is not None:
            weights = jnp.where(jnp.concatenate([keep] * (CHUNK // BLK), axis=1), weights, 0.0)
        weight_ref[slot, rows, span] = weights
        prob_ref[slot, rows, span] = prob_grad
        sum_ref[slot, :, span] += fold(weights)
        dot_ref[slot, :, span] += fold(weights * prob_grad)


def grad_pass(weight_ref, prob_ref, query_ref, grad_ref, slot, rows, inverse_ref, delta_ref, low_ref,
              score_ref, score_rows, key_acc, value_acc, acc_rows):
    columns = query_ref.shape[1]
    for c in range(0, columns, CHUNK):
        span = slice(c, c + CHUNK)
        shape = (BLK // SUB, SUB, CHUNK)
        attention = weight_ref[slot, rows, span].reshape(shape) * inverse_ref[slot, :, span][None]
        lifted = prob_ref[slot, rows, span].reshape(shape) - delta_ref[slot, :, span][None]
        score_grad = (attention * lifted).reshape(BLK, CHUNK)
        low_ref[:, span] = attention.reshape(BLK, CHUNK).astype(BF16)
        score_ref[slot, score_rows, span] = score_grad.astype(BF16)
    value_acc[acc_rows, :] += nn_dot(low_ref[...], grad_ref[slot])
    key_acc[acc_rows, :] += nn_dot(score_ref[slot, score_rows, :], query_ref[slot])


def block_rows(index):
    return pl.ds(pl.multiple_of(index * BLK, BLK), BLK)


def local_kernel(sizes, assistant, turn_first, query_hbm, grad_hbm, kv_ref, query_ref, grad_ref,
                 weight_ref, prob_ref, sum_ref, dot_ref, sem):
    block_count, slot_count, head_count, width, scale = sizes
    base = lax.axis_index("ctx") * block_count
    slots = slots_of(assistant, turn_first, base, block_count, slot_count)

    def copies(s, block):
        for i, (source, target) in enumerate(((query_hbm, query_ref), (grad_hbm, grad_ref))):
            for h in range(head_count):
                yield pltpu.make_async_copy(
                    source.at[0, block_rows(block), pl.ds(h * width, width)],
                    target.at[s, pl.ds(h * BLK, BLK)],
                    sem.at[s, i, h],
                )

    for s, (block, live, start) in enumerate(slots):
        @pl.when(live)
        def _():
            for copy in copies(s, block):
                copy.start()
    sum_ref[...] = jnp.zeros_like(sum_ref)
    dot_ref[...] = jnp.zeros_like(dot_ref)
    ahead = lax.broadcasted_iota(jnp.int32, (BLK, BLK), 1) - lax.broadcasted_iota(
        jnp.int32, (BLK, BLK), 0
    )
    for s, (block, live, start) in enumerate(slots):
        @pl.when(live)
        def _():
            for copy in copies(s, block):
                copy.wait()

            def step(k, carry):
                rows = block_rows(k)
                keep = ahead >= (k - block) * BLK
                score_pass(kv_ref[0, rows, :], kv_ref[1, rows, :], query_ref, grad_ref, s, keep,
                           weight_ref, prob_ref, rows, sum_ref, dot_ref, scale * math.log2(math.e))
                return carry

            lax.fori_loop(jnp.maximum(start, 0), block + 1, step, 0)


def remote_kernel(sizes, assistant, turn_first, query_ref, grad_ref, sum_in, dot_in, gathered,
                  near_out, far_out, score_ref, inverse_ref, delta_ref, window,
                  weight_ref, prob_ref, sum_ref, dot_ref, low_ref, key_acc, value_acc, sem):
    block_count, slot_count, head_count, width, scale = sizes
    base = lax.axis_index("ctx") * block_count
    slots = slots_of(assistant, turn_first, base, block_count, slot_count)
    far_rows = far_out.shape[1]
    near_rows = near_out.shape[1]
    reach = window.shape[1] // BLK
    rank = lax.axis_index("ctx")
    fetches = []
    for i in range(2):
        fetches.append(
            pltpu.make_async_copy(
                gathered.at[jnp.maximum(rank - 2, 0), i, pl.ds(near_rows - far_rows, far_rows)],
                window.at[i, pl.ds(0, far_rows)],
                sem.at[2 * i],
            )
        )
        fetches.append(
            pltpu.make_async_copy(
                gathered.at[jnp.maximum(rank - 1, 0), i],
                window.at[i, pl.ds(far_rows, near_rows)],
                sem.at[2 * i + 1],
            )
        )
    for fetch in fetches:
        fetch.start()
    key_acc[...] = jnp.zeros_like(key_acc)
    value_acc[...] = jnp.zeros_like(value_acc)
    sum_ref[...] = sum_in[...]
    dot_ref[...] = dot_in[...]
    for fetch in fetches:
        fetch.wait()
    for s, (block, live, start) in enumerate(slots):
        @pl.when(live)
        def _():
            first = jnp.minimum(start + reach, reach)

            def score_step(k, carry):
                rows = block_rows(k)
                score_pass(window[0, rows, :], window[1, rows, :], query_ref, grad_ref, s, None,
                           weight_ref, prob_ref, rows, sum_ref, dot_ref, scale * math.log2(math.e))
                return carry

            lax.fori_loop(first, reach, score_step, 0)
            inverse = 1.0 / jnp.sum(sum_ref[s], axis=0, keepdims=True)
            delta = jnp.sum(dot_ref[s], axis=0, keepdims=True) * inverse
            inverse_ref[s] = jnp.broadcast_to(inverse, inverse_ref.shape[1:])
            delta_ref[s] = jnp.broadcast_to(delta, delta_ref.shape[1:])

            def grad_step(k, carry):
                rows = block_rows(k)
                grad_pass(weight_ref, prob_ref, query_ref, grad_ref, s, rows, inverse_ref, delta_ref,
                          low_ref, score_ref, rows, key_acc, value_acc, rows)
                return carry

            lax.fori_loop(first, reach, grad_step, 0)
    key_low = (key_acc[...] * scale).astype(BF16)
    value_low = value_acc[...].astype(BF16)
    far_out[0] = key_low[:far_rows]
    far_out[1] = value_low[:far_rows]
    near_out[0] = key_low[far_rows:]
    near_out[1] = value_low[far_rows:]


def finish_kernel(sizes, assistant, turn_first, query_ref, grad_ref, weight_ref, prob_ref, score_in,
                  inverse_ref, delta_ref, kv_ref, window, query_out, key_acc, value_acc,
                  score_ref, low_ref, query_acc):
    block_count, slot_count, head_count, width, scale = sizes
    base = lax.axis_index("ctx") * block_count
    slots = slots_of(assistant, turn_first, base, block_count, slot_count)
    reach = window.shape[1] // BLK
    key_acc[...] = jnp.zeros_like(key_acc)
    value_acc[...] = jnp.zeros_like(value_acc)
    query_out[...] = jnp.zeros_like(query_out)
    for s, (block, live, start) in enumerate(slots):
        @pl.when(live)
        def _():
            query_acc[...] = jnp.zeros_like(query_acc)

            def add_query(key_tile, score_source, rows):
                turned = key_tile.T
                for c in range(0, query_acc.shape[1], CHUNK):
                    span = slice(c, c + CHUNK)
                    query_acc[:, span] += nn_dot(turned, score_source[s, rows, span])

            def window_step(k, carry):
                add_query(window[0, block_rows(k), :], score_in, block_rows(k))
                return carry

            def local_step(k, carry):
                rows = block_rows(k)
                grad_pass(weight_ref, prob_ref, query_ref, grad_ref, s, rows, inverse_ref, delta_ref,
                          low_ref, score_ref, rows, key_acc, value_acc, rows)
                add_query(kv_ref[0, rows, :], score_ref, rows)
                return carry

            first = jnp.minimum(start + reach, reach)
            lax.fori_loop(first, reach, window_step, 0)
            lax.fori_loop(jnp.maximum(start, 0), block + 1, local_step, 0)
            for h in range(head_count):
                turned = (query_acc[:, h * BLK:(h + 1) * BLK] * scale).T
                query_out[0, block_rows(block), h * width:(h + 1) * width] = turned.astype(BF16)
    key_acc[...] = key_acc[...] * scale


def total_kernel(key_acc, value_acc, near_ref, far_ref, key_out, value_out):
    far_rows = far_ref.shape[1]
    split = near_ref.shape[1] - far_rows
    for i, (acc, out) in enumerate(((key_acc, key_out), (value_acc, value_out))):
        total = acc[...] + near_ref[i].astype(F32)
        out[0, :split] = total[:split].astype(BF16)
        out[0, split:] = (total[split:] + far_ref[i].astype(F32)).astype(BF16)


def per_device(query_rows, key_rows, value_rows, out_grad, assistant, turn_first):
    token_count = query_rows.shape[1]
    width = key_rows.shape[2]
    head_count = query_rows.shape[2] // width
    block_count = token_count // BLK
    far_rows = block_count // 2 * BLK
    reach_rows = token_count + far_rows
    slot_count = (block_count + 1) // 2
    columns = head_count * BLK
    sizes = (block_count, slot_count, head_count, width, 1.0 / math.sqrt(width))
    any_spec = pl.BlockSpec(memory_space=pl.ANY)
    smem_spec = pl.BlockSpec(memory_space=pltpu.SMEM)
    vmem_spec = pl.BlockSpec(memory_space=pltpu.VMEM)

    def call(kernel, inputs, in_specs, outputs, out_specs, scratch, limit, macs):
        return pl.pallas_call(
            kernel,
            out_shape=outputs,
            in_specs=in_specs,
            out_specs=out_specs,
            scratch_shapes=scratch,
            compiler_params=pltpu.CompilerParams(vmem_limit_bytes=limit * MIB),
            cost_estimate=pl.CostEstimate(flops=2 * macs, bytes_accessed=2 * MIB, transcendentals=0),
        )(*inputs)

    pair = columns * BLK * width
    near, far, assistant, turn_first = call(
        pack_kernel,
        tuple(hbm(a) for a in (key_rows, value_rows, assistant, turn_first)),
        [any_spec] * 4,
        (
            pltpu.VMEM((2, token_count, width), BF16),
            pltpu.VMEM((2, far_rows, width), BF16),
            pltpu.SMEM(assistant.shape, jnp.int32),
            pltpu.SMEM(turn_first.shape, jnp.int32),
        ),
        [vmem_spec] * 2 + [smem_spec] * 2,
        [pltpu.SemaphoreType.DMA((6,))],
        8,
        BLK,
    )
    assistant, turn_first = smem(assistant), smem(turn_first)
    gathered = lax.all_gather(near, "ctx")
    slot_rows = (slot_count, columns, width)
    stat_rows = (slot_count, SUB, columns)
    query_slots, grad_slots, weights, prob_grad, sums, dots = call(
        lambda *refs: local_kernel(sizes, *refs),
        (assistant, turn_first, hbm(query_rows), hbm(out_grad), vmem(near)),
        [smem_spec] * 2 + [any_spec] * 2 + [vmem_spec],
        (
            pltpu.VMEM(slot_rows, BF16),
            pltpu.VMEM(slot_rows, BF16),
            pltpu.VMEM((slot_count, token_count, columns), F32),
            pltpu.VMEM((slot_count, token_count, columns), F32),
            pltpu.VMEM(stat_rows, F32),
            pltpu.VMEM(stat_rows, F32),
        ),
        [vmem_spec] * 6,
        [pltpu.SemaphoreType.DMA((slot_count, 2, head_count))],
        16,
        10 * pair,
    )
    near_grad, far_grad, score_grad, inverse, delta, window = call(
        lambda *refs: remote_kernel(sizes, *refs),
        (assistant, turn_first)
        + tuple(vmem(a) for a in (query_slots, grad_slots, sums, dots)) + (hbm(gathered),),
        [smem_spec] * 2 + [vmem_spec] * 4 + [any_spec],
        (
            pltpu.VMEM((2, token_count, width), BF16),
            pltpu.VMEM((2, far_rows, width), BF16),
            pltpu.VMEM((slot_count, reach_rows, columns), BF16),
            pltpu.VMEM(stat_rows, F32),
            pltpu.VMEM(stat_rows, F32),
            pltpu.VMEM((2, reach_rows, width), BF16),
        ),
        [vmem_spec] * 6,
        [
            pltpu.VMEM((slot_count, reach_rows, columns), F32),
            pltpu.VMEM((slot_count, reach_rows, columns), F32),
            pltpu.VMEM(stat_rows, F32),
            pltpu.VMEM(stat_rows, F32),
            pltpu.VMEM((BLK, columns), BF16),
            pltpu.VMEM((reach_rows, width), F32),
            pltpu.VMEM((reach_rows, width), F32),
            pltpu.SemaphoreType.DMA((4,)),
        ],
        20,
        20 * pair,
    )
    near_back = shifted(near_grad, "ctx", -1)
    far_back = shifted(far_grad, "ctx", -2)
    query_grad, key_acc, value_acc = call(
        lambda *refs: finish_kernel(sizes, *refs),
        (assistant, turn_first)
        + tuple(
            vmem(a)
            for a in (query_slots, grad_slots, weights, prob_grad, score_grad, inverse, delta, near,
                      window)
        ),
        [smem_spec] * 2 + [vmem_spec] * 9,
        (
            jax.ShapeDtypeStruct(query_rows.shape, BF16),
            pltpu.VMEM((token_count, width), F32),
            pltpu.VMEM((token_count, width), F32),
        ),
        [vmem_spec] * 3,
        [
            pltpu.VMEM((slot_count, token_count, columns), BF16),
            pltpu.VMEM((BLK, columns), BF16),
            pltpu.VMEM((BLK, columns), F32),
        ],
        16,
        25 * pair,
    )
    key_grad, value_grad = call(
        total_kernel,
        tuple(vmem(a) for a in (key_acc, value_acc, near_back, far_back)),
        [vmem_spec] * 4,
        (
            jax.ShapeDtypeStruct(key_rows.shape, BF16),
            jax.ShapeDtypeStruct(value_rows.shape, BF16),
        ),
        [vmem_spec] * 2,
        [],
        8,
        BLK,
    )
    return (query_grad, key_grad, value_grad)


def solution(mesh):
    return jax.shard_map(
        per_device,
        mesh=mesh,
        in_specs=(
            P("dp", "ctx", "tp"),
            P("dp", "ctx", "tp"),
            P("dp", "ctx", "tp"),
            P("dp", "ctx", "tp"),
            P("dp", None),
            P("dp", None),
        ),
        out_specs=(P("dp", "ctx", "tp"), P("dp", "ctx", "tp"), P("dp", "ctx", "tp")),
        check_vma=False,
    )
```

```python
import math

import jax
import jax.numpy as jnp
from jax import lax
from jax.experimental import pallas as pl
from jax.experimental.pallas import tpu as pltpu
from jax.sharding import PartitionSpec as P

BLK = 128
SUB = 8
CHUNK = 256
F32 = jnp.float32
BF16 = jnp.bfloat16
MIB = 1 << 20


def shifted(block, axis, distance):
    devices = range(lax.axis_size(axis))
    route = [(i - distance, i) for i in devices if i - distance in devices]
    return lax.ppermute(block, axis, route)


def vmem(array):
    return pltpu.with_memory_space_constraint(array, pltpu.VMEM)


def smem(array):
    return pltpu.with_memory_space_constraint(array, pltpu.SMEM)


def hbm(array):
    return pltpu.with_memory_space_constraint(array, pltpu.HBM)


def nt_dot(left, right):
    return lax.dot_general(left, right, (((1,), (1,)), ((), ())), preferred_element_type=F32)


def nn_dot(left, right):
    return lax.dot_general(left, right, (((1,), (0,)), ((), ())), preferred_element_type=F32)


def fold(tile):
    return jnp.sum(tile.reshape(tile.shape[0] // SUB, SUB, tile.shape[1]), axis=0)


def slots_of(assistant, turn_first, base, block_count, slot_count):
    found = jnp.int32(0)
    blocks = [jnp.int32(0)] * slot_count
    starts = [jnp.int32(0)] * slot_count
    for i in range(block_count):
        mark = assistant[0, base + i]
        start = turn_first[0, base + i] - base
        for s in range(slot_count):
            here = (mark == 1) & (found == s)
            blocks[s] = jnp.where(here, i, blocks[s])
            starts[s] = jnp.where(here, start, starts[s])
        found = found + jnp.where(mark == 1, 1, 0)
    return [(blocks[s], found > s, starts[s]) for s in range(slot_count)]


def pack_kernel(key_ref, value_ref, assistant_ref, turn_ref, near_ref, far_ref, assistant, turn_first,
                sem):
    far_rows = far_ref.shape[1]
    first = near_ref.shape[1] - far_rows
    copies = [
        pltpu.make_async_copy(assistant_ref, assistant, sem.at[4]),
        pltpu.make_async_copy(turn_ref, turn_first, sem.at[5]),
    ]
    for i, source in enumerate((key_ref, value_ref)):
        copies.append(pltpu.make_async_copy(source.at[0], near_ref.at[i], sem.at[2 * i]))
        copies.append(
            pltpu.make_async_copy(
                source.at[0, pl.ds(first, far_rows)], far_ref.at[i], sem.at[2 * i + 1]
            )
        )
    for copy in copies:
        copy.start()
    for copy in copies:
        copy.wait()


def score_pass(key_tile, value_tile, query_ref, grad_ref, slot, keep, weight_ref, prob_ref, at, sum_ref,
               dot_ref, scale):
    columns = query_ref.shape[1]
    height = key_tile.shape[0]
    for c in range(0, columns, CHUNK):
        span = slice(c, c + CHUNK)
        scores = nt_dot(key_tile, query_ref[slot, span, :])
        prob_grad = nt_dot(value_tile, grad_ref[slot, span, :])
        weights = jnp.exp2(scores * scale)
        if keep is not None:
            wide = jnp.concatenate([keep] * (CHUNK // BLK), axis=1)
            last = jnp.where(wide, weights[height - BLK:], 0.0)
            weights = jnp.concatenate([weights[:height - BLK], last], axis=0) if height > BLK else last
        weight_ref[at + (span,)] = weights
        prob_ref[at + (span,)] = prob_grad
        sum_ref[slot, :, span] = fold(weights)
        dot_ref[slot, :, span] = fold(weights * prob_grad)


def grad_pass(weight_ref, prob_ref, at, query_ref, grad_ref, slot, inverse_ref, delta_ref, low_ref,
              score_ref, score_rows, key_acc, value_acc, acc_rows):
    columns = query_ref.shape[1]
    height = acc_rows.size
    for c in range(0, columns, CHUNK):
        span = slice(c, c + CHUNK)
        shape = (height // SUB, SUB, CHUNK)
        attention = weight_ref[at + (span,)].reshape(shape) * inverse_ref[slot, :, span][None]
        lifted = prob_ref[at + (span,)].reshape(shape) - delta_ref[slot, :, span][None]
        score_grad = (attention * lifted).reshape(height, CHUNK)
        low_ref[:height, span] = attention.reshape(height, CHUNK).astype(BF16)
        score_ref[slot, score_rows, span] = score_grad.astype(BF16)
    value_acc[acc_rows, :] += nn_dot(low_ref[:height], grad_ref[slot])
    key_acc[acc_rows, :] += nn_dot(score_ref[slot, score_rows, :], query_ref[slot])


def block_rows(index, count=1):
    return pl.ds(pl.multiple_of(index * BLK, BLK), count * BLK)


def pick(values, s):
    chosen = values[0]
    for i in range(1, len(values)):
        chosen = jnp.where(s == i, values[i], chosen)
    return chosen


def over_slots(slots, body):
    def step(s, carry):
        block, start = (pick([slot[i] for slot in slots], s) for i in (0, 2))

        @pl.when(pick([jnp.where(slot[1], 1, 0) for slot in slots], s) == 1)
        def _():
            body(s, block, start)

        return carry

    lax.fori_loop(0, len(slots), step, 0)


def local_kernel(sizes, early, assistant, turn_first, query_hbm, grad_hbm, kv_ref, *rest):
    query_ref, grad_ref, weight_ref, prob_ref, sum_ref, dot_ref, sem = rest[-7:]
    block_count, slot_count, head_count, width, scale = sizes
    rank = lax.axis_index("ctx")
    first_half = rank * 2 < lax.axis_size("ctx")

    def run():
        slots = slots_of(assistant, turn_first, rank * block_count, block_count, slot_count)

        def copies(s, block):
            for i, (source, target) in enumerate(((query_hbm, query_ref), (grad_hbm, grad_ref))):
                for h in range(head_count):
                    yield pltpu.make_async_copy(
                        source.at[0, block_rows(block), pl.ds(h * width, width)],
                        target.at[s, pl.ds(h * BLK, BLK)],
                        sem.at[s, i, h],
                    )

        for s, (block, live, start) in enumerate(slots):
            @pl.when(live)
            def _():
                for copy in copies(s, block):
                    copy.start()
        keep = lax.broadcasted_iota(jnp.int32, (BLK, BLK), 0) <= lax.broadcasted_iota(
            jnp.int32, (BLK, BLK), 1
        )

        def body(s, block, start):
            for copy in copies(s, block):
                copy.wait()
            low = jnp.maximum(start, 0)
            for count in range(1, block_count + 1):
                @pl.when(block + 1 - low == count)
                def _():
                    rows = block_rows(low, count)
                    score_pass(kv_ref[0, rows, :], kv_ref[1, rows, :], query_ref, grad_ref, s, keep,
                               weight_ref, prob_ref, (s, rows), sum_ref, dot_ref,
                               scale * math.log2(math.e))

        over_slots(slots, body)

    pl.when(first_half if early else jnp.logical_not(first_half))(run)


def near_kernel(sizes, assistant, turn_first, query_ref, grad_ref, near_ref, weight_ref, prob_ref, sum_ref,
                dot_ref):
    block_count, slot_count, head_count, width, scale = sizes
    base = lax.axis_index("ctx") * block_count
    slots = slots_of(assistant, turn_first, base, block_count, slot_count)
    sum_ref[...] = jnp.zeros_like(sum_ref)
    dot_ref[...] = jnp.zeros_like(dot_ref)

    def body(s, block, start):
        for count in range(1, block_count + 1):
            last = start <= -count if count == block_count else start == -count

            @pl.when(last)
            def _():
                rows = pl.ds((block_count - count) * BLK, count * BLK)
                score_pass(near_ref[0, rows, :], near_ref[1, rows, :], query_ref, grad_ref, s, None,
                           weight_ref, prob_ref, (s, rows), sum_ref, dot_ref, scale * math.log2(math.e))

    over_slots(slots, body)


def remote_kernel(sizes, assistant, turn_first, query_ref, grad_ref, sum_local, dot_local, sum_near,
                  dot_near, weight_near, prob_near, far_ref, near_out, far_out, score_ref, inverse_ref,
                  delta_ref, weight_far, prob_far, sum_far, dot_far, low_ref, key_acc, value_acc):
    block_count, slot_count, head_count, width, scale = sizes
    base = lax.axis_index("ctx") * block_count
    slots = slots_of(assistant, turn_first, base, block_count, slot_count)
    far_rows = far_ref.shape[1]
    far_blocks = far_rows // BLK
    key_acc[...] = jnp.zeros_like(key_acc)
    value_acc[...] = jnp.zeros_like(value_acc)
    sum_far[...] = jnp.zeros_like(sum_far)
    dot_far[...] = jnp.zeros_like(dot_far)

    def body(s, block, start):
        for count in range(1, far_blocks + 1):
            @pl.when(start == -block_count - count)
            def _():
                rows = pl.ds((far_blocks - count) * BLK, count * BLK)
                score_pass(far_ref[0, rows, :], far_ref[1, rows, :], query_ref, grad_ref, s, None,
                           weight_far, prob_far, (s, rows), sum_far, dot_far, scale * math.log2(math.e))

        sums = sum_local[s] + sum_near[s] + sum_far[s]
        dots = dot_local[s] + dot_near[s] + dot_far[s]
        inverse = 1.0 / jnp.sum(sums, axis=0, keepdims=True)
        delta = jnp.sum(dots, axis=0, keepdims=True) * inverse
        inverse_ref[s] = jnp.broadcast_to(inverse, inverse_ref.shape[1:])
        delta_ref[s] = jnp.broadcast_to(delta, delta_ref.shape[1:])
        for count in range(1, far_blocks + 1):
            @pl.when(start == -block_count - count)
            def _():
                rows = pl.ds((far_blocks - count) * BLK, count * BLK)
                grad_pass(weight_far, prob_far, (s, rows), query_ref, grad_ref, s, inverse_ref, delta_ref,
                          low_ref, score_ref, rows, key_acc, value_acc, rows)

        for count in range(1, block_count + 1):
            last = start <= -count if count == block_count else start == -count

            @pl.when(last)
            def _():
                rows = pl.ds((block_count - count) * BLK, count * BLK)
                window = pl.ds(far_rows + (block_count - count) * BLK, count * BLK)
                grad_pass(weight_near, prob_near, (s, rows), query_ref, grad_ref, s, inverse_ref,
                          delta_ref, low_ref, score_ref, window, key_acc, value_acc, window)

    over_slots(slots, body)
    key_low = (key_acc[...] * scale).astype(BF16)
    value_low = value_acc[...].astype(BF16)
    far_out[0] = key_low[:far_rows]
    far_out[1] = value_low[:far_rows]
    near_out[0] = key_low[far_rows:]
    near_out[1] = value_low[far_rows:]


def finish_kernel(sizes, assistant, turn_first, query_ref, grad_ref, weight_ref, prob_ref, score_in,
                  inverse_ref, delta_ref, kv_ref, near_ref, far_ref, query_out, key_acc, value_acc,
                  score_ref, low_ref, query_acc):
    block_count, slot_count, head_count, width, scale = sizes
    base = lax.axis_index("ctx") * block_count
    slots = slots_of(assistant, turn_first, base, block_count, slot_count)
    far_blocks = far_ref.shape[1] // BLK
    reach = block_count + far_blocks
    key_acc[...] = jnp.zeros_like(key_acc)
    value_acc[...] = jnp.zeros_like(value_acc)
    query_out[...] = jnp.zeros_like(query_out)

    def body(s, block, start):
        query_acc[...] = jnp.zeros_like(query_acc)

        def add_query(key_tile, score_source, rows):
            turned = key_tile.T
            for c in range(0, query_acc.shape[1], CHUNK):
                span = slice(c, c + CHUNK)
                query_acc[:, span] += nn_dot(turned, score_source[s, rows, span])

        def far_step(k, carry):
            add_query(far_ref[0, block_rows(k), :], score_in, block_rows(k))
            return carry

        def near_step(k, carry):
            add_query(near_ref[0, block_rows(k - far_blocks), :], score_in, block_rows(k))
            return carry

        first = jnp.minimum(start + reach, reach)
        lax.fori_loop(first, far_blocks, far_step, 0)
        lax.fori_loop(jnp.maximum(first, far_blocks), reach, near_step, 0)
        low = jnp.maximum(start, 0)
        for count in range(1, block_count + 1):
            @pl.when(block + 1 - low == count)
            def _():
                rows = block_rows(low, count)
                grad_pass(weight_ref, prob_ref, (s, rows), query_ref, grad_ref, s, inverse_ref, delta_ref,
                          low_ref, score_ref, rows, key_acc, value_acc, rows)
                add_query(kv_ref[0, rows, :], score_ref, rows)

        for h in range(head_count):
            turned = (query_acc[:, h * BLK:(h + 1) * BLK] * scale).T
            query_out[0, block_rows(block), h * width:(h + 1) * width] = turned.astype(BF16)

    over_slots(slots, body)
    key_acc[...] = key_acc[...] * scale


def total_kernel(key_acc, value_acc, near_ref, far_ref, key_out, value_out):
    far_rows = far_ref.shape[1]
    split = near_ref.shape[1] - far_rows
    for i, (acc, out) in enumerate(((key_acc, key_out), (value_acc, value_out))):
        total = acc[...] + near_ref[i].astype(F32)
        out[0, :split] = total[:split].astype(BF16)
        out[0, split:] = (total[split:] + far_ref[i].astype(F32)).astype(BF16)


def per_device(query_rows, key_rows, value_rows, out_grad, assistant, turn_first):
    token_count = query_rows.shape[1]
    width = key_rows.shape[2]
    head_count = query_rows.shape[2] // width
    block_count = token_count // BLK
    far_rows = block_count // 2 * BLK
    reach_rows = token_count + far_rows
    slot_count = (block_count + 1) // 2
    columns = head_count * BLK
    sizes = (block_count, slot_count, head_count, width, 1.0 / math.sqrt(width))
    any_spec = pl.BlockSpec(memory_space=pl.ANY)
    smem_spec = pl.BlockSpec(memory_space=pltpu.SMEM)
    vmem_spec = pl.BlockSpec(memory_space=pltpu.VMEM)

    def call(kernel, inputs, in_specs, outputs, out_specs, scratch, limit, macs, aliases={}):
        return pl.pallas_call(
            kernel,
            out_shape=outputs,
            in_specs=in_specs,
            out_specs=out_specs,
            scratch_shapes=scratch,
            input_output_aliases=aliases,
            compiler_params=pltpu.CompilerParams(vmem_limit_bytes=limit * MIB),
            cost_estimate=pl.CostEstimate(flops=2 * macs, bytes_accessed=2 * MIB, transcendentals=0),
        )(*inputs)

    pair = columns * BLK * width
    near, far, assistant, turn_first = call(
        pack_kernel,
        tuple(hbm(a) for a in (key_rows, value_rows, assistant, turn_first)),
        [any_spec] * 4,
        (
            pltpu.VMEM((2, token_count, width), BF16),
            pltpu.VMEM((2, far_rows, width), BF16),
            pltpu.SMEM(assistant.shape, jnp.int32),
            pltpu.SMEM(turn_first.shape, jnp.int32),
        ),
        [vmem_spec] * 2 + [smem_spec] * 2,
        [pltpu.SemaphoreType.DMA((6,))],
        8,
        BLK,
    )
    assistant, turn_first = smem(assistant), smem(turn_first)
    slot_rows = (slot_count, columns, width)
    stat_rows = (slot_count, SUB, columns)
    local_rows = (slot_count, token_count, columns)
    local_shapes = (
        pltpu.VMEM(slot_rows, BF16),
        pltpu.VMEM(slot_rows, BF16),
        pltpu.VMEM(local_rows, F32),
        pltpu.VMEM(local_rows, F32),
        pltpu.VMEM(stat_rows, F32),
        pltpu.VMEM(stat_rows, F32),
    )
    local_inputs = (assistant, turn_first, hbm(query_rows), hbm(out_grad), vmem(near))
    local_specs = [smem_spec] * 2 + [any_spec] * 2 + [vmem_spec]
    local_sems = [pltpu.SemaphoreType.DMA((slot_count, 2, head_count))]
    local_state = call(
        lambda *refs: local_kernel(sizes, True, *refs),
        local_inputs,
        local_specs,
        local_shapes,
        [vmem_spec] * 6,
        local_sems,
        16,
        10 * pair,
    )
    near, far, local_state = lax.optimization_barrier((near, far, local_state))
    near_in = shifted(near, "ctx", 1)
    far_in = shifted(far, "ctx", 2)
    local_state = call(
        lambda *refs: local_kernel(sizes, False, *refs),
        local_inputs + tuple(vmem(a) for a in local_state),
        local_specs + [vmem_spec] * 6,
        local_shapes,
        [vmem_spec] * 6,
        local_sems,
        16,
        10 * pair,
        {5 + i: i for i in range(6)},
    )
    query_slots, grad_slots, weights, prob_grad, sums, dots = local_state
    weight_near, prob_near, sum_near, dot_near = call(
        lambda *refs: near_kernel(sizes, *refs),
        (assistant, turn_first) + tuple(vmem(a) for a in (query_slots, grad_slots, near_in)),
        [smem_spec] * 2 + [vmem_spec] * 3,
        local_shapes[2:],
        [vmem_spec] * 4,
        [],
        16,
        10 * pair,
    )
    near_grad, far_grad, score_grad, inverse, delta = call(
        lambda *refs: remote_kernel(sizes, *refs),
        (assistant, turn_first)
        + tuple(
            vmem(a)
            for a in (query_slots, grad_slots, sums, dots, sum_near, dot_near, weight_near, prob_near,
                      far_in)
        ),
        [smem_spec] * 2 + [vmem_spec] * 9,
        (
            pltpu.VMEM((2, token_count, width), BF16),
            pltpu.VMEM((2, far_rows, width), BF16),
            pltpu.VMEM((slot_count, reach_rows, columns), BF16),
            pltpu.VMEM(stat_rows, F32),
            pltpu.VMEM(stat_rows, F32),
        ),
        [vmem_spec] * 5,
        [
            pltpu.VMEM((slot_count, far_rows, columns), F32),
            pltpu.VMEM((slot_count, far_rows, columns), F32),
            pltpu.VMEM(stat_rows, F32),
            pltpu.VMEM(stat_rows, F32),
            pltpu.VMEM((token_count, columns), BF16),
            pltpu.VMEM((reach_rows, width), F32),
            pltpu.VMEM((reach_rows, width), F32),
        ],
        20,
        14 * pair,
    )
    near_back = shifted(near_grad, "ctx", -1)
    far_back = shifted(far_grad, "ctx", -2)
    query_grad, key_acc, value_acc = call(
        lambda *refs: finish_kernel(sizes, *refs),
        (assistant, turn_first)
        + tuple(
            vmem(a)
            for a in (query_slots, grad_slots, weights, prob_grad, score_grad, inverse, delta, near,
                      near_in, far_in)
        ),
        [smem_spec] * 2 + [vmem_spec] * 10,
        (
            jax.ShapeDtypeStruct(query_rows.shape, BF16),
            pltpu.VMEM((token_count, width), F32),
            pltpu.VMEM((token_count, width), F32),
        ),
        [vmem_spec] * 3,
        [
            pltpu.VMEM((slot_count, token_count, columns), BF16),
            pltpu.VMEM((token_count, columns), BF16),
            pltpu.VMEM((BLK, columns), F32),
        ],
        16,
        25 * pair,
    )
    key_grad, value_grad = call(
        total_kernel,
        tuple(vmem(a) for a in (key_acc, value_acc, near_back, far_back)),
        [vmem_spec] * 4,
        (
            jax.ShapeDtypeStruct(key_rows.shape, BF16),
            jax.ShapeDtypeStruct(value_rows.shape, BF16),
        ),
        [vmem_spec] * 2,
        [],
        8,
        BLK,
    )
    return (query_grad, key_grad, value_grad)


def solution(mesh):
    return jax.shard_map(
        per_device,
        mesh=mesh,
        in_specs=(
            P("dp", "ctx", "tp"),
            P("dp", "ctx", "tp"),
            P("dp", "ctx", "tp"),
            P("dp", "ctx", "tp"),
            P("dp", None),
            P("dp", None),
        ),
        out_specs=(P("dp", "ctx", "tp"), P("dp", "ctx", "tp"), P("dp", "ctx", "tp")),
        check_vma=False,
    )
```

```python
import math

import jax
import jax.numpy as jnp
from jax import lax
from jax.experimental import pallas as pl
from jax.experimental.pallas import tpu as pltpu
from jax.sharding import PartitionSpec as P

BLK = 128
SUB = 8
CHUNK = 256
F32 = jnp.float32
BF16 = jnp.bfloat16
MIB = 1 << 20


def shifted(block, axis, distance):
    devices = range(lax.axis_size(axis))
    route = [(i - distance, i) for i in devices if i - distance in devices]
    return lax.ppermute(block, axis, route)


def vmem(array):
    return pltpu.with_memory_space_constraint(array, pltpu.VMEM)


def smem(array):
    return pltpu.with_memory_space_constraint(array, pltpu.SMEM)


def hbm(array):
    return pltpu.with_memory_space_constraint(array, pltpu.HBM)


def nt_dot(left, right):
    return lax.dot_general(left, right, (((1,), (1,)), ((), ())), preferred_element_type=F32)


def nn_dot(left, right):
    return lax.dot_general(left, right, (((1,), (0,)), ((), ())), preferred_element_type=F32)


def fold(tile):
    return jnp.sum(tile.reshape(tile.shape[0] // SUB, SUB, tile.shape[1]), axis=0)


def slots_of(assistant, turn_first, base, block_count, slot_count):
    found = jnp.int32(0)
    blocks = [jnp.int32(0)] * slot_count
    starts = [jnp.int32(0)] * slot_count
    for i in range(block_count):
        mark = assistant[0, base + i]
        start = turn_first[0, base + i] - base
        for s in range(slot_count):
            here = (mark == 1) & (found == s)
            blocks[s] = jnp.where(here, i, blocks[s])
            starts[s] = jnp.where(here, start, starts[s])
        found = found + jnp.where(mark == 1, 1, 0)
    return [(blocks[s], found > s, starts[s]) for s in range(slot_count)]


def pack_kernel(block_count, key_ref, value_ref, assistant_ref, turn_ref, *rest):
    packs, (assistant, turn_first, need_ref, sem) = rest[:block_count], rest[block_count:]
    token_count = key_ref.shape[1]
    marks = [
        pltpu.make_async_copy(assistant_ref, assistant, sem.at[0]),
        pltpu.make_async_copy(turn_ref, turn_first, sem.at[1]),
    ]
    copies = []
    for pack in reversed(packs):
        rows = pack.shape[1]
        for i, source in enumerate((key_ref, value_ref)):
            copies.append(
                pltpu.make_async_copy(
                    source.at[0, pl.ds(token_count - rows, rows)], pack.at[i], sem.at[2 + len(copies)]
                )
            )
    for copy in marks + copies:
        copy.start()
    for copy in marks:
        copy.wait()
    need = jnp.int32(1)
    for i in range(block_count, assistant.shape[1]):
        behind = i // block_count * block_count - turn_first[0, i]
        need = jnp.maximum(need, jnp.where(assistant[0, i] == 1, behind, 1))
    need_ref[0] = jnp.minimum(need - 1, block_count)
    for copy in copies:
        copy.wait()


def score_pass(key_tile, value_tile, query_ref, grad_ref, slot, keep, weight_ref, prob_ref, at, sum_ref,
               dot_ref, scale):
    columns = query_ref.shape[1]
    height = key_tile.shape[0]
    for c in range(0, columns, CHUNK):
        span = slice(c, c + CHUNK)
        scores = nt_dot(key_tile, query_ref[slot, span, :])
        prob_grad = nt_dot(value_tile, grad_ref[slot, span, :])
        weights = jnp.exp2(scores * scale)
        if keep is not None:
            wide = jnp.concatenate([keep] * (CHUNK // BLK), axis=1)
            last = jnp.where(wide, weights[height - BLK:], 0.0)
            weights = jnp.concatenate([weights[:height - BLK], last], axis=0) if height > BLK else last
        weight_ref[at + (span,)] = weights
        prob_ref[at + (span,)] = prob_grad
        sum_ref[slot, :, span] = fold(weights)
        dot_ref[slot, :, span] = fold(weights * prob_grad)


def grad_pass(weight_ref, prob_ref, at, query_ref, grad_ref, slot, inverse_ref, delta_ref, low_ref,
              score_ref, score_rows, key_acc, value_acc, acc_rows):
    columns = query_ref.shape[1]
    height = acc_rows.size
    for c in range(0, columns, CHUNK):
        span = slice(c, c + CHUNK)
        shape = (height // SUB, SUB, CHUNK)
        attention = weight_ref[at + (span,)].reshape(shape) * inverse_ref[slot, :, span][None]
        lifted = prob_ref[at + (span,)].reshape(shape) - delta_ref[slot, :, span][None]
        score_grad = (attention * lifted).reshape(height, CHUNK)
        low_ref[:height, span] = attention.reshape(height, CHUNK).astype(BF16)
        score_ref[slot, score_rows, span] = score_grad.astype(BF16)
    value_acc[acc_rows, :] += nn_dot(low_ref[:height], grad_ref[slot])
    key_acc[acc_rows, :] += nn_dot(score_ref[slot, score_rows, :], query_ref[slot])


def block_rows(index, count=1):
    return pl.ds(pl.multiple_of(index * BLK, BLK), count * BLK)


def pick(values, s):
    chosen = values[0]
    for i in range(1, len(values)):
        chosen = jnp.where(s == i, values[i], chosen)
    return chosen


def over_slots(slots, body):
    def step(s, carry):
        block, start = (pick([slot[i] for slot in slots], s) for i in (0, 2))

        @pl.when(pick([jnp.where(slot[1], 1, 0) for slot in slots], s) == 1)
        def _():
            body(s, block, start)

        return carry

    lax.fori_loop(0, len(slots), step, 0)


def local_kernel(sizes, early, assistant, turn_first, query_hbm, grad_hbm, kv_ref, *rest):
    query_ref, grad_ref, weight_ref, prob_ref, sum_ref, dot_ref, sem = rest[-7:]
    block_count, slot_count, head_count, width, scale = sizes
    rank = lax.axis_index("ctx")
    first_half = rank * 2 < lax.axis_size("ctx")

    def run():
        slots = slots_of(assistant, turn_first, rank * block_count, block_count, slot_count)

        def copies(s, block):
            for i, (source, target) in enumerate(((query_hbm, query_ref), (grad_hbm, grad_ref))):
                for h in range(head_count):
                    yield pltpu.make_async_copy(
                        source.at[0, block_rows(block), pl.ds(h * width, width)],
                        target.at[s, pl.ds(h * BLK, BLK)],
                        sem.at[s, i, h],
                    )

        for s, (block, live, start) in enumerate(slots):
            @pl.when(live)
            def _():
                for copy in copies(s, block):
                    copy.start()
        keep = lax.broadcasted_iota(jnp.int32, (BLK, BLK), 0) <= lax.broadcasted_iota(
            jnp.int32, (BLK, BLK), 1
        )

        def body(s, block, start):
            for copy in copies(s, block):
                copy.wait()
            low = jnp.maximum(start, 0)
            for count in range(1, block_count + 1):
                @pl.when(block + 1 - low == count)
                def _():
                    rows = block_rows(low, count)
                    score_pass(kv_ref[0, rows, :], kv_ref[1, rows, :], query_ref, grad_ref, s, keep,
                               weight_ref, prob_ref, (s, rows), sum_ref, dot_ref,
                               scale * math.log2(math.e))

        over_slots(slots, body)

    pl.when(first_half if early else jnp.logical_not(first_half))(run)


def near_kernel(sizes, assistant, turn_first, query_ref, grad_ref, near_ref, weight_ref, prob_ref, sum_ref,
                dot_ref):
    block_count, slot_count, head_count, width, scale = sizes
    base = lax.axis_index("ctx") * block_count
    slots = slots_of(assistant, turn_first, base, block_count, slot_count)
    sent = near_ref.shape[1] // BLK
    sum_ref[...] = jnp.zeros_like(sum_ref)
    dot_ref[...] = jnp.zeros_like(dot_ref)

    def body(s, block, start):
        for count in range(1, sent + 1):
            last = start <= -count if count == sent else start == -count

            @pl.when(last)
            def _():
                rows = pl.ds((sent - count) * BLK, count * BLK)
                score_pass(near_ref[0, rows, :], near_ref[1, rows, :], query_ref, grad_ref, s, None,
                           weight_ref, prob_ref, (s, rows), sum_ref, dot_ref, scale * math.log2(math.e))

    over_slots(slots, body)


def remote_kernel(sizes, assistant, turn_first, query_ref, grad_ref, sum_local, dot_local, sum_near,
                  dot_near, weight_near, prob_near, *rest):
    far_ref = far_out = sum_far = dot_far = None
    if len(rest) > 7:
        far_ref, far_out, weight_far, prob_far, sum_far, dot_far = rest[:1] + rest[-5:]
        rest = rest[1:-5]
    near_out, score_ref, inverse_ref, delta_ref, low_ref, key_acc, value_acc = rest
    block_count, slot_count, head_count, width, scale = sizes
    base = lax.axis_index("ctx") * block_count
    slots = slots_of(assistant, turn_first, base, block_count, slot_count)
    far_blocks = 0 if far_ref is None else far_ref.shape[1] // BLK
    far_rows = far_blocks * BLK
    sent = near_out.shape[1] // BLK
    key_acc[...] = jnp.zeros_like(key_acc)
    value_acc[...] = jnp.zeros_like(value_acc)
    if far_blocks:
        sum_far[...] = jnp.zeros_like(sum_far)
        dot_far[...] = jnp.zeros_like(dot_far)

    def body(s, block, start):
        sums = sum_local[s] + sum_near[s]
        dots = dot_local[s] + dot_near[s]
        for count in range(1, far_blocks + 1):
            @pl.when(start == -block_count - count)
            def _():
                rows = pl.ds((far_blocks - count) * BLK, count * BLK)
                score_pass(far_ref[0, rows, :], far_ref[1, rows, :], query_ref, grad_ref, s, None,
                           weight_far, prob_far, (s, rows), sum_far, dot_far, scale * math.log2(math.e))

        if far_blocks:
            sums = sums + sum_far[s]
            dots = dots + dot_far[s]
        inverse = 1.0 / jnp.sum(sums, axis=0, keepdims=True)
        delta = jnp.sum(dots, axis=0, keepdims=True) * inverse
        inverse_ref[s] = jnp.broadcast_to(inverse, inverse_ref.shape[1:])
        delta_ref[s] = jnp.broadcast_to(delta, delta_ref.shape[1:])
        for count in range(1, far_blocks + 1):
            @pl.when(start == -block_count - count)
            def _():
                rows = pl.ds((far_blocks - count) * BLK, count * BLK)
                grad_pass(weight_far, prob_far, (s, rows), query_ref, grad_ref, s, inverse_ref, delta_ref,
                          low_ref, score_ref, rows, key_acc, value_acc, rows)

        for count in range(1, sent + 1):
            last = start <= -count if count == sent else start == -count

            @pl.when(last)
            def _():
                rows = pl.ds((sent - count) * BLK, count * BLK)
                window = pl.ds(far_rows + (sent - count) * BLK, count * BLK)
                grad_pass(weight_near, prob_near, (s, rows), query_ref, grad_ref, s, inverse_ref,
                          delta_ref, low_ref, score_ref, window, key_acc, value_acc, window)

    over_slots(slots, body)
    key_low = (key_acc[...] * scale).astype(BF16)
    value_low = value_acc[...].astype(BF16)
    if far_blocks:
        far_out[0] = key_low[:far_rows]
        far_out[1] = value_low[:far_rows]
    near_out[0] = key_low[far_rows:]
    near_out[1] = value_low[far_rows:]


def finish_kernel(sizes, assistant, turn_first, query_ref, grad_ref, weight_ref, prob_ref, score_in,
                  inverse_ref, delta_ref, kv_ref, near_ref, *rest):
    far_ref = rest[0] if len(rest) > 6 else None
    query_out, key_acc, value_acc, score_ref, low_ref, query_acc = rest[-6:]
    block_count, slot_count, head_count, width, scale = sizes
    base = lax.axis_index("ctx") * block_count
    slots = slots_of(assistant, turn_first, base, block_count, slot_count)
    far_blocks = 0 if far_ref is None else far_ref.shape[1] // BLK
    reach = near_ref.shape[1] // BLK + far_blocks
    key_acc[...] = jnp.zeros_like(key_acc)
    value_acc[...] = jnp.zeros_like(value_acc)
    query_out[...] = jnp.zeros_like(query_out)

    def body(s, block, start):
        query_acc[...] = jnp.zeros_like(query_acc)

        def add_query(key_tile, score_source, rows):
            turned = key_tile.T
            for c in range(0, query_acc.shape[1], CHUNK):
                span = slice(c, c + CHUNK)
                query_acc[:, span] += nn_dot(turned, score_source[s, rows, span])

        def far_step(k, carry):
            add_query(far_ref[0, block_rows(k), :], score_in, block_rows(k))
            return carry

        def near_step(k, carry):
            add_query(near_ref[0, block_rows(k - far_blocks), :], score_in, block_rows(k))
            return carry

        first = jnp.minimum(start + reach, reach)
        if far_blocks:
            lax.fori_loop(first, far_blocks, far_step, 0)
        lax.fori_loop(jnp.maximum(first, far_blocks), reach, near_step, 0)
        low = jnp.maximum(start, 0)
        for count in range(1, block_count + 1):
            @pl.when(block + 1 - low == count)
            def _():
                rows = block_rows(low, count)
                grad_pass(weight_ref, prob_ref, (s, rows), query_ref, grad_ref, s, inverse_ref, delta_ref,
                          low_ref, score_ref, rows, key_acc, value_acc, rows)
                add_query(kv_ref[0, rows, :], score_ref, rows)

        for h in range(head_count):
            turned = (query_acc[:, h * BLK:(h + 1) * BLK] * scale).T
            query_out[0, block_rows(block), h * width:(h + 1) * width] = turned.astype(BF16)

    over_slots(slots, body)
    key_acc[...] = key_acc[...] * scale


def total_kernel(*refs):
    key_acc, value_acc, near_ref = refs[:3]
    key_out, value_out = refs[-2:]
    token_count = key_acc.shape[0]
    for i, (acc, out) in enumerate(((key_acc, key_out), (value_acc, value_out))):
        cuts = sorted({0, token_count} | {token_count - ref.shape[1] for ref in refs[2:-2]})
        for low, high in zip(cuts, cuts[1:]):
            total = acc[low:high, :]
            for ref in refs[2:-2]:
                first = token_count - ref.shape[1]
                if first <= low:
                    total = total + ref[i, low - first:high - first, :].astype(F32)
            out[0, low:high, :] = total.astype(BF16)


def call(kernel, inputs, in_specs, outputs, out_specs, scratch, limit, macs, aliases={}):
    return pl.pallas_call(
        kernel,
        out_shape=outputs,
        in_specs=in_specs,
        out_specs=out_specs,
        scratch_shapes=scratch,
        input_output_aliases=aliases,
        compiler_params=pltpu.CompilerParams(vmem_limit_bytes=limit * MIB),
        cost_estimate=pl.CostEstimate(flops=2 * macs, bytes_accessed=2 * MIB, transcendentals=0),
    )(*inputs)


ANY_SPEC = pl.BlockSpec(memory_space=pl.ANY)
SMEM_SPEC = pl.BlockSpec(memory_space=pltpu.SMEM)
VMEM_SPEC = pl.BlockSpec(memory_space=pltpu.VMEM)


def gradients(sizes, with_far, near, far, own, assistant, turn_first, query_rows, out_grad):
    block_count, slot_count, head_count, width, scale = sizes
    token_count = block_count * BLK
    columns = head_count * BLK
    sent_rows = near.shape[1]
    far_rows = far.shape[1] if with_far else 0
    reach_rows = sent_rows + far_rows
    pair = columns * BLK * width
    assistant, turn_first = smem(assistant), smem(turn_first)
    slot_rows = (slot_count, columns, width)
    stat_rows = (slot_count, SUB, columns)

    def score_shapes(rows):
        return (
            pltpu.VMEM((slot_count, rows, columns), F32),
            pltpu.VMEM((slot_count, rows, columns), F32),
            pltpu.VMEM(stat_rows, F32),
            pltpu.VMEM(stat_rows, F32),
        )

    local_shapes = (pltpu.VMEM(slot_rows, BF16), pltpu.VMEM(slot_rows, BF16)) + score_shapes(token_count)
    local_inputs = (assistant, turn_first, hbm(query_rows), hbm(out_grad), vmem(own))
    local_specs = [SMEM_SPEC] * 2 + [ANY_SPEC] * 2 + [VMEM_SPEC]
    local_sems = [pltpu.SemaphoreType.DMA((slot_count, 2, head_count))]
    local_state = call(
        lambda *refs: local_kernel(sizes, True, *refs),
        local_inputs,
        local_specs,
        local_shapes,
        [VMEM_SPEC] * 6,
        local_sems,
        16,
        10 * pair,
    )
    near, far, local_state = lax.optimization_barrier((near, far, local_state))
    near_in = shifted(near, "ctx", 1)
    far_in = (shifted(far, "ctx", 2),) if with_far else ()
    local_state = call(
        lambda *refs: local_kernel(sizes, False, *refs),
        local_inputs + tuple(vmem(a) for a in local_state),
        local_specs + [VMEM_SPEC] * 6,
        local_shapes,
        [VMEM_SPEC] * 6,
        local_sems,
        16,
        10 * pair,
        {5 + i: i for i in range(6)},
    )
    query_slots, grad_slots, weights, prob_grad, sums, dots = local_state
    weight_near, prob_near, sum_near, dot_near = call(
        lambda *refs: near_kernel(sizes, *refs),
        (assistant, turn_first) + tuple(vmem(a) for a in (query_slots, grad_slots, near_in)),
        [SMEM_SPEC] * 2 + [VMEM_SPEC] * 3,
        score_shapes(sent_rows),
        [VMEM_SPEC] * 4,
        [],
        16,
        10 * pair,
    )
    outputs = [
        pltpu.VMEM((2, sent_rows, width), BF16),
        pltpu.VMEM((slot_count, reach_rows, columns), BF16),
        pltpu.VMEM(stat_rows, F32),
        pltpu.VMEM(stat_rows, F32),
    ]
    scratch = [
        pltpu.VMEM((token_count, columns), BF16),
        pltpu.VMEM((reach_rows, width), F32),
        pltpu.VMEM((reach_rows, width), F32),
    ]
    if with_far:
        outputs.append(pltpu.VMEM((2, far_rows, width), BF16))
        scratch.extend(score_shapes(far_rows))

    def remote(*refs):
        if with_far:
            fixed, (near_out, score_ref, inverse_ref, delta_ref, far_out), scratch_refs = (
                refs[:11], refs[11:16], refs[16:]
            )
            refs = fixed + (near_out, score_ref, inverse_ref, delta_ref) + scratch_refs[:3] + (
                (far_out,) + scratch_refs[3:]
            )
        return remote_kernel(sizes, *refs)

    near_grad, score_grad, inverse, delta, *far_grad = call(
        remote,
        (assistant, turn_first)
        + tuple(
            vmem(a)
            for a in (query_slots, grad_slots, sums, dots, sum_near, dot_near, weight_near, prob_near)
            + far_in
        ),
        [SMEM_SPEC] * 2 + [VMEM_SPEC] * (8 + len(far_in)),
        tuple(outputs),
        [VMEM_SPEC] * len(outputs),
        scratch,
        20,
        14 * pair,
    )
    returned = [shifted(a, "ctx", -2) for a in far_grad] + [shifted(near_grad, "ctx", -1)]
    query_grad, key_acc, value_acc = call(
        lambda *refs: finish_kernel(sizes, *refs),
        (assistant, turn_first)
        + tuple(
            vmem(a)
            for a in (query_slots, grad_slots, weights, prob_grad, score_grad, inverse, delta, own,
                      near_in) + far_in
        ),
        [SMEM_SPEC] * 2 + [VMEM_SPEC] * (9 + len(far_in)),
        (
            jax.ShapeDtypeStruct(query_rows.shape, BF16),
            pltpu.VMEM((token_count, width), F32),
            pltpu.VMEM((token_count, width), F32),
        ),
        [VMEM_SPEC] * 3,
        [
            pltpu.VMEM((slot_count, token_count, columns), BF16),
            pltpu.VMEM((token_count, columns), BF16),
            pltpu.VMEM((BLK, columns), F32),
        ],
        16,
        25 * pair,
    )
    key_grad, value_grad = call(
        total_kernel,
        tuple(vmem(a) for a in [key_acc, value_acc] + returned[::-1]),
        [VMEM_SPEC] * (2 + len(returned)),
        (jax.ShapeDtypeStruct((1, token_count, width), BF16),) * 2,
        [VMEM_SPEC] * 2,
        [],
        8,
        BLK,
    )
    return (query_grad, key_grad, value_grad)


def per_device(query_rows, key_rows, value_rows, out_grad, assistant, turn_first):
    token_count = query_rows.shape[1]
    width = key_rows.shape[2]
    head_count = query_rows.shape[2] // width
    block_count = token_count // BLK
    far_blocks = block_count // 2
    slot_count = (block_count + 1) // 2
    sizes = (block_count, slot_count, head_count, width, 1.0 / math.sqrt(width))
    *packs, assistant, turn_first, need = call(
        lambda *refs: pack_kernel(block_count, *refs),
        tuple(hbm(a) for a in (key_rows, value_rows, assistant, turn_first)),
        [ANY_SPEC] * 4,
        tuple(pltpu.VMEM((2, (i + 1) * BLK, width), BF16) for i in range(block_count))
        + (
            pltpu.SMEM(assistant.shape, jnp.int32),
            pltpu.SMEM(turn_first.shape, jnp.int32),
            pltpu.SMEM((1,), jnp.int32),
        ),
        [VMEM_SPEC] * block_count + [SMEM_SPEC] * 3,
        [pltpu.SemaphoreType.DMA((2 + 2 * block_count,))],
        8,
        BLK,
    )

    def branch(sent, with_far):
        def run(packs, *rest):
            return gradients(sizes, with_far, packs[sent - 1], packs[far_blocks - 1], packs[-1], *rest)

        return run

    branches = [branch(sent, False) for sent in range(1, block_count + 1)] + [branch(block_count, True)]
    return lax.switch(need[0], branches, packs, assistant, turn_first, query_rows, out_grad)


def solution(mesh):
    return jax.shard_map(
        per_device,
        mesh=mesh,
        in_specs=(
            P("dp", "ctx", "tp"),
            P("dp", "ctx", "tp"),
            P("dp", "ctx", "tp"),
            P("dp", "ctx", "tp"),
            P("dp", None),
            P("dp", None),
        ),
        out_specs=(P("dp", "ctx", "tp"), P("dp", "ctx", "tp"), P("dp", "ctx", "tp")),
        check_vma=False,
    )
```

```python
import math

import jax
import jax.numpy as jnp
from jax import lax
from jax.experimental import pallas as pl
from jax.experimental.pallas import tpu as pltpu
from jax.sharding import PartitionSpec as P

BLK = 128
SUB = 8
CHUNK = 256
F32 = jnp.float32
BF16 = jnp.bfloat16
MIB = 1 << 20


def shifted(block, axis, distance):
    devices = range(lax.axis_size(axis))
    route = [(i - distance, i) for i in devices if i - distance in devices]
    return lax.ppermute(block, axis, route)


def pair_shift(block, axis, distance, parity):
    pairs = [(i - 1, i) for i in range(1, lax.axis_size(axis)) if i % 2 == parity]
    return lax.ppermute(block, axis, pairs if distance == 1 else [pair[::-1] for pair in pairs])


def vmem(array):
    return pltpu.with_memory_space_constraint(array, pltpu.VMEM)


def smem(array):
    return pltpu.with_memory_space_constraint(array, pltpu.SMEM)


def hbm(array):
    return pltpu.with_memory_space_constraint(array, pltpu.HBM)


def nt_dot(left, right):
    return lax.dot_general(left, right, (((1,), (1,)), ((), ())), preferred_element_type=F32)


def nn_dot(left, right):
    return lax.dot_general(left, right, (((1,), (0,)), ((), ())), preferred_element_type=F32)


def fold(tile):
    return jnp.sum(tile.reshape(tile.shape[0] // SUB, SUB, tile.shape[1]), axis=0)


def slots_of(assistant, turn_first, base, block_count, slot_count):
    found = jnp.int32(0)
    blocks = [jnp.int32(0)] * slot_count
    starts = [jnp.int32(0)] * slot_count
    for i in range(block_count):
        mark = assistant[0, base + i]
        start = turn_first[0, base + i] - base
        for s in range(slot_count):
            here = (mark == 1) & (found == s)
            blocks[s] = jnp.where(here, i, blocks[s])
            starts[s] = jnp.where(here, start, starts[s])
        found = found + jnp.where(mark == 1, 1, 0)
    return [(blocks[s], found > s, starts[s]) for s in range(slot_count)]


def pack_kernel(block_count, key_ref, value_ref, assistant_ref, turn_ref, last_ref, all_ref, assistant,
                turn_first, need_ref, sem):
    token_count = key_ref.shape[1]
    marks = [
        pltpu.make_async_copy(assistant_ref, assistant, sem.at[0]),
        pltpu.make_async_copy(turn_ref, turn_first, sem.at[1]),
    ]
    copies = []
    for pack in (all_ref, last_ref):
        rows = pack.shape[1]
        for i, source in enumerate((key_ref, value_ref)):
            copies.append(
                pltpu.make_async_copy(
                    source.at[0, pl.ds(token_count - rows, rows)], pack.at[i], sem.at[2 + len(copies)]
                )
            )
    for copy in marks + copies:
        copy.start()
    for copy in marks:
        copy.wait()
    outer = far = jnp.int32(0)
    for i in range(block_count, assistant.shape[1]):
        device = i // block_count
        behind = jnp.where(assistant[0, i] == 1, device * block_count - turn_first[0, i], 0)
        far = jnp.where(behind > block_count, 1, far)
        if device % 2 == 0:
            outer = jnp.maximum(outer, behind)
    need_ref[0] = jnp.where((outer > 0) | (far > 0), 1 + jnp.where(outer > 1, 1, 0) + 2 * far, 0)
    for copy in copies:
        copy.wait()


def score_pass(key_tile, value_tile, query_ref, grad_ref, slot, keep, weight_ref, prob_ref, at, sum_ref,
               dot_ref, scale):
    columns = query_ref.shape[1]
    height = key_tile.shape[0]
    for c in range(0, columns, CHUNK):
        span = slice(c, c + CHUNK)
        scores = nt_dot(key_tile, query_ref[slot, span, :])
        prob_grad = nt_dot(value_tile, grad_ref[slot, span, :])
        weights = jnp.exp2(scores * scale)
        if keep is not None:
            wide = jnp.concatenate([keep] * (CHUNK // BLK), axis=1)
            last = jnp.where(wide, weights[height - BLK:], 0.0)
            weights = jnp.concatenate([weights[:height - BLK], last], axis=0) if height > BLK else last
        weight_ref[at + (span,)] = weights
        prob_ref[at + (span,)] = prob_grad
        sum_ref[slot, :, span] = fold(weights)
        dot_ref[slot, :, span] = fold(weights * prob_grad)


def grad_pass(weight_ref, prob_ref, at, query_ref, grad_ref, slot, inverse_ref, delta_ref, low_ref,
              score_ref, score_rows, key_acc, value_acc, acc_rows):
    columns = query_ref.shape[1]
    height = acc_rows.size
    for c in range(0, columns, CHUNK):
        span = slice(c, c + CHUNK)
        shape = (height // SUB, SUB, CHUNK)
        attention = weight_ref[at + (span,)].reshape(shape) * inverse_ref[slot, :, span][None]
        lifted = prob_ref[at + (span,)].reshape(shape) - delta_ref[slot, :, span][None]
        score_grad = (attention * lifted).reshape(height, CHUNK)
        low_ref[:height, span] = attention.reshape(height, CHUNK).astype(BF16)
        score_ref[slot, score_rows, span] = score_grad.astype(BF16)
    value_acc[acc_rows, :] += nn_dot(low_ref[:height], grad_ref[slot])
    key_acc[acc_rows, :] += nn_dot(score_ref[slot, score_rows, :], query_ref[slot])


def block_rows(index, count=1):
    return pl.ds(pl.multiple_of(index * BLK, BLK), count * BLK)


def pick(values, s):
    chosen = values[0]
    for i in range(1, len(values)):
        chosen = jnp.where(s == i, values[i], chosen)
    return chosen


def over_slots(slots, body):
    def step(s, carry):
        block, start = (pick([slot[i] for slot in slots], s) for i in (0, 2))

        @pl.when(pick([jnp.where(slot[1], 1, 0) for slot in slots], s) == 1)
        def _():
            body(s, block, start)

        return carry

    lax.fori_loop(0, len(slots), step, 0)


def local_kernel(sizes, halves, assistant, turn_first, query_hbm, grad_hbm, kv_ref, *rest):
    query_ref, grad_ref, weight_ref, prob_ref, sum_ref, dot_ref, sem = rest[-7:]
    block_count, slot_count, head_count, width, scale = sizes
    rank = lax.axis_index("ctx")
    first_half = rank * 2 < lax.axis_size("ctx")

    def run():
        slots = slots_of(assistant, turn_first, rank * block_count, block_count, slot_count)

        def copies(s, block):
            for i, (source, target) in enumerate(((query_hbm, query_ref), (grad_hbm, grad_ref))):
                for h in range(head_count):
                    yield pltpu.make_async_copy(
                        source.at[0, block_rows(block), pl.ds(h * width, width)],
                        target.at[s, pl.ds(h * BLK, BLK)],
                        sem.at[s, i, h],
                    )

        for s, (block, live, start) in enumerate(slots):
            @pl.when(live)
            def _():
                for copy in copies(s, block):
                    copy.start()
        keep = lax.broadcasted_iota(jnp.int32, (BLK, BLK), 0) <= lax.broadcasted_iota(
            jnp.int32, (BLK, BLK), 1
        )

        def body(s, block, start):
            for copy in copies(s, block):
                copy.wait()
            low = jnp.maximum(start, 0)
            for count in range(1, block_count + 1):
                @pl.when(block + 1 - low == count)
                def _():
                    rows = block_rows(low, count)
                    score_pass(kv_ref[0, rows, :], kv_ref[1, rows, :], query_ref, grad_ref, s, keep,
                               weight_ref, prob_ref, (s, rows), sum_ref, dot_ref,
                               scale * math.log2(math.e))

        over_slots(slots, body)

    if halves == "both":
        run()
    else:
        pl.when(first_half if halves == "first" else jnp.logical_not(first_half))(run)


def near_kernel(sizes, parity, assistant, turn_first, query_ref, grad_ref, source, *rest):
    weight_ref, prob_ref, sum_ref, dot_ref, window = rest[-5:]
    block_count, slot_count, head_count, width, scale = sizes
    rank = lax.axis_index("ctx")
    slots = slots_of(assistant, turn_first, rank * block_count, block_count, slot_count)
    top = window.shape[0] // BLK
    sent = source.shape[1] // BLK
    if len(rest) == 5:
        sum_ref[...] = jnp.zeros_like(sum_ref)
        dot_ref[...] = jnp.zeros_like(dot_ref)

    def body(s, block, start):
        for count in range(1, sent + 1):
            last = start <= -count if count == sent else start == -count

            @pl.when(last)
            def _():
                taken = pl.ds((sent - count) * BLK, count * BLK)
                rows = pl.ds((top - count) * BLK, count * BLK)
                score_pass(source[0, taken, :], source[1, taken, :], query_ref, grad_ref, s, None,
                           weight_ref, prob_ref, (s, rows), sum_ref, dot_ref, scale * math.log2(math.e))

    @pl.when(lax.rem(rank, 2) == parity)
    def _():
        window[window.shape[0] - source.shape[1]:, :] = source[0]
        over_slots(slots, body)


def remote_kernel(sizes, with_outer, assistant, turn_first, query_ref, grad_ref, sum_local, dot_local,
                  sum_near, dot_near, weight_near, prob_near, *rest):
    rest = list(rest)
    block_count, slot_count, head_count, width, scale = sizes
    low_ref, key_acc, value_acc = rest[-3:]
    far_ref = far_out = sum_far = dot_far = outer_out = None
    if len(rest) > 7 + with_outer:
        far_ref, far_out = rest.pop(0), rest.pop(0)
        weight_far, prob_far, sum_far, dot_far = rest[-7:-3]
    inner_out, score_ref, inverse_ref, delta_ref = rest[:4]
    if with_outer:
        outer_out = rest[4]
    rank = lax.axis_index("ctx")
    slots = slots_of(assistant, turn_first, rank * block_count, block_count, slot_count)
    far_blocks = 0 if far_ref is None else far_ref.shape[1] // BLK
    far_rows = far_blocks * BLK
    top = weight_near.shape[1] // BLK
    key_acc[...] = jnp.zeros_like(key_acc)
    value_acc[...] = jnp.zeros_like(value_acc)
    if far_blocks:
        sum_far[...] = jnp.zeros_like(sum_far)
        dot_far[...] = jnp.zeros_like(dot_far)

    def body(s, block, start):
        sums = sum_local[s] + sum_near[s]
        dots = dot_local[s] + dot_near[s]
        for count in range(1, far_blocks + 1):
            @pl.when(start == -block_count - count)
            def _():
                rows = pl.ds((far_blocks - count) * BLK, count * BLK)
                score_pass(far_ref[0, rows, :], far_ref[1, rows, :], query_ref, grad_ref, s, None,
                           weight_far, prob_far, (s, rows), sum_far, dot_far, scale * math.log2(math.e))

        if far_blocks:
            sums = sums + sum_far[s]
            dots = dots + dot_far[s]
        inverse = 1.0 / jnp.sum(sums, axis=0, keepdims=True)
        delta = jnp.sum(dots, axis=0, keepdims=True) * inverse
        inverse_ref[s] = jnp.broadcast_to(inverse, inverse_ref.shape[1:])
        delta_ref[s] = jnp.broadcast_to(delta, delta_ref.shape[1:])
        for count in range(1, far_blocks + 1):
            @pl.when(start == -block_count - count)
            def _():
                rows = pl.ds((far_blocks - count) * BLK, count * BLK)
                grad_pass(weight_far, prob_far, (s, rows), query_ref, grad_ref, s, inverse_ref, delta_ref,
                          low_ref, score_ref, rows, key_acc, value_acc, rows)

        for count in range(1, top + 1):
            last = start <= -count if count == top else start == -count

            @pl.when(last)
            def _():
                rows = pl.ds((top - count) * BLK, count * BLK)
                window = pl.ds(far_rows + (top - count) * BLK, count * BLK)
                grad_pass(weight_near, prob_near, (s, rows), query_ref, grad_ref, s, inverse_ref,
                          delta_ref, low_ref, score_ref, window, key_acc, value_acc, window)

    over_slots(slots, body)
    if far_blocks:
        far_out[0] = (key_acc[:far_rows, :] * scale).astype(BF16)
        far_out[1] = value_acc[:far_rows, :].astype(BF16)
    odd = lax.rem(rank, 2) == 1
    for out, mine in ((inner_out, odd), (outer_out, jnp.logical_not(odd))):
        if out is not None:
            @pl.when(mine)
            def _():
                first = key_acc.shape[0] - out.shape[1]
                out[0] = (key_acc[first:, :] * scale).astype(BF16)
                out[1] = value_acc[first:, :].astype(BF16)


def finish_kernel(sizes, assistant, turn_first, query_ref, grad_ref, weight_ref, prob_ref, score_in,
                  inverse_ref, delta_ref, kv_ref, window, *rest):
    far_ref = rest[0] if len(rest) > 9 else None
    query_hbm, key_acc, value_acc, score_ref, low_ref, query_acc, stage, blank, sem = rest[-9:]
    block_count, slot_count, head_count, width, scale = sizes
    base = lax.axis_index("ctx") * block_count
    slots = slots_of(assistant, turn_first, base, block_count, slot_count)
    far_blocks = 0 if far_ref is None else far_ref.shape[1] // BLK
    top = window.shape[0] // BLK
    columns = query_acc.shape[1]
    blank[...] = jnp.zeros_like(blank)

    def blank_copy(i):
        return pltpu.make_async_copy(blank, query_hbm.at[0, pl.ds(i * BLK, BLK)], sem.at[slot_count + i])

    def stage_copy(s, block):
        return pltpu.make_async_copy(stage.at[s], query_hbm.at[0, block_rows(block)], sem.at[s])

    for i in range(block_count):
        @pl.when(assistant[0, base + i] != 1)
        def _():
            blank_copy(i).start()
    key_acc[...] = jnp.zeros_like(key_acc)
    value_acc[...] = jnp.zeros_like(value_acc)

    def body(s, block, start):
        def query_part(keys, source, rows, span):
            return nn_dot(keys.T, source[s, rows, span])

        @pl.when(start >= 0)
        def _():
            query_acc[...] = jnp.zeros_like(query_acc)

        for count in range(1, top + 1):
            last = start <= -count if count == top else start == -count

            @pl.when(last)
            def _():
                keys = window[(top - count) * BLK:, :]
                rows = pl.ds((far_blocks + top - count) * BLK, count * BLK)
                for c in range(0, columns, CHUNK):
                    span = slice(c, c + CHUNK)
                    query_acc[:, span] = query_part(keys, score_in, rows, span)

        for count in range(1, far_blocks + 1):
            @pl.when(start == -block_count - count)
            def _():
                rows = pl.ds((far_blocks - count) * BLK, count * BLK)
                for c in range(0, columns, CHUNK):
                    span = slice(c, c + CHUNK)
                    query_acc[:, span] += query_part(far_ref[0, rows, :], score_in, rows, span)

        low = jnp.maximum(start, 0)
        for count in range(1, block_count + 1):
            @pl.when(block + 1 - low == count)
            def _():
                rows = block_rows(low, count)
                grad_pass(weight_ref, prob_ref, (s, rows), query_ref, grad_ref, s, inverse_ref, delta_ref,
                          low_ref, score_ref, rows, key_acc, value_acc, rows)
                keys = kv_ref[0, rows, :]
                for c in range(0, columns, CHUNK):
                    span = slice(c, c + CHUNK)
                    total = query_acc[:, span] + query_part(keys, score_ref, rows, span)
                    for h in range(0, CHUNK, BLK):
                        place = slice((c + h) // BLK * width, ((c + h) // BLK + 1) * width)
                        stage[s, :, place] = (total[:, h:h + BLK] * scale).T.astype(BF16)

        stage_copy(s, block).start()

    over_slots(slots, body)
    key_acc[...] = key_acc[...] * scale
    for s, (block, live, start) in enumerate(slots):
        @pl.when(live)
        def _():
            stage_copy(s, block).wait()

    for i in range(block_count):
        @pl.when(assistant[0, base + i] != 1)
        def _():
            blank_copy(i).wait()


def total_kernel(*refs):
    key_acc, value_acc, near_ref = refs[:3]
    key_out, value_out = refs[-2:]
    token_count = key_acc.shape[0]
    for i, (acc, out) in enumerate(((key_acc, key_out), (value_acc, value_out))):
        cuts = sorted({0, token_count} | {token_count - ref.shape[1] for ref in refs[2:-2]})
        for low, high in zip(cuts, cuts[1:]):
            total = acc[low:high, :]
            for ref in refs[2:-2]:
                first = token_count - ref.shape[1]
                if first <= low:
                    total = total + ref[i, low - first:high - first, :].astype(F32)
            out[0, low:high, :] = total.astype(BF16)


def call(kernel, inputs, in_specs, outputs, out_specs, scratch, limit, macs, aliases={}):
    return pl.pallas_call(
        kernel,
        out_shape=outputs,
        in_specs=in_specs,
        out_specs=out_specs,
        scratch_shapes=scratch,
        input_output_aliases=aliases,
        compiler_params=pltpu.CompilerParams(vmem_limit_bytes=limit * MIB),
        cost_estimate=pl.CostEstimate(flops=2 * macs, bytes_accessed=2 * MIB, transcendentals=0),
    )(*inputs)


ANY_SPEC = pl.BlockSpec(memory_space=pl.ANY)
SMEM_SPEC = pl.BlockSpec(memory_space=pltpu.SMEM)
VMEM_SPEC = pl.BlockSpec(memory_space=pltpu.VMEM)


def gradients(sizes, with_outer, with_far, outer, far, own, assistant, turn_first, query_rows, out_grad):
    block_count, slot_count, head_count, width, scale = sizes
    token_count = block_count * BLK
    columns = head_count * BLK
    outer_rows = outer.shape[1]
    far_rows = far.shape[1] if with_far else 0
    reach_rows = token_count + far_rows
    pair = columns * BLK * width
    assistant, turn_first = smem(assistant), smem(turn_first)
    slot_rows = (slot_count, columns, width)
    stat_rows = (slot_count, SUB, columns)

    def score_shapes(rows):
        return (
            pltpu.VMEM((slot_count, rows, columns), F32),
            pltpu.VMEM((slot_count, rows, columns), F32),
            pltpu.VMEM(stat_rows, F32),
            pltpu.VMEM(stat_rows, F32),
        )

    def local(halves, state):
        return call(
            lambda *refs: local_kernel(sizes, halves, *refs),
            (assistant, turn_first, hbm(query_rows), hbm(out_grad), vmem(own)) + tuple(vmem(a) for a in state),
            [SMEM_SPEC] * 2 + [ANY_SPEC] * 2 + [VMEM_SPEC] * (1 + len(state)),
            (pltpu.VMEM(slot_rows, BF16), pltpu.VMEM(slot_rows, BF16)) + score_shapes(token_count),
            [VMEM_SPEC] * 6,
            [pltpu.SemaphoreType.DMA((slot_count, 2, head_count))],
            16,
            10 * pair,
            {5 + i: i for i in range(len(state))},
        )

    inner_in = pair_shift(own, "ctx", 1, 1)
    outer_in = far_in = ()
    if with_outer:
        local_state = local("first", ())
        outer, far, local_state = lax.optimization_barrier((outer, far, local_state))
        outer_in = (pair_shift(outer, "ctx", 1, 0),)
        if with_far:
            far_in = (shifted(far, "ctx", 2),)
        local_state = local("second", local_state)
    else:
        local_state = local("both", ())
    query_slots, grad_slots, weights, prob_grad, sums, dots = local_state
    near_state = ()
    for parity, source in ((1, inner_in),) + tuple((0, a) for a in outer_in):
        near_state = call(
            lambda *refs: near_kernel(sizes, parity, *refs),
            (assistant, turn_first) + tuple(vmem(a) for a in (query_slots, grad_slots, source) + tuple(near_state)),
            [SMEM_SPEC] * 2 + [VMEM_SPEC] * (3 + len(near_state)),
            score_shapes(token_count) + (pltpu.VMEM((token_count, width), BF16),),
            [VMEM_SPEC] * 5,
            [],
            16,
            10 * pair,
            {5 + i: i for i in range(len(near_state))},
        )
    weight_near, prob_near, sum_near, dot_near, window = near_state
    far_out = (pltpu.VMEM((2, far_rows, width), BF16),) if with_far else ()
    outer_out = (pltpu.VMEM((2, outer_rows, width), BF16),) if with_outer else ()
    outputs = far_out + (
        pltpu.VMEM((2, token_count, width), BF16),
        pltpu.VMEM((slot_count, reach_rows, columns), BF16),
        pltpu.VMEM(stat_rows, F32),
        pltpu.VMEM(stat_rows, F32),
    ) + outer_out
    results = call(
        lambda *refs: remote_kernel(sizes, with_outer, *refs),
        (assistant, turn_first)
        + tuple(
            vmem(a)
            for a in (query_slots, grad_slots, sums, dots, sum_near, dot_near, weight_near, prob_near)
            + far_in
        ),
        [SMEM_SPEC] * 2 + [VMEM_SPEC] * (8 + len(far_in)),
        outputs,
        [VMEM_SPEC] * len(outputs),
        (list(score_shapes(far_rows)) if with_far else [])
        + [
            pltpu.VMEM((token_count, columns), BF16),
            pltpu.VMEM((reach_rows, width), F32),
            pltpu.VMEM((reach_rows, width), F32),
        ],
        20,
        14 * pair,
    )
    first = len(far_out)
    inner_grad, score_grad, inverse, delta = results[first:first + 4]
    returned = [pair_shift(a, "ctx", -1, 0) for a in results[first + 4:]]
    returned += [shifted(a, "ctx", -2) for a in results[:first]]
    returned += [pair_shift(inner_grad, "ctx", -1, 1)]
    query_grad, key_acc, value_acc = call(
        lambda *refs: finish_kernel(sizes, *refs),
        (assistant, turn_first)
        + tuple(
            vmem(a)
            for a in (query_slots, grad_slots, weights, prob_grad, score_grad, inverse, delta, own,
                      window) + far_in
        ),
        [SMEM_SPEC] * 2 + [VMEM_SPEC] * (9 + len(far_in)),
        (
            jax.ShapeDtypeStruct(query_rows.shape, BF16),
            pltpu.VMEM((token_count, width), F32),
            pltpu.VMEM((token_count, width), F32),
        ),
        [ANY_SPEC] + [VMEM_SPEC] * 2,
        [
            pltpu.VMEM((slot_count, token_count, columns), BF16),
            pltpu.VMEM((token_count, columns), BF16),
            pltpu.VMEM((BLK, columns), F32),
            pltpu.VMEM((slot_count, BLK, head_count * width), BF16),
            pltpu.VMEM((BLK, head_count * width), BF16),
            pltpu.SemaphoreType.DMA((slot_count + block_count,)),
        ],
        16,
        25 * pair,
    )
    key_grad, value_grad = call(
        total_kernel,
        tuple(vmem(a) for a in [key_acc, value_acc] + returned),
        [VMEM_SPEC] * (2 + len(returned)),
        (jax.ShapeDtypeStruct((1, token_count, width), BF16),) * 2,
        [VMEM_SPEC] * 2,
        [],
        8,
        BLK,
    )
    return (query_grad, key_grad, value_grad)


def per_device(query_rows, key_rows, value_rows, out_grad, assistant, turn_first):
    token_count = query_rows.shape[1]
    width = key_rows.shape[2]
    head_count = query_rows.shape[2] // width
    block_count = token_count // BLK
    far_blocks = block_count // 2
    slot_count = (block_count + 1) // 2
    sizes = (block_count, slot_count, head_count, width, 1.0 / math.sqrt(width))
    last, own, assistant, turn_first, need = call(
        lambda *refs: pack_kernel(block_count, *refs),
        tuple(hbm(a) for a in (key_rows, value_rows, assistant, turn_first)),
        [ANY_SPEC] * 4,
        (
            pltpu.VMEM((2, far_blocks * BLK, width), BF16),
            pltpu.VMEM((2, token_count, width), BF16),
            pltpu.SMEM(assistant.shape, jnp.int32),
            pltpu.SMEM(turn_first.shape, jnp.int32),
            pltpu.SMEM((1,), jnp.int32),
        ),
        [VMEM_SPEC] * 2 + [SMEM_SPEC] * 3,
        [pltpu.SemaphoreType.DMA((6,))],
        8,
        BLK,
    )

    def branch(with_outer, whole, with_far):
        def run(last, own, *rest):
            return gradients(sizes, with_outer, with_far, own if whole else last, last, own, *rest)

        return run

    branches = [
        branch(False, False, False),
        branch(True, False, False),
        branch(True, True, False),
        branch(True, False, True),
        branch(True, True, True),
    ]
    return lax.switch(need[0], branches, last, own, assistant, turn_first, query_rows, out_grad)


def solution(mesh):
    return jax.shard_map(
        per_device,
        mesh=mesh,
        in_specs=(
            P("dp", "ctx", "tp"),
            P("dp", "ctx", "tp"),
            P("dp", "ctx", "tp"),
            P("dp", "ctx", "tp"),
            P("dp", None),
            P("dp", None),
        ),
        out_specs=(P("dp", "ctx", "tp"), P("dp", "ctx", "tp"), P("dp", "ctx", "tp")),
        check_vma=False,
    )
```

```python
import math

import jax
import jax.numpy as jnp
from jax import lax
from jax.experimental import pallas as pl
from jax.experimental.pallas import tpu as pltpu
from jax.sharding import PartitionSpec as P

BLK = 128
SUB = 8
CHUNK = 256
F32 = jnp.float32
BF16 = jnp.bfloat16
MIB = 1 << 20
NEAR_HINT = 400
CROSS_HINT = 60


def shifted(block, axis, distance):
    devices = range(lax.axis_size(axis))
    route = [(i - distance, i) for i in devices if i - distance in devices]
    return lax.ppermute(block, axis, route)


def pair_shift(block, axis, distance, parity):
    pairs = [(i - 1, i) for i in range(1, lax.axis_size(axis)) if i % 2 == parity]
    return lax.ppermute(block, axis, pairs if distance == 1 else [pair[::-1] for pair in pairs])


def vmem(array):
    return pltpu.with_memory_space_constraint(array, pltpu.VMEM)


def smem(array):
    return pltpu.with_memory_space_constraint(array, pltpu.SMEM)


def hbm(array):
    return pltpu.with_memory_space_constraint(array, pltpu.HBM)


def nt_dot(left, right):
    return lax.dot_general(left, right, (((1,), (1,)), ((), ())), preferred_element_type=F32)


def nn_dot(left, right):
    return lax.dot_general(left, right, (((1,), (0,)), ((), ())), preferred_element_type=F32)


def fold(tile):
    return jnp.sum(tile.reshape(tile.shape[0] // SUB, SUB, tile.shape[1]), axis=0)


def slots_of(assistant, turn_first, base, block_count, slot_count):
    found = jnp.int32(0)
    blocks = [jnp.int32(0)] * slot_count
    starts = [jnp.int32(0)] * slot_count
    for i in range(block_count):
        mark = assistant[0, base + i]
        start = turn_first[0, base + i] - base
        for s in range(slot_count):
            here = (mark == 1) & (found == s)
            blocks[s] = jnp.where(here, i, blocks[s])
            starts[s] = jnp.where(here, start, starts[s])
        found = found + jnp.where(mark == 1, 1, 0)
    return [(blocks[s], found > s, starts[s]) for s in range(slot_count)]


def score_pass(key_tile, value_tile, query_ref, grad_ref, slot, keep, weight_ref, prob_ref, at, sum_ref,
               dot_ref, scale):
    columns = query_ref.shape[1]
    height = key_tile.shape[0]
    for c in range(0, columns, CHUNK):
        span = slice(c, c + CHUNK)
        scores = nt_dot(key_tile, query_ref[slot, span, :])
        prob_grad = nt_dot(value_tile, grad_ref[slot, span, :])
        weights = jnp.exp2(scores * scale)
        if keep is not None:
            wide = jnp.concatenate([keep] * (CHUNK // BLK), axis=1)
            last = jnp.where(wide, weights[height - BLK:], 0.0)
            weights = jnp.concatenate([weights[:height - BLK], last], axis=0) if height > BLK else last
        weight_ref[at + (span,)] = weights
        prob_ref[at + (span,)] = prob_grad
        sum_ref[slot, :, span] = fold(weights)
        dot_ref[slot, :, span] = fold(weights * prob_grad)


def grad_pass(weight_ref, prob_ref, at, query_ref, grad_ref, slot, inverse_ref, delta_ref, low_ref,
              score_ref, score_rows, key_acc, value_acc, acc_rows):
    columns = query_ref.shape[1]
    height = acc_rows.size
    for c in range(0, columns, CHUNK):
        span = slice(c, c + CHUNK)
        shape = (height // SUB, SUB, CHUNK)
        attention = weight_ref[at + (span,)].reshape(shape) * inverse_ref[slot, :, span][None]
        lifted = prob_ref[at + (span,)].reshape(shape) - delta_ref[slot, :, span][None]
        score_grad = (attention * lifted).reshape(height, CHUNK)
        low_ref[:height, span] = attention.reshape(height, CHUNK).astype(BF16)
        score_ref[slot, score_rows, span] = score_grad.astype(BF16)
    value_acc[acc_rows, :] += nn_dot(low_ref[:height], grad_ref[slot])
    key_acc[acc_rows, :] += nn_dot(score_ref[slot, score_rows, :], query_ref[slot])


def block_rows(index, count=1):
    return pl.ds(pl.multiple_of(index * BLK, BLK), count * BLK)


def pick(values, s):
    chosen = values[0]
    for i in range(1, len(values)):
        chosen = jnp.where(s == i, values[i], chosen)
    return chosen


def over_slots(slots, body):
    def step(s, carry):
        block, start = (pick([slot[i] for slot in slots], s) for i in (0, 2))

        @pl.when(pick([jnp.where(slot[1], 1, 0) for slot in slots], s) == 1)
        def _():
            body(s, block, start)

        return carry

    lax.fori_loop(0, len(slots), step, 0)


def local_scores(sizes, assistant, turn_first, query_hbm, grad_hbm, kv_ref, query_ref, grad_ref,
                 weight_ref, prob_ref, sum_ref, dot_ref, sem, ready=lambda: None):
    block_count, slot_count, head_count, width, scale = sizes
    base = lax.axis_index("ctx") * block_count
    slots = slots_of(assistant, turn_first, base, block_count, slot_count)

    def copies(s, block):
        for i, (source, target) in enumerate(((query_hbm, query_ref), (grad_hbm, grad_ref))):
            for h in range(head_count):
                yield pltpu.make_async_copy(
                    source.at[0, block_rows(block), pl.ds(h * width, width)],
                    target.at[s, pl.ds(h * BLK, BLK)],
                    sem.at[s, i, h],
                )

    for s, (block, live, start) in enumerate(slots):
        @pl.when(live)
        def _():
            for copy in copies(s, block):
                copy.start()
    keep = lax.broadcasted_iota(jnp.int32, (BLK, BLK), 0) <= lax.broadcasted_iota(
        jnp.int32, (BLK, BLK), 1
    )
    ready()

    def body(s, block, start):
        for copy in copies(s, block):
            copy.wait()
        low = jnp.maximum(start, 0)
        for count in range(1, block_count + 1):
            @pl.when(block + 1 - low == count)
            def _():
                rows = block_rows(low, count)
                score_pass(kv_ref[0, rows, :], kv_ref[1, rows, :], query_ref, grad_ref, s, keep,
                           weight_ref, prob_ref, (s, rows), sum_ref, dot_ref, scale * math.log2(math.e))

    over_slots(slots, body)


def in_first_half():
    return lax.axis_index("ctx") * 2 < lax.axis_size("ctx")


def local_kernel(sizes, *refs):
    inputs, results = refs[:5], refs[-7:]
    pl.when(jnp.logical_not(in_first_half()))(lambda: local_scores(sizes, *inputs, *results))


def pack_kernel(sizes, key_ref, value_ref, assistant_ref, turn_ref, query_hbm, grad_hbm, last_ref, all_ref,
                assistant, turn_first, need_ref, *state):
    state, pack_sem = state[:-1], state[-1]
    block_count = sizes[0]
    token_count = key_ref.shape[1]
    marks = [
        pltpu.make_async_copy(assistant_ref, assistant, pack_sem.at[0]),
        pltpu.make_async_copy(turn_ref, turn_first, pack_sem.at[1]),
    ]
    copies = []
    for pack in (all_ref, last_ref):
        rows = pack.shape[1]
        for i, source in enumerate((key_ref, value_ref)):
            copies.append(
                pltpu.make_async_copy(
                    source.at[0, pl.ds(token_count - rows, rows)], pack.at[i], pack_sem.at[2 + len(copies)]
                )
            )
    for copy in marks + copies:
        copy.start()
    for copy in marks:
        copy.wait()
    outer = far = jnp.int32(0)
    for i in range(block_count, assistant.shape[1]):
        device = i // block_count
        behind = jnp.where(assistant[0, i] == 1, device * block_count - turn_first[0, i], 0)
        far = jnp.where(behind > block_count, 1, far)
        if device % 2 == 0:
            outer = jnp.maximum(outer, behind)
    need_ref[0] = jnp.where((outer > 1) | (far > 0), 2, outer)

    def ready():
        for copy in copies:
            copy.wait()

    @pl.when(in_first_half())
    def _():
        local_scores(sizes, assistant, turn_first, query_hbm, grad_hbm, all_ref, *state, ready=ready)

    pl.when(jnp.logical_not(in_first_half()))(ready)


def near_kernel(sizes, parity, assistant, turn_first, query_ref, grad_ref, source, *rest):
    weight_ref, prob_ref, sum_ref, dot_ref, window = rest[-5:]
    block_count, slot_count, head_count, width, scale = sizes
    rank = lax.axis_index("ctx")
    slots = slots_of(assistant, turn_first, rank * block_count, block_count, slot_count)
    top = window.shape[0] // BLK
    sent = source.shape[1] // BLK
    if len(rest) == 5:
        sum_ref[...] = jnp.zeros_like(sum_ref)
        dot_ref[...] = jnp.zeros_like(dot_ref)

    def body(s, block, start):
        for count in range(1, sent + 1):
            last = start <= -count if count == sent else start == -count

            @pl.when(last)
            def _():
                taken = pl.ds((sent - count) * BLK, count * BLK)
                rows = pl.ds((top - count) * BLK, count * BLK)
                score_pass(source[0, taken, :], source[1, taken, :], query_ref, grad_ref, s, None,
                           weight_ref, prob_ref, (s, rows), sum_ref, dot_ref, scale * math.log2(math.e))

    @pl.when(lax.rem(rank, 2) == parity)
    def _():
        window[window.shape[0] - source.shape[1]:, :] = source[0]
        over_slots(slots, body)


def remote_kernel(sizes, with_outer, with_far, assistant, turn_first, query_ref, grad_ref, sum_local, dot_local,
                  sum_near, dot_near, weight_near, prob_near, *rest):
    rest = list(rest)
    block_count, slot_count, head_count, width, scale = sizes
    far_ref = far_out = sum_far = dot_far = outer_out = None
    if with_far:
        far_ref, far_out = rest.pop(0), rest.pop(0)
        weight_far, prob_far, sum_far, dot_far = rest[-7:-3]
    if with_outer:
        outer_out = rest.pop(0)
    inner_out, score_ref, inverse_ref, delta_ref = rest[:4]
    low_ref, key_acc, value_acc = rest[-3:]
    rank = lax.axis_index("ctx")
    slots = slots_of(assistant, turn_first, rank * block_count, block_count, slot_count)
    far_blocks = 0 if far_ref is None else far_ref.shape[1] // BLK
    far_rows = far_blocks * BLK
    top = weight_near.shape[1] // BLK
    key_acc[...] = jnp.zeros_like(key_acc)
    value_acc[...] = jnp.zeros_like(value_acc)
    if far_blocks:
        sum_far[...] = jnp.zeros_like(sum_far)
        dot_far[...] = jnp.zeros_like(dot_far)

    def body(s, block, start):
        sums = sum_local[s] + sum_near[s]
        dots = dot_local[s] + dot_near[s]
        for count in range(1, far_blocks + 1):
            @pl.when(start == -block_count - count)
            def _():
                rows = pl.ds((far_blocks - count) * BLK, count * BLK)
                score_pass(far_ref[0, rows, :], far_ref[1, rows, :], query_ref, grad_ref, s, None,
                           weight_far, prob_far, (s, rows), sum_far, dot_far, scale * math.log2(math.e))

        if far_blocks:
            sums = sums + sum_far[s]
            dots = dots + dot_far[s]
        inverse = 1.0 / jnp.sum(sums, axis=0, keepdims=True)
        delta = jnp.sum(dots, axis=0, keepdims=True) * inverse
        inverse_ref[s] = jnp.broadcast_to(inverse, inverse_ref.shape[1:])
        delta_ref[s] = jnp.broadcast_to(delta, delta_ref.shape[1:])
        for count in range(1, far_blocks + 1):
            @pl.when(start == -block_count - count)
            def _():
                rows = pl.ds((far_blocks - count) * BLK, count * BLK)
                grad_pass(weight_far, prob_far, (s, rows), query_ref, grad_ref, s, inverse_ref, delta_ref,
                          low_ref, score_ref, rows, key_acc, value_acc, rows)

        for count in range(1, top + 1):
            last = start <= -count if count == top else start == -count

            @pl.when(last)
            def _():
                rows = pl.ds((top - count) * BLK, count * BLK)
                window = pl.ds(far_rows + (top - count) * BLK, count * BLK)
                grad_pass(weight_near, prob_near, (s, rows), query_ref, grad_ref, s, inverse_ref,
                          delta_ref, low_ref, score_ref, window, key_acc, value_acc, window)

    over_slots(slots, body)
    if far_blocks:
        far_out[0] = (key_acc[:far_rows, :] * scale).astype(BF16)
        far_out[1] = value_acc[:far_rows, :].astype(BF16)
    odd = lax.rem(rank, 2) == 1
    for out, mine in ((inner_out, odd), (outer_out, jnp.logical_not(odd))):
        if out is not None:
            @pl.when(mine)
            def _():
                first = key_acc.shape[0] - out.shape[1]
                out[0] = (key_acc[first:, :] * scale).astype(BF16)
                out[1] = value_acc[first:, :].astype(BF16)


def finish_kernel(sizes, assistant, turn_first, query_ref, grad_ref, weight_ref, prob_ref, score_in,
                  inverse_ref, delta_ref, kv_ref, window, *rest):
    far_ref = rest[0] if len(rest) > 9 else None
    query_hbm, key_acc, value_acc, score_ref, low_ref, query_acc, stage, blank, sem = rest[-9:]
    block_count, slot_count, head_count, width, scale = sizes
    base = lax.axis_index("ctx") * block_count
    slots = slots_of(assistant, turn_first, base, block_count, slot_count)
    far_blocks = 0 if far_ref is None else far_ref.shape[1] // BLK
    top = window.shape[0] // BLK
    columns = query_acc.shape[1]
    blank[...] = jnp.zeros_like(blank)

    def blank_copy(i):
        return pltpu.make_async_copy(blank, query_hbm.at[0, pl.ds(i * BLK, BLK)], sem.at[slot_count + i])

    def stage_copy(s, block):
        return pltpu.make_async_copy(stage.at[s], query_hbm.at[0, block_rows(block)], sem.at[s])

    for i in range(block_count):
        @pl.when(assistant[0, base + i] != 1)
        def _():
            blank_copy(i).start()
    key_acc[...] = jnp.zeros_like(key_acc)
    value_acc[...] = jnp.zeros_like(value_acc)

    def body(s, block, start):
        def query_part(keys, source, rows, span):
            return nn_dot(keys.T, source[s, rows, span])

        @pl.when(start >= 0)
        def _():
            query_acc[...] = jnp.zeros_like(query_acc)

        for count in range(1, top + 1):
            last = start <= -count if count == top else start == -count

            @pl.when(last)
            def _():
                keys = window[(top - count) * BLK:, :]
                rows = pl.ds((far_blocks + top - count) * BLK, count * BLK)
                for c in range(0, columns, CHUNK):
                    span = slice(c, c + CHUNK)
                    query_acc[:, span] = query_part(keys, score_in, rows, span)

        for count in range(1, far_blocks + 1):
            @pl.when(start == -block_count - count)
            def _():
                rows = pl.ds((far_blocks - count) * BLK, count * BLK)
                for c in range(0, columns, CHUNK):
                    span = slice(c, c + CHUNK)
                    query_acc[:, span] += query_part(far_ref[0, rows, :], score_in, rows, span)

        low = jnp.maximum(start, 0)
        for count in range(1, block_count + 1):
            @pl.when(block + 1 - low == count)
            def _():
                rows = block_rows(low, count)
                grad_pass(weight_ref, prob_ref, (s, rows), query_ref, grad_ref, s, inverse_ref, delta_ref,
                          low_ref, score_ref, rows, key_acc, value_acc, rows)
                keys = kv_ref[0, rows, :]
                for c in range(0, columns, CHUNK):
                    span = slice(c, c + CHUNK)
                    total = query_acc[:, span] + query_part(keys, score_ref, rows, span)
                    for h in range(0, CHUNK, BLK):
                        place = slice((c + h) // BLK * width, ((c + h) // BLK + 1) * width)
                        stage[s, :, place] = (total[:, h:h + BLK] * scale).T.astype(BF16)

        stage_copy(s, block).start()

    over_slots(slots, body)
    key_acc[...] = key_acc[...] * scale
    for s, (block, live, start) in enumerate(slots):
        @pl.when(live)
        def _():
            stage_copy(s, block).wait()

    for i in range(block_count):
        @pl.when(assistant[0, base + i] != 1)
        def _():
            blank_copy(i).wait()


def add_kernel(*refs):
    for i, out in enumerate(refs[-2:]):
        for ref in refs[2:-2]:
            first = out.shape[0] - ref.shape[1]
            out[first:, :] += ref[i].astype(F32)


def total_kernel(key_acc, value_acc, returned, key_out, value_out):
    for i, (acc, out) in enumerate(((key_acc, key_out), (value_acc, value_out))):
        out[0] = (acc[...] + returned[i].astype(F32)).astype(BF16)


def call(kernel, inputs, in_specs, outputs, out_specs, scratch, limit, macs, aliases={},
         traffic=2 * MIB):
    return pl.pallas_call(
        kernel,
        out_shape=outputs,
        in_specs=in_specs,
        out_specs=out_specs,
        scratch_shapes=scratch,
        input_output_aliases=aliases,
        compiler_params=pltpu.CompilerParams(vmem_limit_bytes=limit * MIB),
        cost_estimate=pl.CostEstimate(flops=2 * macs, bytes_accessed=traffic, transcendentals=0),
    )(*inputs)


ANY_SPEC = pl.BlockSpec(memory_space=pl.ANY)
SMEM_SPEC = pl.BlockSpec(memory_space=pltpu.SMEM)
VMEM_SPEC = pl.BlockSpec(memory_space=pltpu.VMEM)


def score_shapes(sizes, rows):
    block_count, slot_count, head_count, width, scale = sizes
    columns = head_count * BLK
    return (
        pltpu.VMEM((slot_count, rows, columns), F32),
        pltpu.VMEM((slot_count, rows, columns), F32),
        pltpu.VMEM((slot_count, SUB, columns), F32),
        pltpu.VMEM((slot_count, SUB, columns), F32),
    )


def local_shapes(sizes):
    block_count, slot_count, head_count, width, scale = sizes
    rows = pltpu.VMEM((slot_count, head_count * BLK, width), BF16)
    return (rows, rows) + score_shapes(sizes, block_count * BLK)


def local_sems(sizes):
    return pltpu.SemaphoreType.DMA((sizes[1], 2, sizes[2]))


def gradients(sizes, with_outer, with_far, outer, far, own, assistant, turn_first, query_rows, out_grad,
              local_state):
    block_count, slot_count, head_count, width, scale = sizes
    token_count = block_count * BLK
    columns = head_count * BLK
    outer_rows = outer.shape[1]
    far_rows = far.shape[1] if with_far else 0
    reach_rows = token_count + far_rows
    pair = columns * BLK * width
    assistant, turn_first = smem(assistant), smem(turn_first)
    stat_rows = (slot_count, SUB, columns)
    outer_in = (pair_shift(outer, "ctx", 1, 0),) if with_outer else ()
    far_in = (shifted(far, "ctx", 2),) if with_far else ()
    local_state = call(
        lambda *refs: local_kernel(sizes, *refs),
        (assistant, turn_first, hbm(query_rows), hbm(out_grad), vmem(own))
        + tuple(vmem(a) for a in local_state),
        [SMEM_SPEC] * 2 + [ANY_SPEC] * 2 + [VMEM_SPEC] * 7,
        local_shapes(sizes),
        [VMEM_SPEC] * 6,
        [local_sems(sizes)],
        16,
        pair,
        {5 + i: i for i in range(6)},
    )
    inner_in = pair_shift(own, "ctx", 1, 1)
    query_slots, grad_slots, weights, prob_grad, sums, dots = local_state
    near_state = ()
    for parity, source in tuple((0, a) for a in outer_in) + ((1, inner_in),):
        near_state = call(
            lambda *refs: near_kernel(sizes, parity, *refs),
            (assistant, turn_first)
            + tuple(vmem(a) for a in (query_slots, grad_slots, source) + tuple(near_state)),
            [SMEM_SPEC] * 2 + [VMEM_SPEC] * (3 + len(near_state)),
            score_shapes(sizes, token_count) + (pltpu.VMEM((token_count, width), BF16),),
            [VMEM_SPEC] * 5,
            [],
            16,
            10 * pair if parity else NEAR_HINT * pair,
            {5 + i: i for i in range(len(near_state))},
            1,
        )
    weight_near, prob_near, sum_near, dot_near, window = near_state
    far_out = (pltpu.VMEM((2, far_rows, width), BF16),) if with_far else ()
    outer_out = (pltpu.VMEM((2, outer_rows, width), BF16),) if with_outer else ()
    outputs = far_out + outer_out + (
        pltpu.VMEM((2, token_count, width), BF16),
        pltpu.VMEM((slot_count, reach_rows, columns), BF16),
        pltpu.VMEM(stat_rows, F32),
        pltpu.VMEM(stat_rows, F32),
    )
    results = call(
        lambda *refs: remote_kernel(sizes, with_outer, with_far, *refs),
        (assistant, turn_first)
        + tuple(
            vmem(a)
            for a in (query_slots, grad_slots, sums, dots, sum_near, dot_near, weight_near, prob_near)
            + far_in
        ),
        [SMEM_SPEC] * 2 + [VMEM_SPEC] * (8 + len(far_in)),
        outputs,
        [VMEM_SPEC] * len(outputs),
        (list(score_shapes(sizes, far_rows)) if with_far else [])
        + [
            pltpu.VMEM((token_count, columns), BF16),
            pltpu.VMEM((reach_rows, width), F32),
            pltpu.VMEM((reach_rows, width), F32),
        ],
        20,
        14 * pair,
    )
    inner_grad, score_grad, inverse, delta = results[-4:]
    crossed = [shifted(a, "ctx", -2) for a in results[:len(far_out)]]
    crossed += [pair_shift(a, "ctx", -1, 0) for a in results[len(far_out):-4]]
    returned = pair_shift(inner_grad, "ctx", -1, 1)
    query_grad, key_acc, value_acc = call(
        lambda *refs: finish_kernel(sizes, *refs),
        (assistant, turn_first)
        + tuple(
            vmem(a)
            for a in (query_slots, grad_slots, weights, prob_grad, score_grad, inverse, delta, own,
                      window) + far_in
        ),
        [SMEM_SPEC] * 2 + [VMEM_SPEC] * (9 + len(far_in)),
        (
            jax.ShapeDtypeStruct(query_rows.shape, BF16),
            pltpu.VMEM((token_count, width), F32),
            pltpu.VMEM((token_count, width), F32),
        ),
        [ANY_SPEC] + [VMEM_SPEC] * 2,
        [
            pltpu.VMEM((slot_count, token_count, columns), BF16),
            pltpu.VMEM((token_count, columns), BF16),
            pltpu.VMEM((BLK, columns), F32),
            pltpu.VMEM((slot_count, BLK, head_count * width), BF16),
            pltpu.VMEM((BLK, head_count * width), BF16),
            pltpu.SemaphoreType.DMA((slot_count + block_count,)),
        ],
        16,
        pair,
        {},
        1,
    )
    if crossed:
        key_acc, value_acc = call(
            add_kernel,
            tuple(vmem(a) for a in [key_acc, value_acc] + crossed),
            [VMEM_SPEC] * (2 + len(crossed)),
            (pltpu.VMEM((token_count, width), F32),) * 2,
            [VMEM_SPEC] * 2,
            [],
            8,
            CROSS_HINT * pair,
            {0: 0, 1: 1},
            1,
        )
    key_grad, value_grad = call(
        total_kernel,
        tuple(vmem(a) for a in (key_acc, value_acc, returned)),
        [VMEM_SPEC] * 3,
        (jax.ShapeDtypeStruct((1, token_count, width), BF16),) * 2,
        [VMEM_SPEC] * 2,
        [],
        8,
        BLK,
    )
    return (query_grad, key_grad, value_grad)


def per_device(query_rows, key_rows, value_rows, out_grad, assistant, turn_first):
    token_count = query_rows.shape[1]
    width = key_rows.shape[2]
    head_count = query_rows.shape[2] // width
    block_count = token_count // BLK
    far_blocks = block_count // 2
    slot_count = (block_count + 1) // 2
    sizes = (block_count, slot_count, head_count, width, 1.0 / math.sqrt(width))
    last, own, assistant, turn_first, need, *local_state = call(
        lambda *refs: pack_kernel(sizes, *refs),
        tuple(hbm(a) for a in (key_rows, value_rows, assistant, turn_first, query_rows, out_grad)),
        [ANY_SPEC] * 6,
        (
            pltpu.VMEM((2, far_blocks * BLK, width), BF16),
            pltpu.VMEM((2, token_count, width), BF16),
            pltpu.SMEM(assistant.shape, jnp.int32),
            pltpu.SMEM(turn_first.shape, jnp.int32),
            pltpu.SMEM((1,), jnp.int32),
        )
        + local_shapes(sizes),
        [VMEM_SPEC] * 2 + [SMEM_SPEC] * 3 + [VMEM_SPEC] * 6,
        [local_sems(sizes), pltpu.SemaphoreType.DMA((6,))],
        16,
        10 * head_count * BLK * BLK * width,
    )

    def branch(with_outer, whole, with_far):
        def run(last, own, *rest):
            return gradients(sizes, with_outer, with_far, own if whole else last, last, own, *rest)

        return run

    branches = [branch(False, False, False), branch(True, False, False), branch(True, True, True)]
    return lax.switch(
        need[0], branches, last, own, assistant, turn_first, query_rows, out_grad, tuple(local_state)
    )


def solution(mesh):
    return jax.shard_map(
        per_device,
        mesh=mesh,
        in_specs=(
            P("dp", "ctx", "tp"),
            P("dp", "ctx", "tp"),
            P("dp", "ctx", "tp"),
            P("dp", "ctx", "tp"),
            P("dp", None),
            P("dp", None),
        ),
        out_specs=(P("dp", "ctx", "tp"), P("dp", "ctx", "tp"), P("dp", "ctx", "tp")),
        check_vma=False,
    )
```

```python
import math

import jax
import jax.numpy as jnp
from jax import lax
from jax.experimental import pallas as pl
from jax.experimental.pallas import tpu as pltpu
from jax.sharding import PartitionSpec as P

BLK = 128
SUB = 8
CHUNK = 256
F32 = jnp.float32
BF16 = jnp.bfloat16
MIB = 1 << 20
NEAR_HINT = (400, 10)
REMOTE_HINT = (14, 14)
CROSS_HINT = 60


def shifted(block, axis, distance):
    devices = range(lax.axis_size(axis))
    route = [(i - distance, i) for i in devices if i - distance in devices]
    return lax.ppermute(block, axis, route)


def pair_shift(block, axis, distance, parity):
    pairs = [(i - 1, i) for i in range(1, lax.axis_size(axis)) if i % 2 == parity]
    return lax.ppermute(block, axis, pairs if distance == 1 else [pair[::-1] for pair in pairs])


def vmem(array):
    return pltpu.with_memory_space_constraint(array, pltpu.VMEM)


def smem(array):
    return pltpu.with_memory_space_constraint(array, pltpu.SMEM)


def hbm(array):
    return pltpu.with_memory_space_constraint(array, pltpu.HBM)


def nt_dot(left, right):
    return lax.dot_general(left, right, (((1,), (1,)), ((), ())), preferred_element_type=F32)


def nn_dot(left, right):
    return lax.dot_general(left, right, (((1,), (0,)), ((), ())), preferred_element_type=F32)


def fold(tile):
    return jnp.sum(tile.reshape(tile.shape[0] // SUB, SUB, tile.shape[1]), axis=0)


def slots_of(assistant, turn_first, base, block_count, slot_count):
    found = jnp.int32(0)
    blocks = [jnp.int32(0)] * slot_count
    starts = [jnp.int32(0)] * slot_count
    for i in range(block_count):
        mark = assistant[0, base + i]
        start = turn_first[0, base + i] - base
        for s in range(slot_count):
            here = (mark == 1) & (found == s)
            blocks[s] = jnp.where(here, i, blocks[s])
            starts[s] = jnp.where(here, start, starts[s])
        found = found + jnp.where(mark == 1, 1, 0)
    return [(blocks[s], found > s, starts[s]) for s in range(slot_count)]


def score_pass(key_tile, value_tile, query_ref, grad_ref, slot, keep, weight_ref, prob_ref, at, sum_ref,
               dot_ref, scale):
    columns = query_ref.shape[1]
    height = key_tile.shape[0]
    for c in range(0, columns, CHUNK):
        span = slice(c, c + CHUNK)
        scores = nt_dot(key_tile, query_ref[slot, span, :])
        prob_grad = nt_dot(value_tile, grad_ref[slot, span, :])
        weights = jnp.exp2(scores * scale)
        if keep is not None:
            wide = jnp.concatenate([keep] * (CHUNK // BLK), axis=1)
            last = jnp.where(wide, weights[height - BLK:], 0.0)
            weights = jnp.concatenate([weights[:height - BLK], last], axis=0) if height > BLK else last
        weight_ref[at + (span,)] = weights
        prob_ref[at + (span,)] = prob_grad
        sum_ref[slot, :, span] = fold(weights)
        dot_ref[slot, :, span] = fold(weights * prob_grad)


def grad_pass(weight_ref, prob_ref, at, query_ref, grad_ref, slot, inverse_ref, delta_ref, low_ref,
              score_ref, score_rows, key_acc, value_acc, acc_rows):
    columns = query_ref.shape[1]
    height = acc_rows.size
    for c in range(0, columns, CHUNK):
        span = slice(c, c + CHUNK)
        shape = (height // SUB, SUB, CHUNK)
        attention = weight_ref[at + (span,)].reshape(shape) * inverse_ref[slot, :, span][None]
        lifted = prob_ref[at + (span,)].reshape(shape) - delta_ref[slot, :, span][None]
        score_grad = (attention * lifted).reshape(height, CHUNK)
        low_ref[:height, span] = attention.reshape(height, CHUNK).astype(BF16)
        score_ref[slot, score_rows, span] = score_grad.astype(BF16)
    value_acc[acc_rows, :] += nn_dot(low_ref[:height], grad_ref[slot])
    key_acc[acc_rows, :] += nn_dot(score_ref[slot, score_rows, :], query_ref[slot])


def block_rows(index, count=1):
    return pl.ds(pl.multiple_of(index * BLK, BLK), count * BLK)


def pick(values, s):
    chosen = values[0]
    for i in range(1, len(values)):
        chosen = jnp.where(s == i, values[i], chosen)
    return chosen


def over_slots(slots, body):
    def step(s, carry):
        block, start = (pick([slot[i] for slot in slots], s) for i in (0, 2))

        @pl.when(pick([jnp.where(slot[1], 1, 0) for slot in slots], s) == 1)
        def _():
            body(s, block, start)

        return carry

    lax.fori_loop(0, len(slots), step, 0)


def local_scores(sizes, assistant, turn_first, query_hbm, grad_hbm, kv_ref, query_ref, grad_ref,
                 weight_ref, prob_ref, sum_ref, dot_ref, sem, ready=lambda: None):
    block_count, slot_count, head_count, width, scale = sizes
    base = lax.axis_index("ctx") * block_count
    slots = slots_of(assistant, turn_first, base, block_count, slot_count)

    def copies(s, block):
        for i, (source, target) in enumerate(((query_hbm, query_ref), (grad_hbm, grad_ref))):
            for h in range(head_count):
                yield pltpu.make_async_copy(
                    source.at[0, block_rows(block), pl.ds(h * width, width)],
                    target.at[s, pl.ds(h * BLK, BLK)],
                    sem.at[s, i, h],
                )

    for s, (block, live, start) in enumerate(slots):
        @pl.when(live)
        def _():
            for copy in copies(s, block):
                copy.start()
    keep = lax.broadcasted_iota(jnp.int32, (BLK, BLK), 0) <= lax.broadcasted_iota(
        jnp.int32, (BLK, BLK), 1
    )
    ready()

    def body(s, block, start):
        for copy in copies(s, block):
            copy.wait()
        low = jnp.maximum(start, 0)
        for count in range(1, block_count + 1):
            @pl.when(block + 1 - low == count)
            def _():
                rows = block_rows(low, count)
                score_pass(kv_ref[0, rows, :], kv_ref[1, rows, :], query_ref, grad_ref, s, keep,
                           weight_ref, prob_ref, (s, rows), sum_ref, dot_ref, scale * math.log2(math.e))

    over_slots(slots, body)


def in_first_half():
    return lax.axis_index("ctx") * 2 < lax.axis_size("ctx")


def local_kernel(sizes, *refs):
    inputs, results = refs[:5], refs[-7:]
    pl.when(jnp.logical_not(in_first_half()))(lambda: local_scores(sizes, *inputs, *results))


def pack_kernel(sizes, key_ref, value_ref, assistant_ref, turn_ref, query_hbm, grad_hbm, last_ref, all_ref,
                assistant, turn_first, need_ref, *state):
    state, pack_sem = state[:-1], state[-1]
    block_count = sizes[0]
    token_count = key_ref.shape[1]
    marks = [
        pltpu.make_async_copy(assistant_ref, assistant, pack_sem.at[0]),
        pltpu.make_async_copy(turn_ref, turn_first, pack_sem.at[1]),
    ]
    copies = []
    for pack in (all_ref, last_ref):
        rows = pack.shape[1]
        for i, source in enumerate((key_ref, value_ref)):
            copies.append(
                pltpu.make_async_copy(
                    source.at[0, pl.ds(token_count - rows, rows)], pack.at[i], pack_sem.at[2 + len(copies)]
                )
            )
    for copy in marks + copies:
        copy.start()
    for copy in marks:
        copy.wait()
    outer = far = jnp.int32(0)
    for i in range(block_count, assistant.shape[1]):
        device = i // block_count
        behind = jnp.where(assistant[0, i] == 1, device * block_count - turn_first[0, i], 0)
        far = jnp.where(behind > block_count, 1, far)
        if device % 2 == 0:
            outer = jnp.maximum(outer, behind)
    need_ref[0] = jnp.where((outer > 1) | (far > 0), 2, outer)

    def ready():
        for copy in copies:
            copy.wait()

    @pl.when(in_first_half())
    def _():
        local_scores(sizes, assistant, turn_first, query_hbm, grad_hbm, all_ref, *state, ready=ready)

    pl.when(jnp.logical_not(in_first_half()))(ready)


def near_kernel(sizes, parity, assistant, turn_first, query_ref, grad_ref, source, *rest):
    weight_ref, prob_ref, sum_ref, dot_ref, window = rest[-5:]
    block_count, slot_count, head_count, width, scale = sizes
    rank = lax.axis_index("ctx")
    slots = slots_of(assistant, turn_first, rank * block_count, block_count, slot_count)
    sent = source.shape[1] // BLK

    def body(s, block, start):
        for count in range(1, sent + 1):
            last = start <= -count if count == sent else start == -count

            @pl.when(last)
            def _():
                rows = pl.ds((sent - count) * BLK, count * BLK)
                score_pass(source[0, rows, :], source[1, rows, :], query_ref, grad_ref, s, None,
                           weight_ref, prob_ref, (s, rows), sum_ref, dot_ref, scale * math.log2(math.e))

    @pl.when(lax.rem(rank, 2) == parity)
    def _():
        window[window.shape[0] - source.shape[1]:, :] = source[0]
        over_slots(slots, body)


def remote_kernel(sizes, parity, with_far, assistant, turn_first, query_ref, grad_ref, sum_local, dot_local,
                  *rest):
    block_count, slot_count, head_count, width, scale = sizes
    near_refs, rest = rest[:4], rest[4:]
    weight_near, prob_near, sum_near, dot_near = near_refs
    low_ref, key_acc, value_acc = rest[-3:]
    far_ref = None
    if with_far:
        far_ref, far_out = rest[0], rest[-8]
        weight_far, prob_far, sum_far, dot_far = rest[-7:-3]
        rest = rest[:-8] + rest[-3:]
    score_ref, inverse_ref, delta_ref, near_out = rest[-7:-3]
    rank = lax.axis_index("ctx")
    slots = slots_of(assistant, turn_first, rank * block_count, block_count, slot_count)
    far_blocks = 0 if far_ref is None else far_ref.shape[1] // BLK
    far_rows = far_blocks * BLK
    sent = weight_near.shape[1] // BLK

    def body(s, block, start):
        sums = sum_local[s] + jnp.where(start < 0, sum_near[s], 0.0)
        dots = dot_local[s] + jnp.where(start < 0, dot_near[s], 0.0)
        for count in range(1, far_blocks + 1):
            @pl.when(start == -block_count - count)
            def _():
                rows = pl.ds((far_blocks - count) * BLK, count * BLK)
                score_pass(far_ref[0, rows, :], far_ref[1, rows, :], query_ref, grad_ref, s, None,
                           weight_far, prob_far, (s, rows), sum_far, dot_far, scale * math.log2(math.e))

        if far_blocks:
            sums = sums + jnp.where(start < -block_count, sum_far[s], 0.0)
            dots = dots + jnp.where(start < -block_count, dot_far[s], 0.0)
        inverse = 1.0 / jnp.sum(sums, axis=0, keepdims=True)
        delta = jnp.sum(dots, axis=0, keepdims=True) * inverse
        inverse_ref[s] = jnp.broadcast_to(inverse, inverse_ref.shape[1:])
        delta_ref[s] = jnp.broadcast_to(delta, delta_ref.shape[1:])
        for count in range(1, far_blocks + 1):
            @pl.when(start == -block_count - count)
            def _():
                rows = pl.ds((far_blocks - count) * BLK, count * BLK)
                grad_pass(weight_far, prob_far, (s, rows), query_ref, grad_ref, s, inverse_ref, delta_ref,
                          low_ref, score_ref, rows, key_acc, value_acc, rows)

        for count in range(1, sent + 1):
            last = start <= -count if count == sent else start == -count

            @pl.when(last)
            def _():
                rows = pl.ds((sent - count) * BLK, count * BLK)
                window = pl.ds(far_rows + (block_count - count) * BLK, count * BLK)
                grad_pass(weight_near, prob_near, (s, rows), query_ref, grad_ref, s, inverse_ref,
                          delta_ref, low_ref, score_ref, window, key_acc, value_acc, window)

    def run():
        key_acc[...] = jnp.zeros_like(key_acc)
        value_acc[...] = jnp.zeros_like(value_acc)
        over_slots(slots, body)
        if far_blocks:
            far_out[0] = (key_acc[:far_rows, :] * scale).astype(BF16)
            far_out[1] = value_acc[:far_rows, :].astype(BF16)
        first = key_acc.shape[0] - near_out.shape[1]
        near_out[0] = (key_acc[first:, :] * scale).astype(BF16)
        near_out[1] = value_acc[first:, :].astype(BF16)

    if parity is None:
        run()
    else:
        pl.when(lax.rem(rank, 2) == parity)(run)


def finish_kernel(sizes, assistant, turn_first, query_ref, grad_ref, weight_ref, prob_ref, score_in,
                  inverse_ref, delta_ref, kv_ref, window, *rest):
    far_ref = rest[0] if len(rest) > 9 else None
    query_hbm, key_acc, value_acc, score_ref, low_ref, query_acc, stage, blank, sem = rest[-9:]
    block_count, slot_count, head_count, width, scale = sizes
    base = lax.axis_index("ctx") * block_count
    slots = slots_of(assistant, turn_first, base, block_count, slot_count)
    far_blocks = 0 if far_ref is None else far_ref.shape[1] // BLK
    top = window.shape[0] // BLK
    columns = query_acc.shape[1]
    blank[...] = jnp.zeros_like(blank)

    def blank_copy(i):
        return pltpu.make_async_copy(blank, query_hbm.at[0, pl.ds(i * BLK, BLK)], sem.at[slot_count + i])

    def stage_copy(s, block):
        return pltpu.make_async_copy(stage.at[s], query_hbm.at[0, block_rows(block)], sem.at[s])

    for i in range(block_count):
        @pl.when(assistant[0, base + i] != 1)
        def _():
            blank_copy(i).start()
    key_acc[...] = jnp.zeros_like(key_acc)
    value_acc[...] = jnp.zeros_like(value_acc)

    def body(s, block, start):
        def query_part(keys, source, rows, span):
            return nn_dot(keys.T, source[s, rows, span])

        @pl.when(start >= 0)
        def _():
            query_acc[...] = jnp.zeros_like(query_acc)

        for count in range(1, top + 1):
            last = start <= -count if count == top else start == -count

            @pl.when(last)
            def _():
                keys = window[(top - count) * BLK:, :]
                rows = pl.ds((far_blocks + top - count) * BLK, count * BLK)
                for c in range(0, columns, CHUNK):
                    span = slice(c, c + CHUNK)
                    query_acc[:, span] = query_part(keys, score_in, rows, span)

        for count in range(1, far_blocks + 1):
            @pl.when(start == -block_count - count)
            def _():
                rows = pl.ds((far_blocks - count) * BLK, count * BLK)
                for c in range(0, columns, CHUNK):
                    span = slice(c, c + CHUNK)
                    query_acc[:, span] += query_part(far_ref[0, rows, :], score_in, rows, span)

        low = jnp.maximum(start, 0)
        for count in range(1, block_count + 1):
            @pl.when(block + 1 - low == count)
            def _():
                rows = block_rows(low, count)
                grad_pass(weight_ref, prob_ref, (s, rows), query_ref, grad_ref, s, inverse_ref, delta_ref,
                          low_ref, score_ref, rows, key_acc, value_acc, rows)
                keys = kv_ref[0, rows, :]
                for c in range(0, columns, CHUNK):
                    span = slice(c, c + CHUNK)
                    total = query_acc[:, span] + query_part(keys, score_ref, rows, span)
                    for h in range(0, CHUNK, BLK):
                        place = slice((c + h) // BLK * width, ((c + h) // BLK + 1) * width)
                        stage[s, :, place] = (total[:, h:h + BLK] * scale).T.astype(BF16)

        stage_copy(s, block).start()

    over_slots(slots, body)
    key_acc[...] = key_acc[...] * scale
    for s, (block, live, start) in enumerate(slots):
        @pl.when(live)
        def _():
            stage_copy(s, block).wait()

    for i in range(block_count):
        @pl.when(assistant[0, base + i] != 1)
        def _():
            blank_copy(i).wait()


def add_kernel(*refs):
    for i, out in enumerate(refs[-2:]):
        for ref in refs[2:-2]:
            first = out.shape[0] - ref.shape[1]
            out[first:, :] += ref[i].astype(F32)


def total_kernel(key_acc, value_acc, returned, key_out, value_out):
    for i, (acc, out) in enumerate(((key_acc, key_out), (value_acc, value_out))):
        out[0] = (acc[...] + returned[i].astype(F32)).astype(BF16)


def call(kernel, inputs, in_specs, outputs, out_specs, scratch, limit, macs, aliases={},
         traffic=2 * MIB):
    return pl.pallas_call(
        kernel,
        out_shape=outputs,
        in_specs=in_specs,
        out_specs=out_specs,
        scratch_shapes=scratch,
        input_output_aliases=aliases,
        compiler_params=pltpu.CompilerParams(vmem_limit_bytes=limit * MIB),
        cost_estimate=pl.CostEstimate(flops=2 * macs, bytes_accessed=traffic, transcendentals=0),
    )(*inputs)


ANY_SPEC = pl.BlockSpec(memory_space=pl.ANY)
SMEM_SPEC = pl.BlockSpec(memory_space=pltpu.SMEM)
VMEM_SPEC = pl.BlockSpec(memory_space=pltpu.VMEM)


def score_shapes(sizes, rows):
    block_count, slot_count, head_count, width, scale = sizes
    columns = head_count * BLK
    return (
        pltpu.VMEM((slot_count, rows, columns), F32),
        pltpu.VMEM((slot_count, rows, columns), F32),
        pltpu.VMEM((slot_count, SUB, columns), F32),
        pltpu.VMEM((slot_count, SUB, columns), F32),
    )


def local_shapes(sizes):
    block_count, slot_count, head_count, width, scale = sizes
    rows = pltpu.VMEM((slot_count, head_count * BLK, width), BF16)
    return (rows, rows) + score_shapes(sizes, block_count * BLK)


def local_sems(sizes):
    return pltpu.SemaphoreType.DMA((sizes[1], 2, sizes[2]))


def gradients(sizes, with_outer, with_far, outer, far, own, assistant, turn_first, query_rows, out_grad,
              local_state):
    block_count, slot_count, head_count, width, scale = sizes
    token_count = block_count * BLK
    columns = head_count * BLK
    outer_rows = outer.shape[1]
    far_rows = far.shape[1] if with_far else 0
    reach_rows = token_count + far_rows
    pair = columns * BLK * width
    assistant, turn_first = smem(assistant), smem(turn_first)
    stat_rows = (slot_count, SUB, columns)
    outer_in = (pair_shift(outer, "ctx", 1, 0),) if with_outer else ()
    far_in = (shifted(far, "ctx", 2),) if with_far else ()
    local_state = call(
        lambda *refs: local_kernel(sizes, *refs),
        (assistant, turn_first, hbm(query_rows), hbm(out_grad), vmem(own))
        + tuple(vmem(a) for a in local_state),
        [SMEM_SPEC] * 2 + [ANY_SPEC] * 2 + [VMEM_SPEC] * 7,
        local_shapes(sizes),
        [VMEM_SPEC] * 6,
        [local_sems(sizes)],
        16,
        pair,
        {5 + i: i for i in range(6)},
    )
    inner_in = pair_shift(own, "ctx", 1, 1)
    query_slots, grad_slots, weights, prob_grad, sums, dots = local_state
    window = ()
    remote_state = ()
    near_grads = []
    for parity, source in tuple((0, a) for a in outer_in) + ((1, inner_in),):
        rows = source.shape[1]
        *near_state, window = call(
            lambda *refs: near_kernel(sizes, parity, *refs),
            (assistant, turn_first) + tuple(vmem(a) for a in (query_slots, grad_slots, source) + window),
            [SMEM_SPEC] * 2 + [VMEM_SPEC] * (3 + len(window)),
            score_shapes(sizes, rows) + (pltpu.VMEM((token_count, width), BF16),),
            [VMEM_SPEC] * 5,
            [],
            16,
            NEAR_HINT[parity] * pair,
            {5: 4} if window else {},
            1,
        )
        window = (window,)
        outputs = (
            pltpu.VMEM((slot_count, reach_rows, columns), BF16),
            pltpu.VMEM(stat_rows, F32),
            pltpu.VMEM(stat_rows, F32),
            pltpu.VMEM((2, rows, width), BF16),
        )
        if with_far:
            outputs += (pltpu.VMEM((2, far_rows, width), BF16),)
        inputs = (query_slots, grad_slots, sums, dots) + tuple(near_state) + far_in
        aliases = {2 + len(inputs) + i: i if i < 3 else 4 for i in range(len(remote_state))}
        results = call(
            lambda *refs: remote_kernel(sizes, parity if with_outer else None, with_far, *refs),
            (assistant, turn_first) + tuple(vmem(a) for a in inputs + remote_state),
            [SMEM_SPEC] * 2 + [VMEM_SPEC] * (len(inputs) + len(remote_state)),
            outputs,
            [VMEM_SPEC] * len(outputs),
            (list(score_shapes(sizes, far_rows)) if with_far else [])
            + [
                pltpu.VMEM((token_count, columns), BF16),
                pltpu.VMEM((reach_rows, width), F32),
                pltpu.VMEM((reach_rows, width), F32),
            ],
            20,
            REMOTE_HINT[parity] * pair,
            aliases,
            1,
        )
        remote_state = results[:3] + results[4:]
        near_grads.append(pair_shift(results[3], "ctx", -1, parity))
    score_grad, inverse, delta, *far_grad = remote_state
    *crossed, returned = near_grads
    crossed += [shifted(a, "ctx", -2) for a in far_grad]
    query_grad, key_acc, value_acc = call(
        lambda *refs: finish_kernel(sizes, *refs),
        (assistant, turn_first)
        + tuple(
            vmem(a)
            for a in (query_slots, grad_slots, weights, prob_grad, score_grad, inverse, delta, own)
            + window + far_in
        ),
        [SMEM_SPEC] * 2 + [VMEM_SPEC] * (9 + len(far_in)),
        (
            jax.ShapeDtypeStruct(query_rows.shape, BF16),
            pltpu.VMEM((token_count, width), F32),
            pltpu.VMEM((token_count, width), F32),
        ),
        [ANY_SPEC] + [VMEM_SPEC] * 2,
        [
            pltpu.VMEM((slot_count, token_count, columns), BF16),
            pltpu.VMEM((token_count, columns), BF16),
            pltpu.VMEM((BLK, columns), F32),
            pltpu.VMEM((slot_count, BLK, head_count * width), BF16),
            pltpu.VMEM((BLK, head_count * width), BF16),
            pltpu.SemaphoreType.DMA((slot_count + block_count,)),
        ],
        16,
        pair,
        {},
        1,
    )
    if crossed:
        key_acc, value_acc = call(
            add_kernel,
            tuple(vmem(a) for a in [key_acc, value_acc] + crossed),
            [VMEM_SPEC] * (2 + len(crossed)),
            (pltpu.VMEM((token_count, width), F32),) * 2,
            [VMEM_SPEC] * 2,
            [],
            8,
            CROSS_HINT * pair,
            {0: 0, 1: 1},
            1,
        )
    key_grad, value_grad = call(
        total_kernel,
        tuple(vmem(a) for a in (key_acc, value_acc, returned)),
        [VMEM_SPEC] * 3,
        (jax.ShapeDtypeStruct((1, token_count, width), BF16),) * 2,
        [VMEM_SPEC] * 2,
        [],
        8,
        BLK,
    )
    return (query_grad, key_grad, value_grad)


def per_device(query_rows, key_rows, value_rows, out_grad, assistant, turn_first):
    token_count = query_rows.shape[1]
    width = key_rows.shape[2]
    head_count = query_rows.shape[2] // width
    block_count = token_count // BLK
    far_blocks = block_count // 2
    slot_count = (block_count + 1) // 2
    sizes = (block_count, slot_count, head_count, width, 1.0 / math.sqrt(width))
    last, own, assistant, turn_first, need, *local_state = call(
        lambda *refs: pack_kernel(sizes, *refs),
        tuple(hbm(a) for a in (key_rows, value_rows, assistant, turn_first, query_rows, out_grad)),
        [ANY_SPEC] * 6,
        (
            pltpu.VMEM((2, far_blocks * BLK, width), BF16),
            pltpu.VMEM((2, token_count, width), BF16),
            pltpu.SMEM(assistant.shape, jnp.int32),
            pltpu.SMEM(turn_first.shape, jnp.int32),
            pltpu.SMEM((1,), jnp.int32),
        )
        + local_shapes(sizes),
        [VMEM_SPEC] * 2 + [SMEM_SPEC] * 3 + [VMEM_SPEC] * 6,
        [local_sems(sizes), pltpu.SemaphoreType.DMA((6,))],
        16,
        10 * head_count * BLK * BLK * width,
    )

    def branch(with_outer, whole, with_far):
        def run(last, own, *rest):
            return gradients(sizes, with_outer, with_far, own if whole else last, last, own, *rest)

        return run

    branches = [branch(False, False, False), branch(True, False, False), branch(True, True, True)]
    return lax.switch(
        need[0], branches, last, own, assistant, turn_first, query_rows, out_grad, tuple(local_state)
    )


def solution(mesh):
    return jax.shard_map(
        per_device,
        mesh=mesh,
        in_specs=(
            P("dp", "ctx", "tp"),
            P("dp", "ctx", "tp"),
            P("dp", "ctx", "tp"),
            P("dp", "ctx", "tp"),
            P("dp", None),
            P("dp", None),
        ),
        out_specs=(P("dp", "ctx", "tp"), P("dp", "ctx", "tp"), P("dp", "ctx", "tp")),
        check_vma=False,
    )
```

```python
import math

import jax
import jax.numpy as jnp
from jax import lax
from jax.experimental import pallas as pl
from jax.experimental.pallas import tpu as pltpu
from jax.sharding import PartitionSpec as P

BLK = 128
SUB = 8
CHUNK = 256
F32 = jnp.float32
BF16 = jnp.bfloat16
MIB = 1 << 20
NEAR_HINT = (400, 10)
REMOTE_HINT = (14, 14)
CROSS_HINT = 60


def shifted(block, axis, distance):
    devices = range(lax.axis_size(axis))
    route = [(i - distance, i) for i in devices if i - distance in devices]
    return lax.ppermute(block, axis, route)


def pair_shift(block, axis, distance, parity):
    pairs = [(i - 1, i) for i in range(1, lax.axis_size(axis)) if i % 2 == parity]
    return lax.ppermute(block, axis, pairs if distance == 1 else [pair[::-1] for pair in pairs])


def vmem(array):
    return pltpu.with_memory_space_constraint(array, pltpu.VMEM)


def smem(array):
    return pltpu.with_memory_space_constraint(array, pltpu.SMEM)


def hbm(array):
    return pltpu.with_memory_space_constraint(array, pltpu.HBM)


def nt_dot(left, right):
    return lax.dot_general(left, right, (((1,), (1,)), ((), ())), preferred_element_type=F32)


def nn_dot(left, right):
    return lax.dot_general(left, right, (((1,), (0,)), ((), ())), preferred_element_type=F32)


def fold(tile):
    return jnp.sum(tile.reshape(tile.shape[0] // SUB, SUB, tile.shape[1]), axis=0)


def slots_of(assistant, turn_first, base, block_count, slot_count):
    found = jnp.int32(0)
    blocks = [jnp.int32(0)] * slot_count
    starts = [jnp.int32(0)] * slot_count
    for i in range(block_count):
        mark = assistant[0, base + i]
        start = turn_first[0, base + i] - base
        for s in range(slot_count):
            here = (mark == 1) & (found == s)
            blocks[s] = jnp.where(here, i, blocks[s])
            starts[s] = jnp.where(here, start, starts[s])
        found = found + jnp.where(mark == 1, 1, 0)
    return [(blocks[s], found > s, starts[s]) for s in range(slot_count)]


def score_pass(key_tile, value_tile, query_ref, grad_ref, slot, keep, weight_ref, prob_ref, at, sum_ref,
               dot_ref, scale):
    columns = query_ref.shape[1]
    for c in range(0, columns, CHUNK):
        span = slice(c, c + CHUNK)
        scores = nt_dot(key_tile, query_ref[slot, span, :])
        prob_grad = nt_dot(value_tile, grad_ref[slot, span, :])
        weights = jnp.exp2(scores * scale)
        if keep is not None:
            weights = jnp.where(jnp.concatenate([keep] * (CHUNK // BLK), axis=1), weights, 0.0)
        weight_ref[at + (span,)] = weights
        prob_ref[at + (span,)] = prob_grad
        sum_ref[slot, :, span] += fold(weights)
        dot_ref[slot, :, span] += fold(weights * prob_grad)


def grad_pass(weight_ref, prob_ref, at, query_ref, grad_ref, slot, inverse_ref, delta_ref, low_ref,
              score_ref, score_rows, key_acc, value_acc, acc_rows):
    columns = query_ref.shape[1]
    height = acc_rows.size
    for c in range(0, columns, CHUNK):
        span = slice(c, c + CHUNK)
        shape = (height // SUB, SUB, CHUNK)
        attention = weight_ref[at + (span,)].reshape(shape) * inverse_ref[slot, :, span][None]
        lifted = prob_ref[at + (span,)].reshape(shape) - delta_ref[slot, :, span][None]
        score_grad = (attention * lifted).reshape(height, CHUNK)
        low_ref[:height, span] = attention.reshape(height, CHUNK).astype(BF16)
        score_ref[slot, score_rows, span] = score_grad.astype(BF16)
    value_acc[acc_rows, :] += nn_dot(low_ref[:height], grad_ref[slot])
    key_acc[acc_rows, :] += nn_dot(score_ref[slot, score_rows, :], query_ref[slot])


def block_rows(index, count=1):
    return pl.ds(pl.multiple_of(index * BLK, BLK), count * BLK)


def pick(values, s):
    chosen = values[0]
    for i in range(1, len(values)):
        chosen = jnp.where(s == i, values[i], chosen)
    return chosen


def over_slots(slots, body):
    def step(s, carry):
        block, start = (pick([slot[i] for slot in slots], s) for i in (0, 2))

        @pl.when(pick([jnp.where(slot[1], 1, 0) for slot in slots], s) == 1)
        def _():
            body(s, block, start)

        return carry

    lax.fori_loop(0, len(slots), step, 0)


def local_scores(sizes, assistant, turn_first, query_hbm, grad_hbm, kv_ref, query_ref, grad_ref,
                 weight_ref, prob_ref, sum_ref, dot_ref, sem, ready=lambda: None):
    block_count, slot_count, head_count, width, scale = sizes
    base = lax.axis_index("ctx") * block_count
    slots = slots_of(assistant, turn_first, base, block_count, slot_count)

    def copies(s, block):
        for i, (source, target) in enumerate(((query_hbm, query_ref), (grad_hbm, grad_ref))):
            for h in range(head_count):
                yield pltpu.make_async_copy(
                    source.at[0, block_rows(block), pl.ds(h * width, width)],
                    target.at[s, pl.ds(h * BLK, BLK)],
                    sem.at[s, i, h],
                )

    for s, (block, live, start) in enumerate(slots):
        @pl.when(live)
        def _():
            for copy in copies(s, block):
                copy.start()
    sum_ref[...] = jnp.zeros_like(sum_ref)
    dot_ref[...] = jnp.zeros_like(dot_ref)
    ahead = lax.broadcasted_iota(jnp.int32, (BLK, BLK), 1) - lax.broadcasted_iota(
        jnp.int32, (BLK, BLK), 0
    )
    ready()

    def body(s, block, start):
        for copy in copies(s, block):
            copy.wait()

        def step(k, carry):
            rows = block_rows(k)
            score_pass(kv_ref[0, rows, :], kv_ref[1, rows, :], query_ref, grad_ref, s,
                       ahead >= (k - block) * BLK, weight_ref, prob_ref, (s, rows), sum_ref, dot_ref,
                       scale * math.log2(math.e))
            return carry

        lax.fori_loop(jnp.maximum(start, 0), block + 1, step, 0)

    over_slots(slots, body)


def in_first_half():
    return lax.axis_index("ctx") * 2 < lax.axis_size("ctx")


def local_kernel(sizes, *refs):
    inputs, results = refs[:5], refs[-7:]
    pl.when(jnp.logical_not(in_first_half()))(lambda: local_scores(sizes, *inputs, *results))


def pack_kernel(sizes, key_ref, value_ref, assistant_ref, turn_ref, query_hbm, grad_hbm, last_ref, all_ref,
                assistant, turn_first, need_ref, *state):
    state, pack_sem = state[:-1], state[-1]
    block_count = sizes[0]
    token_count = key_ref.shape[1]
    marks = [
        pltpu.make_async_copy(assistant_ref, assistant, pack_sem.at[0]),
        pltpu.make_async_copy(turn_ref, turn_first, pack_sem.at[1]),
    ]
    copies = []
    for pack in (all_ref, last_ref):
        rows = pack.shape[1]
        for i, source in enumerate((key_ref, value_ref)):
            copies.append(
                pltpu.make_async_copy(
                    source.at[0, pl.ds(token_count - rows, rows)], pack.at[i], pack_sem.at[2 + len(copies)]
                )
            )
    for copy in marks + copies:
        copy.start()
    for copy in marks:
        copy.wait()
    outer = far = jnp.int32(0)
    for i in range(block_count, assistant.shape[1]):
        device = i // block_count
        behind = jnp.where(assistant[0, i] == 1, device * block_count - turn_first[0, i], 0)
        far = jnp.where(behind > block_count, 1, far)
        if device % 2 == 0:
            outer = jnp.maximum(outer, behind)
    need_ref[0] = jnp.where((outer > 1) | (far > 0), 1, 0)

    def ready():
        for copy in copies:
            copy.wait()

    @pl.when(in_first_half())
    def _():
        local_scores(sizes, assistant, turn_first, query_hbm, grad_hbm, all_ref, *state, ready=ready)

    pl.when(jnp.logical_not(in_first_half()))(ready)


def over_window(block_count, reach, start, whole, body):
    first = jnp.maximum(start + reach, 0)
    last = reach
    if whole:
        @pl.when(start <= -block_count)
        def _():
            body(pl.ds((reach - block_count) * BLK, block_count * BLK))

        last = jnp.where(start <= -block_count, reach - block_count, reach)

    def step(k, carry):
        body(block_rows(k))
        return carry

    lax.fori_loop(first, last, step, 0)


def near_kernel(sizes, parity, assistant, turn_first, need, query_ref, grad_ref, far_ref, *rest):
    weight_ref, prob_ref, sum_ref, dot_ref, window, values = rest[-6:]
    block_count, slot_count, head_count, width, scale = sizes
    rank = lax.axis_index("ctx")
    reach = window.shape[0] // BLK
    near = pl.ds((reach - block_count) * BLK, block_count * BLK)

    def fill(rows, source):
        window[rows, :] = source[0]
        values[rows, :] = source[1]

    def body(s, block, start):
        def scores(rows):
            score_pass(window[rows, :], values[rows, :], query_ref, grad_ref, s, None, weight_ref,
                       prob_ref, (s, rows), sum_ref, dot_ref, scale * math.log2(math.e))

        over_window(block_count, reach, start, parity == 1, scores)

    @pl.when(lax.rem(rank, 2) == parity)
    def _():
        if parity == 1:
            fill(near, rest[0])
        else:
            fill(block_rows(reach - 1), rest[0])

        @pl.when(need[0] > 0)
        def _():
            fill(pl.ds(0, far_ref.shape[1]), far_ref)
            if parity == 0:
                fill(near, rest[1])

        sum_ref[...] = jnp.zeros_like(sum_ref)
        dot_ref[...] = jnp.zeros_like(dot_ref)
        over_slots(slots_of(assistant, turn_first, rank * block_count, block_count, slot_count), body)


def remote_kernel(sizes, parity, assistant, turn_first, need, query_ref, grad_ref, sum_local, dot_local,
                  weight_near, prob_near, sum_near, dot_near, *rest):
    block_count, slot_count, head_count, width, scale = sizes
    score_ref, inverse_ref, delta_ref, beyond_out, near_out, low_ref, key_acc, value_acc = rest[-8:]
    rank = lax.axis_index("ctx")
    reach = weight_near.shape[1] // BLK

    def body(s, block, start):
        inverse = 1.0 / jnp.sum(sum_local[s] + sum_near[s], axis=0, keepdims=True)
        delta = jnp.sum(dot_local[s] + dot_near[s], axis=0, keepdims=True) * inverse
        inverse_ref[s] = jnp.broadcast_to(inverse, inverse_ref.shape[1:])
        delta_ref[s] = jnp.broadcast_to(delta, delta_ref.shape[1:])

        def gradients_of(rows):
            grad_pass(weight_near, prob_near, (s, rows), query_ref, grad_ref, s, inverse_ref, delta_ref,
                      low_ref, score_ref, rows, key_acc, value_acc, rows)

        over_window(block_count, reach, start, parity == 1, gradients_of)

    @pl.when(lax.rem(rank, 2) == parity)
    def _():
        key_acc[...] = jnp.zeros_like(key_acc)
        value_acc[...] = jnp.zeros_like(value_acc)
        over_slots(slots_of(assistant, turn_first, rank * block_count, block_count, slot_count), body)

        def round_to(out, first, rows):
            out[0] = (key_acc[first:first + rows, :] * scale).astype(BF16)
            out[1] = value_acc[first:first + rows, :].astype(BF16)

        total = reach * BLK
        round_to(near_out, total - near_out.shape[1], near_out.shape[1])

        @pl.when(need[0] > 0)
        def _():
            round_to(beyond_out, 0, beyond_out.shape[1])


def finish_kernel(sizes, assistant, turn_first, query_ref, grad_ref, weight_ref, prob_ref, score_in,
                  inverse_ref, delta_ref, kv_ref, window, *rest):
    query_hbm, key_acc, value_acc, score_ref, low_ref, query_acc, stage, blank, sem = rest
    block_count, slot_count, head_count, width, scale = sizes
    base = lax.axis_index("ctx") * block_count
    slots = slots_of(assistant, turn_first, base, block_count, slot_count)
    reach = window.shape[0] // BLK
    columns = query_acc.shape[1]
    blank[...] = jnp.zeros_like(blank)

    def blank_copy(i):
        return pltpu.make_async_copy(blank, query_hbm.at[0, pl.ds(i * BLK, BLK)], sem.at[slot_count + i])

    def stage_copy(s, block):
        return pltpu.make_async_copy(stage.at[s], query_hbm.at[0, block_rows(block)], sem.at[s])

    for i in range(block_count):
        @pl.when(assistant[0, base + i] != 1)
        def _():
            blank_copy(i).start()
    key_acc[...] = jnp.zeros_like(key_acc)
    value_acc[...] = jnp.zeros_like(value_acc)

    def body(s, block, start):
        def query_part(keys, source, rows, span):
            return nn_dot(keys.T, source[s, rows, span])

        query_acc[...] = jnp.zeros_like(query_acc)

        def remote_part(rows):
            keys = window[rows, :]
            for c in range(0, columns, CHUNK):
                span = slice(c, c + CHUNK)
                query_acc[:, span] += query_part(keys, score_in, rows, span)

        over_window(block_count, reach, start, True, remote_part)
        low = jnp.maximum(start, 0)
        for count in range(1, block_count + 1):
            @pl.when(block + 1 - low == count)
            def _():
                rows = block_rows(low, count)
                grad_pass(weight_ref, prob_ref, (s, rows), query_ref, grad_ref, s, inverse_ref, delta_ref,
                          low_ref, score_ref, rows, key_acc, value_acc, rows)
                keys = kv_ref[0, rows, :]
                for c in range(0, columns, CHUNK):
                    span = slice(c, c + CHUNK)
                    total = query_acc[:, span] + query_part(keys, score_ref, rows, span)
                    for h in range(0, CHUNK, BLK):
                        place = slice((c + h) // BLK * width, ((c + h) // BLK + 1) * width)
                        stage[s, :, place] = (total[:, h:h + BLK] * scale).T.astype(BF16)

        stage_copy(s, block).start()

    over_slots(slots, body)
    key_acc[...] = key_acc[...] * scale
    for s, (block, live, start) in enumerate(slots):
        @pl.when(live)
        def _():
            stage_copy(s, block).wait()

    for i in range(block_count):
        @pl.when(assistant[0, base + i] != 1)
        def _():
            blank_copy(i).wait()


def add_kernel(far_rows, need, key_in, value_in, outer_ref, rest_ref, far_ref, key_acc, value_acc):
    for i, acc in enumerate((key_acc, value_acc)):
        last = acc.shape[0] - outer_ref.shape[1]
        acc[last:, :] += outer_ref[i].astype(F32)

        @pl.when(need[0] > 0)
        def _():
            acc[:last, :] += rest_ref[i, far_rows:, :].astype(F32)
            acc[acc.shape[0] - far_rows:, :] += far_ref[i].astype(F32)


def total_kernel(key_acc, value_acc, returned, key_out, value_out):
    for i, (acc, out) in enumerate(((key_acc, key_out), (value_acc, value_out))):
        out[0] = (acc[...] + returned[i].astype(F32)).astype(BF16)


def call(kernel, inputs, in_specs, outputs, out_specs, scratch, limit, macs, aliases={},
         traffic=2 * MIB):
    return pl.pallas_call(
        kernel,
        out_shape=outputs,
        in_specs=in_specs,
        out_specs=out_specs,
        scratch_shapes=scratch,
        input_output_aliases=aliases,
        compiler_params=pltpu.CompilerParams(vmem_limit_bytes=limit * MIB),
        cost_estimate=pl.CostEstimate(flops=2 * macs, bytes_accessed=traffic, transcendentals=0),
    )(*inputs)


ANY_SPEC = pl.BlockSpec(memory_space=pl.ANY)
SMEM_SPEC = pl.BlockSpec(memory_space=pltpu.SMEM)
VMEM_SPEC = pl.BlockSpec(memory_space=pltpu.VMEM)


def score_shapes(sizes, rows):
    block_count, slot_count, head_count, width, scale = sizes
    columns = head_count * BLK
    return (
        pltpu.VMEM((slot_count, rows, columns), F32),
        pltpu.VMEM((slot_count, rows, columns), F32),
        pltpu.VMEM((slot_count, SUB, columns), F32),
        pltpu.VMEM((slot_count, SUB, columns), F32),
    )


def local_shapes(sizes):
    block_count, slot_count, head_count, width, scale = sizes
    rows = pltpu.VMEM((slot_count, head_count * BLK, width), BF16)
    return (rows, rows) + score_shapes(sizes, block_count * BLK)


def local_sems(sizes):
    return pltpu.SemaphoreType.DMA((sizes[1], 2, sizes[2]))


def skip_kernel(*refs):
    pass


def rarely(need, exchange, operands, shapes):
    def skipped(*operands):
        return call(skip_kernel, (), [], tuple(pltpu.VMEM(s, BF16) for s in shapes),
                    [VMEM_SPEC] * len(shapes), [], 8, 1, {}, 1)

    return tuple(lax.switch(need[0], [skipped, lambda *operands: tuple(exchange(*operands))], *operands))


def per_device(query_rows, key_rows, value_rows, out_grad, assistant, turn_first):
    token_count = query_rows.shape[1]
    width = key_rows.shape[2]
    head_count = query_rows.shape[2] // width
    block_count = token_count // BLK
    far_rows = block_count // 2 * BLK
    reach_rows = token_count + far_rows
    slot_count = (block_count + 1) // 2
    columns = head_count * BLK
    pair = columns * BLK * width
    sizes = (block_count, slot_count, head_count, width, 1.0 / math.sqrt(width))
    stat_rows = (slot_count, SUB, columns)
    last, own, assistant, turn_first, need, *local_state = call(
        lambda *refs: pack_kernel(sizes, *refs),
        tuple(hbm(a) for a in (key_rows, value_rows, assistant, turn_first, query_rows, out_grad)),
        [ANY_SPEC] * 6,
        (
            pltpu.VMEM((2, far_rows, width), BF16),
            pltpu.VMEM((2, token_count, width), BF16),
            pltpu.SMEM(assistant.shape, jnp.int32),
            pltpu.SMEM(turn_first.shape, jnp.int32),
            pltpu.SMEM((1,), jnp.int32),
        )
        + local_shapes(sizes),
        [VMEM_SPEC] * 2 + [SMEM_SPEC] * 3 + [VMEM_SPEC] * 6,
        [local_sems(sizes), pltpu.SemaphoreType.DMA((6,))],
        16,
        10 * pair,
    )
    marks = (smem(assistant), smem(turn_first))
    flag = smem(need)
    outer_in = pair_shift(last, "ctx", 1, 0)
    inner_in = pair_shift(own, "ctx", 1, 1)
    local_state = call(
        lambda *refs: local_kernel(sizes, *refs),
        marks + (hbm(query_rows), hbm(out_grad), vmem(own)) + tuple(vmem(a) for a in local_state),
        [SMEM_SPEC] * 2 + [ANY_SPEC] * 2 + [VMEM_SPEC] * 7,
        local_shapes(sizes),
        [VMEM_SPEC] * 6,
        [local_sems(sizes)],
        16,
        pair,
        {5 + i: i for i in range(6)},
    )
    far_source, whole_source, local_state = lax.optimization_barrier((last, own, local_state))
    far_in, whole_in = rarely(
        need,
        lambda far, whole: (shifted(far, "ctx", 2), pair_shift(whole, "ctx", 1, 0)),
        (far_source, whole_source),
        [far_source.shape, whole_source.shape],
    )
    query_slots, grad_slots, weights, prob_grad, sums, dots = local_state
    window = remote_state = ()
    near_grads = []
    for parity, sources in ((0, (outer_in, whole_in)), (1, (inner_in,))):
        *near_state, window = call(
            lambda *refs: near_kernel(sizes, parity, *refs),
            marks + (flag,)
            + tuple(vmem(a) for a in (query_slots, grad_slots, far_in) + sources + window),
            [SMEM_SPEC] * 3 + [VMEM_SPEC] * (3 + len(sources) + len(window)),
            score_shapes(sizes, reach_rows) + (pltpu.VMEM((reach_rows, width), BF16),),
            [VMEM_SPEC] * 5,
            [pltpu.VMEM((reach_rows, width), BF16)],
            16,
            NEAR_HINT[parity] * pair,
            {6 + len(sources): 4} if window else {},
            1,
        )
        window = (window,)
        inputs = (query_slots, grad_slots, sums, dots) + tuple(near_state)
        *remote_state, near_grad = call(
            lambda *refs: remote_kernel(sizes, parity, *refs),
            marks + (flag,) + tuple(vmem(a) for a in inputs + tuple(remote_state)),
            [SMEM_SPEC] * 3 + [VMEM_SPEC] * (len(inputs) + len(remote_state)),
            (
                pltpu.VMEM((slot_count, reach_rows, columns), BF16),
                pltpu.VMEM(stat_rows, F32),
                pltpu.VMEM(stat_rows, F32),
                pltpu.VMEM((2, token_count, width), BF16),
                pltpu.VMEM((2, sources[0].shape[1], width), BF16),
            ),
            [VMEM_SPEC] * 5,
            [
                pltpu.VMEM((token_count, columns), BF16),
                pltpu.VMEM((reach_rows, width), F32),
                pltpu.VMEM((reach_rows, width), F32),
            ],
            20,
            REMOTE_HINT[parity] * pair,
            {3 + len(inputs) + i: i for i in range(len(remote_state))},
            1,
        )
        near_grads.append(pair_shift(near_grad, "ctx", -1, parity))
    score_grad, inverse, delta, beyond = remote_state
    outer_back, inner_back = near_grads
    query_grad, key_acc, value_acc = call(
        lambda *refs: finish_kernel(sizes, *refs),
        marks
        + tuple(
            vmem(a)
            for a in (query_slots, grad_slots, weights, prob_grad, score_grad, inverse, delta, own) + window
        ),
        [SMEM_SPEC] * 2 + [VMEM_SPEC] * 9,
        (
            jax.ShapeDtypeStruct(query_rows.shape, BF16),
            pltpu.VMEM((token_count, width), F32),
            pltpu.VMEM((token_count, width), F32),
        ),
        [ANY_SPEC] + [VMEM_SPEC] * 2,
        [
            pltpu.VMEM((slot_count, token_count, columns), BF16),
            pltpu.VMEM((token_count, columns), BF16),
            pltpu.VMEM((BLK, columns), F32),
            pltpu.VMEM((slot_count, BLK, head_count * width), BF16),
            pltpu.VMEM((BLK, head_count * width), BF16),
            pltpu.SemaphoreType.DMA((slot_count + block_count,)),
        ],
        16,
        pair,
        {},
        1,
    )
    beyond, key_acc, value_acc = lax.optimization_barrier((beyond, key_acc, value_acc))
    rest_back, far_back = rarely(
        need,
        lambda beyond: (
            pair_shift(beyond, "ctx", -1, 0),
            shifted(beyond[:, :far_rows], "ctx", -2),
        ),
        (beyond,),
        [beyond.shape, far_in.shape],
    )
    key_acc, value_acc = call(
        lambda *refs: add_kernel(far_rows, *refs),
        (flag,) + tuple(vmem(a) for a in (key_acc, value_acc, outer_back, rest_back, far_back)),
        [SMEM_SPEC] + [VMEM_SPEC] * 5,
        (pltpu.VMEM((token_count, width), F32),) * 2,
        [VMEM_SPEC] * 2,
        [],
        8,
        CROSS_HINT * pair,
        {1: 0, 2: 1},
        1,
    )
    key_grad, value_grad = call(
        total_kernel,
        tuple(vmem(a) for a in (key_acc, value_acc, inner_back)),
        [VMEM_SPEC] * 3,
        (jax.ShapeDtypeStruct(key_rows.shape, BF16), jax.ShapeDtypeStruct(value_rows.shape, BF16)),
        [VMEM_SPEC] * 2,
        [],
        8,
        BLK,
    )
    return (query_grad, key_grad, value_grad)


def solution(mesh):
    return jax.shard_map(
        per_device,
        mesh=mesh,
        in_specs=(
            P("dp", "ctx", "tp"),
            P("dp", "ctx", "tp"),
            P("dp", "ctx", "tp"),
            P("dp", "ctx", "tp"),
            P("dp", None),
            P("dp", None),
        ),
        out_specs=(P("dp", "ctx", "tp"), P("dp", "ctx", "tp"), P("dp", "ctx", "tp")),
        check_vma=False,
    )
```

```python
import math

import jax
import jax.numpy as jnp
from jax import lax
from jax.experimental import pallas as pl
from jax.experimental.pallas import tpu as pltpu
from jax.sharding import PartitionSpec as P

BLK = 128
SUB = 8
CHUNK = 256
F32 = jnp.float32
BF16 = jnp.bfloat16
MIB = 1 << 20
NEAR_HINT = (400, 10)
REMOTE_HINT = (14, 14)
CROSS_HINT = 60


def shifted(block, axis, distance):
    devices = range(lax.axis_size(axis))
    route = [(i - distance, i) for i in devices if i - distance in devices]
    return lax.ppermute(block, axis, route)


def pair_shift(block, axis, distance, parity):
    pairs = [(i - 1, i) for i in range(1, lax.axis_size(axis)) if i % 2 == parity]
    return lax.ppermute(block, axis, pairs if distance == 1 else [pair[::-1] for pair in pairs])


def vmem(array):
    return pltpu.with_memory_space_constraint(array, pltpu.VMEM)


def smem(array):
    return pltpu.with_memory_space_constraint(array, pltpu.SMEM)


def hbm(array):
    return pltpu.with_memory_space_constraint(array, pltpu.HBM)


def nt_dot(left, right):
    return lax.dot_general(left, right, (((1,), (1,)), ((), ())), preferred_element_type=F32)


def nn_dot(left, right):
    return lax.dot_general(left, right, (((1,), (0,)), ((), ())), preferred_element_type=F32)


def fold(tile):
    return jnp.sum(tile.reshape(tile.shape[0] // SUB, SUB, tile.shape[1]), axis=0)


def slots_of(assistant, turn_first, base, block_count, slot_count):
    found = jnp.int32(0)
    blocks = [jnp.int32(0)] * slot_count
    starts = [jnp.int32(0)] * slot_count
    for i in range(block_count):
        mark = assistant[0, base + i]
        start = turn_first[0, base + i] - base
        for s in range(slot_count):
            here = (mark == 1) & (found == s)
            blocks[s] = jnp.where(here, i, blocks[s])
            starts[s] = jnp.where(here, start, starts[s])
        found = found + jnp.where(mark == 1, 1, 0)
    return [(blocks[s], found > s, starts[s]) for s in range(slot_count)]


def score_pass(key_tile, value_tile, query_ref, grad_ref, slot, keep, weight_ref, prob_ref, at, sum_ref,
               dot_ref, scale):
    columns = query_ref.shape[1]
    for c in range(0, columns, CHUNK):
        span = slice(c, c + CHUNK)
        scores = nt_dot(key_tile, query_ref[slot, span, :])
        prob_grad = nt_dot(value_tile, grad_ref[slot, span, :])
        weights = jnp.exp2(scores * scale)
        if keep is not None:
            weights = jnp.where(jnp.concatenate([keep] * (CHUNK // BLK), axis=1), weights, 0.0)
        weight_ref[at + (span,)] = weights
        prob_ref[at + (span,)] = prob_grad
        sum_ref[slot, :, span] += fold(weights)
        dot_ref[slot, :, span] += fold(weights * prob_grad)


def grad_pass(weight_ref, prob_ref, at, query_ref, grad_ref, slot, inverse_ref, delta_ref, low_ref,
              score_ref, score_rows, key_acc, value_acc, acc_rows):
    columns = query_ref.shape[1]
    height = acc_rows.size
    for c in range(0, columns, CHUNK):
        span = slice(c, c + CHUNK)
        shape = (height // SUB, SUB, CHUNK)
        attention = weight_ref[at + (span,)].reshape(shape) * inverse_ref[slot, :, span][None]
        lifted = prob_ref[at + (span,)].reshape(shape) - delta_ref[slot, :, span][None]
        score_grad = (attention * lifted).reshape(height, CHUNK)
        low_ref[:height, span] = attention.reshape(height, CHUNK).astype(BF16)
        score_ref[slot, score_rows, span] = score_grad.astype(BF16)
    value_acc[acc_rows, :] += nn_dot(low_ref[:height], grad_ref[slot])
    key_acc[acc_rows, :] += nn_dot(score_ref[slot, score_rows, :], query_ref[slot])


def block_rows(index, count=1):
    return pl.ds(pl.multiple_of(index * BLK, BLK), count * BLK)


def pick(values, s):
    chosen = values[0]
    for i in range(1, len(values)):
        chosen = jnp.where(s == i, values[i], chosen)
    return chosen


def over_slots(slots, body):
    def step(s, carry):
        block, start = (pick([slot[i] for slot in slots], s) for i in (0, 2))

        @pl.when(pick([jnp.where(slot[1], 1, 0) for slot in slots], s) == 1)
        def _():
            body(s, block, start)

        return carry

    lax.fori_loop(0, len(slots), step, 0)


def local_scores(sizes, assistant, turn_first, query_hbm, grad_hbm, kv_ref, query_ref, grad_ref,
                 weight_ref, prob_ref, sum_ref, dot_ref, sem, ready=lambda: None):
    block_count, slot_count, head_count, width, scale = sizes
    base = lax.axis_index("ctx") * block_count
    slots = slots_of(assistant, turn_first, base, block_count, slot_count)

    def copies(s, block):
        for i, (source, target) in enumerate(((query_hbm, query_ref), (grad_hbm, grad_ref))):
            for h in range(head_count):
                yield pltpu.make_async_copy(
                    source.at[0, block_rows(block), pl.ds(h * width, width)],
                    target.at[s, pl.ds(h * BLK, BLK)],
                    sem.at[s, i, h],
                )

    for s, (block, live, start) in enumerate(slots):
        @pl.when(live)
        def _():
            for copy in copies(s, block):
                copy.start()
    sum_ref[...] = jnp.zeros_like(sum_ref)
    dot_ref[...] = jnp.zeros_like(dot_ref)
    ahead = lax.broadcasted_iota(jnp.int32, (BLK, BLK), 1) - lax.broadcasted_iota(
        jnp.int32, (BLK, BLK), 0
    )
    ready()

    def body(s, block, start):
        for copy in copies(s, block):
            copy.wait()

        def step(k, carry):
            rows = block_rows(k)
            score_pass(kv_ref[0, rows, :], kv_ref[1, rows, :], query_ref, grad_ref, s,
                       ahead >= (k - block) * BLK, weight_ref, prob_ref, (s, rows), sum_ref, dot_ref,
                       scale * math.log2(math.e))
            return carry

        lax.fori_loop(jnp.maximum(start, 0), block + 1, step, 0)

    over_slots(slots, body)


def in_first_half():
    return lax.axis_index("ctx") * 2 < lax.axis_size("ctx")


def local_kernel(sizes, *refs):
    inputs, results = refs[:5], refs[-7:]
    pl.when(jnp.logical_not(in_first_half()))(lambda: local_scores(sizes, *inputs, *results))


def pack_kernel(sizes, key_ref, value_ref, assistant_ref, turn_ref, query_hbm, grad_hbm, last_ref, all_ref,
                assistant, turn_first, need_ref, *state):
    state, pack_sem = state[:-1], state[-1]
    block_count = sizes[0]
    token_count = key_ref.shape[1]
    marks = [
        pltpu.make_async_copy(assistant_ref, assistant, pack_sem.at[0]),
        pltpu.make_async_copy(turn_ref, turn_first, pack_sem.at[1]),
    ]
    copies = []
    for pack in (all_ref, last_ref):
        rows = pack.shape[1]
        for i, source in enumerate((key_ref, value_ref)):
            copies.append(
                pltpu.make_async_copy(
                    source.at[0, pl.ds(token_count - rows, rows)], pack.at[i], pack_sem.at[2 + len(copies)]
                )
            )
    for copy in marks + copies:
        copy.start()
    for copy in marks:
        copy.wait()
    outer = far = jnp.int32(0)
    for i in range(block_count, assistant.shape[1]):
        device = i // block_count
        behind = jnp.where(assistant[0, i] == 1, device * block_count - turn_first[0, i], 0)
        far = jnp.where(behind > block_count, 1, far)
        if device % 2 == 0:
            outer = jnp.maximum(outer, behind)
    need_ref[0] = jnp.where((outer > 1) | (far > 0), 1, 0)

    def ready():
        for copy in copies:
            copy.wait()

    @pl.when(in_first_half())
    def _():
        local_scores(sizes, assistant, turn_first, query_hbm, grad_hbm, all_ref, *state, ready=ready)

    pl.when(jnp.logical_not(in_first_half()))(ready)


def over_window(block_count, reach, start, whole, body):
    first = jnp.maximum(start + reach, 0)
    last = reach
    if whole:
        @pl.when(start <= -block_count)
        def _():
            body(pl.ds((reach - block_count) * BLK, block_count * BLK))

        last = jnp.where(start <= -block_count, reach - block_count, reach)

    def step(k, carry):
        body(block_rows(k))
        return carry

    lax.fori_loop(first, last, step, 0)


def near_kernel(sizes, parity, assistant, turn_first, need, query_ref, grad_ref, far_hbm, *rest):
    weight_ref, prob_ref, sum_ref, dot_ref, window, values, sem = rest[-7:]
    block_count, slot_count, head_count, width, scale = sizes
    rank = lax.axis_index("ctx")
    reach = window.shape[0] // BLK
    near = pl.ds((reach - block_count) * BLK, block_count * BLK)

    def fill(rows, source):
        window[rows, :] = source[0]
        values[rows, :] = source[1]

    def fetch(rows, source, first_sem):
        return [
            pltpu.make_async_copy(source.at[i], target.at[rows], sem.at[first_sem + i])
            for i, target in enumerate((window, values))
        ]

    def body(s, block, start):
        def scores(rows):
            score_pass(window[rows, :], values[rows, :], query_ref, grad_ref, s, None, weight_ref,
                       prob_ref, (s, rows), sum_ref, dot_ref, scale * math.log2(math.e))

        over_window(block_count, reach, start, parity == 1, scores)

    @pl.when(lax.rem(rank, 2) == parity)
    def _():
        if parity == 1:
            fill(near, rest[0])
        else:
            fill(block_rows(reach - 1), rest[0])

        @pl.when(need[0] > 0)
        def _():
            copies = fetch(pl.ds(0, far_hbm.shape[1]), far_hbm, 0)
            if parity == 0:
                copies += fetch(near, rest[1], 2)
            for copy in copies:
                copy.start()
            for copy in copies:
                copy.wait()

        sum_ref[...] = jnp.zeros_like(sum_ref)
        dot_ref[...] = jnp.zeros_like(dot_ref)
        over_slots(slots_of(assistant, turn_first, rank * block_count, block_count, slot_count), body)


def remote_kernel(sizes, parity, assistant, turn_first, need, query_ref, grad_ref, sum_local, dot_local,
                  weight_near, prob_near, sum_near, dot_near, *rest):
    block_count, slot_count, head_count, width, scale = sizes
    (score_ref, inverse_ref, delta_ref, beyond_hbm, *_, near_out, low_ref, key_acc, value_acc, beyond) = (
        rest[-11 + 2 * parity:]
    )
    rank = lax.axis_index("ctx")
    reach = weight_near.shape[1] // BLK

    def body(s, block, start):
        inverse = 1.0 / jnp.sum(sum_local[s] + sum_near[s], axis=0, keepdims=True)
        delta = jnp.sum(dot_local[s] + dot_near[s], axis=0, keepdims=True) * inverse
        inverse_ref[s] = jnp.broadcast_to(inverse, inverse_ref.shape[1:])
        delta_ref[s] = jnp.broadcast_to(delta, delta_ref.shape[1:])

        def gradients_of(rows):
            grad_pass(weight_near, prob_near, (s, rows), query_ref, grad_ref, s, inverse_ref, delta_ref,
                      low_ref, score_ref, rows, key_acc, value_acc, rows)

        over_window(block_count, reach, start, parity == 1, gradients_of)

    @pl.when(lax.rem(rank, 2) == parity)
    def _():
        key_acc[...] = jnp.zeros_like(key_acc)
        value_acc[...] = jnp.zeros_like(value_acc)
        over_slots(slots_of(assistant, turn_first, rank * block_count, block_count, slot_count), body)

        def round_to(out, first, rows):
            out[0] = (key_acc[first:first + rows, :] * scale).astype(BF16)
            out[1] = value_acc[first:first + rows, :].astype(BF16)

        total = reach * BLK
        round_to(near_out, total - near_out.shape[1], near_out.shape[1])

        @pl.when(need[0] > 0)
        def _():
            round_to(beyond, 0, beyond.shape[1])
            pltpu.sync_copy(beyond, beyond_hbm)


def finish_kernel(sizes, assistant, turn_first, query_ref, grad_ref, weight_ref, prob_ref, score_in,
                  inverse_ref, delta_ref, kv_ref, window, *rest):
    query_hbm, key_acc, value_acc, score_ref, low_ref, query_acc, stage, blank, sem = rest
    block_count, slot_count, head_count, width, scale = sizes
    base = lax.axis_index("ctx") * block_count
    slots = slots_of(assistant, turn_first, base, block_count, slot_count)
    reach = window.shape[0] // BLK
    columns = query_acc.shape[1]
    blank[...] = jnp.zeros_like(blank)

    def blank_copy(i):
        return pltpu.make_async_copy(blank, query_hbm.at[0, pl.ds(i * BLK, BLK)], sem.at[slot_count + i])

    def stage_copy(s, block):
        return pltpu.make_async_copy(stage.at[s], query_hbm.at[0, block_rows(block)], sem.at[s])

    for i in range(block_count):
        @pl.when(assistant[0, base + i] != 1)
        def _():
            blank_copy(i).start()
    key_acc[...] = jnp.zeros_like(key_acc)
    value_acc[...] = jnp.zeros_like(value_acc)

    def body(s, block, start):
        def query_part(keys, source, rows, span):
            return nn_dot(keys.T, source[s, rows, span])

        query_acc[...] = jnp.zeros_like(query_acc)

        def remote_part(rows):
            keys = window[rows, :]
            for c in range(0, columns, CHUNK):
                span = slice(c, c + CHUNK)
                query_acc[:, span] += query_part(keys, score_in, rows, span)

        over_window(block_count, reach, start, True, remote_part)
        low = jnp.maximum(start, 0)
        for count in range(1, block_count + 1):
            @pl.when(block + 1 - low == count)
            def _():
                rows = block_rows(low, count)
                grad_pass(weight_ref, prob_ref, (s, rows), query_ref, grad_ref, s, inverse_ref, delta_ref,
                          low_ref, score_ref, rows, key_acc, value_acc, rows)
                keys = kv_ref[0, rows, :]
                for c in range(0, columns, CHUNK):
                    span = slice(c, c + CHUNK)
                    total = query_acc[:, span] + query_part(keys, score_ref, rows, span)
                    for h in range(0, CHUNK, BLK):
                        place = slice((c + h) // BLK * width, ((c + h) // BLK + 1) * width)
                        stage[s, :, place] = (total[:, h:h + BLK] * scale).T.astype(BF16)

        stage_copy(s, block).start()

    over_slots(slots, body)
    key_acc[...] = key_acc[...] * scale
    for s, (block, live, start) in enumerate(slots):
        @pl.when(live)
        def _():
            stage_copy(s, block).wait()

    for i in range(block_count):
        @pl.when(assistant[0, base + i] != 1)
        def _():
            blank_copy(i).wait()


def add_kernel(far_rows, need, key_in, value_in, outer_ref, rest_hbm, far_hbm, key_acc, value_acc, rest, far):
    for i, acc in enumerate((key_acc, value_acc)):
        last = acc.shape[0] - outer_ref.shape[1]
        acc[last:, :] += outer_ref[i].astype(F32)

    @pl.when(need[0] > 0)
    def _():
        pltpu.sync_copy(rest_hbm, rest)
        pltpu.sync_copy(far_hbm, far)
        for i, acc in enumerate((key_acc, value_acc)):
            last = acc.shape[0] - outer_ref.shape[1]
            acc[:last, :] += rest[i, far_rows:, :].astype(F32)
            acc[acc.shape[0] - far_rows:, :] += far[i].astype(F32)


def total_kernel(key_acc, value_acc, returned, key_out, value_out):
    for i, (acc, out) in enumerate(((key_acc, key_out), (value_acc, value_out))):
        out[0] = (acc[...] + returned[i].astype(F32)).astype(BF16)


def call(kernel, inputs, in_specs, outputs, out_specs, scratch, limit, macs, aliases={},
         traffic=2 * MIB):
    return pl.pallas_call(
        kernel,
        out_shape=outputs,
        in_specs=in_specs,
        out_specs=out_specs,
        scratch_shapes=scratch,
        input_output_aliases=aliases,
        compiler_params=pltpu.CompilerParams(vmem_limit_bytes=limit * MIB),
        cost_estimate=pl.CostEstimate(flops=2 * macs, bytes_accessed=traffic, transcendentals=0),
    )(*inputs)


ANY_SPEC = pl.BlockSpec(memory_space=pl.ANY)
SMEM_SPEC = pl.BlockSpec(memory_space=pltpu.SMEM)
VMEM_SPEC = pl.BlockSpec(memory_space=pltpu.VMEM)


def score_shapes(sizes, rows):
    block_count, slot_count, head_count, width, scale = sizes
    columns = head_count * BLK
    return (
        pltpu.VMEM((slot_count, rows, columns), F32),
        pltpu.VMEM((slot_count, rows, columns), F32),
        pltpu.VMEM((slot_count, SUB, columns), F32),
        pltpu.VMEM((slot_count, SUB, columns), F32),
    )


def local_shapes(sizes):
    block_count, slot_count, head_count, width, scale = sizes
    rows = pltpu.VMEM((slot_count, head_count * BLK, width), BF16)
    return (rows, rows) + score_shapes(sizes, block_count * BLK)


def local_sems(sizes):
    return pltpu.SemaphoreType.DMA((sizes[1], 2, sizes[2]))


def skip_kernel(*refs):
    pass


def rarely(need, exchange, operands, shapes):
    def skipped(*operands):
        return call(skip_kernel, (), [], tuple(jax.ShapeDtypeStruct(s, BF16) for s in shapes),
                    [ANY_SPEC] * len(shapes), [], 4, 1, {}, 1)

    return tuple(lax.switch(need[0], [skipped, lambda *operands: tuple(exchange(*operands))], *operands))


def per_device(query_rows, key_rows, value_rows, out_grad, assistant, turn_first):
    token_count = query_rows.shape[1]
    width = key_rows.shape[2]
    head_count = query_rows.shape[2] // width
    block_count = token_count // BLK
    far_rows = block_count // 2 * BLK
    reach_rows = token_count + far_rows
    slot_count = (block_count + 1) // 2
    columns = head_count * BLK
    pair = columns * BLK * width
    sizes = (block_count, slot_count, head_count, width, 1.0 / math.sqrt(width))
    stat_rows = (slot_count, SUB, columns)
    last, own, assistant, turn_first, need, *local_state = call(
        lambda *refs: pack_kernel(sizes, *refs),
        tuple(hbm(a) for a in (key_rows, value_rows, assistant, turn_first, query_rows, out_grad)),
        [ANY_SPEC] * 6,
        (
            pltpu.VMEM((2, far_rows, width), BF16),
            pltpu.VMEM((2, token_count, width), BF16),
            pltpu.SMEM(assistant.shape, jnp.int32),
            pltpu.SMEM(turn_first.shape, jnp.int32),
            pltpu.SMEM((1,), jnp.int32),
        )
        + local_shapes(sizes),
        [VMEM_SPEC] * 2 + [SMEM_SPEC] * 3 + [VMEM_SPEC] * 6,
        [local_sems(sizes), pltpu.SemaphoreType.DMA((6,))],
        8,
        10 * pair,
    )
    marks = (smem(assistant), smem(turn_first))
    flag = smem(need)
    outer_in = pair_shift(last, "ctx", 1, 0)
    inner_in = pair_shift(own, "ctx", 1, 1)
    local_state = call(
        lambda *refs: local_kernel(sizes, *refs),
        marks + (hbm(query_rows), hbm(out_grad), vmem(own)) + tuple(vmem(a) for a in local_state),
        [SMEM_SPEC] * 2 + [ANY_SPEC] * 2 + [VMEM_SPEC] * 7,
        local_shapes(sizes),
        [VMEM_SPEC] * 6,
        [local_sems(sizes)],
        8,
        pair,
        {5 + i: i for i in range(6)},
    )
    key_source, value_source, local_state = lax.optimization_barrier((key_rows, value_rows, local_state))

    def exchange(keys, values):
        whole = jnp.stack([keys[0], values[0]])
        return shifted(whole[:, token_count - far_rows:], "ctx", 2), pair_shift(whole, "ctx", 1, 0)

    far_in, whole_in = rarely(
        need,
        exchange,
        (key_source, value_source),
        [(2, far_rows, width), (2, token_count, width)],
    )
    query_slots, grad_slots, weights, prob_grad, sums, dots = local_state
    near_state = window = remote_state = ()
    near_grads = []
    for parity, sources in ((0, (vmem(outer_in), hbm(whole_in))), (1, (vmem(inner_in),))):
        inputs = marks + (flag, vmem(query_slots), vmem(grad_slots), hbm(far_in)) + sources
        kept = tuple(vmem(a) for a in tuple(near_state) + window)
        *near_state, sum_near, dot_near, window = call(
            lambda *refs: near_kernel(sizes, parity, *refs),
            inputs + kept,
            [SMEM_SPEC] * 3 + [VMEM_SPEC] * 2 + [ANY_SPEC, VMEM_SPEC]
            + [ANY_SPEC] * (len(sources) - 1) + [VMEM_SPEC] * len(kept),
            score_shapes(sizes, reach_rows) + (pltpu.VMEM((reach_rows, width), BF16),),
            [VMEM_SPEC] * 5,
            [pltpu.VMEM((reach_rows, width), BF16), pltpu.SemaphoreType.DMA((4,))],
            8,
            NEAR_HINT[parity] * pair,
            {len(inputs) + i: i if i < 2 else 4 for i in range(len(kept))},
            1,
        )
        window = (window,)
        inputs = marks + (flag,) + tuple(vmem(a) for a in (query_slots, grad_slots, sums, dots))
        near_inputs = tuple(vmem(a) for a in tuple(near_state) + (sum_near, dot_near))
        kept = tuple(vmem(a) for a in remote_state[:3]) + tuple(hbm(a) for a in remote_state[3:])
        score_arrays = score_shapes(sizes, reach_rows)[:2] if parity == 0 else ()
        aliases = {len(inputs) + 4 + i: i for i in range(len(kept))}
        aliases.update({len(inputs) + i: 4 + i for i in range(len(score_arrays))})
        *remote_state, near_grad = call(
            lambda *refs: remote_kernel(sizes, parity, *refs),
            inputs + near_inputs + kept,
            [SMEM_SPEC] * 3 + [VMEM_SPEC] * (8 + len(kept[:3])) + [ANY_SPEC] * len(kept[3:]),
            (
                pltpu.VMEM((slot_count, reach_rows, columns), BF16),
                pltpu.VMEM(stat_rows, F32),
                pltpu.VMEM(stat_rows, F32),
                jax.ShapeDtypeStruct((2, token_count, width), BF16),
            )
            + score_arrays
            + (pltpu.VMEM((2, sources[0].shape[1], width), BF16),),
            [VMEM_SPEC] * 3 + [ANY_SPEC] + [VMEM_SPEC] * (1 + len(score_arrays)),
            [
                pltpu.VMEM((token_count, columns), BF16),
                pltpu.VMEM((reach_rows, width), F32),
                pltpu.VMEM((reach_rows, width), F32),
                pltpu.VMEM((2, token_count, width), BF16),
            ],
            8,
            REMOTE_HINT[parity] * pair,
            aliases,
            1,
        )
        near_state = remote_state[4:]
        remote_state = tuple(remote_state[:4])
        near_grads.append(pair_shift(near_grad, "ctx", -1, parity))
    score_grad, inverse, delta, beyond = remote_state
    outer_back, inner_back = near_grads
    query_grad, key_acc, value_acc = call(
        lambda *refs: finish_kernel(sizes, *refs),
        marks
        + tuple(
            vmem(a)
            for a in (query_slots, grad_slots, weights, prob_grad, score_grad, inverse, delta, own) + window
        ),
        [SMEM_SPEC] * 2 + [VMEM_SPEC] * 9,
        (
            jax.ShapeDtypeStruct(query_rows.shape, BF16),
            pltpu.VMEM((token_count, width), F32),
            pltpu.VMEM((token_count, width), F32),
        ),
        [ANY_SPEC] + [VMEM_SPEC] * 2,
        [
            pltpu.VMEM((slot_count, token_count, columns), BF16),
            pltpu.VMEM((token_count, columns), BF16),
            pltpu.VMEM((BLK, columns), F32),
            pltpu.VMEM((slot_count, BLK, head_count * width), BF16),
            pltpu.VMEM((BLK, head_count * width), BF16),
            pltpu.SemaphoreType.DMA((slot_count + block_count,)),
        ],
        10,
        pair,
        {},
        1,
    )
    beyond, query_grad = lax.optimization_barrier((beyond, query_grad))
    rest_back, far_back = rarely(
        need,
        lambda beyond: (
            pair_shift(beyond, "ctx", -1, 0),
            shifted(beyond[:, :far_rows], "ctx", -2),
        ),
        (beyond,),
        [beyond.shape, far_in.shape],
    )
    key_acc, value_acc = call(
        lambda *refs: add_kernel(far_rows, *refs),
        (flag,) + tuple(vmem(a) for a in (key_acc, value_acc, outer_back)) + (hbm(rest_back), hbm(far_back)),
        [SMEM_SPEC] + [VMEM_SPEC] * 3 + [ANY_SPEC] * 2,
        (pltpu.VMEM((token_count, width), F32),) * 2,
        [VMEM_SPEC] * 2,
        [pltpu.VMEM(beyond.shape, BF16), pltpu.VMEM(far_in.shape, BF16)],
        4,
        CROSS_HINT * pair,
        {1: 0, 2: 1},
        1,
    )
    key_grad, value_grad = call(
        total_kernel,
        tuple(vmem(a) for a in (key_acc, value_acc, inner_back)),
        [VMEM_SPEC] * 3,
        (jax.ShapeDtypeStruct(key_rows.shape, BF16), jax.ShapeDtypeStruct(value_rows.shape, BF16)),
        [VMEM_SPEC] * 2,
        [],
        8,
        BLK,
    )
    return (query_grad, key_grad, value_grad)


def solution(mesh):
    return jax.shard_map(
        per_device,
        mesh=mesh,
        in_specs=(
            P("dp", "ctx", "tp"),
            P("dp", "ctx", "tp"),
            P("dp", "ctx", "tp"),
            P("dp", "ctx", "tp"),
            P("dp", None),
            P("dp", None),
        ),
        out_specs=(P("dp", "ctx", "tp"), P("dp", "ctx", "tp"), P("dp", "ctx", "tp")),
        check_vma=False,
    )
```

```python
import math

import jax
import jax.numpy as jnp
from jax import lax
from jax.experimental import pallas as pl
from jax.experimental.pallas import tpu as pltpu
from jax.sharding import PartitionSpec as P

BLK = 128
SUB = 8
CHUNK = 256
F32 = jnp.float32
BF16 = jnp.bfloat16
MIB = 1 << 20
NEAR_HINT = (400, 10)
REMOTE_HINT = (14, 14)
CROSS_HINT = 60


def shifted(block, axis, distance):
    devices = range(lax.axis_size(axis))
    route = [(i - distance, i) for i in devices if i - distance in devices]
    return lax.ppermute(block, axis, route)


def pair_shift(block, axis, distance, parity):
    pairs = [(i - 1, i) for i in range(1, lax.axis_size(axis)) if i % 2 == parity]
    return lax.ppermute(block, axis, pairs if distance == 1 else [pair[::-1] for pair in pairs])


def vmem(array):
    return pltpu.with_memory_space_constraint(array, pltpu.VMEM)


def smem(array):
    return pltpu.with_memory_space_constraint(array, pltpu.SMEM)


def hbm(array):
    return pltpu.with_memory_space_constraint(array, pltpu.HBM)


def nt_dot(left, right):
    return lax.dot_general(left, right, (((1,), (1,)), ((), ())), preferred_element_type=F32)


def nn_dot(left, right):
    return lax.dot_general(left, right, (((1,), (0,)), ((), ())), preferred_element_type=F32)


def fold(tile):
    return jnp.sum(tile.reshape(tile.shape[0] // SUB, SUB, tile.shape[1]), axis=0)


def slots_of(assistant, turn_first, base, block_count, slot_count):
    found = jnp.int32(0)
    blocks = [jnp.int32(0)] * slot_count
    starts = [jnp.int32(0)] * slot_count
    for i in range(block_count):
        mark = assistant[0, base + i]
        start = turn_first[0, base + i] - base
        for s in range(slot_count):
            here = (mark == 1) & (found == s)
            blocks[s] = jnp.where(here, i, blocks[s])
            starts[s] = jnp.where(here, start, starts[s])
        found = found + jnp.where(mark == 1, 1, 0)
    return [(blocks[s], found > s, starts[s]) for s in range(slot_count)]


def score_pass(key_tile, value_tile, query_ref, grad_ref, slot, keep, weight_ref, prob_ref, at, sum_ref,
               dot_ref, scale):
    columns = query_ref.shape[1]
    for c in range(0, columns, CHUNK):
        span = slice(c, c + CHUNK)
        scores = nt_dot(key_tile, query_ref[slot, span, :])
        prob_grad = nt_dot(value_tile, grad_ref[slot, span, :])
        weights = jnp.exp2(scores * scale)
        if keep is not None:
            weights = jnp.where(jnp.concatenate([keep] * (CHUNK // BLK), axis=1), weights, 0.0)
        weight_ref[at + (span,)] = weights
        prob_ref[at + (span,)] = prob_grad
        sum_ref[slot, :, span] += fold(weights)
        dot_ref[slot, :, span] += fold(weights * prob_grad)


def grad_pass(weight_ref, prob_ref, at, query_ref, grad_ref, slot, inverse_ref, delta_ref, low_ref,
              score_ref, score_rows, key_acc, value_acc, acc_rows):
    columns = query_ref.shape[1]
    height = acc_rows.size
    for c in range(0, columns, CHUNK):
        span = slice(c, c + CHUNK)
        shape = (height // SUB, SUB, CHUNK)
        attention = weight_ref[at + (span,)].reshape(shape) * inverse_ref[slot, :, span][None]
        lifted = prob_ref[at + (span,)].reshape(shape) - delta_ref[slot, :, span][None]
        score_grad = (attention * lifted).reshape(height, CHUNK)
        low_ref[:height, span] = attention.reshape(height, CHUNK).astype(BF16)
        score_ref[slot, score_rows, span] = score_grad.astype(BF16)
    value_acc[acc_rows, :] += nn_dot(low_ref[:height], grad_ref[slot])
    key_acc[acc_rows, :] += nn_dot(score_ref[slot, score_rows, :], query_ref[slot])


def block_rows(index, count=1):
    return pl.ds(pl.multiple_of(index * BLK, BLK), count * BLK)


def pick(values, s):
    chosen = values[0]
    for i in range(1, len(values)):
        chosen = jnp.where(s == i, values[i], chosen)
    return chosen


def over_slots(slots, body):
    def step(s, carry):
        block, start = (pick([slot[i] for slot in slots], s) for i in (0, 2))

        @pl.when(pick([jnp.where(slot[1], 1, 0) for slot in slots], s) == 1)
        def _():
            body(s, block, start)

        return carry

    lax.fori_loop(0, len(slots), step, 0)


def local_scores(sizes, assistant, turn_first, query_hbm, grad_hbm, kv_ref, query_ref, grad_ref,
                 weight_ref, prob_ref, sum_ref, dot_ref, sem, ready=lambda: None):
    block_count, slot_count, head_count, width, scale = sizes
    base = lax.axis_index("ctx") * block_count
    slots = slots_of(assistant, turn_first, base, block_count, slot_count)

    def copies(s, block):
        for i, (source, target) in enumerate(((query_hbm, query_ref), (grad_hbm, grad_ref))):
            for h in range(head_count):
                yield pltpu.make_async_copy(
                    source.at[0, block_rows(block), pl.ds(h * width, width)],
                    target.at[s, pl.ds(h * BLK, BLK)],
                    sem.at[s, i, h],
                )

    for s, (block, live, start) in enumerate(slots):
        @pl.when(live)
        def _():
            for copy in copies(s, block):
                copy.start()
    sum_ref[...] = jnp.zeros_like(sum_ref)
    dot_ref[...] = jnp.zeros_like(dot_ref)
    ahead = lax.broadcasted_iota(jnp.int32, (BLK, BLK), 1) - lax.broadcasted_iota(
        jnp.int32, (BLK, BLK), 0
    )
    ready()

    def body(s, block, start):
        for copy in copies(s, block):
            copy.wait()

        def step(k, carry):
            rows = block_rows(k)
            score_pass(kv_ref[0, rows, :], kv_ref[1, rows, :], query_ref, grad_ref, s,
                       ahead >= (k - block) * BLK, weight_ref, prob_ref, (s, rows), sum_ref, dot_ref,
                       scale * math.log2(math.e))
            return carry

        lax.fori_loop(jnp.maximum(start, 0), block + 1, step, 0)

    over_slots(slots, body)


def in_first_half():
    return lax.axis_index("ctx") * 2 < lax.axis_size("ctx")


def local_kernel(sizes, *refs):
    inputs, results = refs[:5], refs[-7:]
    pl.when(jnp.logical_not(in_first_half()))(lambda: local_scores(sizes, *inputs, *results))


def pack_kernel(sizes, key_ref, value_ref, assistant_ref, turn_ref, query_hbm, grad_hbm, last_ref, all_ref,
                assistant, turn_first, need_ref, *state):
    state, pack_sem = state[:-1], state[-1]
    block_count = sizes[0]
    token_count = key_ref.shape[1]
    marks = [
        pltpu.make_async_copy(assistant_ref, assistant, pack_sem.at[0]),
        pltpu.make_async_copy(turn_ref, turn_first, pack_sem.at[1]),
    ]
    copies = []
    for pack in (all_ref, last_ref):
        rows = pack.shape[1]
        for i, source in enumerate((key_ref, value_ref)):
            copies.append(
                pltpu.make_async_copy(
                    source.at[0, pl.ds(token_count - rows, rows)], pack.at[i], pack_sem.at[2 + len(copies)]
                )
            )
    for copy in marks + copies:
        copy.start()
    for copy in marks:
        copy.wait()
    outer = far = jnp.int32(0)
    for i in range(block_count, assistant.shape[1]):
        device = i // block_count
        behind = jnp.where(assistant[0, i] == 1, device * block_count - turn_first[0, i], 0)
        far = jnp.where(behind > block_count, 1, far)
        if device % 2 == 0:
            outer = jnp.maximum(outer, behind)
    need_ref[0] = jnp.where((outer > 1) | (far > 0), 1, 0)

    def ready():
        for copy in copies:
            copy.wait()

    @pl.when(in_first_half())
    def _():
        local_scores(sizes, assistant, turn_first, query_hbm, grad_hbm, all_ref, *state, ready=ready)

    pl.when(jnp.logical_not(in_first_half()))(ready)


def over_window(block_count, reach, start, whole, body):
    first = jnp.maximum(start + reach, 0)
    last = reach
    if whole:
        @pl.when(start <= -block_count)
        def _():
            body(pl.ds((reach - block_count) * BLK, block_count * BLK))

        last = jnp.where(start <= -block_count, reach - block_count, reach)

    def step(k, carry):
        body(block_rows(k))
        return carry

    lax.fori_loop(first, last, step, 0)


def near_kernel(sizes, parity, assistant, turn_first, need, query_ref, grad_ref, far_hbm, *rest):
    weight_ref, prob_ref, sum_ref, dot_ref, window, values, sem = rest[-7:]
    block_count, slot_count, head_count, width, scale = sizes
    rank = lax.axis_index("ctx")
    reach = window.shape[0] // BLK
    near = pl.ds((reach - block_count) * BLK, block_count * BLK)

    def fill(rows, source):
        window[rows, :] = source[0]
        values[rows, :] = source[1]

    def fetch(rows, source, first_sem):
        return [
            pltpu.make_async_copy(source.at[i], target.at[rows], sem.at[first_sem + i])
            for i, target in enumerate((window, values))
        ]

    def body(s, block, start):
        def scores(rows):
            score_pass(window[rows, :], values[rows, :], query_ref, grad_ref, s, None, weight_ref,
                       prob_ref, (s, rows), sum_ref, dot_ref, scale * math.log2(math.e))

        over_window(block_count, reach, start, parity == 1, scores)

    @pl.when(lax.rem(rank, 2) == parity)
    def _():
        if parity == 1:
            fill(near, rest[0])
        else:
            fill(block_rows(reach - 1), rest[0])

        @pl.when(need[0] > 0)
        def _():
            copies = fetch(pl.ds(0, far_hbm.shape[1]), far_hbm, 0)
            if parity == 0:
                copies += fetch(near, rest[1], 2)
            for copy in copies:
                copy.start()
            for copy in copies:
                copy.wait()

        sum_ref[...] = jnp.zeros_like(sum_ref)
        dot_ref[...] = jnp.zeros_like(dot_ref)
        over_slots(slots_of(assistant, turn_first, rank * block_count, block_count, slot_count), body)


def remote_kernel(sizes, parity, assistant, turn_first, need, query_ref, grad_ref, sum_local, dot_local,
                  weight_near, prob_near, sum_near, dot_near, *rest):
    block_count, slot_count, head_count, width, scale = sizes
    (score_ref, inverse_ref, delta_ref, beyond_hbm, *_, near_out, low_ref, key_acc, value_acc, beyond) = (
        rest[-11 + 2 * parity:]
    )
    rank = lax.axis_index("ctx")
    reach = weight_near.shape[1] // BLK

    def body(s, block, start):
        inverse = 1.0 / jnp.sum(sum_local[s] + sum_near[s], axis=0, keepdims=True)
        delta = jnp.sum(dot_local[s] + dot_near[s], axis=0, keepdims=True) * inverse
        inverse_ref[s] = jnp.broadcast_to(inverse, inverse_ref.shape[1:])
        delta_ref[s] = jnp.broadcast_to(delta, delta_ref.shape[1:])

        def gradients_of(rows):
            grad_pass(weight_near, prob_near, (s, rows), query_ref, grad_ref, s, inverse_ref, delta_ref,
                      low_ref, score_ref, rows, key_acc, value_acc, rows)

        over_window(block_count, reach, start, parity == 1, gradients_of)

    @pl.when(lax.rem(rank, 2) == parity)
    def _():
        key_acc[...] = jnp.zeros_like(key_acc)
        value_acc[...] = jnp.zeros_like(value_acc)
        over_slots(slots_of(assistant, turn_first, rank * block_count, block_count, slot_count), body)

        def round_to(out, first, rows):
            out[0] = (key_acc[first:first + rows, :] * scale).astype(BF16)
            out[1] = value_acc[first:first + rows, :].astype(BF16)

        total = reach * BLK
        round_to(near_out, total - near_out.shape[1], near_out.shape[1])

        @pl.when(need[0] > 0)
        def _():
            round_to(beyond, 0, beyond.shape[1])
            pltpu.sync_copy(beyond, beyond_hbm)


def finish_kernel(sizes, assistant, turn_first, query_ref, grad_ref, weight_ref, prob_ref, score_in,
                  inverse_ref, delta_ref, kv_ref, window, *rest):
    query_hbm, key_acc, value_acc, score_ref, low_ref, query_acc, stage, blank, sem = rest
    block_count, slot_count, head_count, width, scale = sizes
    base = lax.axis_index("ctx") * block_count
    slots = slots_of(assistant, turn_first, base, block_count, slot_count)
    reach = window.shape[0] // BLK
    columns = query_acc.shape[1]
    blank[...] = jnp.zeros_like(blank)

    def blank_copy(i):
        return pltpu.make_async_copy(blank, query_hbm.at[0, pl.ds(i * BLK, BLK)], sem.at[slot_count + i])

    def stage_copy(s, block):
        return pltpu.make_async_copy(stage.at[s], query_hbm.at[0, block_rows(block)], sem.at[s])

    for i in range(block_count):
        @pl.when(assistant[0, base + i] != 1)
        def _():
            blank_copy(i).start()
    key_acc[...] = jnp.zeros_like(key_acc)
    value_acc[...] = jnp.zeros_like(value_acc)

    def body(s, block, start):
        def query_part(keys, source, rows, span):
            return nn_dot(keys.T, source[s, rows, span])

        query_acc[...] = jnp.zeros_like(query_acc)

        def remote_part(rows):
            keys = window[rows, :]
            for c in range(0, columns, CHUNK):
                span = slice(c, c + CHUNK)
                query_acc[:, span] += query_part(keys, score_in, rows, span)

        over_window(block_count, reach, start, True, remote_part)
        low = jnp.maximum(start, 0)
        for count in range(1, block_count + 1):
            @pl.when(block + 1 - low == count)
            def _():
                rows = block_rows(low, count)
                grad_pass(weight_ref, prob_ref, (s, rows), query_ref, grad_ref, s, inverse_ref, delta_ref,
                          low_ref, score_ref, rows, key_acc, value_acc, rows)
                keys = kv_ref[0, rows, :]
                for c in range(0, columns, CHUNK):
                    span = slice(c, c + CHUNK)
                    total = query_acc[:, span] + query_part(keys, score_ref, rows, span)
                    for h in range(0, CHUNK, BLK):
                        place = slice((c + h) // BLK * width, ((c + h) // BLK + 1) * width)
                        stage[s, :, place] = (total[:, h:h + BLK] * scale).T.astype(BF16)

        stage_copy(s, block).start()

    over_slots(slots, body)
    key_acc[...] = key_acc[...] * scale
    for s, (block, live, start) in enumerate(slots):
        @pl.when(live)
        def _():
            stage_copy(s, block).wait()

    for i in range(block_count):
        @pl.when(assistant[0, base + i] != 1)
        def _():
            blank_copy(i).wait()


def add_kernel(far_rows, need, key_in, value_in, outer_ref, rest_hbm, far_hbm, key_acc, value_acc, rest, far):
    for i, acc in enumerate((key_acc, value_acc)):
        last = acc.shape[0] - outer_ref.shape[1]
        acc[last:, :] += outer_ref[i].astype(F32)

    @pl.when(need[0] > 0)
    def _():
        pltpu.sync_copy(rest_hbm, rest)
        pltpu.sync_copy(far_hbm, far)
        for i, acc in enumerate((key_acc, value_acc)):
            last = acc.shape[0] - outer_ref.shape[1]
            acc[:last, :] += rest[i, far_rows:, :].astype(F32)
            acc[acc.shape[0] - far_rows:, :] += far[i].astype(F32)


def total_kernel(key_acc, value_acc, returned, key_out, value_out):
    for i, (acc, out) in enumerate(((key_acc, key_out), (value_acc, value_out))):
        out[0] = (acc[...] + returned[i].astype(F32)).astype(BF16)


def call(kernel, inputs, in_specs, outputs, out_specs, scratch, limit, macs, aliases={},
         traffic=2 * MIB):
    return pl.pallas_call(
        kernel,
        out_shape=outputs,
        in_specs=in_specs,
        out_specs=out_specs,
        scratch_shapes=scratch,
        input_output_aliases=aliases,
        compiler_params=pltpu.CompilerParams(vmem_limit_bytes=limit * MIB),
        cost_estimate=pl.CostEstimate(flops=2 * macs, bytes_accessed=traffic, transcendentals=0),
    )(*inputs)


ANY_SPEC = pl.BlockSpec(memory_space=pl.ANY)
SMEM_SPEC = pl.BlockSpec(memory_space=pltpu.SMEM)
VMEM_SPEC = pl.BlockSpec(memory_space=pltpu.VMEM)


def score_shapes(sizes, rows):
    block_count, slot_count, head_count, width, scale = sizes
    columns = head_count * BLK
    return (
        pltpu.VMEM((slot_count, rows, columns), F32),
        pltpu.VMEM((slot_count, rows, columns), F32),
        pltpu.VMEM((slot_count, SUB, columns), F32),
        pltpu.VMEM((slot_count, SUB, columns), F32),
    )


def local_shapes(sizes):
    block_count, slot_count, head_count, width, scale = sizes
    rows = pltpu.VMEM((slot_count, head_count * BLK, width), BF16)
    return (rows, rows) + score_shapes(sizes, block_count * BLK)


def local_sems(sizes):
    return pltpu.SemaphoreType.DMA((sizes[1], 2, sizes[2]))


def skip_kernel(*refs):
    pass


def whole_kernel(key_ref, value_ref, far_ref, whole_ref):
    first = whole_ref.shape[1] - far_ref.shape[1]
    for i, source in enumerate((key_ref, value_ref)):
        pltpu.sync_copy(source.at[0], whole_ref.at[i])
        pltpu.sync_copy(source.at[0, pl.ds(first, far_ref.shape[1])], far_ref.at[i])


def head_kernel(source_ref, head_ref):
    for i in range(head_ref.shape[0]):
        pltpu.sync_copy(source_ref.at[i, pl.ds(0, head_ref.shape[1])], head_ref.at[i])


def rarely(need, exchange, operands, shapes):
    def skipped(*operands):
        return call(skip_kernel, (), [], tuple(jax.ShapeDtypeStruct(s, BF16) for s in shapes),
                    [ANY_SPEC] * len(shapes), [], 4, 1, {}, 1)

    return tuple(lax.switch(need[0], [skipped, lambda *operands: tuple(exchange(*operands))], *operands))


def per_device(query_rows, key_rows, value_rows, out_grad, assistant, turn_first):
    token_count = query_rows.shape[1]
    width = key_rows.shape[2]
    head_count = query_rows.shape[2] // width
    block_count = token_count // BLK
    far_rows = block_count // 2 * BLK
    reach_rows = token_count + far_rows
    slot_count = (block_count + 1) // 2
    columns = head_count * BLK
    pair = columns * BLK * width
    sizes = (block_count, slot_count, head_count, width, 1.0 / math.sqrt(width))
    stat_rows = (slot_count, SUB, columns)
    last, own, assistant, turn_first, need, *local_state = call(
        lambda *refs: pack_kernel(sizes, *refs),
        tuple(hbm(a) for a in (key_rows, value_rows, assistant, turn_first, query_rows, out_grad)),
        [ANY_SPEC] * 6,
        (
            pltpu.VMEM((2, far_rows, width), BF16),
            pltpu.VMEM((2, token_count, width), BF16),
            pltpu.SMEM(assistant.shape, jnp.int32),
            pltpu.SMEM(turn_first.shape, jnp.int32),
            pltpu.SMEM((1,), jnp.int32),
        )
        + local_shapes(sizes),
        [VMEM_SPEC] * 2 + [SMEM_SPEC] * 3 + [VMEM_SPEC] * 6,
        [local_sems(sizes), pltpu.SemaphoreType.DMA((6,))],
        8,
        10 * pair,
    )
    marks = (smem(assistant), smem(turn_first))
    flag = smem(need)
    outer_in = pair_shift(last, "ctx", 1, 0)
    inner_in = pair_shift(own, "ctx", 1, 1)
    local_state = call(
        lambda *refs: local_kernel(sizes, *refs),
        marks + (hbm(query_rows), hbm(out_grad), vmem(own)) + tuple(vmem(a) for a in local_state),
        [SMEM_SPEC] * 2 + [ANY_SPEC] * 2 + [VMEM_SPEC] * 7,
        local_shapes(sizes),
        [VMEM_SPEC] * 6,
        [local_sems(sizes)],
        8,
        pair,
        {5 + i: i for i in range(6)},
    )
    key_source, value_source, local_state = lax.optimization_barrier((key_rows, value_rows, local_state))

    far_shape = jax.ShapeDtypeStruct((2, far_rows, width), BF16)
    whole_shape = jax.ShapeDtypeStruct((2, token_count, width), BF16)

    def exchange(keys, values):
        far, whole = call(whole_kernel, (keys, values), [ANY_SPEC] * 2, (far_shape, whole_shape),
                          [ANY_SPEC] * 2, [], 4, 1, {}, 1)
        return shifted(far, "ctx", 2), pair_shift(whole, "ctx", 1, 0)

    def exchange_back(beyond):
        far = call(head_kernel, (beyond,), [ANY_SPEC], far_shape, ANY_SPEC, [], 4, 1, {}, 1)
        return pair_shift(beyond, "ctx", -1, 0), shifted(far, "ctx", -2)

    far_in, whole_in = rarely(
        need,
        exchange,
        (key_source, value_source),
        [far_shape.shape, whole_shape.shape],
    )
    query_slots, grad_slots, weights, prob_grad, sums, dots = local_state
    near_state = window = remote_state = ()
    near_grads = []
    for parity, sources in ((0, (vmem(outer_in), hbm(whole_in))), (1, (vmem(inner_in),))):
        inputs = marks + (flag, vmem(query_slots), vmem(grad_slots), hbm(far_in)) + sources
        kept = tuple(vmem(a) for a in tuple(near_state) + window)
        *near_state, sum_near, dot_near, window = call(
            lambda *refs: near_kernel(sizes, parity, *refs),
            inputs + kept,
            [SMEM_SPEC] * 3 + [VMEM_SPEC] * 2 + [ANY_SPEC, VMEM_SPEC]
            + [ANY_SPEC] * (len(sources) - 1) + [VMEM_SPEC] * len(kept),
            score_shapes(sizes, reach_rows) + (pltpu.VMEM((reach_rows, width), BF16),),
            [VMEM_SPEC] * 5,
            [pltpu.VMEM((reach_rows, width), BF16), pltpu.SemaphoreType.DMA((4,))],
            8,
            NEAR_HINT[parity] * pair,
            {len(inputs) + i: i if i < 2 else 4 for i in range(len(kept))},
            1,
        )
        window = (window,)
        inputs = marks + (flag,) + tuple(vmem(a) for a in (query_slots, grad_slots, sums, dots))
        near_inputs = tuple(vmem(a) for a in tuple(near_state) + (sum_near, dot_near))
        kept = tuple(vmem(a) for a in remote_state[:3]) + tuple(hbm(a) for a in remote_state[3:])
        score_arrays = score_shapes(sizes, reach_rows)[:2] if parity == 0 else ()
        aliases = {len(inputs) + 4 + i: i for i in range(len(kept))}
        aliases.update({len(inputs) + i: 4 + i for i in range(len(score_arrays))})
        *remote_state, near_grad = call(
            lambda *refs: remote_kernel(sizes, parity, *refs),
            inputs + near_inputs + kept,
            [SMEM_SPEC] * 3 + [VMEM_SPEC] * (8 + len(kept[:3])) + [ANY_SPEC] * len(kept[3:]),
            (
                pltpu.VMEM((slot_count, reach_rows, columns), BF16),
                pltpu.VMEM(stat_rows, F32),
                pltpu.VMEM(stat_rows, F32),
                jax.ShapeDtypeStruct((2, token_count, width), BF16),
            )
            + score_arrays
            + (pltpu.VMEM((2, sources[0].shape[1], width), BF16),),
            [VMEM_SPEC] * 3 + [ANY_SPEC] + [VMEM_SPEC] * (1 + len(score_arrays)),
            [
                pltpu.VMEM((token_count, columns), BF16),
                pltpu.VMEM((reach_rows, width), F32),
                pltpu.VMEM((reach_rows, width), F32),
                pltpu.VMEM((2, token_count, width), BF16),
            ],
            8,
            REMOTE_HINT[parity] * pair,
            aliases,
            1,
        )
        near_state = remote_state[4:]
        remote_state = tuple(remote_state[:4])
        near_grads.append(pair_shift(near_grad, "ctx", -1, parity))
    score_grad, inverse, delta, beyond = remote_state
    outer_back, inner_back = near_grads
    query_grad, key_acc, value_acc = call(
        lambda *refs: finish_kernel(sizes, *refs),
        marks
        + tuple(
            vmem(a)
            for a in (query_slots, grad_slots, weights, prob_grad, score_grad, inverse, delta, own) + window
        ),
        [SMEM_SPEC] * 2 + [VMEM_SPEC] * 9,
        (
            jax.ShapeDtypeStruct(query_rows.shape, BF16),
            pltpu.VMEM((token_count, width), F32),
            pltpu.VMEM((token_count, width), F32),
        ),
        [ANY_SPEC] + [VMEM_SPEC] * 2,
        [
            pltpu.VMEM((slot_count, token_count, columns), BF16),
            pltpu.VMEM((token_count, columns), BF16),
            pltpu.VMEM((BLK, columns), F32),
            pltpu.VMEM((slot_count, BLK, head_count * width), BF16),
            pltpu.VMEM((BLK, head_count * width), BF16),
            pltpu.SemaphoreType.DMA((slot_count + block_count,)),
        ],
        10,
        pair,
        {},
        1,
    )
    beyond, query_grad = lax.optimization_barrier((beyond, query_grad))
    rest_back, far_back = rarely(
        need,
        exchange_back,
        (beyond,),
        [beyond.shape, far_in.shape],
    )
    key_acc, value_acc = call(
        lambda *refs: add_kernel(far_rows, *refs),
        (flag,) + tuple(vmem(a) for a in (key_acc, value_acc, outer_back)) + (hbm(rest_back), hbm(far_back)),
        [SMEM_SPEC] + [VMEM_SPEC] * 3 + [ANY_SPEC] * 2,
        (pltpu.VMEM((token_count, width), F32),) * 2,
        [VMEM_SPEC] * 2,
        [pltpu.VMEM(beyond.shape, BF16), pltpu.VMEM(far_in.shape, BF16)],
        4,
        CROSS_HINT * pair,
        {1: 0, 2: 1},
        1,
    )
    key_grad, value_grad = call(
        total_kernel,
        tuple(vmem(a) for a in (key_acc, value_acc, inner_back)),
        [VMEM_SPEC] * 3,
        (jax.ShapeDtypeStruct(key_rows.shape, BF16), jax.ShapeDtypeStruct(value_rows.shape, BF16)),
        [VMEM_SPEC] * 2,
        [],
        8,
        BLK,
    )
    return (query_grad, key_grad, value_grad)


def solution(mesh):
    return jax.shard_map(
        per_device,
        mesh=mesh,
        in_specs=(
            P("dp", "ctx", "tp"),
            P("dp", "ctx", "tp"),
            P("dp", "ctx", "tp"),
            P("dp", "ctx", "tp"),
            P("dp", None),
            P("dp", None),
        ),
        out_specs=(P("dp", "ctx", "tp"), P("dp", "ctx", "tp"), P("dp", "ctx", "tp")),
        check_vma=False,
    )
```

```python
import math

import jax
import jax.numpy as jnp
from jax import lax
from jax.experimental import pallas as pl
from jax.experimental.pallas import tpu as pltpu
from jax.sharding import PartitionSpec as P

BLK = 128
SUB = 8
CHUNK = 256
F32 = jnp.float32
BF16 = jnp.bfloat16
MIB = 1 << 20
NEAR_HINT = (400, 10)
REMOTE_HINT = (14, 14)
CROSS_HINT = 60


def shifted(block, axis, distance):
    devices = range(lax.axis_size(axis))
    route = [(i - distance, i) for i in devices if i - distance in devices]
    return lax.ppermute(block, axis, route)


def pair_shift(block, axis, distance, parity):
    pairs = [(i - 1, i) for i in range(1, lax.axis_size(axis)) if i % 2 == parity]
    return lax.ppermute(block, axis, pairs if distance == 1 else [pair[::-1] for pair in pairs])


def vmem(array):
    return pltpu.with_memory_space_constraint(array, pltpu.VMEM)


def smem(array):
    return pltpu.with_memory_space_constraint(array, pltpu.SMEM)


def hbm(array):
    return pltpu.with_memory_space_constraint(array, pltpu.HBM)


def nt_dot(left, right):
    return lax.dot_general(left, right, (((1,), (1,)), ((), ())), preferred_element_type=F32)


def nn_dot(left, right):
    return lax.dot_general(left, right, (((1,), (0,)), ((), ())), preferred_element_type=F32)


def fold(tile):
    return jnp.sum(tile.reshape(tile.shape[0] // SUB, SUB, tile.shape[1]), axis=0)


def slots_of(assistant, turn_first, base, block_count, slot_count):
    found = jnp.int32(0)
    blocks = [jnp.int32(0)] * slot_count
    starts = [jnp.int32(0)] * slot_count
    for i in range(block_count):
        mark = assistant[0, base + i]
        start = turn_first[0, base + i] - base
        for s in range(slot_count):
            here = (mark == 1) & (found == s)
            blocks[s] = jnp.where(here, i, blocks[s])
            starts[s] = jnp.where(here, start, starts[s])
        found = found + jnp.where(mark == 1, 1, 0)
    return [(blocks[s], found > s, starts[s]) for s in range(slot_count)]


def score_pass(key_tile, value_tile, query_ref, grad_ref, slot, keep, weight_ref, prob_ref, at, sum_ref,
               dot_ref, scale):
    columns = query_ref.shape[1]
    for c in range(0, columns, CHUNK):
        span = slice(c, c + CHUNK)
        scores = nt_dot(key_tile, query_ref[slot, span, :])
        prob_grad = nt_dot(value_tile, grad_ref[slot, span, :])
        weights = jnp.exp2(scores * scale)
        if keep is not None:
            weights = jnp.where(jnp.concatenate([keep] * (CHUNK // BLK), axis=1), weights, 0.0)
        weight_ref[at + (span,)] = weights
        prob_ref[at + (span,)] = prob_grad
        sum_ref[slot, :, span] += fold(weights)
        dot_ref[slot, :, span] += fold(weights * prob_grad)


def grad_pass(weight_ref, prob_ref, at, query_ref, grad_ref, slot, inverse_ref, delta_ref, low_ref,
              score_ref, score_rows, key_acc, value_acc, acc_rows):
    columns = query_ref.shape[1]
    height = acc_rows.size
    for c in range(0, columns, CHUNK):
        span = slice(c, c + CHUNK)
        shape = (height // SUB, SUB, CHUNK)
        attention = weight_ref[at + (span,)].reshape(shape) * inverse_ref[slot, :, span][None]
        lifted = prob_ref[at + (span,)].reshape(shape) - delta_ref[slot, :, span][None]
        score_grad = (attention * lifted).reshape(height, CHUNK)
        low_ref[:height, span] = attention.reshape(height, CHUNK).astype(BF16)
        score_ref[slot, score_rows, span] = score_grad.astype(BF16)
    value_acc[acc_rows, :] += nn_dot(low_ref[:height], grad_ref[slot])
    key_acc[acc_rows, :] += nn_dot(score_ref[slot, score_rows, :], query_ref[slot])


def block_rows(index, count=1):
    return pl.ds(pl.multiple_of(index * BLK, BLK), count * BLK)


def pick(values, s):
    chosen = values[0]
    for i in range(1, len(values)):
        chosen = jnp.where(s == i, values[i], chosen)
    return chosen


def over_slots(slots, body):
    def step(s, carry):
        block, start = (pick([slot[i] for slot in slots], s) for i in (0, 2))

        @pl.when(pick([jnp.where(slot[1], 1, 0) for slot in slots], s) == 1)
        def _():
            body(s, block, start)

        return carry

    lax.fori_loop(0, len(slots), step, 0)


def local_scores(sizes, assistant, turn_first, query_hbm, grad_hbm, kv_ref, query_ref, grad_ref,
                 weight_ref, prob_ref, sum_ref, dot_ref, sem):
    block_count, slot_count, head_count, width, scale = sizes
    base = lax.axis_index("ctx") * block_count
    slots = slots_of(assistant, turn_first, base, block_count, slot_count)

    def copies(s, block):
        for i, (source, target) in enumerate(((query_hbm, query_ref), (grad_hbm, grad_ref))):
            for h in range(head_count):
                yield pltpu.make_async_copy(
                    source.at[0, block_rows(block), pl.ds(h * width, width)],
                    target.at[s, pl.ds(h * BLK, BLK)],
                    sem.at[s, i],
                )

    for s, (block, live, start) in enumerate(slots):
        @pl.when(live)
        def _():
            for copy in copies(s, block):
                copy.start()
    sum_ref[...] = jnp.zeros_like(sum_ref)
    dot_ref[...] = jnp.zeros_like(dot_ref)
    ahead = lax.broadcasted_iota(jnp.int32, (BLK, BLK), 1) - lax.broadcasted_iota(
        jnp.int32, (BLK, BLK), 0
    )
    def body(s, block, start):
        for i, target in enumerate((query_ref, grad_ref)):
            pltpu.make_async_copy(target.at[s], target.at[s], sem.at[s, i]).wait()

        def step(k, carry):
            rows = block_rows(k)
            score_pass(kv_ref[0, rows, :], kv_ref[1, rows, :], query_ref, grad_ref, s,
                       ahead >= (k - block) * BLK, weight_ref, prob_ref, (s, rows), sum_ref, dot_ref,
                       scale * math.log2(math.e))
            return carry

        lax.fori_loop(jnp.maximum(start, 0), block + 1, step, 0)

    over_slots(slots, body)


def in_first_half():
    return lax.axis_index("ctx") * 2 < lax.axis_size("ctx")


def local_kernel(sizes, early, *refs):
    inputs, results = refs[:5], refs[-7:]
    here = in_first_half() if early else jnp.logical_not(in_first_half())
    pl.when(here)(lambda: local_scores(sizes, *inputs, *results))


def pack_kernel(block_count, key_ref, value_ref, assistant_ref, turn_ref, last_ref, all_ref, assistant,
                turn_first, need_ref, pack_sem):
    token_count = key_ref.shape[1]
    marks = [
        pltpu.make_async_copy(assistant_ref, assistant, pack_sem.at[0]),
        pltpu.make_async_copy(turn_ref, turn_first, pack_sem.at[1]),
    ]
    copies = []
    for pack in (all_ref, last_ref):
        rows = pack.shape[1]
        for i, source in enumerate((key_ref, value_ref)):
            copies.append(
                pltpu.make_async_copy(
                    source.at[0, pl.ds(token_count - rows, rows)], pack.at[i], pack_sem.at[2 + len(copies)]
                )
            )
    for copy in marks + copies:
        copy.start()
    for copy in marks:
        copy.wait()
    outer = far = jnp.int32(0)
    for i in range(block_count, assistant.shape[1]):
        device = i // block_count
        behind = jnp.where(assistant[0, i] == 1, device * block_count - turn_first[0, i], 0)
        far = jnp.where(behind > block_count, 1, far)
        if device % 2 == 0:
            outer = jnp.maximum(outer, behind)
    need_ref[0] = jnp.where((outer > 1) | (far > 0), 1, 0)

    for copy in copies:
        copy.wait()


def over_window(block_count, reach, start, whole, body):
    first = jnp.maximum(start + reach, 0)
    last = reach
    if whole:
        @pl.when(start <= -block_count)
        def _():
            body(pl.ds((reach - block_count) * BLK, block_count * BLK))

        last = jnp.where(start <= -block_count, reach - block_count, reach)

    def step(k, carry):
        body(block_rows(k))
        return carry

    lax.fori_loop(first, last, step, 0)


def near_kernel(sizes, parity, assistant, turn_first, need, query_ref, grad_ref, far_hbm, *rest):
    weight_ref, prob_ref, sum_ref, dot_ref, window, values, sem = rest[-7:]
    block_count, slot_count, head_count, width, scale = sizes
    rank = lax.axis_index("ctx")
    reach = window.shape[0] // BLK
    near = pl.ds((reach - block_count) * BLK, block_count * BLK)

    def fill(rows, source):
        window[rows, :] = source[0]
        values[rows, :] = source[1]

    def fetch(rows, source, first_sem):
        return [
            pltpu.make_async_copy(source.at[i], target.at[rows], sem.at[first_sem + i])
            for i, target in enumerate((window, values))
        ]

    def body(s, block, start):
        def scores(rows):
            score_pass(window[rows, :], values[rows, :], query_ref, grad_ref, s, None, weight_ref,
                       prob_ref, (s, rows), sum_ref, dot_ref, scale * math.log2(math.e))

        over_window(block_count, reach, start, parity == 1, scores)

    @pl.when(lax.rem(rank, 2) == parity)
    def _():
        if parity == 1:
            fill(near, rest[0])
        else:
            fill(block_rows(reach - 1), rest[0])

        @pl.when(need[0] > 0)
        def _():
            copies = fetch(pl.ds(0, far_hbm.shape[1]), far_hbm, 0)
            if parity == 0:
                copies += fetch(near, rest[1], 2)
            for copy in copies:
                copy.start()
            for copy in copies:
                copy.wait()

        sum_ref[...] = jnp.zeros_like(sum_ref)
        dot_ref[...] = jnp.zeros_like(dot_ref)
        over_slots(slots_of(assistant, turn_first, rank * block_count, block_count, slot_count), body)


def remote_kernel(sizes, parity, assistant, turn_first, need, query_ref, grad_ref, sum_local, dot_local,
                  weight_near, prob_near, sum_near, dot_near, *rest):
    block_count, slot_count, head_count, width, scale = sizes
    (score_ref, inverse_ref, delta_ref, beyond_hbm, *_, near_out, low_ref, key_acc, value_acc, beyond) = (
        rest[-11 + 2 * parity:]
    )
    rank = lax.axis_index("ctx")
    reach = weight_near.shape[1] // BLK

    def body(s, block, start):
        inverse = 1.0 / jnp.sum(sum_local[s] + sum_near[s], axis=0, keepdims=True)
        delta = jnp.sum(dot_local[s] + dot_near[s], axis=0, keepdims=True) * inverse
        inverse_ref[s] = jnp.broadcast_to(inverse, inverse_ref.shape[1:])
        delta_ref[s] = jnp.broadcast_to(delta, delta_ref.shape[1:])

        def gradients_of(rows):
            grad_pass(weight_near, prob_near, (s, rows), query_ref, grad_ref, s, inverse_ref, delta_ref,
                      low_ref, score_ref, rows, key_acc, value_acc, rows)

        over_window(block_count, reach, start, parity == 1, gradients_of)

    @pl.when(lax.rem(rank, 2) == parity)
    def _():
        key_acc[...] = jnp.zeros_like(key_acc)
        value_acc[...] = jnp.zeros_like(value_acc)
        over_slots(slots_of(assistant, turn_first, rank * block_count, block_count, slot_count), body)

        def round_to(out, first, rows):
            out[0] = (key_acc[first:first + rows, :] * scale).astype(BF16)
            out[1] = value_acc[first:first + rows, :].astype(BF16)

        total = reach * BLK
        round_to(near_out, total - near_out.shape[1], near_out.shape[1])

        @pl.when(need[0] > 0)
        def _():
            round_to(beyond, 0, beyond.shape[1])
            pltpu.sync_copy(beyond, beyond_hbm)


def finish_kernel(sizes, assistant, turn_first, query_ref, grad_ref, weight_ref, prob_ref, score_in,
                  inverse_ref, delta_ref, kv_ref, window, *rest):
    query_hbm, key_acc, value_acc, score_ref, low_ref, query_acc, stage, blank, sem = rest
    block_count, slot_count, head_count, width, scale = sizes
    base = lax.axis_index("ctx") * block_count
    slots = slots_of(assistant, turn_first, base, block_count, slot_count)
    reach = window.shape[0] // BLK
    columns = query_acc.shape[1]
    blank[...] = jnp.zeros_like(blank)

    def blank_copy(i):
        return pltpu.make_async_copy(blank, query_hbm.at[0, pl.ds(i * BLK, BLK)], sem.at[slot_count + i])

    def stage_copy(s, block):
        return pltpu.make_async_copy(stage.at[s], query_hbm.at[0, block_rows(block)], sem.at[s])

    for i in range(block_count):
        @pl.when(assistant[0, base + i] != 1)
        def _():
            blank_copy(i).start()
    key_acc[...] = jnp.zeros_like(key_acc)
    value_acc[...] = jnp.zeros_like(value_acc)

    def body(s, block, start):
        def query_part(keys, source, rows, span):
            return nn_dot(keys.T, source[s, rows, span])

        query_acc[...] = jnp.zeros_like(query_acc)

        def remote_part(rows):
            keys = window[rows, :]
            for c in range(0, columns, CHUNK):
                span = slice(c, c + CHUNK)
                query_acc[:, span] += query_part(keys, score_in, rows, span)

        over_window(block_count, reach, start, True, remote_part)
        low = jnp.maximum(start, 0)
        for count in range(1, block_count + 1):
            @pl.when(block + 1 - low == count)
            def _():
                rows = block_rows(low, count)
                grad_pass(weight_ref, prob_ref, (s, rows), query_ref, grad_ref, s, inverse_ref, delta_ref,
                          low_ref, score_ref, rows, key_acc, value_acc, rows)
                keys = kv_ref[0, rows, :]
                for c in range(0, columns, CHUNK):
                    span = slice(c, c + CHUNK)
                    total = query_acc[:, span] + query_part(keys, score_ref, rows, span)
                    for h in range(0, CHUNK, BLK):
                        place = slice((c + h) // BLK * width, ((c + h) // BLK + 1) * width)
                        stage[s, :, place] = (total[:, h:h + BLK] * scale).T.astype(BF16)

        stage_copy(s, block).start()

    over_slots(slots, body)
    key_acc[...] = key_acc[...] * scale
    for s, (block, live, start) in enumerate(slots):
        @pl.when(live)
        def _():
            stage_copy(s, block).wait()

    for i in range(block_count):
        @pl.when(assistant[0, base + i] != 1)
        def _():
            blank_copy(i).wait()


def add_kernel(far_rows, need, key_in, value_in, outer_ref, rest_hbm, far_hbm, key_acc, value_acc, rest, far):
    for i, acc in enumerate((key_acc, value_acc)):
        last = acc.shape[0] - outer_ref.shape[1]
        acc[last:, :] += outer_ref[i].astype(F32)

    @pl.when(need[0] > 0)
    def _():
        pltpu.sync_copy(rest_hbm, rest)
        pltpu.sync_copy(far_hbm, far)
        for i, acc in enumerate((key_acc, value_acc)):
            last = acc.shape[0] - outer_ref.shape[1]
            acc[:last, :] += rest[i, far_rows:, :].astype(F32)
            acc[acc.shape[0] - far_rows:, :] += far[i].astype(F32)


def total_kernel(key_acc, value_acc, returned, key_out, value_out):
    for i, (acc, out) in enumerate(((key_acc, key_out), (value_acc, value_out))):
        out[0] = (acc[...] + returned[i].astype(F32)).astype(BF16)


def call(kernel, inputs, in_specs, outputs, out_specs, scratch, limit, macs, aliases={},
         traffic=2 * MIB):
    return pl.pallas_call(
        kernel,
        out_shape=outputs,
        in_specs=in_specs,
        out_specs=out_specs,
        scratch_shapes=scratch,
        input_output_aliases=aliases,
        compiler_params=pltpu.CompilerParams(vmem_limit_bytes=limit * MIB),
        cost_estimate=pl.CostEstimate(flops=2 * macs, bytes_accessed=traffic, transcendentals=0),
    )(*inputs)


ANY_SPEC = pl.BlockSpec(memory_space=pl.ANY)
SMEM_SPEC = pl.BlockSpec(memory_space=pltpu.SMEM)
VMEM_SPEC = pl.BlockSpec(memory_space=pltpu.VMEM)


def score_shapes(sizes, rows):
    block_count, slot_count, head_count, width, scale = sizes
    columns = head_count * BLK
    return (
        pltpu.VMEM((slot_count, rows, columns), F32),
        pltpu.VMEM((slot_count, rows, columns), F32),
        pltpu.VMEM((slot_count, SUB, columns), F32),
        pltpu.VMEM((slot_count, SUB, columns), F32),
    )


def local_shapes(sizes):
    block_count, slot_count, head_count, width, scale = sizes
    rows = pltpu.VMEM((slot_count, head_count * BLK, width), BF16)
    return (rows, rows) + score_shapes(sizes, block_count * BLK)


def local_sems(sizes):
    return pltpu.SemaphoreType.DMA((sizes[1], 2))


def skip_kernel(*refs):
    pass


def whole_kernel(key_ref, value_ref, far_ref, whole_ref):
    first = whole_ref.shape[1] - far_ref.shape[1]
    for i, source in enumerate((key_ref, value_ref)):
        pltpu.sync_copy(source.at[0], whole_ref.at[i])
        pltpu.sync_copy(source.at[0, pl.ds(first, far_ref.shape[1])], far_ref.at[i])


def head_kernel(source_ref, head_ref):
    for i in range(head_ref.shape[0]):
        pltpu.sync_copy(source_ref.at[i, pl.ds(0, head_ref.shape[1])], head_ref.at[i])


def rarely(need, exchange, operands, shapes):
    def skipped(*operands):
        return call(skip_kernel, (), [], tuple(jax.ShapeDtypeStruct(s, BF16) for s in shapes),
                    [ANY_SPEC] * len(shapes), [], 4, 1, {}, 1)

    return tuple(lax.switch(need[0], [skipped, lambda *operands: tuple(exchange(*operands))], *operands))


def per_device(query_rows, key_rows, value_rows, out_grad, assistant, turn_first):
    token_count = query_rows.shape[1]
    width = key_rows.shape[2]
    head_count = query_rows.shape[2] // width
    block_count = token_count // BLK
    far_rows = block_count // 2 * BLK
    reach_rows = token_count + far_rows
    slot_count = (block_count + 1) // 2
    columns = head_count * BLK
    pair = columns * BLK * width
    sizes = (block_count, slot_count, head_count, width, 1.0 / math.sqrt(width))
    stat_rows = (slot_count, SUB, columns)
    last, own, assistant, turn_first, need = call(
        lambda *refs: pack_kernel(block_count, *refs),
        tuple(hbm(a) for a in (key_rows, value_rows, assistant, turn_first)),
        [ANY_SPEC] * 4,
        (
            pltpu.VMEM((2, far_rows, width), BF16),
            pltpu.VMEM((2, token_count, width), BF16),
            pltpu.SMEM(assistant.shape, jnp.int32),
            pltpu.SMEM(turn_first.shape, jnp.int32),
            pltpu.SMEM((1,), jnp.int32),
        ),
        [VMEM_SPEC] * 2 + [SMEM_SPEC] * 3,
        [pltpu.SemaphoreType.DMA((6,))],
        4,
        BLK,
    )
    marks = (smem(assistant), smem(turn_first))
    flag = smem(need)
    far_shape = jax.ShapeDtypeStruct((2, far_rows, width), BF16)
    whole_shape = jax.ShapeDtypeStruct((2, token_count, width), BF16)

    def exchange(keys, values):
        far, whole = call(whole_kernel, (keys, values), [ANY_SPEC] * 2, (far_shape, whole_shape),
                          [ANY_SPEC] * 2, [], 4, 1, {}, 1)
        return shifted(far, "ctx", 2), pair_shift(whole, "ctx", 1, 0)

    def exchange_back(beyond):
        far = call(head_kernel, (beyond,), [ANY_SPEC], far_shape, ANY_SPEC, [], 4, 1, {}, 1)
        return pair_shift(beyond, "ctx", -1, 0), shifted(far, "ctx", -2)

    far_in, whole_in = rarely(
        need,
        exchange,
        (key_rows, value_rows),
        [far_shape.shape, whole_shape.shape],
    )
    own, far_in, whole_in = lax.optimization_barrier((own, far_in, whole_in))

    def local(early, state):
        return call(
            lambda *refs: local_kernel(sizes, early, *refs),
            marks + (hbm(query_rows), hbm(out_grad), vmem(own)) + tuple(vmem(a) for a in state),
            [SMEM_SPEC] * 2 + [ANY_SPEC] * 2 + [VMEM_SPEC] * (1 + len(state)),
            local_shapes(sizes),
            [VMEM_SPEC] * 6,
            [local_sems(sizes)],
            8,
            pair,
            {5 + i: i for i in range(len(state))},
            1,
        )

    local_state = local(True, ())
    last, own, local_state = lax.optimization_barrier((last, own, local_state))
    outer_in = pair_shift(last, "ctx", 1, 0)
    inner_in = pair_shift(own, "ctx", 1, 1)
    local_state = local(False, local_state)
    query_slots, grad_slots, weights, prob_grad, sums, dots = local_state
    near_state = window = remote_state = ()
    near_grads = []
    for parity, sources in ((0, (vmem(outer_in), hbm(whole_in))), (1, (vmem(inner_in),))):
        inputs = marks + (flag, vmem(query_slots), vmem(grad_slots), hbm(far_in)) + sources
        kept = tuple(vmem(a) for a in tuple(near_state) + window)
        *near_state, sum_near, dot_near, window = call(
            lambda *refs: near_kernel(sizes, parity, *refs),
            inputs + kept,
            [SMEM_SPEC] * 3 + [VMEM_SPEC] * 2 + [ANY_SPEC, VMEM_SPEC]
            + [ANY_SPEC] * (len(sources) - 1) + [VMEM_SPEC] * len(kept),
            score_shapes(sizes, reach_rows) + (pltpu.VMEM((reach_rows, width), BF16),),
            [VMEM_SPEC] * 5,
            [pltpu.VMEM((reach_rows, width), BF16), pltpu.SemaphoreType.DMA((4,))],
            8,
            NEAR_HINT[parity] * pair,
            {len(inputs) + i: i if i < 2 else 4 for i in range(len(kept))},
            1,
        )
        window = (window,)
        inputs = marks + (flag,) + tuple(vmem(a) for a in (query_slots, grad_slots, sums, dots))
        near_inputs = tuple(vmem(a) for a in tuple(near_state) + (sum_near, dot_near))
        kept = tuple(vmem(a) for a in remote_state[:3]) + tuple(hbm(a) for a in remote_state[3:])
        score_arrays = score_shapes(sizes, reach_rows)[:2] if parity == 0 else ()
        aliases = {len(inputs) + 4 + i: i for i in range(len(kept))}
        aliases.update({len(inputs) + i: 4 + i for i in range(len(score_arrays))})
        *remote_state, near_grad = call(
            lambda *refs: remote_kernel(sizes, parity, *refs),
            inputs + near_inputs + kept,
            [SMEM_SPEC] * 3 + [VMEM_SPEC] * (8 + len(kept[:3])) + [ANY_SPEC] * len(kept[3:]),
            (
                pltpu.VMEM((slot_count, reach_rows, columns), BF16),
                pltpu.VMEM(stat_rows, F32),
                pltpu.VMEM(stat_rows, F32),
                jax.ShapeDtypeStruct((2, token_count, width), BF16),
            )
            + score_arrays
            + (pltpu.VMEM((2, sources[0].shape[1], width), BF16),),
            [VMEM_SPEC] * 3 + [ANY_SPEC] + [VMEM_SPEC] * (1 + len(score_arrays)),
            [
                pltpu.VMEM((token_count, columns), BF16),
                pltpu.VMEM((reach_rows, width), F32),
                pltpu.VMEM((reach_rows, width), F32),
                pltpu.VMEM((2, token_count, width), BF16),
            ],
            8,
            REMOTE_HINT[parity] * pair,
            aliases,
            1,
        )
        near_state = remote_state[4:]
        remote_state = tuple(remote_state[:4])
        near_grads.append(pair_shift(near_grad, "ctx", -1, parity))
    score_grad, inverse, delta, beyond = remote_state
    outer_back, inner_back = near_grads
    query_grad, key_acc, value_acc = call(
        lambda *refs: finish_kernel(sizes, *refs),
        marks
        + tuple(
            vmem(a)
            for a in (query_slots, grad_slots, weights, prob_grad, score_grad, inverse, delta, own) + window
        ),
        [SMEM_SPEC] * 2 + [VMEM_SPEC] * 9,
        (
            jax.ShapeDtypeStruct(query_rows.shape, BF16),
            pltpu.VMEM((token_count, width), F32),
            pltpu.VMEM((token_count, width), F32),
        ),
        [ANY_SPEC] + [VMEM_SPEC] * 2,
        [
            pltpu.VMEM((slot_count, token_count, columns), BF16),
            pltpu.VMEM((token_count, columns), BF16),
            pltpu.VMEM((BLK, columns), F32),
            pltpu.VMEM((slot_count, BLK, head_count * width), BF16),
            pltpu.VMEM((BLK, head_count * width), BF16),
            pltpu.SemaphoreType.DMA((slot_count + block_count,)),
        ],
        10,
        pair,
        {},
        1,
    )
    beyond, query_grad = lax.optimization_barrier((beyond, query_grad))
    rest_back, far_back = rarely(
        need,
        exchange_back,
        (beyond,),
        [beyond.shape, far_in.shape],
    )
    key_acc, value_acc = call(
        lambda *refs: add_kernel(far_rows, *refs),
        (flag,) + tuple(vmem(a) for a in (key_acc, value_acc, outer_back)) + (hbm(rest_back), hbm(far_back)),
        [SMEM_SPEC] + [VMEM_SPEC] * 3 + [ANY_SPEC] * 2,
        (pltpu.VMEM((token_count, width), F32),) * 2,
        [VMEM_SPEC] * 2,
        [pltpu.VMEM(beyond.shape, BF16), pltpu.VMEM(far_in.shape, BF16)],
        4,
        CROSS_HINT * pair,
        {1: 0, 2: 1},
        1,
    )
    key_grad, value_grad = call(
        total_kernel,
        tuple(vmem(a) for a in (key_acc, value_acc, inner_back)),
        [VMEM_SPEC] * 3,
        (jax.ShapeDtypeStruct(key_rows.shape, BF16), jax.ShapeDtypeStruct(value_rows.shape, BF16)),
        [VMEM_SPEC] * 2,
        [],
        8,
        BLK,
    )
    return (query_grad, key_grad, value_grad)


def solution(mesh):
    return jax.shard_map(
        per_device,
        mesh=mesh,
        in_specs=(
            P("dp", "ctx", "tp"),
            P("dp", "ctx", "tp"),
            P("dp", "ctx", "tp"),
            P("dp", "ctx", "tp"),
            P("dp", None),
            P("dp", None),
        ),
        out_specs=(P("dp", "ctx", "tp"), P("dp", "ctx", "tp"), P("dp", "ctx", "tp")),
        check_vma=False,
    )
```

```python
import math

import jax
import jax.numpy as jnp
from jax import lax
from jax.experimental import pallas as pl
from jax.experimental.pallas import tpu as pltpu
from jax.sharding import PartitionSpec as P

BLK = 128
SUB = 8
CHUNK = 256
F32 = jnp.float32
BF16 = jnp.bfloat16
MIB = 1 << 20
NEAR_HINT = (400, 10)
REMOTE_HINT = (14, 14)
CROSS_HINT = 60


def shifted(block, axis, distance):
    devices = range(lax.axis_size(axis))
    route = [(i - distance, i) for i in devices if i - distance in devices]
    return lax.ppermute(block, axis, route)


def pair_shift(block, axis, distance, parity):
    pairs = [(i - 1, i) for i in range(1, lax.axis_size(axis)) if i % 2 == parity]
    return lax.ppermute(block, axis, pairs if distance == 1 else [pair[::-1] for pair in pairs])


def vmem(array):
    return pltpu.with_memory_space_constraint(array, pltpu.VMEM)


def smem(array):
    return pltpu.with_memory_space_constraint(array, pltpu.SMEM)


def hbm(array):
    return pltpu.with_memory_space_constraint(array, pltpu.HBM)


def nt_dot(left, right):
    return lax.dot_general(left, right, (((1,), (1,)), ((), ())), preferred_element_type=F32)


def nn_dot(left, right):
    return lax.dot_general(left, right, (((1,), (0,)), ((), ())), preferred_element_type=F32)


def fold(tile):
    return jnp.sum(tile.reshape(tile.shape[0] // SUB, SUB, tile.shape[1]), axis=0)


def slots_of(assistant, turn_first, base, block_count, slot_count):
    found = jnp.int32(0)
    blocks = [jnp.int32(0)] * slot_count
    starts = [jnp.int32(0)] * slot_count
    for i in range(block_count):
        mark = assistant[0, base + i]
        start = turn_first[0, base + i] - base
        for s in range(slot_count):
            here = (mark == 1) & (found == s)
            blocks[s] = jnp.where(here, i, blocks[s])
            starts[s] = jnp.where(here, start, starts[s])
        found = found + jnp.where(mark == 1, 1, 0)
    return [(blocks[s], found > s, starts[s]) for s in range(slot_count)]


def score_pass(key_tile, value_tile, query_ref, grad_ref, slot, keep, weight_ref, prob_ref, at, sum_ref,
               dot_ref, scale):
    columns = query_ref.shape[1]
    for c in range(0, columns, CHUNK):
        span = slice(c, c + CHUNK)
        scores = nt_dot(key_tile, query_ref[slot, span, :])
        prob_grad = nt_dot(value_tile, grad_ref[slot, span, :])
        weights = jnp.exp2(scores * scale)
        if keep is not None:
            weights = jnp.where(jnp.concatenate([keep] * (CHUNK // BLK), axis=1), weights, 0.0)
        weight_ref[at + (span,)] = weights
        prob_ref[at + (span,)] = prob_grad
        sum_ref[slot, :, span] += fold(weights)
        dot_ref[slot, :, span] += fold(weights * prob_grad)


def grad_pass(weight_ref, prob_ref, at, query_ref, grad_ref, slot, inverse_ref, delta_ref, low_ref,
              score_ref, score_rows, key_acc, value_acc, acc_rows):
    columns = query_ref.shape[1]
    height = acc_rows.size
    for c in range(0, columns, CHUNK):
        span = slice(c, c + CHUNK)
        shape = (height // SUB, SUB, CHUNK)
        attention = weight_ref[at + (span,)].reshape(shape) * inverse_ref[slot, :, span][None]
        lifted = prob_ref[at + (span,)].reshape(shape) - delta_ref[slot, :, span][None]
        score_grad = (attention * lifted).reshape(height, CHUNK)
        low_ref[:height, span] = attention.reshape(height, CHUNK).astype(BF16)
        score_ref[slot, score_rows, span] = score_grad.astype(BF16)
    value_acc[acc_rows, :] += nn_dot(low_ref[:height], grad_ref[slot])
    key_acc[acc_rows, :] += nn_dot(score_ref[slot, score_rows, :], query_ref[slot])


def block_rows(index, count=1):
    return pl.ds(pl.multiple_of(index * BLK, BLK), count * BLK)


def pick(values, s):
    chosen = values[0]
    for i in range(1, len(values)):
        chosen = jnp.where(s == i, values[i], chosen)
    return chosen


def over_slots(slots, body):
    def step(s, carry):
        block, start = (pick([slot[i] for slot in slots], s) for i in (0, 2))

        @pl.when(pick([jnp.where(slot[1], 1, 0) for slot in slots], s) == 1)
        def _():
            body(s, block, start)

        return carry

    lax.fori_loop(0, len(slots), step, 0)


def local_scores(sizes, assistant, turn_first, query_hbm, grad_hbm, kv_ref, query_ref, grad_ref,
                 weight_ref, prob_ref, sum_ref, dot_ref, sem):
    block_count, slot_count, head_count, width, scale = sizes
    base = lax.axis_index("ctx") * block_count
    slots = slots_of(assistant, turn_first, base, block_count, slot_count)

    def copies(s, block):
        for i, (source, target) in enumerate(((query_hbm, query_ref), (grad_hbm, grad_ref))):
            for h in range(head_count):
                yield pltpu.make_async_copy(
                    source.at[0, block_rows(block), pl.ds(h * width, width)],
                    target.at[s, pl.ds(h * BLK, BLK)],
                    sem.at[s, i],
                )

    for s, (block, live, start) in enumerate(slots):
        @pl.when(live)
        def _():
            for copy in copies(s, block):
                copy.start()
    sum_ref[...] = jnp.zeros_like(sum_ref)
    dot_ref[...] = jnp.zeros_like(dot_ref)
    ahead = lax.broadcasted_iota(jnp.int32, (BLK, BLK), 1) - lax.broadcasted_iota(
        jnp.int32, (BLK, BLK), 0
    )
    def body(s, block, start):
        for i, target in enumerate((query_ref, grad_ref)):
            pltpu.make_async_copy(target.at[s], target.at[s], sem.at[s, i]).wait()

        def step(k, carry):
            rows = block_rows(k)
            score_pass(kv_ref[0, rows, :], kv_ref[1, rows, :], query_ref, grad_ref, s,
                       ahead >= (k - block) * BLK, weight_ref, prob_ref, (s, rows), sum_ref, dot_ref,
                       scale * math.log2(math.e))
            return carry

        lax.fori_loop(jnp.maximum(start, 0), block + 1, step, 0)

    over_slots(slots, body)


def in_first_half():
    return lax.axis_index("ctx") * 2 < lax.axis_size("ctx")


def local_kernel(sizes, early, *refs):
    inputs, results = refs[:5], refs[-7:]
    here = in_first_half() if early else jnp.logical_not(in_first_half())
    pl.when(here)(lambda: local_scores(sizes, *inputs, *results))


def pack_kernel(block_count, key_ref, value_ref, assistant_ref, turn_ref, last_ref, all_ref, assistant,
                turn_first, need_ref, pack_sem):
    token_count = key_ref.shape[1]
    marks = [
        pltpu.make_async_copy(assistant_ref, assistant, pack_sem.at[0]),
        pltpu.make_async_copy(turn_ref, turn_first, pack_sem.at[1]),
    ]
    copies = []
    for pack in (all_ref, last_ref):
        rows = pack.shape[1]
        for i, source in enumerate((key_ref, value_ref)):
            copies.append(
                pltpu.make_async_copy(
                    source.at[0, pl.ds(token_count - rows, rows)], pack.at[i], pack_sem.at[2 + len(copies)]
                )
            )
    for copy in marks + copies:
        copy.start()
    for copy in marks:
        copy.wait()
    outer = far = jnp.int32(0)
    for i in range(block_count, assistant.shape[1]):
        device = i // block_count
        behind = jnp.where(assistant[0, i] == 1, device * block_count - turn_first[0, i], 0)
        far = jnp.where(behind > block_count, 1, far)
        if device % 2 == 0:
            outer = jnp.maximum(outer, behind)
    need_ref[0] = jnp.where((outer > 1) | (far > 0), 1, 0)

    for copy in copies:
        copy.wait()


def over_window(block_count, reach, start, whole, body):
    first = jnp.maximum(start + reach, 0)
    last = reach
    if whole:
        @pl.when(start <= -block_count)
        def _():
            body(pl.ds((reach - block_count) * BLK, block_count * BLK))

        last = jnp.where(start <= -block_count, reach - block_count, reach)

    def step(k, carry):
        body(block_rows(k))
        return carry

    lax.fori_loop(first, last, step, 0)


def near_kernel(sizes, parity, assistant, turn_first, need, query_ref, grad_ref, far_hbm, *rest):
    weight_ref, prob_ref, sum_ref, dot_ref, window, values, sem = rest[-7:]
    block_count, slot_count, head_count, width, scale = sizes
    rank = lax.axis_index("ctx")
    reach = window.shape[0] // BLK
    near = pl.ds((reach - block_count) * BLK, block_count * BLK)

    def fill(rows, source):
        window[rows, :] = source[0]
        values[rows, :] = source[1]

    def fetch(rows, source, first_sem):
        return [
            pltpu.make_async_copy(source.at[i], target.at[rows], sem.at[first_sem + i])
            for i, target in enumerate((window, values))
        ]

    def body(s, block, start):
        def scores(rows):
            score_pass(window[rows, :], values[rows, :], query_ref, grad_ref, s, None, weight_ref,
                       prob_ref, (s, rows), sum_ref, dot_ref, scale * math.log2(math.e))

        over_window(block_count, reach, start, parity == 1, scores)

    @pl.when(lax.rem(rank, 2) == parity)
    def _():
        if parity == 1:
            fill(near, rest[0])
        else:
            fill(block_rows(reach - 1), rest[0])

        @pl.when(need[0] > 0)
        def _():
            copies = fetch(pl.ds(0, far_hbm.shape[1]), far_hbm, 0)
            if parity == 0:
                copies += fetch(near, rest[1], 2)
            for copy in copies:
                copy.start()
            for copy in copies:
                copy.wait()

        sum_ref[...] = jnp.zeros_like(sum_ref)
        dot_ref[...] = jnp.zeros_like(dot_ref)
        over_slots(slots_of(assistant, turn_first, rank * block_count, block_count, slot_count), body)


def remote_kernel(sizes, parity, assistant, turn_first, need, query_ref, grad_ref, sum_local, dot_local,
                  weight_near, prob_near, sum_near, dot_near, *rest):
    block_count, slot_count, head_count, width, scale = sizes
    (score_ref, inverse_ref, delta_ref, beyond_hbm, *_, near_out, low_ref, key_acc, value_acc, beyond) = (
        rest[-11 + 2 * parity:]
    )
    rank = lax.axis_index("ctx")
    reach = weight_near.shape[1] // BLK

    def body(s, block, start):
        inverse = 1.0 / jnp.sum(sum_local[s] + sum_near[s], axis=0, keepdims=True)
        delta = jnp.sum(dot_local[s] + dot_near[s], axis=0, keepdims=True) * inverse
        inverse_ref[s] = jnp.broadcast_to(inverse, inverse_ref.shape[1:])
        delta_ref[s] = jnp.broadcast_to(delta, delta_ref.shape[1:])

        def gradients_of(rows):
            grad_pass(weight_near, prob_near, (s, rows), query_ref, grad_ref, s, inverse_ref, delta_ref,
                      low_ref, score_ref, rows, key_acc, value_acc, rows)

        over_window(block_count, reach, start, parity == 1, gradients_of)

    @pl.when(lax.rem(rank, 2) == parity)
    def _():
        key_acc[...] = jnp.zeros_like(key_acc)
        value_acc[...] = jnp.zeros_like(value_acc)
        over_slots(slots_of(assistant, turn_first, rank * block_count, block_count, slot_count), body)

        def round_to(out, first, rows):
            out[0] = (key_acc[first:first + rows, :] * scale).astype(BF16)
            out[1] = value_acc[first:first + rows, :].astype(BF16)

        total = reach * BLK
        round_to(near_out, total - near_out.shape[1], near_out.shape[1])

        @pl.when(need[0] > 0)
        def _():
            round_to(beyond, 0, beyond.shape[1])
            pltpu.sync_copy(beyond, beyond_hbm)


def sends_late(rank):
    return (lax.rem(rank, 2) == 1) & (rank > 1)


def finish_kernel(sizes, early, assistant, turn_first, query_ref, grad_ref, weight_ref, prob_ref, score_in,
                  inverse_ref, delta_ref, kv_ref, window, *rest):
    query_hbm, key_acc, value_acc, stage, score_ref, low_ref, query_acc, blank, sem = rest[-9:]
    block_count, slot_count, head_count, width, scale = sizes
    rank = lax.axis_index("ctx")
    base = rank * block_count
    reach = window.shape[0] // BLK
    columns = query_acc.shape[1]

    def blank_copy(i):
        return pltpu.make_async_copy(blank, query_hbm.at[0, pl.ds(i * BLK, BLK)], sem.at[slot_count + i])

    def run():
        slots = slots_of(assistant, turn_first, base, block_count, slot_count)
        more = [live for _, live, _ in slots[1:]]

        def stage_copy(s):
            return pltpu.make_async_copy(stage.at[s], query_hbm.at[0, block_rows(slots[s][0])], sem.at[s])

        blank[...] = jnp.zeros_like(blank)
        for i in range(block_count):
            @pl.when(assistant[0, base + i] != 1)
            def _():
                blank_copy(i).start()
        key_acc[...] = jnp.zeros_like(key_acc)
        value_acc[...] = jnp.zeros_like(value_acc)

        def body(s, block, start):
            def query_part(keys, source, rows, span):
                return nn_dot(keys.T, source[s, rows, span])

            query_acc[...] = jnp.zeros_like(query_acc)

            def remote_part(rows):
                keys = window[rows, :]
                for c in range(0, columns, CHUNK):
                    span = slice(c, c + CHUNK)
                    query_acc[:, span] += query_part(keys, score_in, rows, span)

            over_window(block_count, reach, start, True, remote_part)
            low = jnp.maximum(start, 0)
            for count in range(1, block_count + 1):
                @pl.when(block + 1 - low == count)
                def _():
                    rows = block_rows(low, count)
                    grad_pass(weight_ref, prob_ref, (s, rows), query_ref, grad_ref, s, inverse_ref, delta_ref,
                              low_ref, score_ref, rows, key_acc, value_acc, rows)
                    keys = kv_ref[0, rows, :]
                    for c in range(0, columns, CHUNK):
                        span = slice(c, c + CHUNK)
                        total = query_acc[:, span] + query_part(keys, score_ref, rows, span)
                        for h in range(0, CHUNK, BLK):
                            place = slice((c + h) // BLK * width, ((c + h) // BLK + 1) * width)
                            stage[s, :, place] = (total[:, h:h + BLK] * scale).T.astype(BF16)

            for i in range(slot_count - 1):
                @pl.when((s == i) & more[i])
                def _():
                    stage_copy(i).start()

        over_slots(slots, body)
        key_acc[...] = key_acc[...] * scale
        for i in range(slot_count - 1):
            @pl.when(more[i])
            def _():
                stage_copy(i).wait()

        for i in range(block_count):
            @pl.when(assistant[0, base + i] != 1)
            def _():
                blank_copy(i).wait()

    pl.when(sends_late(rank) if early else jnp.logical_not(sends_late(rank)))(run)


def add_kernel(far_rows, need, key_in, value_in, outer_ref, rest_hbm, far_hbm, key_acc, value_acc, rest, far):
    for i, acc in enumerate((key_acc, value_acc)):
        last = acc.shape[0] - outer_ref.shape[1]
        acc[last:, :] += outer_ref[i].astype(F32)

    @pl.when(need[0] > 0)
    def _():
        pltpu.sync_copy(rest_hbm, rest)
        pltpu.sync_copy(far_hbm, far)
        for i, acc in enumerate((key_acc, value_acc)):
            last = acc.shape[0] - outer_ref.shape[1]
            acc[:last, :] += rest[i, far_rows:, :].astype(F32)
            acc[acc.shape[0] - far_rows:, :] += far[i].astype(F32)


def total_kernel(sizes, parity, assistant, turn_first, key_acc, value_acc, stage, *rest):
    query_hbm, key_hbm, value_hbm, low, sem = rest[-5:]
    block_count, slot_count, head_count, width, scale = sizes
    rank = lax.axis_index("ctx")

    @pl.when(lax.rem(rank, 2) == parity)
    def _():
        slots = slots_of(assistant, turn_first, rank * block_count, block_count, slot_count)
        ends = [
            live & jnp.logical_not(slots[s + 1][1]) if s + 1 < slot_count else live
            for s, (_, live, _) in enumerate(slots)
        ]

        def stage_copy(s):
            rows = block_rows(slots[s][0])
            return pltpu.make_async_copy(stage.at[s], query_hbm.at[0, rows], sem.at[2 + s])

        for s in range(slot_count):
            @pl.when(ends[s])
            def _():
                stage_copy(s).start()

        copies = []
        for i, (acc, out) in enumerate(((key_acc, key_hbm), (value_acc, value_hbm))):
            total = acc[...] if parity == 1 else acc[...] + rest[0][i].astype(F32)
            low[i] = total.astype(BF16)
            copies.append(pltpu.make_async_copy(low.at[i], out.at[0], sem.at[i]))
            copies[i].start()
        for copy in copies:
            copy.wait()
        for s in range(slot_count):
            @pl.when(ends[s])
            def _():
                stage_copy(s).wait()


def call(kernel, inputs, in_specs, outputs, out_specs, scratch, limit, macs, aliases={},
         traffic=2 * MIB):
    return pl.pallas_call(
        kernel,
        out_shape=outputs,
        in_specs=in_specs,
        out_specs=out_specs,
        scratch_shapes=scratch,
        input_output_aliases=aliases,
        compiler_params=pltpu.CompilerParams(vmem_limit_bytes=limit * MIB),
        cost_estimate=pl.CostEstimate(flops=2 * macs, bytes_accessed=traffic, transcendentals=0),
    )(*inputs)


ANY_SPEC = pl.BlockSpec(memory_space=pl.ANY)
SMEM_SPEC = pl.BlockSpec(memory_space=pltpu.SMEM)
VMEM_SPEC = pl.BlockSpec(memory_space=pltpu.VMEM)


def score_shapes(sizes, rows):
    block_count, slot_count, head_count, width, scale = sizes
    columns = head_count * BLK
    return (
        pltpu.VMEM((slot_count, rows, columns), F32),
        pltpu.VMEM((slot_count, rows, columns), F32),
        pltpu.VMEM((slot_count, SUB, columns), F32),
        pltpu.VMEM((slot_count, SUB, columns), F32),
    )


def local_shapes(sizes):
    block_count, slot_count, head_count, width, scale = sizes
    rows = pltpu.VMEM((slot_count, head_count * BLK, width), BF16)
    return (rows, rows) + score_shapes(sizes, block_count * BLK)


def local_sems(sizes):
    return pltpu.SemaphoreType.DMA((sizes[1], 2))


def skip_kernel(*refs):
    pass


def whole_kernel(key_ref, value_ref, far_ref, whole_ref):
    first = whole_ref.shape[1] - far_ref.shape[1]
    for i, source in enumerate((key_ref, value_ref)):
        pltpu.sync_copy(source.at[0], whole_ref.at[i])
        pltpu.sync_copy(source.at[0, pl.ds(first, far_ref.shape[1])], far_ref.at[i])


def head_kernel(source_ref, head_ref):
    for i in range(head_ref.shape[0]):
        pltpu.sync_copy(source_ref.at[i, pl.ds(0, head_ref.shape[1])], head_ref.at[i])


def rarely(need, exchange, operands, shapes):
    def skipped(*operands):
        return call(skip_kernel, (), [], tuple(jax.ShapeDtypeStruct(s, BF16) for s in shapes),
                    [ANY_SPEC] * len(shapes), [], 4, 1, {}, 1)

    return tuple(lax.switch(need[0], [skipped, lambda *operands: tuple(exchange(*operands))], *operands))


def per_device(query_rows, key_rows, value_rows, out_grad, assistant, turn_first):
    token_count = query_rows.shape[1]
    width = key_rows.shape[2]
    head_count = query_rows.shape[2] // width
    block_count = token_count // BLK
    far_rows = block_count // 2 * BLK
    reach_rows = token_count + far_rows
    slot_count = (block_count + 1) // 2
    columns = head_count * BLK
    pair = columns * BLK * width
    sizes = (block_count, slot_count, head_count, width, 1.0 / math.sqrt(width))
    stat_rows = (slot_count, SUB, columns)
    last, own, assistant, turn_first, need = call(
        lambda *refs: pack_kernel(block_count, *refs),
        tuple(hbm(a) for a in (key_rows, value_rows, assistant, turn_first)),
        [ANY_SPEC] * 4,
        (
            pltpu.VMEM((2, far_rows, width), BF16),
            pltpu.VMEM((2, token_count, width), BF16),
            pltpu.SMEM(assistant.shape, jnp.int32),
            pltpu.SMEM(turn_first.shape, jnp.int32),
            pltpu.SMEM((1,), jnp.int32),
        ),
        [VMEM_SPEC] * 2 + [SMEM_SPEC] * 3,
        [pltpu.SemaphoreType.DMA((6,))],
        4,
        BLK,
    )
    marks = (smem(assistant), smem(turn_first))
    flag = smem(need)
    far_shape = jax.ShapeDtypeStruct((2, far_rows, width), BF16)
    whole_shape = jax.ShapeDtypeStruct((2, token_count, width), BF16)

    def exchange(keys, values):
        far, whole = call(whole_kernel, (keys, values), [ANY_SPEC] * 2, (far_shape, whole_shape),
                          [ANY_SPEC] * 2, [], 4, 1, {}, 1)
        return shifted(far, "ctx", 2), pair_shift(whole, "ctx", 1, 0)

    def exchange_back(beyond):
        far = call(head_kernel, (beyond,), [ANY_SPEC], far_shape, ANY_SPEC, [], 4, 1, {}, 1)
        return pair_shift(beyond, "ctx", -1, 0), shifted(far, "ctx", -2)

    far_in, whole_in = rarely(
        need,
        exchange,
        (key_rows, value_rows),
        [far_shape.shape, whole_shape.shape],
    )
    own, far_in, whole_in = lax.optimization_barrier((own, far_in, whole_in))

    def local(early, state):
        return call(
            lambda *refs: local_kernel(sizes, early, *refs),
            marks + (hbm(query_rows), hbm(out_grad), vmem(own)) + tuple(vmem(a) for a in state),
            [SMEM_SPEC] * 2 + [ANY_SPEC] * 2 + [VMEM_SPEC] * (1 + len(state)),
            local_shapes(sizes),
            [VMEM_SPEC] * 6,
            [local_sems(sizes)],
            8,
            pair,
            {5 + i: i for i in range(len(state))},
            1,
        )

    local_state = local(True, ())
    last, own, local_state = lax.optimization_barrier((last, own, local_state))
    outer_in = pair_shift(last, "ctx", 1, 0)
    inner_in = pair_shift(own, "ctx", 1, 1)
    local_state = local(False, local_state)
    query_slots, grad_slots, weights, prob_grad, sums, dots = local_state
    near_state = window = remote_state = ()
    near_grads = []
    for parity, sources in ((0, (vmem(outer_in), hbm(whole_in))), (1, (vmem(inner_in),))):
        inputs = marks + (flag, vmem(query_slots), vmem(grad_slots), hbm(far_in)) + sources
        kept = tuple(vmem(a) for a in tuple(near_state) + window)
        *near_state, sum_near, dot_near, window = call(
            lambda *refs: near_kernel(sizes, parity, *refs),
            inputs + kept,
            [SMEM_SPEC] * 3 + [VMEM_SPEC] * 2 + [ANY_SPEC, VMEM_SPEC]
            + [ANY_SPEC] * (len(sources) - 1) + [VMEM_SPEC] * len(kept),
            score_shapes(sizes, reach_rows) + (pltpu.VMEM((reach_rows, width), BF16),),
            [VMEM_SPEC] * 5,
            [pltpu.VMEM((reach_rows, width), BF16), pltpu.SemaphoreType.DMA((4,))],
            8,
            NEAR_HINT[parity] * pair,
            {len(inputs) + i: i if i < 2 else 4 for i in range(len(kept))},
            1,
        )
        window = (window,)
        inputs = marks + (flag,) + tuple(vmem(a) for a in (query_slots, grad_slots, sums, dots))
        near_inputs = tuple(vmem(a) for a in tuple(near_state) + (sum_near, dot_near))
        kept = tuple(vmem(a) for a in remote_state[:3]) + tuple(hbm(a) for a in remote_state[3:])
        score_arrays = score_shapes(sizes, reach_rows)[:2] if parity == 0 else ()
        aliases = {len(inputs) + 4 + i: i for i in range(len(kept))}
        aliases.update({len(inputs) + i: 4 + i for i in range(len(score_arrays))})
        *remote_state, near_grad = call(
            lambda *refs: remote_kernel(sizes, parity, *refs),
            inputs + near_inputs + kept,
            [SMEM_SPEC] * 3 + [VMEM_SPEC] * (8 + len(kept[:3])) + [ANY_SPEC] * len(kept[3:]),
            (
                pltpu.VMEM((slot_count, reach_rows, columns), BF16),
                pltpu.VMEM(stat_rows, F32),
                pltpu.VMEM(stat_rows, F32),
                jax.ShapeDtypeStruct((2, token_count, width), BF16),
            )
            + score_arrays
            + (pltpu.VMEM((2, sources[0].shape[1], width), BF16),),
            [VMEM_SPEC] * 3 + [ANY_SPEC] + [VMEM_SPEC] * (1 + len(score_arrays)),
            [
                pltpu.VMEM((token_count, columns), BF16),
                pltpu.VMEM((reach_rows, width), F32),
                pltpu.VMEM((reach_rows, width), F32),
                pltpu.VMEM((2, token_count, width), BF16),
            ],
            8,
            REMOTE_HINT[parity] * pair,
            aliases,
            1,
        )
        near_state = remote_state[4:]
        remote_state = tuple(remote_state[:4])
        near_grads.append(near_grad)
        if parity == 0:
            outer_back = pair_shift(near_grad, "ctx", -1, 0)
    score_grad, inverse, delta, beyond = remote_state

    def finish(early, state):
        inputs = marks + tuple(
            vmem(a)
            for a in (query_slots, grad_slots, weights, prob_grad, score_grad, inverse, delta, own) + window
        )
        return call(
            lambda *refs: finish_kernel(sizes, early, *refs),
            inputs + tuple(hbm(a) for a in state[:1]) + tuple(vmem(a) for a in state[1:]),
            [SMEM_SPEC] * 2 + [VMEM_SPEC] * 9 + [ANY_SPEC] * len(state[:1]) + [VMEM_SPEC] * len(state[1:]),
            (
                jax.ShapeDtypeStruct(query_rows.shape, BF16),
                pltpu.VMEM((token_count, width), F32),
                pltpu.VMEM((token_count, width), F32),
                pltpu.VMEM((slot_count, BLK, head_count * width), BF16),
            ),
            [ANY_SPEC] + [VMEM_SPEC] * 3,
            [
                pltpu.VMEM((slot_count, token_count, columns), BF16),
                pltpu.VMEM((token_count, columns), BF16),
                pltpu.VMEM((BLK, columns), F32),
                pltpu.VMEM((BLK, head_count * width), BF16),
                pltpu.SemaphoreType.DMA((slot_count + block_count,)),
            ],
            10,
            pair,
            {len(inputs) + i: i for i in range(len(state))},
            1,
        )

    state = finish(True, ())
    inner_grad, state = lax.optimization_barrier((near_grads[1], state))
    inner_back = pair_shift(inner_grad, "ctx", -1, 1)
    query_grad, key_acc, value_acc, stage = finish(False, tuple(state))
    beyond, query_grad = lax.optimization_barrier((beyond, query_grad))
    rest_back, far_back = rarely(
        need,
        exchange_back,
        (beyond,),
        [beyond.shape, far_in.shape],
    )
    key_acc, value_acc = call(
        lambda *refs: add_kernel(far_rows, *refs),
        (flag,) + tuple(vmem(a) for a in (key_acc, value_acc, outer_back)) + (hbm(rest_back), hbm(far_back)),
        [SMEM_SPEC] + [VMEM_SPEC] * 3 + [ANY_SPEC] * 2,
        (pltpu.VMEM((token_count, width), F32),) * 2,
        [VMEM_SPEC] * 2,
        [pltpu.VMEM(beyond.shape, BF16), pltpu.VMEM(far_in.shape, BF16)],
        4,
        CROSS_HINT * pair,
        {1: 0, 2: 1},
        1,
    )
    results = (query_grad,)
    for parity, received in ((1, ()), (0, (vmem(inner_back),))):
        inputs = marks + tuple(vmem(a) for a in (key_acc, value_acc, stage)) + received
        results = call(
            lambda *refs: total_kernel(sizes, parity, *refs),
            inputs + tuple(hbm(a) for a in results),
            [SMEM_SPEC] * 2 + [VMEM_SPEC] * (len(inputs) - 2) + [ANY_SPEC] * len(results),
            tuple(jax.ShapeDtypeStruct(a.shape, BF16) for a in (query_rows, key_rows, value_rows)),
            [ANY_SPEC] * 3,
            [pltpu.VMEM((2, token_count, width), BF16), pltpu.SemaphoreType.DMA((2 + slot_count,))],
            8,
            pair,
            {len(inputs) + i: i for i in range(len(results))},
            1,
        )
    return tuple(results)


def solution(mesh):
    return jax.shard_map(
        per_device,
        mesh=mesh,
        in_specs=(
            P("dp", "ctx", "tp"),
            P("dp", "ctx", "tp"),
            P("dp", "ctx", "tp"),
            P("dp", "ctx", "tp"),
            P("dp", None),
            P("dp", None),
        ),
        out_specs=(P("dp", "ctx", "tp"), P("dp", "ctx", "tp"), P("dp", "ctx", "tp")),
        check_vma=False,
    )
```

```python
import math

import jax
import jax.numpy as jnp
from jax import lax
from jax.experimental import pallas as pl
from jax.experimental.pallas import tpu as pltpu
from jax.sharding import PartitionSpec as P

BLK = 128
SUB = 8
CHUNK = 256
F32 = jnp.float32
BF16 = jnp.bfloat16
MIB = 1 << 20
NEAR_HINT = (400, 10)
REMOTE_HINT = (14, 14)
CROSS_HINT = 60


def shifted(block, axis, distance):
    devices = range(lax.axis_size(axis))
    route = [(i - distance, i) for i in devices if i - distance in devices]
    return lax.ppermute(block, axis, route)


def pair_shift(block, axis, distance, parity):
    pairs = [(i - 1, i) for i in range(1, lax.axis_size(axis)) if i % 2 == parity]
    return lax.ppermute(block, axis, pairs if distance == 1 else [pair[::-1] for pair in pairs])


def vmem(array):
    return pltpu.with_memory_space_constraint(array, pltpu.VMEM)


def smem(array):
    return pltpu.with_memory_space_constraint(array, pltpu.SMEM)


def hbm(array):
    return pltpu.with_memory_space_constraint(array, pltpu.HBM)


def nt_dot(left, right):
    return lax.dot_general(left, right, (((1,), (1,)), ((), ())), preferred_element_type=F32)


def nn_dot(left, right):
    return lax.dot_general(left, right, (((1,), (0,)), ((), ())), preferred_element_type=F32)


def fold(tile):
    return jnp.sum(tile.reshape(tile.shape[0] // SUB, SUB, tile.shape[1]), axis=0)


def slots_of(assistant, turn_first, base, block_count, slot_count):
    found = jnp.int32(0)
    blocks = [jnp.int32(0)] * slot_count
    starts = [jnp.int32(0)] * slot_count
    for i in range(block_count):
        mark = assistant[0, base + i]
        start = turn_first[0, base + i] - base
        for s in range(slot_count):
            here = (mark == 1) & (found == s)
            blocks[s] = jnp.where(here, i, blocks[s])
            starts[s] = jnp.where(here, start, starts[s])
        found = found + jnp.where(mark == 1, 1, 0)
    return [(blocks[s], found > s, starts[s]) for s in range(slot_count)]


def score_pass(key_tile, value_tile, query_ref, grad_ref, slot, keep, weight_ref, prob_ref, at, sum_ref,
               dot_ref, scale):
    columns = query_ref.shape[1]
    for c in range(0, columns, CHUNK):
        span = slice(c, c + CHUNK)
        scores = nt_dot(key_tile, query_ref[slot, span, :])
        prob_grad = nt_dot(value_tile, grad_ref[slot, span, :])
        weights = jnp.exp2(scores * scale)
        if keep is not None:
            weights = jnp.where(jnp.concatenate([keep] * (CHUNK // BLK), axis=1), weights, 0.0)
        weight_ref[at + (span,)] = weights
        prob_ref[at + (span,)] = prob_grad
        sum_ref[slot, :, span] += fold(weights)
        dot_ref[slot, :, span] += fold(weights * prob_grad)


def grad_pass(weight_ref, prob_ref, at, query_ref, grad_ref, slot, inverse_ref, delta_ref, low_ref,
              score_ref, score_rows, key_acc, value_acc, acc_rows):
    columns = query_ref.shape[1]
    height = acc_rows.size
    for c in range(0, columns, CHUNK):
        span = slice(c, c + CHUNK)
        shape = (height // SUB, SUB, CHUNK)
        attention = weight_ref[at + (span,)].reshape(shape) * inverse_ref[slot, :, span][None]
        lifted = prob_ref[at + (span,)].reshape(shape) - delta_ref[slot, :, span][None]
        score_grad = (attention * lifted).reshape(height, CHUNK)
        low_ref[:height, span] = attention.reshape(height, CHUNK).astype(BF16)
        score_ref[slot, score_rows, span] = score_grad.astype(BF16)
    value_acc[acc_rows, :] += nn_dot(low_ref[:height], grad_ref[slot])
    key_acc[acc_rows, :] += nn_dot(score_ref[slot, score_rows, :], query_ref[slot])


def block_rows(index, count=1):
    return pl.ds(pl.multiple_of(index * BLK, BLK), count * BLK)


def pick(values, s):
    chosen = values[0]
    for i in range(1, len(values)):
        chosen = jnp.where(s == i, values[i], chosen)
    return chosen


def over_slots(slots, body):
    def step(s, carry):
        block, start = (pick([slot[i] for slot in slots], s) for i in (0, 2))

        @pl.when(pick([jnp.where(slot[1], 1, 0) for slot in slots], s) == 1)
        def _():
            body(s, block, start)

        return carry

    lax.fori_loop(0, len(slots), step, 0)


def local_scores(sizes, assistant, turn_first, query_hbm, grad_hbm, kv_ref, query_ref, grad_ref,
                 weight_ref, prob_ref, sum_ref, dot_ref, sem):
    block_count, slot_count, head_count, width, scale = sizes
    base = lax.axis_index("ctx") * block_count
    slots = slots_of(assistant, turn_first, base, block_count, slot_count)

    def copies(s, block):
        for i, (source, target) in enumerate(((query_hbm, query_ref), (grad_hbm, grad_ref))):
            for h in range(head_count):
                yield pltpu.make_async_copy(
                    source.at[0, block_rows(block), pl.ds(h * width, width)],
                    target.at[s, pl.ds(h * BLK, BLK)],
                    sem.at[s, i],
                )

    for s, (block, live, start) in enumerate(slots):
        @pl.when(live)
        def _():
            for copy in copies(s, block):
                copy.start()
    sum_ref[...] = jnp.zeros_like(sum_ref)
    dot_ref[...] = jnp.zeros_like(dot_ref)
    ahead = lax.broadcasted_iota(jnp.int32, (BLK, BLK), 1) - lax.broadcasted_iota(
        jnp.int32, (BLK, BLK), 0
    )
    def body(s, block, start):
        for i, target in enumerate((query_ref, grad_ref)):
            pltpu.make_async_copy(target.at[s], target.at[s], sem.at[s, i]).wait()

        def step(k, carry):
            rows = block_rows(k)
            score_pass(kv_ref[0, rows, :], kv_ref[1, rows, :], query_ref, grad_ref, s,
                       ahead >= (k - block) * BLK, weight_ref, prob_ref, (s, rows), sum_ref, dot_ref,
                       scale * math.log2(math.e))
            return carry

        lax.fori_loop(jnp.maximum(start, 0), block + 1, step, 0)

    over_slots(slots, body)


def in_first_half():
    return lax.axis_index("ctx") * 2 < lax.axis_size("ctx")


def local_kernel(sizes, early, *refs):
    inputs, results = refs[:5], refs[-7:]
    here = in_first_half() if early else jnp.logical_not(in_first_half())
    pl.when(here)(lambda: local_scores(sizes, *inputs, *results))


def pack_kernel(block_count, key_ref, value_ref, assistant_ref, turn_ref, last_ref, all_ref, assistant,
                turn_first, need_ref, pack_sem):
    token_count = key_ref.shape[1]
    marks = [
        pltpu.make_async_copy(assistant_ref, assistant, pack_sem.at[0]),
        pltpu.make_async_copy(turn_ref, turn_first, pack_sem.at[1]),
    ]
    copies = []
    for pack in (all_ref, last_ref):
        rows = pack.shape[1]
        for i, source in enumerate((key_ref, value_ref)):
            copies.append(
                pltpu.make_async_copy(
                    source.at[0, pl.ds(token_count - rows, rows)], pack.at[i], pack_sem.at[2 + len(copies)]
                )
            )
    for copy in marks + copies:
        copy.start()
    for copy in marks:
        copy.wait()
    outer = far = jnp.int32(0)
    for i in range(block_count, assistant.shape[1]):
        device = i // block_count
        behind = jnp.where(assistant[0, i] == 1, device * block_count - turn_first[0, i], 0)
        far = jnp.where(behind > block_count, 1, far)
        if device % 2 == 0:
            outer = jnp.maximum(outer, behind)
    need_ref[0] = jnp.where(outer > 1, 2, far)

    for copy in copies:
        copy.wait()


def over_window(block_count, reach, start, whole, body):
    first = jnp.maximum(start + reach, 0)
    last = reach
    if whole:
        @pl.when(start <= -block_count)
        def _():
            body(pl.ds((reach - block_count) * BLK, block_count * BLK))

        last = jnp.where(start <= -block_count, reach - block_count, reach)

    def step(k, carry):
        body(block_rows(k))
        return carry

    lax.fori_loop(first, last, step, 0)


def near_kernel(sizes, parity, assistant, turn_first, need, query_ref, grad_ref, far_hbm, *rest):
    weight_ref, prob_ref, sum_ref, dot_ref, window, values, sem = rest[-7:]
    block_count, slot_count, head_count, width, scale = sizes
    rank = lax.axis_index("ctx")
    reach = window.shape[0] // BLK
    near = pl.ds((reach - block_count) * BLK, block_count * BLK)

    def fill(rows, source):
        window[rows, :] = source[0]
        values[rows, :] = source[1]

    def fetch(rows, source, first_sem):
        return [
            pltpu.make_async_copy(source.at[i], target.at[rows], sem.at[first_sem + i])
            for i, target in enumerate((window, values))
        ]

    def body(s, block, start):
        def scores(rows):
            score_pass(window[rows, :], values[rows, :], query_ref, grad_ref, s, None, weight_ref,
                       prob_ref, (s, rows), sum_ref, dot_ref, scale * math.log2(math.e))

        over_window(block_count, reach, start, parity == 1, scores)

    @pl.when(lax.rem(rank, 2) == parity)
    def _():
        if parity == 1:
            fill(near, rest[0])
        else:
            fill(block_rows(reach - 1), rest[0])

        @pl.when(need[0] > 0)
        def _():
            copies = fetch(pl.ds(0, far_hbm.shape[1]), far_hbm, 0)
            for copy in copies:
                copy.start()
            for copy in copies:
                copy.wait()

        if parity == 0:
            @pl.when(need[0] > 1)
            def _():
                copies = fetch(near, rest[1], 2)
                for copy in copies:
                    copy.start()
                for copy in copies:
                    copy.wait()

        sum_ref[...] = jnp.zeros_like(sum_ref)
        dot_ref[...] = jnp.zeros_like(dot_ref)
        over_slots(slots_of(assistant, turn_first, rank * block_count, block_count, slot_count), body)


def remote_kernel(sizes, parity, assistant, turn_first, need, query_ref, grad_ref, sum_local, dot_local,
                  weight_near, prob_near, sum_near, dot_near, *rest):
    block_count, slot_count, head_count, width, scale = sizes
    (score_ref, inverse_ref, delta_ref, far_hbm, rest_hbm, *_, near_out, low_ref, key_acc, value_acc, far_low,
     rest_low) = rest[-13 + 2 * parity:]
    rank = lax.axis_index("ctx")
    reach = weight_near.shape[1] // BLK

    def body(s, block, start):
        inverse = 1.0 / jnp.sum(sum_local[s] + sum_near[s], axis=0, keepdims=True)
        delta = jnp.sum(dot_local[s] + dot_near[s], axis=0, keepdims=True) * inverse
        inverse_ref[s] = jnp.broadcast_to(inverse, inverse_ref.shape[1:])
        delta_ref[s] = jnp.broadcast_to(delta, delta_ref.shape[1:])

        def gradients_of(rows):
            grad_pass(weight_near, prob_near, (s, rows), query_ref, grad_ref, s, inverse_ref, delta_ref,
                      low_ref, score_ref, rows, key_acc, value_acc, rows)

        over_window(block_count, reach, start, parity == 1, gradients_of)

    @pl.when(lax.rem(rank, 2) == parity)
    def _():
        key_acc[...] = jnp.zeros_like(key_acc)
        value_acc[...] = jnp.zeros_like(value_acc)
        over_slots(slots_of(assistant, turn_first, rank * block_count, block_count, slot_count), body)

        def round_to(out, first, rows):
            out[0] = (key_acc[first:first + rows, :] * scale).astype(BF16)
            out[1] = value_acc[first:first + rows, :].astype(BF16)

        total = reach * BLK
        round_to(near_out, total - near_out.shape[1], near_out.shape[1])

        @pl.when(need[0] > 0)
        def _():
            round_to(far_low, 0, far_low.shape[1])
            pltpu.sync_copy(far_low, far_hbm)

        if parity == 0:
            @pl.when(need[0] > 1)
            def _():
                round_to(rest_low, far_low.shape[1], rest_low.shape[1])
                pltpu.sync_copy(rest_low, rest_hbm)


def sends_late(rank):
    return (lax.rem(rank, 2) == 1) & (rank > 1)


def finish_kernel(sizes, early, assistant, turn_first, query_ref, grad_ref, weight_ref, prob_ref, score_in,
                  inverse_ref, delta_ref, kv_ref, window, *rest):
    query_hbm, key_acc, value_acc, stage, score_ref, low_ref, query_acc, blank, sem = rest[-9:]
    block_count, slot_count, head_count, width, scale = sizes
    rank = lax.axis_index("ctx")
    base = rank * block_count
    reach = window.shape[0] // BLK
    columns = query_acc.shape[1]

    def blank_copy(i):
        return pltpu.make_async_copy(blank, query_hbm.at[0, pl.ds(i * BLK, BLK)], sem.at[slot_count + i])

    def run():
        slots = slots_of(assistant, turn_first, base, block_count, slot_count)
        more = [live for _, live, _ in slots[1:]]

        def stage_copy(s):
            return pltpu.make_async_copy(stage.at[s], query_hbm.at[0, block_rows(slots[s][0])], sem.at[s])

        blank[...] = jnp.zeros_like(blank)
        for i in range(block_count):
            @pl.when(assistant[0, base + i] != 1)
            def _():
                blank_copy(i).start()
        key_acc[...] = jnp.zeros_like(key_acc)
        value_acc[...] = jnp.zeros_like(value_acc)

        def body(s, block, start):
            def query_part(keys, source, rows, span):
                return nn_dot(keys.T, source[s, rows, span])

            query_acc[...] = jnp.zeros_like(query_acc)

            def remote_part(rows):
                keys = window[rows, :]
                for c in range(0, columns, CHUNK):
                    span = slice(c, c + CHUNK)
                    query_acc[:, span] += query_part(keys, score_in, rows, span)

            over_window(block_count, reach, start, True, remote_part)
            low = jnp.maximum(start, 0)
            for count in range(1, block_count + 1):
                @pl.when(block + 1 - low == count)
                def _():
                    rows = block_rows(low, count)
                    grad_pass(weight_ref, prob_ref, (s, rows), query_ref, grad_ref, s, inverse_ref, delta_ref,
                              low_ref, score_ref, rows, key_acc, value_acc, rows)
                    keys = kv_ref[0, rows, :]
                    for c in range(0, columns, CHUNK):
                        span = slice(c, c + CHUNK)
                        total = query_acc[:, span] + query_part(keys, score_ref, rows, span)
                        for h in range(0, CHUNK, BLK):
                            place = slice((c + h) // BLK * width, ((c + h) // BLK + 1) * width)
                            stage[s, :, place] = (total[:, h:h + BLK] * scale).T.astype(BF16)

            for i in range(slot_count - 1):
                @pl.when((s == i) & more[i])
                def _():
                    stage_copy(i).start()

        over_slots(slots, body)
        key_acc[...] = key_acc[...] * scale
        for i in range(slot_count - 1):
            @pl.when(more[i])
            def _():
                stage_copy(i).wait()

        for i in range(block_count):
            @pl.when(assistant[0, base + i] != 1)
            def _():
                blank_copy(i).wait()

    pl.when(sends_late(rank) if early else jnp.logical_not(sends_late(rank)))(run)


def add_kernel(need, key_in, value_in, outer_ref, far_hbm, rest_hbm, key_acc, value_acc, far, rest):
    pairs = list(enumerate((key_acc, value_acc)))

    def add_last(source):
        for i, acc in pairs:
            acc[acc.shape[0] - source.shape[1]:, :] += source[i].astype(F32)

    add_last(outer_ref)

    @pl.when(need[0] > 0)
    def _():
        pltpu.sync_copy(far_hbm, far)
        add_last(far)

    @pl.when(need[0] > 1)
    def _():
        pltpu.sync_copy(rest_hbm, rest)
        for i, acc in pairs:
            acc[:rest.shape[1], :] += rest[i].astype(F32)


def total_kernel(sizes, parity, assistant, turn_first, key_acc, value_acc, stage, *rest):
    query_hbm, key_hbm, value_hbm, low, sem = rest[-5:]
    block_count, slot_count, head_count, width, scale = sizes
    rank = lax.axis_index("ctx")

    @pl.when(lax.rem(rank, 2) == parity)
    def _():
        slots = slots_of(assistant, turn_first, rank * block_count, block_count, slot_count)
        ends = [
            live & jnp.logical_not(slots[s + 1][1]) if s + 1 < slot_count else live
            for s, (_, live, _) in enumerate(slots)
        ]

        def stage_copy(s):
            rows = block_rows(slots[s][0])
            return pltpu.make_async_copy(stage.at[s], query_hbm.at[0, rows], sem.at[2 + s])

        for s in range(slot_count):
            @pl.when(ends[s])
            def _():
                stage_copy(s).start()

        copies = []
        for i, (acc, out) in enumerate(((key_acc, key_hbm), (value_acc, value_hbm))):
            total = acc[...] if parity == 1 else acc[...] + rest[0][i].astype(F32)
            low[i] = total.astype(BF16)
            copies.append(pltpu.make_async_copy(low.at[i], out.at[0], sem.at[i]))
            copies[i].start()
        for copy in copies:
            copy.wait()
        for s in range(slot_count):
            @pl.when(ends[s])
            def _():
                stage_copy(s).wait()


def call(kernel, inputs, in_specs, outputs, out_specs, scratch, limit, macs, aliases={},
         traffic=2 * MIB):
    return pl.pallas_call(
        kernel,
        out_shape=outputs,
        in_specs=in_specs,
        out_specs=out_specs,
        scratch_shapes=scratch,
        input_output_aliases=aliases,
        compiler_params=pltpu.CompilerParams(vmem_limit_bytes=limit * MIB),
        cost_estimate=pl.CostEstimate(flops=2 * macs, bytes_accessed=traffic, transcendentals=0),
    )(*inputs)


ANY_SPEC = pl.BlockSpec(memory_space=pl.ANY)
SMEM_SPEC = pl.BlockSpec(memory_space=pltpu.SMEM)
VMEM_SPEC = pl.BlockSpec(memory_space=pltpu.VMEM)


def score_shapes(sizes, rows):
    block_count, slot_count, head_count, width, scale = sizes
    columns = head_count * BLK
    return (
        pltpu.VMEM((slot_count, rows, columns), F32),
        pltpu.VMEM((slot_count, rows, columns), F32),
        pltpu.VMEM((slot_count, SUB, columns), F32),
        pltpu.VMEM((slot_count, SUB, columns), F32),
    )


def local_shapes(sizes):
    block_count, slot_count, head_count, width, scale = sizes
    rows = pltpu.VMEM((slot_count, head_count * BLK, width), BF16)
    return (rows, rows) + score_shapes(sizes, block_count * BLK)


def local_sems(sizes):
    return pltpu.SemaphoreType.DMA((sizes[1], 2))


def skip_kernel(*refs):
    pass


def stack_kernel(key_ref, value_ref, *outs):
    *outs, sem = outs
    copies = []
    for out in outs:
        first = key_ref.shape[1] - out.shape[1]
        for i, source in enumerate((key_ref, value_ref)):
            copies.append(
                pltpu.make_async_copy(
                    source.at[0, pl.ds(first, out.shape[1])], out.at[i], sem.at[len(copies)]
                )
            )
    for copy in copies:
        copy.start()
    for copy in copies:
        copy.wait()


def skipped(*shapes):
    return tuple(call(skip_kernel, (), [], shapes, [ANY_SPEC] * len(shapes), [], 4, 1, {}, 1))


def per_device(query_rows, key_rows, value_rows, out_grad, assistant, turn_first):
    token_count = query_rows.shape[1]
    width = key_rows.shape[2]
    head_count = query_rows.shape[2] // width
    block_count = token_count // BLK
    far_rows = block_count // 2 * BLK
    reach_rows = token_count + far_rows
    slot_count = (block_count + 1) // 2
    columns = head_count * BLK
    pair = columns * BLK * width
    sizes = (block_count, slot_count, head_count, width, 1.0 / math.sqrt(width))
    stat_rows = (slot_count, SUB, columns)
    last, own, assistant, turn_first, need = call(
        lambda *refs: pack_kernel(block_count, *refs),
        tuple(hbm(a) for a in (key_rows, value_rows, assistant, turn_first)),
        [ANY_SPEC] * 4,
        (
            pltpu.VMEM((2, far_rows, width), BF16),
            pltpu.VMEM((2, token_count, width), BF16),
            pltpu.SMEM(assistant.shape, jnp.int32),
            pltpu.SMEM(turn_first.shape, jnp.int32),
            pltpu.SMEM((1,), jnp.int32),
        ),
        [VMEM_SPEC] * 2 + [SMEM_SPEC] * 3,
        [pltpu.SemaphoreType.DMA((6,))],
        4,
        BLK,
    )
    marks = (smem(assistant), smem(turn_first))
    flag = smem(need)
    far_shape = jax.ShapeDtypeStruct((2, far_rows, width), BF16)
    whole_shape = jax.ShapeDtypeStruct((2, token_count, width), BF16)
    rest_shape = jax.ShapeDtypeStruct((2, token_count - far_rows, width), BF16)

    def stacked(sources, *shapes):
        return call(stack_kernel, sources, [ANY_SPEC] * 2, shapes, [ANY_SPEC] * len(shapes),
                    [pltpu.SemaphoreType.DMA((2 * len(shapes),))], 4, 1, {}, 1)

    def far_only(*sources):
        far, = stacked(sources, far_shape)
        return (shifted(far, "ctx", 2),) + skipped(whole_shape)

    def far_and_whole(*sources):
        far, whole = stacked(sources, far_shape, whole_shape)
        return shifted(far, "ctx", 2), pair_shift(whole, "ctx", 1, 0)

    far_in, whole_in = lax.switch(
        need[0], [lambda *_: skipped(far_shape, whole_shape), far_only, far_and_whole], key_rows, value_rows
    )
    own, far_in, whole_in = lax.optimization_barrier((own, far_in, whole_in))

    def local(early, state):
        return call(
            lambda *refs: local_kernel(sizes, early, *refs),
            marks + (hbm(query_rows), hbm(out_grad), vmem(own)) + tuple(vmem(a) for a in state),
            [SMEM_SPEC] * 2 + [ANY_SPEC] * 2 + [VMEM_SPEC] * (1 + len(state)),
            local_shapes(sizes),
            [VMEM_SPEC] * 6,
            [local_sems(sizes)],
            8,
            pair,
            {5 + i: i for i in range(len(state))},
            1,
        )

    local_state = local(True, ())
    last, own, local_state = lax.optimization_barrier((last, own, local_state))
    outer_in = pair_shift(last, "ctx", 1, 0)
    inner_in = pair_shift(own, "ctx", 1, 1)
    local_state = local(False, local_state)
    query_slots, grad_slots, weights, prob_grad, sums, dots = local_state
    near_state = window = remote_state = ()
    near_grads = []
    for parity, sources in ((0, (vmem(outer_in), hbm(whole_in))), (1, (vmem(inner_in),))):
        inputs = marks + (flag, vmem(query_slots), vmem(grad_slots), hbm(far_in)) + sources
        kept = tuple(vmem(a) for a in tuple(near_state) + window)
        *near_state, sum_near, dot_near, window = call(
            lambda *refs: near_kernel(sizes, parity, *refs),
            inputs + kept,
            [SMEM_SPEC] * 3 + [VMEM_SPEC] * 2 + [ANY_SPEC, VMEM_SPEC]
            + [ANY_SPEC] * (len(sources) - 1) + [VMEM_SPEC] * len(kept),
            score_shapes(sizes, reach_rows) + (pltpu.VMEM((reach_rows, width), BF16),),
            [VMEM_SPEC] * 5,
            [pltpu.VMEM((reach_rows, width), BF16), pltpu.SemaphoreType.DMA((4,))],
            8,
            NEAR_HINT[parity] * pair,
            {len(inputs) + i: i if i < 2 else 4 for i in range(len(kept))},
            1,
        )
        window = (window,)
        inputs = marks + (flag,) + tuple(vmem(a) for a in (query_slots, grad_slots, sums, dots))
        near_inputs = tuple(vmem(a) for a in tuple(near_state) + (sum_near, dot_near))
        kept = tuple(vmem(a) for a in remote_state[:3]) + tuple(hbm(a) for a in remote_state[3:])
        score_arrays = score_shapes(sizes, reach_rows)[:2] if parity == 0 else ()
        aliases = {len(inputs) + 4 + i: i for i in range(len(kept))}
        aliases.update({len(inputs) + i: 5 + i for i in range(len(score_arrays))})
        *remote_state, near_grad = call(
            lambda *refs: remote_kernel(sizes, parity, *refs),
            inputs + near_inputs + kept,
            [SMEM_SPEC] * 3 + [VMEM_SPEC] * (8 + len(kept[:3])) + [ANY_SPEC] * len(kept[3:]),
            (
                pltpu.VMEM((slot_count, reach_rows, columns), BF16),
                pltpu.VMEM(stat_rows, F32),
                pltpu.VMEM(stat_rows, F32),
                far_shape,
                rest_shape,
            )
            + score_arrays
            + (pltpu.VMEM((2, sources[0].shape[1], width), BF16),),
            [VMEM_SPEC] * 3 + [ANY_SPEC] * 2 + [VMEM_SPEC] * (1 + len(score_arrays)),
            [
                pltpu.VMEM((token_count, columns), BF16),
                pltpu.VMEM((reach_rows, width), F32),
                pltpu.VMEM((reach_rows, width), F32),
                pltpu.VMEM(far_shape.shape, BF16),
                pltpu.VMEM(rest_shape.shape, BF16),
            ],
            8,
            REMOTE_HINT[parity] * pair,
            aliases,
            1,
        )
        near_state = remote_state[5:]
        remote_state = tuple(remote_state[:5])
        near_grads.append(near_grad)
        if parity == 0:
            outer_back = pair_shift(near_grad, "ctx", -1, 0)
    score_grad, inverse, delta, far_grad, rest_grad = remote_state

    def finish(early, state):
        inputs = marks + tuple(
            vmem(a)
            for a in (query_slots, grad_slots, weights, prob_grad, score_grad, inverse, delta, own) + window
        )
        return call(
            lambda *refs: finish_kernel(sizes, early, *refs),
            inputs + tuple(hbm(a) for a in state[:1]) + tuple(vmem(a) for a in state[1:]),
            [SMEM_SPEC] * 2 + [VMEM_SPEC] * 9 + [ANY_SPEC] * len(state[:1]) + [VMEM_SPEC] * len(state[1:]),
            (
                jax.ShapeDtypeStruct(query_rows.shape, BF16),
                pltpu.VMEM((token_count, width), F32),
                pltpu.VMEM((token_count, width), F32),
                pltpu.VMEM((slot_count, BLK, head_count * width), BF16),
            ),
            [ANY_SPEC] + [VMEM_SPEC] * 3,
            [
                pltpu.VMEM((slot_count, token_count, columns), BF16),
                pltpu.VMEM((token_count, columns), BF16),
                pltpu.VMEM((BLK, columns), F32),
                pltpu.VMEM((BLK, head_count * width), BF16),
                pltpu.SemaphoreType.DMA((slot_count + block_count,)),
            ],
            10,
            pair,
            {len(inputs) + i: i for i in range(len(state))},
            1,
        )

    state = finish(True, ())
    inner_grad, state = lax.optimization_barrier((near_grads[1], state))
    inner_back = pair_shift(inner_grad, "ctx", -1, 1)
    query_grad, key_acc, value_acc, stage = finish(False, tuple(state))
    far_grad, rest_grad, query_grad = lax.optimization_barrier((far_grad, rest_grad, query_grad))
    far_back, rest_back = lax.switch(
        need[0],
        [
            lambda far, rest: skipped(far_shape, rest_shape),
            lambda far, rest: (shifted(far, "ctx", -2),) + skipped(rest_shape),
            lambda far, rest: (shifted(far, "ctx", -2), pair_shift(rest, "ctx", -1, 0)),
        ],
        far_grad,
        rest_grad,
    )
    key_acc, value_acc = call(
        add_kernel,
        (flag,) + tuple(vmem(a) for a in (key_acc, value_acc, outer_back)) + (hbm(far_back), hbm(rest_back)),
        [SMEM_SPEC] + [VMEM_SPEC] * 3 + [ANY_SPEC] * 2,
        (pltpu.VMEM((token_count, width), F32),) * 2,
        [VMEM_SPEC] * 2,
        [pltpu.VMEM(far_shape.shape, BF16), pltpu.VMEM(rest_shape.shape, BF16)],
        4,
        CROSS_HINT * pair,
        {1: 0, 2: 1},
        1,
    )
    results = (query_grad,)
    for parity, received in ((1, ()), (0, (vmem(inner_back),))):
        inputs = marks + tuple(vmem(a) for a in (key_acc, value_acc, stage)) + received
        results = call(
            lambda *refs: total_kernel(sizes, parity, *refs),
            inputs + tuple(hbm(a) for a in results),
            [SMEM_SPEC] * 2 + [VMEM_SPEC] * (len(inputs) - 2) + [ANY_SPEC] * len(results),
            tuple(jax.ShapeDtypeStruct(a.shape, BF16) for a in (query_rows, key_rows, value_rows)),
            [ANY_SPEC] * 3,
            [pltpu.VMEM((2, token_count, width), BF16), pltpu.SemaphoreType.DMA((2 + slot_count,))],
            8,
            pair,
            {len(inputs) + i: i for i in range(len(results))},
            1,
        )
    return tuple(results)


def solution(mesh):
    return jax.shard_map(
        per_device,
        mesh=mesh,
        in_specs=(
            P("dp", "ctx", "tp"),
            P("dp", "ctx", "tp"),
            P("dp", "ctx", "tp"),
            P("dp", "ctx", "tp"),
            P("dp", None),
            P("dp", None),
        ),
        out_specs=(P("dp", "ctx", "tp"), P("dp", "ctx", "tp"), P("dp", "ctx", "tp")),
        check_vma=False,
    )
```

```python
import math

import jax
import jax.numpy as jnp
from jax import lax
from jax.experimental import pallas as pl
from jax.experimental.pallas import tpu as pltpu
from jax.sharding import PartitionSpec as P

BLK = 128
SUB = 8
CHUNK = 256
F32 = jnp.float32
BF16 = jnp.bfloat16
MIB = 1 << 20
NEAR_HINT = (400, 10)
REMOTE_HINT = (14, 14)
CROSS_HINT = 60


def shifted(block, axis, distance):
    devices = range(lax.axis_size(axis))
    route = [(i - distance, i) for i in devices if i - distance in devices]
    return lax.ppermute(block, axis, route)


def pair_shift(block, axis, distance, parity, half=None):
    size = lax.axis_size(axis)
    pairs = [(i - 1, i) for i in range(1, size) if i % 2 == parity and half in (None, int(i * 2 >= size))]
    return lax.ppermute(block, axis, pairs if distance == 1 else [pair[::-1] for pair in pairs])


def vmem(array):
    return pltpu.with_memory_space_constraint(array, pltpu.VMEM)


def smem(array):
    return pltpu.with_memory_space_constraint(array, pltpu.SMEM)


def hbm(array):
    return pltpu.with_memory_space_constraint(array, pltpu.HBM)


def nt_dot(left, right):
    return lax.dot_general(left, right, (((1,), (1,)), ((), ())), preferred_element_type=F32)


def nn_dot(left, right):
    return lax.dot_general(left, right, (((1,), (0,)), ((), ())), preferred_element_type=F32)


def fold(tile):
    return jnp.sum(tile.reshape(tile.shape[0] // SUB, SUB, tile.shape[1]), axis=0)


def slots_of(assistant, turn_first, base, block_count, slot_count):
    found = jnp.int32(0)
    blocks = [jnp.int32(0)] * slot_count
    starts = [jnp.int32(0)] * slot_count
    for i in range(block_count):
        mark = assistant[0, base + i]
        start = turn_first[0, base + i] - base
        for s in range(slot_count):
            here = (mark == 1) & (found == s)
            blocks[s] = jnp.where(here, i, blocks[s])
            starts[s] = jnp.where(here, start, starts[s])
        found = found + jnp.where(mark == 1, 1, 0)
    return [(blocks[s], found > s, starts[s]) for s in range(slot_count)]


def score_pass(key_tile, value_tile, query_ref, grad_ref, slot, keep, weight_ref, prob_ref, at, sum_ref,
               dot_ref, scale):
    columns = query_ref.shape[1]
    for c in range(0, columns, CHUNK):
        span = slice(c, c + CHUNK)
        scores = nt_dot(key_tile, query_ref[slot, span, :])
        prob_grad = nt_dot(value_tile, grad_ref[slot, span, :])
        weights = jnp.exp2(scores * scale)
        if keep is not None:
            weights = jnp.where(jnp.concatenate([keep] * (CHUNK // BLK), axis=1), weights, 0.0)
        weight_ref[at + (span,)] = weights
        prob_ref[at + (span,)] = prob_grad
        sum_ref[slot, :, span] += fold(weights)
        dot_ref[slot, :, span] += fold(weights * prob_grad)


def grad_pass(weight_ref, prob_ref, at, query_ref, grad_ref, slot, inverse_ref, delta_ref, low_ref,
              score_ref, score_rows, key_acc, value_acc, acc_rows):
    columns = query_ref.shape[1]
    height = acc_rows.size
    for c in range(0, columns, CHUNK):
        span = slice(c, c + CHUNK)
        shape = (height // SUB, SUB, CHUNK)
        attention = weight_ref[at + (span,)].reshape(shape) * inverse_ref[slot, :, span][None]
        lifted = prob_ref[at + (span,)].reshape(shape) - delta_ref[slot, :, span][None]
        score_grad = (attention * lifted).reshape(height, CHUNK)
        low_ref[:height, span] = attention.reshape(height, CHUNK).astype(BF16)
        score_ref[slot, score_rows, span] = score_grad.astype(BF16)
    value_acc[acc_rows, :] += nn_dot(low_ref[:height], grad_ref[slot])
    key_acc[acc_rows, :] += nn_dot(score_ref[slot, score_rows, :], query_ref[slot])


def block_rows(index, count=1):
    return pl.ds(pl.multiple_of(index * BLK, BLK), count * BLK)


def pick(values, s):
    chosen = values[0]
    for i in range(1, len(values)):
        chosen = jnp.where(s == i, values[i], chosen)
    return chosen


def over_slots(slots, body):
    def step(s, carry):
        block, start = (pick([slot[i] for slot in slots], s) for i in (0, 2))

        @pl.when(pick([jnp.where(slot[1], 1, 0) for slot in slots], s) == 1)
        def _():
            body(s, block, start)

        return carry

    lax.fori_loop(0, len(slots), step, 0)


def local_scores(sizes, assistant, turn_first, query_hbm, grad_hbm, kv_ref, query_ref, grad_ref,
                 weight_ref, prob_ref, sum_ref, dot_ref, sem):
    block_count, slot_count, head_count, width, scale = sizes
    base = lax.axis_index("ctx") * block_count
    slots = slots_of(assistant, turn_first, base, block_count, slot_count)

    def copies(s, block):
        for i, (source, target) in enumerate(((query_hbm, query_ref), (grad_hbm, grad_ref))):
            for h in range(head_count):
                yield pltpu.make_async_copy(
                    source.at[0, block_rows(block), pl.ds(h * width, width)],
                    target.at[s, pl.ds(h * BLK, BLK)],
                    sem.at[s, i],
                )

    for s, (block, live, start) in enumerate(slots):
        @pl.when(live)
        def _():
            for copy in copies(s, block):
                copy.start()
    sum_ref[...] = jnp.zeros_like(sum_ref)
    dot_ref[...] = jnp.zeros_like(dot_ref)
    ahead = lax.broadcasted_iota(jnp.int32, (BLK, BLK), 1) - lax.broadcasted_iota(
        jnp.int32, (BLK, BLK), 0
    )
    def body(s, block, start):
        for i, target in enumerate((query_ref, grad_ref)):
            pltpu.make_async_copy(target.at[s], target.at[s], sem.at[s, i]).wait()

        def step(k, carry):
            rows = block_rows(k)
            score_pass(kv_ref[0, rows, :], kv_ref[1, rows, :], query_ref, grad_ref, s,
                       ahead >= (k - block) * BLK, weight_ref, prob_ref, (s, rows), sum_ref, dot_ref,
                       scale * math.log2(math.e))
            return carry

        lax.fori_loop(jnp.maximum(start, 0), block + 1, step, 0)

    over_slots(slots, body)


def in_first_half():
    return lax.axis_index("ctx") * 2 < lax.axis_size("ctx")


def local_kernel(sizes, early, *refs):
    inputs, results = refs[:5], refs[-7:]
    here = in_first_half() if early else jnp.logical_not(in_first_half())
    pl.when(here)(lambda: local_scores(sizes, *inputs, *results))


def pack_kernel(block_count, key_ref, value_ref, assistant_ref, turn_ref, last_ref, all_ref, assistant,
                turn_first, need_ref, pack_sem):
    token_count = key_ref.shape[1]
    marks = [
        pltpu.make_async_copy(assistant_ref, assistant, pack_sem.at[0]),
        pltpu.make_async_copy(turn_ref, turn_first, pack_sem.at[1]),
    ]
    copies = []
    for pack in (all_ref, last_ref):
        rows = pack.shape[1]
        for i, source in enumerate((key_ref, value_ref)):
            copies.append(
                pltpu.make_async_copy(
                    source.at[0, pl.ds(token_count - rows, rows)], pack.at[i], pack_sem.at[2 + len(copies)]
                )
            )
    for copy in marks + copies:
        copy.start()
    for copy in marks:
        copy.wait()
    outer = far = jnp.int32(0)
    for i in range(block_count, assistant.shape[1]):
        device = i // block_count
        behind = jnp.where(assistant[0, i] == 1, device * block_count - turn_first[0, i], 0)
        far = jnp.where(behind > block_count, 1, far)
        if device % 2 == 0:
            outer = jnp.maximum(outer, behind)
    need_ref[0] = jnp.where(outer > 1, 2, far)

    for copy in copies:
        copy.wait()


def over_window(block_count, reach, start, whole, body):
    first = jnp.maximum(start + reach, 0)
    last = reach
    if whole:
        @pl.when(start <= -block_count)
        def _():
            body(pl.ds((reach - block_count) * BLK, block_count * BLK))

        last = jnp.where(start <= -block_count, reach - block_count, reach)

    def step(k, carry):
        body(block_rows(k))
        return carry

    lax.fori_loop(first, last, step, 0)


def near_kernel(sizes, parity, half, assistant, turn_first, need, query_ref, grad_ref, far_hbm, *rest):
    weight_ref, prob_ref, sum_ref, dot_ref, window, values, sem = rest[-7:]
    block_count, slot_count, head_count, width, scale = sizes
    rank = lax.axis_index("ctx")
    reach = window.shape[0] // BLK
    near = pl.ds((reach - block_count) * BLK, block_count * BLK)

    def fill(rows, source):
        window[rows, :] = source[0]
        values[rows, :] = source[1]

    def fetch(rows, source, first_sem):
        return [
            pltpu.make_async_copy(source.at[i], target.at[rows], sem.at[first_sem + i])
            for i, target in enumerate((window, values))
        ]

    def body(s, block, start):
        def scores(rows):
            score_pass(window[rows, :], values[rows, :], query_ref, grad_ref, s, None, weight_ref,
                       prob_ref, (s, rows), sum_ref, dot_ref, scale * math.log2(math.e))

        over_window(block_count, reach, start, parity == 1, scores)

    here = lax.rem(rank, 2) == parity
    if half is not None:
        here = here & (in_first_half() if half == 0 else jnp.logical_not(in_first_half()))

    @pl.when(here)
    def _():
        if parity == 1:
            fill(near, rest[0])
        else:
            fill(block_rows(reach - 1), rest[0])

        @pl.when(need[0] > 0)
        def _():
            copies = fetch(pl.ds(0, far_hbm.shape[1]), far_hbm, 0)
            for copy in copies:
                copy.start()
            for copy in copies:
                copy.wait()

        if parity == 0:
            @pl.when(need[0] > 1)
            def _():
                copies = fetch(near, rest[1], 2)
                for copy in copies:
                    copy.start()
                for copy in copies:
                    copy.wait()

        sum_ref[...] = jnp.zeros_like(sum_ref)
        dot_ref[...] = jnp.zeros_like(dot_ref)
        over_slots(slots_of(assistant, turn_first, rank * block_count, block_count, slot_count), body)


def remote_kernel(sizes, parity, assistant, turn_first, need, query_ref, grad_ref, sum_local, dot_local,
                  weight_near, prob_near, sum_near, dot_near, *rest):
    block_count, slot_count, head_count, width, scale = sizes
    (score_ref, inverse_ref, delta_ref, far_hbm, rest_hbm, *_, near_out, low_ref, key_acc, value_acc, far_low,
     rest_low) = rest[-15 + 4 * parity:]
    rank = lax.axis_index("ctx")
    reach = weight_near.shape[1] // BLK

    def body(s, block, start):
        inverse = 1.0 / jnp.sum(sum_local[s] + sum_near[s], axis=0, keepdims=True)
        delta = jnp.sum(dot_local[s] + dot_near[s], axis=0, keepdims=True) * inverse
        inverse_ref[s] = jnp.broadcast_to(inverse, inverse_ref.shape[1:])
        delta_ref[s] = jnp.broadcast_to(delta, delta_ref.shape[1:])

        def gradients_of(rows):
            grad_pass(weight_near, prob_near, (s, rows), query_ref, grad_ref, s, inverse_ref, delta_ref,
                      low_ref, score_ref, rows, key_acc, value_acc, rows)

        over_window(block_count, reach, start, parity == 1, gradients_of)

    @pl.when(lax.rem(rank, 2) == parity)
    def _():
        key_acc[...] = jnp.zeros_like(key_acc)
        value_acc[...] = jnp.zeros_like(value_acc)
        over_slots(slots_of(assistant, turn_first, rank * block_count, block_count, slot_count), body)

        def round_to(out, first, rows):
            out[0] = (key_acc[first:first + rows, :] * scale).astype(BF16)
            out[1] = value_acc[first:first + rows, :].astype(BF16)

        total = reach * BLK
        round_to(near_out, total - near_out.shape[1], near_out.shape[1])

        @pl.when(need[0] > 0)
        def _():
            round_to(far_low, 0, far_low.shape[1])
            pltpu.sync_copy(far_low, far_hbm)

        if parity == 0:
            @pl.when(need[0] > 1)
            def _():
                round_to(rest_low, far_low.shape[1], rest_low.shape[1])
                pltpu.sync_copy(rest_low, rest_hbm)


def sends_late(rank):
    return (lax.rem(rank, 2) == 1) & (rank > 1)


def finish_kernel(sizes, early, assistant, turn_first, query_ref, grad_ref, weight_ref, prob_ref, score_in,
                  inverse_ref, delta_ref, kv_ref, window, *rest):
    query_hbm, key_acc, value_acc, stage, score_ref, low_ref, query_acc, blank, sem = rest[-9:]
    block_count, slot_count, head_count, width, scale = sizes
    rank = lax.axis_index("ctx")
    base = rank * block_count
    reach = window.shape[0] // BLK
    columns = query_acc.shape[1]

    def blank_copy(i):
        return pltpu.make_async_copy(blank, query_hbm.at[0, pl.ds(i * BLK, BLK)], sem.at[slot_count + i])

    def run():
        slots = slots_of(assistant, turn_first, base, block_count, slot_count)
        more = [live for _, live, _ in slots[1:]]

        def stage_copy(s):
            return pltpu.make_async_copy(stage.at[s], query_hbm.at[0, block_rows(slots[s][0])], sem.at[s])

        blank[...] = jnp.zeros_like(blank)
        for i in range(block_count):
            @pl.when(assistant[0, base + i] != 1)
            def _():
                blank_copy(i).start()
        key_acc[...] = jnp.zeros_like(key_acc)
        value_acc[...] = jnp.zeros_like(value_acc)

        def body(s, block, start):
            def query_part(keys, source, rows, span):
                return nn_dot(keys.T, source[s, rows, span])

            query_acc[...] = jnp.zeros_like(query_acc)

            def remote_part(rows):
                keys = window[rows, :]
                for c in range(0, columns, CHUNK):
                    span = slice(c, c + CHUNK)
                    query_acc[:, span] += query_part(keys, score_in, rows, span)

            over_window(block_count, reach, start, True, remote_part)
            low = jnp.maximum(start, 0)
            for count in range(1, block_count + 1):
                @pl.when(block + 1 - low == count)
                def _():
                    rows = block_rows(low, count)
                    grad_pass(weight_ref, prob_ref, (s, rows), query_ref, grad_ref, s, inverse_ref, delta_ref,
                              low_ref, score_ref, rows, key_acc, value_acc, rows)
                    keys = kv_ref[0, rows, :]
                    for c in range(0, columns, CHUNK):
                        span = slice(c, c + CHUNK)
                        total = query_acc[:, span] + query_part(keys, score_ref, rows, span)
                        for h in range(0, CHUNK, BLK):
                            place = slice((c + h) // BLK * width, ((c + h) // BLK + 1) * width)
                            stage[s, :, place] = (total[:, h:h + BLK] * scale).T.astype(BF16)

            for i in range(slot_count - 1):
                @pl.when((s == i) & more[i])
                def _():
                    stage_copy(i).start()

        over_slots(slots, body)
        key_acc[...] = key_acc[...] * scale
        for i in range(slot_count - 1):
            @pl.when(more[i])
            def _():
                stage_copy(i).wait()

        for i in range(block_count):
            @pl.when(assistant[0, base + i] != 1)
            def _():
                blank_copy(i).wait()

    pl.when(sends_late(rank) if early else jnp.logical_not(sends_late(rank)))(run)


def add_kernel(need, key_in, value_in, outer_ref, far_hbm, rest_hbm, key_acc, value_acc, far, rest):
    pairs = list(enumerate((key_acc, value_acc)))

    def add_last(source):
        for i, acc in pairs:
            acc[acc.shape[0] - source.shape[1]:, :] += source[i].astype(F32)

    add_last(outer_ref)

    @pl.when(need[0] > 0)
    def _():
        pltpu.sync_copy(far_hbm, far)
        add_last(far)

    @pl.when(need[0] > 1)
    def _():
        pltpu.sync_copy(rest_hbm, rest)
        for i, acc in pairs:
            acc[:rest.shape[1], :] += rest[i].astype(F32)


def total_kernel(sizes, parity, assistant, turn_first, key_acc, value_acc, stage, *rest):
    query_hbm, key_hbm, value_hbm, low, sem = rest[-5:]
    block_count, slot_count, head_count, width, scale = sizes
    rank = lax.axis_index("ctx")

    @pl.when(lax.rem(rank, 2) == parity)
    def _():
        slots = slots_of(assistant, turn_first, rank * block_count, block_count, slot_count)
        ends = [
            live & jnp.logical_not(slots[s + 1][1]) if s + 1 < slot_count else live
            for s, (_, live, _) in enumerate(slots)
        ]

        def stage_copy(s):
            rows = block_rows(slots[s][0])
            return pltpu.make_async_copy(stage.at[s], query_hbm.at[0, rows], sem.at[2 + s])

        for s in range(slot_count):
            @pl.when(ends[s])
            def _():
                stage_copy(s).start()

        copies = []
        for i, (acc, out) in enumerate(((key_acc, key_hbm), (value_acc, value_hbm))):
            total = acc[...] if parity == 1 else acc[...] + rest[0][i].astype(F32)
            low[i] = total.astype(BF16)
            copies.append(pltpu.make_async_copy(low.at[i], out.at[0], sem.at[i]))
            copies[i].start()
        for copy in copies:
            copy.wait()
        for s in range(slot_count):
            @pl.when(ends[s])
            def _():
                stage_copy(s).wait()


def call(kernel, inputs, in_specs, outputs, out_specs, scratch, limit, macs, aliases={},
         traffic=2 * MIB):
    return pl.pallas_call(
        kernel,
        out_shape=outputs,
        in_specs=in_specs,
        out_specs=out_specs,
        scratch_shapes=scratch,
        input_output_aliases=aliases,
        compiler_params=pltpu.CompilerParams(vmem_limit_bytes=limit * MIB),
        cost_estimate=pl.CostEstimate(flops=2 * macs, bytes_accessed=traffic, transcendentals=0),
    )(*inputs)


ANY_SPEC = pl.BlockSpec(memory_space=pl.ANY)
SMEM_SPEC = pl.BlockSpec(memory_space=pltpu.SMEM)
VMEM_SPEC = pl.BlockSpec(memory_space=pltpu.VMEM)


def score_shapes(sizes, rows):
    block_count, slot_count, head_count, width, scale = sizes
    columns = head_count * BLK
    return (
        pltpu.VMEM((slot_count, rows, columns), F32),
        pltpu.VMEM((slot_count, rows, columns), F32),
        pltpu.VMEM((slot_count, SUB, columns), F32),
        pltpu.VMEM((slot_count, SUB, columns), F32),
    )


def local_shapes(sizes):
    block_count, slot_count, head_count, width, scale = sizes
    rows = pltpu.VMEM((slot_count, head_count * BLK, width), BF16)
    return (rows, rows) + score_shapes(sizes, block_count * BLK)


def local_sems(sizes):
    return pltpu.SemaphoreType.DMA((sizes[1], 2))


def skip_kernel(*refs):
    pass


def stack_kernel(key_ref, value_ref, *outs):
    *outs, sem = outs
    copies = []
    for out in outs:
        first = key_ref.shape[1] - out.shape[1]
        for i, source in enumerate((key_ref, value_ref)):
            copies.append(
                pltpu.make_async_copy(
                    source.at[0, pl.ds(first, out.shape[1])], out.at[i], sem.at[len(copies)]
                )
            )
    for copy in copies:
        copy.start()
    for copy in copies:
        copy.wait()


def skipped(*shapes):
    return tuple(call(skip_kernel, (), [], shapes, [ANY_SPEC] * len(shapes), [], 4, 1, {}, 1))


def per_device(query_rows, key_rows, value_rows, out_grad, assistant, turn_first):
    token_count = query_rows.shape[1]
    width = key_rows.shape[2]
    head_count = query_rows.shape[2] // width
    block_count = token_count // BLK
    far_rows = block_count // 2 * BLK
    reach_rows = token_count + far_rows
    slot_count = (block_count + 1) // 2
    columns = head_count * BLK
    pair = columns * BLK * width
    sizes = (block_count, slot_count, head_count, width, 1.0 / math.sqrt(width))
    stat_rows = (slot_count, SUB, columns)
    last, own, assistant, turn_first, need = call(
        lambda *refs: pack_kernel(block_count, *refs),
        tuple(hbm(a) for a in (key_rows, value_rows, assistant, turn_first)),
        [ANY_SPEC] * 4,
        (
            pltpu.VMEM((2, far_rows, width), BF16),
            pltpu.VMEM((2, token_count, width), BF16),
            pltpu.SMEM(assistant.shape, jnp.int32),
            pltpu.SMEM(turn_first.shape, jnp.int32),
            pltpu.SMEM((1,), jnp.int32),
        ),
        [VMEM_SPEC] * 2 + [SMEM_SPEC] * 3,
        [pltpu.SemaphoreType.DMA((6,))],
        4,
        BLK,
    )
    marks = (smem(assistant), smem(turn_first))
    flag = smem(need)
    far_shape = jax.ShapeDtypeStruct((2, far_rows, width), BF16)
    whole_shape = jax.ShapeDtypeStruct((2, token_count, width), BF16)
    rest_shape = jax.ShapeDtypeStruct((2, token_count - far_rows, width), BF16)

    def stacked(sources, *shapes):
        return call(stack_kernel, sources, [ANY_SPEC] * 2, shapes, [ANY_SPEC] * len(shapes),
                    [pltpu.SemaphoreType.DMA((2 * len(shapes),))], 4, 1, {}, 1)

    def far_only(*sources):
        far, = stacked(sources, far_shape)
        return (shifted(far, "ctx", 2),) + skipped(whole_shape)

    def far_and_whole(*sources):
        far, whole = stacked(sources, far_shape, whole_shape)
        return shifted(far, "ctx", 2), pair_shift(whole, "ctx", 1, 0)

    far_in, whole_in = lax.switch(
        need[0], [lambda *_: skipped(far_shape, whole_shape), far_only, far_and_whole], key_rows, value_rows
    )
    own, far_in, whole_in = lax.optimization_barrier((own, far_in, whole_in))

    def local(early, state):
        return call(
            lambda *refs: local_kernel(sizes, early, *refs),
            marks + (hbm(query_rows), hbm(out_grad), vmem(own)) + tuple(vmem(a) for a in state),
            [SMEM_SPEC] * 2 + [ANY_SPEC] * 2 + [VMEM_SPEC] * (1 + len(state)),
            local_shapes(sizes),
            [VMEM_SPEC] * 6,
            [local_sems(sizes)],
            8,
            pair,
            {5 + i: i for i in range(len(state))},
            1,
        )

    def near(parity, half, sources, local_state, kept):
        inputs = marks + (flag,) + tuple(vmem(a) for a in local_state[:2]) + (hbm(far_in),) + sources
        return tuple(
            call(
                lambda *refs: near_kernel(sizes, parity, half, *refs),
                inputs + tuple(vmem(a) for a in kept),
                [SMEM_SPEC] * 3 + [VMEM_SPEC] * 2 + [ANY_SPEC, VMEM_SPEC]
                + [ANY_SPEC] * (len(sources) - 1) + [VMEM_SPEC] * len(kept),
                score_shapes(sizes, reach_rows) + (pltpu.VMEM((reach_rows, width), BF16),),
                [VMEM_SPEC] * 5,
                [pltpu.VMEM((reach_rows, width), BF16), pltpu.SemaphoreType.DMA((4,))],
                8,
                NEAR_HINT[parity] * pair,
                {len(inputs) + i: i for i in range(len(kept))},
                1,
            )
        )

    def remote(parity, near_rows, near_state, kept):
        inputs = marks + (flag,) + tuple(vmem(a) for a in (query_slots, grad_slots, sums, dots))
        held = tuple(vmem(a) for a in kept[:3]) + tuple(hbm(a) for a in kept[3:])
        passed = score_shapes(sizes, reach_rows) if parity == 0 else ()
        aliases = {len(inputs) + 4 + i: i for i in range(len(held))}
        aliases.update({len(inputs) + i: 5 + i for i in range(len(passed))})
        results = call(
            lambda *refs: remote_kernel(sizes, parity, *refs),
            inputs + tuple(vmem(a) for a in near_state) + held,
            [SMEM_SPEC] * 3 + [VMEM_SPEC] * (8 + len(held[:3])) + [ANY_SPEC] * len(held[3:]),
            (
                pltpu.VMEM((slot_count, reach_rows, columns), BF16),
                pltpu.VMEM(stat_rows, F32),
                pltpu.VMEM(stat_rows, F32),
                far_shape,
                rest_shape,
            )
            + passed
            + (pltpu.VMEM((2, near_rows, width), BF16),),
            [VMEM_SPEC] * 3 + [ANY_SPEC] * 2 + [VMEM_SPEC] * (1 + len(passed)),
            [
                pltpu.VMEM((token_count, columns), BF16),
                pltpu.VMEM((reach_rows, width), F32),
                pltpu.VMEM((reach_rows, width), F32),
                pltpu.VMEM(far_shape.shape, BF16),
                pltpu.VMEM(rest_shape.shape, BF16),
            ],
            8,
            REMOTE_HINT[parity] * pair,
            aliases,
            1,
        )
        return tuple(results[:5]), tuple(results[5:-1]), results[-1]

    inner_first = pair_shift(own, "ctx", 1, 1, 0)
    local_state = local(True, ())
    near_state = near(1, 0, (vmem(inner_first),), local_state, ())
    last, own, local_state, near_state = lax.optimization_barrier((last, own, local_state, near_state))
    outer_in = pair_shift(last, "ctx", 1, 0)
    inner_second = pair_shift(own, "ctx", 1, 1, 1)
    local_state = local(False, local_state)
    query_slots, grad_slots, weights, prob_grad, sums, dots = local_state
    *near_state, window = near(0, None, (vmem(outer_in), hbm(whole_in)), local_state, near_state)
    remote_state, near_state, outer_grad = remote(0, far_rows, near_state, ())
    outer_back = pair_shift(outer_grad, "ctx", -1, 0)
    *near_state, window = near(1, 1, (vmem(inner_second),), local_state, near_state + (window,))
    remote_state, _, inner_grad = remote(1, token_count, near_state, remote_state)
    window = (window,)
    score_grad, inverse, delta, far_grad, rest_grad = remote_state

    def finish(early, state):
        inputs = marks + tuple(
            vmem(a)
            for a in (query_slots, grad_slots, weights, prob_grad, score_grad, inverse, delta, own) + window
        )
        return call(
            lambda *refs: finish_kernel(sizes, early, *refs),
            inputs + tuple(hbm(a) for a in state[:1]) + tuple(vmem(a) for a in state[1:]),
            [SMEM_SPEC] * 2 + [VMEM_SPEC] * 9 + [ANY_SPEC] * len(state[:1]) + [VMEM_SPEC] * len(state[1:]),
            (
                jax.ShapeDtypeStruct(query_rows.shape, BF16),
                pltpu.VMEM((token_count, width), F32),
                pltpu.VMEM((token_count, width), F32),
                pltpu.VMEM((slot_count, BLK, head_count * width), BF16),
            ),
            [ANY_SPEC] + [VMEM_SPEC] * 3,
            [
                pltpu.VMEM((slot_count, token_count, columns), BF16),
                pltpu.VMEM((token_count, columns), BF16),
                pltpu.VMEM((BLK, columns), F32),
                pltpu.VMEM((BLK, head_count * width), BF16),
                pltpu.SemaphoreType.DMA((slot_count + block_count,)),
            ],
            10,
            pair,
            {len(inputs) + i: i for i in range(len(state))},
            1,
        )

    state = finish(True, ())
    inner_grad, state = lax.optimization_barrier((inner_grad, state))
    inner_back = pair_shift(inner_grad, "ctx", -1, 1)
    query_grad, key_acc, value_acc, stage = finish(False, tuple(state))
    far_grad, rest_grad, query_grad = lax.optimization_barrier((far_grad, rest_grad, query_grad))
    far_back, rest_back = lax.switch(
        need[0],
        [
            lambda far, rest: skipped(far_shape, rest_shape),
            lambda far, rest: (shifted(far, "ctx", -2),) + skipped(rest_shape),
            lambda far, rest: (shifted(far, "ctx", -2), pair_shift(rest, "ctx", -1, 0)),
        ],
        far_grad,
        rest_grad,
    )
    key_acc, value_acc = call(
        add_kernel,
        (flag,) + tuple(vmem(a) for a in (key_acc, value_acc, outer_back)) + (hbm(far_back), hbm(rest_back)),
        [SMEM_SPEC] + [VMEM_SPEC] * 3 + [ANY_SPEC] * 2,
        (pltpu.VMEM((token_count, width), F32),) * 2,
        [VMEM_SPEC] * 2,
        [pltpu.VMEM(far_shape.shape, BF16), pltpu.VMEM(rest_shape.shape, BF16)],
        4,
        CROSS_HINT * pair,
        {1: 0, 2: 1},
        1,
    )
    results = (query_grad,)
    for parity, received in ((1, ()), (0, (vmem(inner_back),))):
        inputs = marks + tuple(vmem(a) for a in (key_acc, value_acc, stage)) + received
        results = call(
            lambda *refs: total_kernel(sizes, parity, *refs),
            inputs + tuple(hbm(a) for a in results),
            [SMEM_SPEC] * 2 + [VMEM_SPEC] * (len(inputs) - 2) + [ANY_SPEC] * len(results),
            tuple(jax.ShapeDtypeStruct(a.shape, BF16) for a in (query_rows, key_rows, value_rows)),
            [ANY_SPEC] * 3,
            [pltpu.VMEM((2, token_count, width), BF16), pltpu.SemaphoreType.DMA((2 + slot_count,))],
            8,
            pair,
            {len(inputs) + i: i for i in range(len(results))},
            1,
        )
    return tuple(results)


def solution(mesh):
    return jax.shard_map(
        per_device,
        mesh=mesh,
        in_specs=(
            P("dp", "ctx", "tp"),
            P("dp", "ctx", "tp"),
            P("dp", "ctx", "tp"),
            P("dp", "ctx", "tp"),
            P("dp", None),
            P("dp", None),
        ),
        out_specs=(P("dp", "ctx", "tp"), P("dp", "ctx", "tp"), P("dp", "ctx", "tp")),
        check_vma=False,
    )
```

```python
import math

import jax
import jax.numpy as jnp
from jax import lax
from jax.experimental import pallas as pl
from jax.experimental.pallas import tpu as pltpu
from jax.sharding import PartitionSpec as P

BLK = 128
SUB = 8
CHUNK = 256
F32 = jnp.float32
BF16 = jnp.bfloat16
MIB = 1 << 20
NEAR_HINT = (400, 10)
REMOTE_HINT = (14, 14)
CROSS_HINT = 60


def shifted(block, axis, distance):
    devices = range(lax.axis_size(axis))
    route = [(i - distance, i) for i in devices if i - distance in devices]
    return lax.ppermute(block, axis, route)


def pair_shift(block, axis, distance, parity, half=None):
    size = lax.axis_size(axis)
    pairs = [(i - 1, i) for i in range(1, size) if i % 2 == parity and half in (None, int(i * 2 >= size))]
    return lax.ppermute(block, axis, pairs if distance == 1 else [pair[::-1] for pair in pairs])


def vmem(array):
    return pltpu.with_memory_space_constraint(array, pltpu.VMEM)


def smem(array):
    return pltpu.with_memory_space_constraint(array, pltpu.SMEM)


def hbm(array):
    return pltpu.with_memory_space_constraint(array, pltpu.HBM)


def nt_dot(left, right):
    return lax.dot_general(left, right, (((1,), (1,)), ((), ())), preferred_element_type=F32)


def nn_dot(left, right):
    return lax.dot_general(left, right, (((1,), (0,)), ((), ())), preferred_element_type=F32)


def fold(tile):
    return jnp.sum(tile.reshape(tile.shape[0] // SUB, SUB, tile.shape[1]), axis=0)


def slots_of(assistant, turn_first, base, block_count, slot_count):
    found = jnp.int32(0)
    blocks = [jnp.int32(0)] * slot_count
    starts = [jnp.int32(0)] * slot_count
    for i in range(block_count):
        mark = assistant[0, base + i]
        start = turn_first[0, base + i] - base
        for s in range(slot_count):
            here = (mark == 1) & (found == s)
            blocks[s] = jnp.where(here, i, blocks[s])
            starts[s] = jnp.where(here, start, starts[s])
        found = found + jnp.where(mark == 1, 1, 0)
    return [(blocks[s], found > s, starts[s]) for s in range(slot_count)]


def score_pass(key_tile, value_tile, query_ref, grad_ref, slot, keep, weight_ref, prob_ref, at, sum_ref,
               dot_ref, scale):
    columns = query_ref.shape[1]
    for c in range(0, columns, CHUNK):
        span = slice(c, c + CHUNK)
        scores = nt_dot(key_tile, query_ref[slot, span, :])
        prob_grad = nt_dot(value_tile, grad_ref[slot, span, :])
        weights = jnp.exp2(scores * scale)
        if keep is not None:
            weights = jnp.where(jnp.concatenate([keep] * (CHUNK // BLK), axis=1), weights, 0.0)
        weight_ref[at + (span,)] = weights
        prob_ref[at + (span,)] = prob_grad
        sum_ref[slot, :, span] += fold(weights)
        dot_ref[slot, :, span] += fold(weights * prob_grad)


def grad_pass(weight_ref, prob_ref, at, query_ref, grad_ref, slot, inverse_ref, delta_ref, low_ref,
              score_ref, score_rows, key_acc, value_acc, acc_rows, low_first=0):
    columns = query_ref.shape[1]
    height = acc_rows.size
    low_rows = slice(low_first, low_first + height)
    for c in range(0, columns, CHUNK):
        span = slice(c, c + CHUNK)
        shape = (height // SUB, SUB, CHUNK)
        attention = weight_ref[at + (span,)].reshape(shape) * inverse_ref[slot, :, span][None]
        lifted = prob_ref[at + (span,)].reshape(shape) - delta_ref[slot, :, span][None]
        score_grad = (attention * lifted).reshape(height, CHUNK)
        low_ref[low_rows, span] = attention.reshape(height, CHUNK).astype(BF16)
        score_ref[slot, score_rows, span] = score_grad.astype(BF16)
    value_acc[acc_rows, :] += nn_dot(low_ref[low_rows], grad_ref[slot])
    key_acc[acc_rows, :] += nn_dot(score_ref[slot, score_rows, :], query_ref[slot])


def block_rows(index, count=1):
    return pl.ds(pl.multiple_of(index * BLK, BLK), count * BLK)


def pick(values, s):
    chosen = values[0]
    for i in range(1, len(values)):
        chosen = jnp.where(s == i, values[i], chosen)
    return chosen


def over_slots(slots, body):
    def step(s, carry):
        block, start = (pick([slot[i] for slot in slots], s) for i in (0, 2))

        @pl.when(pick([jnp.where(slot[1], 1, 0) for slot in slots], s) == 1)
        def _():
            body(s, block, start)

        return carry

    lax.fori_loop(0, len(slots), step, 0)


def local_scores(sizes, assistant, turn_first, query_hbm, grad_hbm, kv_ref, query_ref, grad_ref,
                 weight_ref, prob_ref, sum_ref, dot_ref, sem):
    block_count, slot_count, head_count, width, scale = sizes
    base = lax.axis_index("ctx") * block_count
    slots = slots_of(assistant, turn_first, base, block_count, slot_count)

    def copies(s, block):
        for i, (source, target) in enumerate(((query_hbm, query_ref), (grad_hbm, grad_ref))):
            for h in range(head_count):
                yield pltpu.make_async_copy(
                    source.at[0, block_rows(block), pl.ds(h * width, width)],
                    target.at[s, pl.ds(h * BLK, BLK)],
                    sem.at[s, i],
                )

    for s, (block, live, start) in enumerate(slots):
        @pl.when(live)
        def _():
            for copy in copies(s, block):
                copy.start()
    sum_ref[...] = jnp.zeros_like(sum_ref)
    dot_ref[...] = jnp.zeros_like(dot_ref)
    ahead = lax.broadcasted_iota(jnp.int32, (BLK, BLK), 1) - lax.broadcasted_iota(
        jnp.int32, (BLK, BLK), 0
    )
    def body(s, block, start):
        for i, target in enumerate((query_ref, grad_ref)):
            pltpu.make_async_copy(target.at[s], target.at[s], sem.at[s, i]).wait()

        def step(k, carry):
            rows = block_rows(k)
            score_pass(kv_ref[0, rows, :], kv_ref[1, rows, :], query_ref, grad_ref, s,
                       ahead >= (k - block) * BLK, weight_ref, prob_ref, (s, rows), sum_ref, dot_ref,
                       scale * math.log2(math.e))
            return carry

        lax.fori_loop(jnp.maximum(start, 0), block + 1, step, 0)

    over_slots(slots, body)


def in_first_half():
    return lax.axis_index("ctx") * 2 < lax.axis_size("ctx")


def local_kernel(sizes, early, *refs):
    inputs, results = refs[:5], refs[-7:]
    here = in_first_half() if early else jnp.logical_not(in_first_half())
    pl.when(here)(lambda: local_scores(sizes, *inputs, *results))


def pack_kernel(block_count, key_ref, value_ref, assistant_ref, turn_ref, last_ref, all_ref, assistant,
                turn_first, need_ref, pack_sem):
    token_count = key_ref.shape[1]
    marks = [
        pltpu.make_async_copy(assistant_ref, assistant, pack_sem.at[0]),
        pltpu.make_async_copy(turn_ref, turn_first, pack_sem.at[1]),
    ]
    copies = []
    for pack in (all_ref, last_ref):
        rows = pack.shape[1]
        for i, source in enumerate((key_ref, value_ref)):
            copies.append(
                pltpu.make_async_copy(
                    source.at[0, pl.ds(token_count - rows, rows)], pack.at[i], pack_sem.at[2 + len(copies)]
                )
            )
    for copy in marks + copies:
        copy.start()
    for copy in marks:
        copy.wait()
    outer = far = jnp.int32(0)
    for i in range(block_count, assistant.shape[1]):
        device = i // block_count
        behind = jnp.where(assistant[0, i] == 1, device * block_count - turn_first[0, i], 0)
        far = jnp.where(behind > block_count, 1, far)
        if device % 2 == 0:
            outer = jnp.maximum(outer, behind)
    need_ref[0] = jnp.where(outer > 1, 2, far)

    for copy in copies:
        copy.wait()


def over_window(block_count, reach, start, whole, body):
    first = jnp.maximum(start + reach, 0)
    last = reach
    if whole:
        @pl.when(start <= -block_count)
        def _():
            body(pl.ds((reach - block_count) * BLK, block_count * BLK))

        last = jnp.where(start <= -block_count, reach - block_count, reach)

    def step(k, carry):
        body(block_rows(k))
        return carry

    lax.fori_loop(first, last, step, 0)


def all_slots(slots, wanted):
    together = wanted(slots[0][2])
    for _, live, start in slots:
        together = together & live & wanted(start)
    return together


def near_kernel(sizes, parity, half, assistant, turn_first, need, query_ref, grad_ref, far_hbm, *rest):
    weight_ref, prob_ref, sum_ref, dot_ref, window, values, sem = rest[-7:]
    block_count, slot_count, head_count, width, scale = sizes
    rank = lax.axis_index("ctx")
    reach = window.shape[0] // BLK
    near = pl.ds((reach - block_count) * BLK, block_count * BLK)

    def fill(rows, source):
        window[rows, :] = source[0]
        values[rows, :] = source[1]

    def fetch(rows, source, first_sem):
        return [
            pltpu.make_async_copy(source.at[i], target.at[rows], sem.at[first_sem + i])
            for i, target in enumerate((window, values))
        ]

    def body(s, block, start):
        def scores(rows):
            score_pass(window[rows, :], values[rows, :], query_ref, grad_ref, s, None, weight_ref,
                       prob_ref, (s, rows), sum_ref, dot_ref, scale * math.log2(math.e))

        over_window(block_count, reach, start, parity == 1, scores)

    here = lax.rem(rank, 2) == parity
    if half is not None:
        here = here & (in_first_half() if half == 0 else jnp.logical_not(in_first_half()))

    @pl.when(here)
    def _():
        if parity == 1:
            fill(near, rest[0])
        else:
            fill(block_rows(reach - 1), rest[0])

        @pl.when(need[0] > 0)
        def _():
            copies = fetch(pl.ds(0, far_hbm.shape[1]), far_hbm, 0)
            for copy in copies:
                copy.start()
            for copy in copies:
                copy.wait()

        if parity == 0:
            @pl.when(need[0] > 1)
            def _():
                copies = fetch(near, rest[1], 2)
                for copy in copies:
                    copy.start()
                for copy in copies:
                    copy.wait()

        sum_ref[...] = jnp.zeros_like(sum_ref)
        dot_ref[...] = jnp.zeros_like(dot_ref)
        slots = slots_of(assistant, turn_first, rank * block_count, block_count, slot_count)
        if parity == 1:
            over_slots(slots, body)
            return
        together = all_slots(slots, lambda start: start == -1)

        @pl.when(together)
        def _():
            rows = pl.ds((reach - 1) * BLK, BLK)
            for s in range(slot_count):
                score_pass(window[rows, :], values[rows, :], query_ref, grad_ref, s, None, weight_ref,
                           prob_ref, (s, rows), sum_ref, dot_ref, scale * math.log2(math.e))

        pl.when(jnp.logical_not(together))(lambda: over_slots(slots, body))


def remote_kernel(sizes, parity, assistant, turn_first, need, query_ref, grad_ref, sum_local, dot_local,
                  weight_near, prob_near, sum_near, dot_near, *rest):
    block_count, slot_count, head_count, width, scale = sizes
    (score_ref, inverse_ref, delta_ref, far_hbm, rest_hbm, *_, near_out, low_ref, key_acc, value_acc, far_low,
     rest_low) = rest[-15 + 4 * parity:]
    rank = lax.axis_index("ctx")
    reach = weight_near.shape[1] // BLK

    def statistics(s):
        inverse = 1.0 / jnp.sum(sum_local[s] + sum_near[s], axis=0, keepdims=True)
        delta = jnp.sum(dot_local[s] + dot_near[s], axis=0, keepdims=True) * inverse
        inverse_ref[s] = jnp.broadcast_to(inverse, inverse_ref.shape[1:])
        delta_ref[s] = jnp.broadcast_to(delta, delta_ref.shape[1:])

    def gradients_of(s, rows, low_first=0):
        grad_pass(weight_near, prob_near, (s, rows), query_ref, grad_ref, s, inverse_ref, delta_ref,
                  low_ref, score_ref, rows, key_acc, value_acc, rows, low_first)

    def body(s, block, start):
        statistics(s)
        over_window(block_count, reach, start, parity == 1, lambda rows: gradients_of(s, rows))

    @pl.when(lax.rem(rank, 2) == parity)
    def _():
        key_acc[...] = jnp.zeros_like(key_acc)
        value_acc[...] = jnp.zeros_like(value_acc)
        slots = slots_of(assistant, turn_first, rank * block_count, block_count, slot_count)
        count = 1 if parity == 0 else block_count
        together = all_slots(slots, lambda start: start == -count)

        @pl.when(together)
        def _():
            rows = pl.ds((reach - count) * BLK, count * BLK)
            for s in range(slot_count):
                statistics(s)
            for s in range(slot_count):
                gradients_of(s, rows, s * count * BLK)

        pl.when(jnp.logical_not(together))(lambda: over_slots(slots, body))

        def round_to(out, first, rows):
            out[0] = (key_acc[first:first + rows, :] * scale).astype(BF16)
            out[1] = value_acc[first:first + rows, :].astype(BF16)

        total = reach * BLK
        round_to(near_out, total - near_out.shape[1], near_out.shape[1])

        @pl.when(need[0] > 0)
        def _():
            round_to(far_low, 0, far_low.shape[1])
            pltpu.sync_copy(far_low, far_hbm)

        if parity == 0:
            @pl.when(need[0] > 1)
            def _():
                round_to(rest_low, far_low.shape[1], rest_low.shape[1])
                pltpu.sync_copy(rest_low, rest_hbm)


def sends_late(rank):
    return (lax.rem(rank, 2) == 1) & (rank > 1)


def finish_kernel(sizes, early, assistant, turn_first, query_ref, grad_ref, weight_ref, prob_ref, score_in,
                  inverse_ref, delta_ref, kv_ref, window, *rest):
    query_hbm, key_acc, value_acc, stage, score_ref, low_ref, query_acc, blank, sem = rest[-9:]
    block_count, slot_count, head_count, width, scale = sizes
    rank = lax.axis_index("ctx")
    base = rank * block_count
    reach = window.shape[0] // BLK
    columns = query_acc.shape[1]

    def blank_copy(i):
        return pltpu.make_async_copy(blank, query_hbm.at[0, pl.ds(i * BLK, BLK)], sem.at[slot_count + i])

    def run():
        slots = slots_of(assistant, turn_first, base, block_count, slot_count)
        more = [live for _, live, _ in slots[1:]]

        def stage_copy(s):
            return pltpu.make_async_copy(stage.at[s], query_hbm.at[0, block_rows(slots[s][0])], sem.at[s])

        blank[...] = jnp.zeros_like(blank)
        for i in range(block_count):
            @pl.when(assistant[0, base + i] != 1)
            def _():
                blank_copy(i).start()
        key_acc[...] = jnp.zeros_like(key_acc)
        value_acc[...] = jnp.zeros_like(value_acc)

        def body(s, block, start):
            def query_part(keys, source, rows, span):
                return nn_dot(keys.T, source[s, rows, span])

            query_acc[...] = jnp.zeros_like(query_acc)

            def remote_part(rows):
                keys = window[rows, :]
                for c in range(0, columns, CHUNK):
                    span = slice(c, c + CHUNK)
                    query_acc[:, span] += query_part(keys, score_in, rows, span)

            over_window(block_count, reach, start, True, remote_part)
            low = jnp.maximum(start, 0)
            for count in range(1, block_count + 1):
                @pl.when(block + 1 - low == count)
                def _():
                    rows = block_rows(low, count)
                    grad_pass(weight_ref, prob_ref, (s, rows), query_ref, grad_ref, s, inverse_ref, delta_ref,
                              low_ref, score_ref, rows, key_acc, value_acc, rows)
                    keys = kv_ref[0, rows, :]
                    for c in range(0, columns, CHUNK):
                        span = slice(c, c + CHUNK)
                        total = query_acc[:, span] + query_part(keys, score_ref, rows, span)
                        for h in range(0, CHUNK, BLK):
                            place = slice((c + h) // BLK * width, ((c + h) // BLK + 1) * width)
                            stage[s, :, place] = (total[:, h:h + BLK] * scale).T.astype(BF16)

            for i in range(slot_count - 1):
                @pl.when((s == i) & more[i])
                def _():
                    stage_copy(i).start()

        over_slots(slots, body)
        key_acc[...] = key_acc[...] * scale
        for i in range(slot_count - 1):
            @pl.when(more[i])
            def _():
                stage_copy(i).wait()

        for i in range(block_count):
            @pl.when(assistant[0, base + i] != 1)
            def _():
                blank_copy(i).wait()

    pl.when(sends_late(rank) if early else jnp.logical_not(sends_late(rank)))(run)


def add_kernel(need, key_in, value_in, outer_ref, far_hbm, rest_hbm, key_acc, value_acc, far, rest):
    pairs = list(enumerate((key_acc, value_acc)))

    def add_last(source):
        for i, acc in pairs:
            acc[acc.shape[0] - source.shape[1]:, :] += source[i].astype(F32)

    add_last(outer_ref)

    @pl.when(need[0] > 0)
    def _():
        pltpu.sync_copy(far_hbm, far)
        add_last(far)

    @pl.when(need[0] > 1)
    def _():
        pltpu.sync_copy(rest_hbm, rest)
        for i, acc in pairs:
            acc[:rest.shape[1], :] += rest[i].astype(F32)


def total_kernel(sizes, parity, assistant, turn_first, key_acc, value_acc, stage, *rest):
    query_hbm, key_hbm, value_hbm, low, sem = rest[-5:]
    block_count, slot_count, head_count, width, scale = sizes
    rank = lax.axis_index("ctx")

    @pl.when(lax.rem(rank, 2) == parity)
    def _():
        slots = slots_of(assistant, turn_first, rank * block_count, block_count, slot_count)
        ends = [
            live & jnp.logical_not(slots[s + 1][1]) if s + 1 < slot_count else live
            for s, (_, live, _) in enumerate(slots)
        ]

        def stage_copy(s):
            rows = block_rows(slots[s][0])
            return pltpu.make_async_copy(stage.at[s], query_hbm.at[0, rows], sem.at[2 + s])

        for s in range(slot_count):
            @pl.when(ends[s])
            def _():
                stage_copy(s).start()

        copies = []
        for i, (acc, out) in enumerate(((key_acc, key_hbm), (value_acc, value_hbm))):
            total = acc[...] if parity == 1 else acc[...] + rest[0][i].astype(F32)
            low[i] = total.astype(BF16)
            copies.append(pltpu.make_async_copy(low.at[i], out.at[0], sem.at[i]))
            copies[i].start()
        for copy in copies:
            copy.wait()
        for s in range(slot_count):
            @pl.when(ends[s])
            def _():
                stage_copy(s).wait()


def call(kernel, inputs, in_specs, outputs, out_specs, scratch, limit, macs, aliases={},
         traffic=2 * MIB):
    return pl.pallas_call(
        kernel,
        out_shape=outputs,
        in_specs=in_specs,
        out_specs=out_specs,
        scratch_shapes=scratch,
        input_output_aliases=aliases,
        compiler_params=pltpu.CompilerParams(vmem_limit_bytes=limit * MIB),
        cost_estimate=pl.CostEstimate(flops=2 * macs, bytes_accessed=traffic, transcendentals=0),
    )(*inputs)


ANY_SPEC = pl.BlockSpec(memory_space=pl.ANY)
SMEM_SPEC = pl.BlockSpec(memory_space=pltpu.SMEM)
VMEM_SPEC = pl.BlockSpec(memory_space=pltpu.VMEM)


def score_shapes(sizes, rows):
    block_count, slot_count, head_count, width, scale = sizes
    columns = head_count * BLK
    return (
        pltpu.VMEM((slot_count, rows, columns), F32),
        pltpu.VMEM((slot_count, rows, columns), F32),
        pltpu.VMEM((slot_count, SUB, columns), F32),
        pltpu.VMEM((slot_count, SUB, columns), F32),
    )


def local_shapes(sizes):
    block_count, slot_count, head_count, width, scale = sizes
    rows = pltpu.VMEM((slot_count, head_count * BLK, width), BF16)
    return (rows, rows) + score_shapes(sizes, block_count * BLK)


def local_sems(sizes):
    return pltpu.SemaphoreType.DMA((sizes[1], 2))


def skip_kernel(*refs):
    pass


def stack_kernel(key_ref, value_ref, *outs):
    *outs, sem = outs
    copies = []
    for out in outs:
        first = key_ref.shape[1] - out.shape[1]
        for i, source in enumerate((key_ref, value_ref)):
            copies.append(
                pltpu.make_async_copy(
                    source.at[0, pl.ds(first, out.shape[1])], out.at[i], sem.at[len(copies)]
                )
            )
    for copy in copies:
        copy.start()
    for copy in copies:
        copy.wait()


def skipped(*shapes):
    return tuple(call(skip_kernel, (), [], shapes, [ANY_SPEC] * len(shapes), [], 4, 1, {}, 1))


def per_device(query_rows, key_rows, value_rows, out_grad, assistant, turn_first):
    token_count = query_rows.shape[1]
    width = key_rows.shape[2]
    head_count = query_rows.shape[2] // width
    block_count = token_count // BLK
    far_rows = block_count // 2 * BLK
    reach_rows = token_count + far_rows
    slot_count = (block_count + 1) // 2
    columns = head_count * BLK
    pair = columns * BLK * width
    sizes = (block_count, slot_count, head_count, width, 1.0 / math.sqrt(width))
    stat_rows = (slot_count, SUB, columns)
    last, own, assistant, turn_first, need = call(
        lambda *refs: pack_kernel(block_count, *refs),
        tuple(hbm(a) for a in (key_rows, value_rows, assistant, turn_first)),
        [ANY_SPEC] * 4,
        (
            pltpu.VMEM((2, far_rows, width), BF16),
            pltpu.VMEM((2, token_count, width), BF16),
            pltpu.SMEM(assistant.shape, jnp.int32),
            pltpu.SMEM(turn_first.shape, jnp.int32),
            pltpu.SMEM((1,), jnp.int32),
        ),
        [VMEM_SPEC] * 2 + [SMEM_SPEC] * 3,
        [pltpu.SemaphoreType.DMA((6,))],
        4,
        BLK,
    )
    marks = (smem(assistant), smem(turn_first))
    flag = smem(need)
    far_shape = jax.ShapeDtypeStruct((2, far_rows, width), BF16)
    whole_shape = jax.ShapeDtypeStruct((2, token_count, width), BF16)
    rest_shape = jax.ShapeDtypeStruct((2, token_count - far_rows, width), BF16)

    def stacked(sources, *shapes):
        return call(stack_kernel, sources, [ANY_SPEC] * 2, shapes, [ANY_SPEC] * len(shapes),
                    [pltpu.SemaphoreType.DMA((2 * len(shapes),))], 4, 1, {}, 1)

    def far_only(*sources):
        far, = stacked(sources, far_shape)
        return (shifted(far, "ctx", 2),) + skipped(whole_shape)

    def far_and_whole(*sources):
        far, whole = stacked(sources, far_shape, whole_shape)
        return shifted(far, "ctx", 2), pair_shift(whole, "ctx", 1, 0)

    far_in, whole_in = lax.switch(
        need[0], [lambda *_: skipped(far_shape, whole_shape), far_only, far_and_whole], key_rows, value_rows
    )
    own, far_in, whole_in = lax.optimization_barrier((own, far_in, whole_in))

    def local(early, state):
        return call(
            lambda *refs: local_kernel(sizes, early, *refs),
            marks + (hbm(query_rows), hbm(out_grad), vmem(own)) + tuple(vmem(a) for a in state),
            [SMEM_SPEC] * 2 + [ANY_SPEC] * 2 + [VMEM_SPEC] * (1 + len(state)),
            local_shapes(sizes),
            [VMEM_SPEC] * 6,
            [local_sems(sizes)],
            8,
            pair,
            {5 + i: i for i in range(len(state))},
            1,
        )

    def near(parity, half, sources, local_state, kept):
        inputs = marks + (flag,) + tuple(vmem(a) for a in local_state[:2]) + (hbm(far_in),) + sources
        return tuple(
            call(
                lambda *refs: near_kernel(sizes, parity, half, *refs),
                inputs + tuple(vmem(a) for a in kept),
                [SMEM_SPEC] * 3 + [VMEM_SPEC] * 2 + [ANY_SPEC, VMEM_SPEC]
                + [ANY_SPEC] * (len(sources) - 1) + [VMEM_SPEC] * len(kept),
                score_shapes(sizes, reach_rows) + (pltpu.VMEM((reach_rows, width), BF16),),
                [VMEM_SPEC] * 5,
                [pltpu.VMEM((reach_rows, width), BF16), pltpu.SemaphoreType.DMA((4,))],
                8,
                NEAR_HINT[parity] * pair,
                {len(inputs) + i: i for i in range(len(kept))},
                1,
            )
        )

    def remote(parity, near_rows, near_state, kept):
        inputs = marks + (flag,) + tuple(vmem(a) for a in (query_slots, grad_slots, sums, dots))
        held = tuple(vmem(a) for a in kept[:3]) + tuple(hbm(a) for a in kept[3:])
        passed = score_shapes(sizes, reach_rows) if parity == 0 else ()
        aliases = {len(inputs) + 4 + i: i for i in range(len(held))}
        aliases.update({len(inputs) + i: 5 + i for i in range(len(passed))})
        results = call(
            lambda *refs: remote_kernel(sizes, parity, *refs),
            inputs + tuple(vmem(a) for a in near_state) + held,
            [SMEM_SPEC] * 3 + [VMEM_SPEC] * (8 + len(held[:3])) + [ANY_SPEC] * len(held[3:]),
            (
                pltpu.VMEM((slot_count, reach_rows, columns), BF16),
                pltpu.VMEM(stat_rows, F32),
                pltpu.VMEM(stat_rows, F32),
                far_shape,
                rest_shape,
            )
            + passed
            + (pltpu.VMEM((2, near_rows, width), BF16),),
            [VMEM_SPEC] * 3 + [ANY_SPEC] * 2 + [VMEM_SPEC] * (1 + len(passed)),
            [
                pltpu.VMEM((slot_count * token_count, columns), BF16),
                pltpu.VMEM((reach_rows, width), F32),
                pltpu.VMEM((reach_rows, width), F32),
                pltpu.VMEM(far_shape.shape, BF16),
                pltpu.VMEM(rest_shape.shape, BF16),
            ],
            8,
            REMOTE_HINT[parity] * pair,
            aliases,
            1,
        )
        return tuple(results[:5]), tuple(results[5:-1]), results[-1]

    inner_first = pair_shift(own, "ctx", 1, 1, 0)
    local_state = local(True, ())
    near_state = near(1, 0, (vmem(inner_first),), local_state, ())
    last, own, local_state, near_state = lax.optimization_barrier((last, own, local_state, near_state))
    outer_in = pair_shift(last, "ctx", 1, 0)
    inner_second = pair_shift(own, "ctx", 1, 1, 1)
    local_state = local(False, local_state)
    query_slots, grad_slots, weights, prob_grad, sums, dots = local_state
    *near_state, window = near(0, None, (vmem(outer_in), hbm(whole_in)), local_state, near_state)
    remote_state, near_state, outer_grad = remote(0, far_rows, near_state, ())
    outer_back = pair_shift(outer_grad, "ctx", -1, 0)
    *near_state, window = near(1, 1, (vmem(inner_second),), local_state, near_state + (window,))
    remote_state, _, inner_grad = remote(1, token_count, near_state, remote_state)
    window = (window,)
    score_grad, inverse, delta, far_grad, rest_grad = remote_state

    def finish(early, state):
        inputs = marks + tuple(
            vmem(a)
            for a in (query_slots, grad_slots, weights, prob_grad, score_grad, inverse, delta, own) + window
        )
        return call(
            lambda *refs: finish_kernel(sizes, early, *refs),
            inputs + tuple(hbm(a) for a in state[:1]) + tuple(vmem(a) for a in state[1:]),
            [SMEM_SPEC] * 2 + [VMEM_SPEC] * 9 + [ANY_SPEC] * len(state[:1]) + [VMEM_SPEC] * len(state[1:]),
            (
                jax.ShapeDtypeStruct(query_rows.shape, BF16),
                pltpu.VMEM((token_count, width), F32),
                pltpu.VMEM((token_count, width), F32),
                pltpu.VMEM((slot_count, BLK, head_count * width), BF16),
            ),
            [ANY_SPEC] + [VMEM_SPEC] * 3,
            [
                pltpu.VMEM((slot_count, token_count, columns), BF16),
                pltpu.VMEM((token_count, columns), BF16),
                pltpu.VMEM((BLK, columns), F32),
                pltpu.VMEM((BLK, head_count * width), BF16),
                pltpu.SemaphoreType.DMA((slot_count + block_count,)),
            ],
            10,
            pair,
            {len(inputs) + i: i for i in range(len(state))},
            1,
        )

    state = finish(True, ())
    inner_grad, state = lax.optimization_barrier((inner_grad, state))
    inner_back = pair_shift(inner_grad, "ctx", -1, 1)
    query_grad, key_acc, value_acc, stage = finish(False, tuple(state))
    far_grad, rest_grad, query_grad = lax.optimization_barrier((far_grad, rest_grad, query_grad))
    far_back, rest_back = lax.switch(
        need[0],
        [
            lambda far, rest: skipped(far_shape, rest_shape),
            lambda far, rest: (shifted(far, "ctx", -2),) + skipped(rest_shape),
            lambda far, rest: (shifted(far, "ctx", -2), pair_shift(rest, "ctx", -1, 0)),
        ],
        far_grad,
        rest_grad,
    )
    key_acc, value_acc = call(
        add_kernel,
        (flag,) + tuple(vmem(a) for a in (key_acc, value_acc, outer_back)) + (hbm(far_back), hbm(rest_back)),
        [SMEM_SPEC] + [VMEM_SPEC] * 3 + [ANY_SPEC] * 2,
        (pltpu.VMEM((token_count, width), F32),) * 2,
        [VMEM_SPEC] * 2,
        [pltpu.VMEM(far_shape.shape, BF16), pltpu.VMEM(rest_shape.shape, BF16)],
        4,
        CROSS_HINT * pair,
        {1: 0, 2: 1},
        1,
    )
    results = (query_grad,)
    for parity, received in ((1, ()), (0, (vmem(inner_back),))):
        inputs = marks + tuple(vmem(a) for a in (key_acc, value_acc, stage)) + received
        results = call(
            lambda *refs: total_kernel(sizes, parity, *refs),
            inputs + tuple(hbm(a) for a in results),
            [SMEM_SPEC] * 2 + [VMEM_SPEC] * (len(inputs) - 2) + [ANY_SPEC] * len(results),
            tuple(jax.ShapeDtypeStruct(a.shape, BF16) for a in (query_rows, key_rows, value_rows)),
            [ANY_SPEC] * 3,
            [pltpu.VMEM((2, token_count, width), BF16), pltpu.SemaphoreType.DMA((2 + slot_count,))],
            8,
            pair,
            {len(inputs) + i: i for i in range(len(results))},
            1,
        )
    return tuple(results)


def solution(mesh):
    return jax.shard_map(
        per_device,
        mesh=mesh,
        in_specs=(
            P("dp", "ctx", "tp"),
            P("dp", "ctx", "tp"),
            P("dp", "ctx", "tp"),
            P("dp", "ctx", "tp"),
            P("dp", None),
            P("dp", None),
        ),
        out_specs=(P("dp", "ctx", "tp"), P("dp", "ctx", "tp"), P("dp", "ctx", "tp")),
        check_vma=False,
    )
```

```python
import math

import jax
import jax.numpy as jnp
from jax import lax
from jax.experimental import pallas as pl
from jax.experimental.pallas import tpu as pltpu
from jax.sharding import PartitionSpec as P

BLK = 128
SUB = 8
CHUNK = 256
F32 = jnp.float32
BF16 = jnp.bfloat16
MIB = 1 << 20
NEAR_HINT = (400, 10)
REMOTE_HINT = (14, 14)
CROSS_HINT = 60


def shifted(block, axis, distance):
    devices = range(lax.axis_size(axis))
    route = [(i - distance, i) for i in devices if i - distance in devices]
    return lax.ppermute(block, axis, route)


def pair_shift(block, axis, distance, parity):
    pairs = [(i - 1, i) for i in range(1, lax.axis_size(axis)) if i % 2 == parity]
    return lax.ppermute(block, axis, pairs if distance == 1 else [pair[::-1] for pair in pairs])


def vmem(array):
    return pltpu.with_memory_space_constraint(array, pltpu.VMEM)


def smem(array):
    return pltpu.with_memory_space_constraint(array, pltpu.SMEM)


def hbm(array):
    return pltpu.with_memory_space_constraint(array, pltpu.HBM)


def nt_dot(left, right):
    return lax.dot_general(left, right, (((1,), (1,)), ((), ())), preferred_element_type=F32)


def nn_dot(left, right):
    return lax.dot_general(left, right, (((1,), (0,)), ((), ())), preferred_element_type=F32)


def fold(tile):
    return jnp.sum(tile.reshape(tile.shape[0] // SUB, SUB, tile.shape[1]), axis=0)


def slots_of(assistant, turn_first, base, block_count, slot_count):
    found = jnp.int32(0)
    blocks = [jnp.int32(0)] * slot_count
    starts = [jnp.int32(0)] * slot_count
    for i in range(block_count):
        mark = assistant[0, base + i]
        start = turn_first[0, base + i] - base
        for s in range(slot_count):
            here = (mark == 1) & (found == s)
            blocks[s] = jnp.where(here, i, blocks[s])
            starts[s] = jnp.where(here, start, starts[s])
        found = found + jnp.where(mark == 1, 1, 0)
    return [(blocks[s], found > s, starts[s]) for s in range(slot_count)]


def score_pass(key_tile, value_tile, query_ref, grad_ref, slot, keep, weight_ref, prob_ref, at, sum_ref,
               dot_ref, scale):
    columns = query_ref.shape[1]
    for c in range(0, columns, CHUNK):
        span = slice(c, c + CHUNK)
        scores = nt_dot(key_tile, query_ref[slot, span, :])
        prob_grad = nt_dot(value_tile, grad_ref[slot, span, :])
        weights = jnp.exp2(scores * scale)
        if keep is not None:
            weights = jnp.where(jnp.concatenate([keep] * (CHUNK // BLK), axis=1), weights, 0.0)
        weight_ref[at + (span,)] = weights
        prob_ref[at + (span,)] = prob_grad
        sum_ref[slot, :, span] += fold(weights)
        dot_ref[slot, :, span] += fold(weights * prob_grad)


def grad_pass(weight_ref, prob_ref, at, query_ref, grad_ref, slot, inverse_ref, delta_ref, low_ref,
              score_ref, score_rows, key_acc, value_acc, acc_rows, low_first=0):
    columns = query_ref.shape[1]
    height = acc_rows.size
    low_rows = slice(low_first, low_first + height)
    for c in range(0, columns, CHUNK):
        span = slice(c, c + CHUNK)
        shape = (height // SUB, SUB, CHUNK)
        attention = weight_ref[at + (span,)].reshape(shape) * inverse_ref[slot, :, span][None]
        lifted = prob_ref[at + (span,)].reshape(shape) - delta_ref[slot, :, span][None]
        score_grad = (attention * lifted).reshape(height, CHUNK)
        low_ref[low_rows, span] = attention.reshape(height, CHUNK).astype(BF16)
        score_ref[slot, score_rows, span] = score_grad.astype(BF16)
    value_acc[acc_rows, :] += nn_dot(low_ref[low_rows], grad_ref[slot])
    key_acc[acc_rows, :] += nn_dot(score_ref[slot, score_rows, :], query_ref[slot])


def block_rows(index, count=1):
    return pl.ds(pl.multiple_of(index * BLK, BLK), count * BLK)


def pick(values, s):
    chosen = values[0]
    for i in range(1, len(values)):
        chosen = jnp.where(s == i, values[i], chosen)
    return chosen


def over_slots(slots, body):
    def step(s, carry):
        block, start = (pick([slot[i] for slot in slots], s) for i in (0, 2))

        @pl.when(pick([jnp.where(slot[1], 1, 0) for slot in slots], s) == 1)
        def _():
            body(s, block, start)

        return carry

    lax.fori_loop(0, len(slots), step, 0)


def local_scores(sizes, assistant, turn_first, query_hbm, grad_hbm, kv_ref, query_ref, grad_ref,
                 weight_ref, prob_ref, sum_ref, dot_ref, sem):
    block_count, slot_count, head_count, width, scale = sizes
    base = lax.axis_index("ctx") * block_count
    slots = slots_of(assistant, turn_first, base, block_count, slot_count)

    def copies(s, block):
        for i, (source, target) in enumerate(((query_hbm, query_ref), (grad_hbm, grad_ref))):
            for h in range(head_count):
                yield pltpu.make_async_copy(
                    source.at[0, block_rows(block), pl.ds(h * width, width)],
                    target.at[s, pl.ds(h * BLK, BLK)],
                    sem.at[s, i],
                )

    for s, (block, live, start) in enumerate(slots):
        @pl.when(live)
        def _():
            for copy in copies(s, block):
                copy.start()
    sum_ref[...] = jnp.zeros_like(sum_ref)
    dot_ref[...] = jnp.zeros_like(dot_ref)
    ahead = lax.broadcasted_iota(jnp.int32, (BLK, BLK), 1) - lax.broadcasted_iota(
        jnp.int32, (BLK, BLK), 0
    )
    def body(s, block, start):
        for i, target in enumerate((query_ref, grad_ref)):
            pltpu.make_async_copy(target.at[s], target.at[s], sem.at[s, i]).wait()

        def step(k, carry):
            rows = block_rows(k)
            score_pass(kv_ref[0, rows, :], kv_ref[1, rows, :], query_ref, grad_ref, s,
                       ahead >= (k - block) * BLK, weight_ref, prob_ref, (s, rows), sum_ref, dot_ref,
                       scale * math.log2(math.e))
            return carry

        lax.fori_loop(jnp.maximum(start, 0), block + 1, step, 0)

    over_slots(slots, body)


def in_first_half():
    return lax.axis_index("ctx") * 2 < lax.axis_size("ctx")


def local_kernel(sizes, early, *refs):
    inputs, results = refs[:5], refs[-7:]
    here = in_first_half() if early else jnp.logical_not(in_first_half())
    pl.when(here)(lambda: local_scores(sizes, *inputs, *results))


def pack_kernel(block_count, key_ref, value_ref, assistant_ref, turn_ref, last_ref, all_ref, assistant,
                turn_first, need_ref, pack_sem):
    token_count = key_ref.shape[1]
    marks = [
        pltpu.make_async_copy(assistant_ref, assistant, pack_sem.at[0]),
        pltpu.make_async_copy(turn_ref, turn_first, pack_sem.at[1]),
    ]
    copies = []
    for pack in (all_ref, last_ref):
        rows = pack.shape[1]
        for i, source in enumerate((key_ref, value_ref)):
            copies.append(
                pltpu.make_async_copy(
                    source.at[0, pl.ds(token_count - rows, rows)], pack.at[i], pack_sem.at[2 + len(copies)]
                )
            )
    for copy in marks + copies:
        copy.start()
    for copy in marks:
        copy.wait()
    outer = far = jnp.int32(0)
    for i in range(block_count, assistant.shape[1]):
        device = i // block_count
        behind = jnp.where(assistant[0, i] == 1, device * block_count - turn_first[0, i], 0)
        far = jnp.where(behind > block_count, 1, far)
        if device % 2 == 0:
            outer = jnp.maximum(outer, behind)
    need_ref[0] = jnp.where(outer > 1, 2, far)

    for copy in copies:
        copy.wait()


def over_window(block_count, reach, start, whole, body):
    first = jnp.maximum(start + reach, 0)
    last = reach
    if whole:
        @pl.when(start <= -block_count)
        def _():
            body(pl.ds((reach - block_count) * BLK, block_count * BLK))

        last = jnp.where(start <= -block_count, reach - block_count, reach)

    def step(k, carry):
        body(block_rows(k))
        return carry

    lax.fori_loop(first, last, step, 0)


def all_slots(slots, wanted):
    together = wanted(slots[0][2])
    for _, live, start in slots:
        together = together & live & wanted(start)
    return together


def near_kernel(sizes, parity, assistant, turn_first, need, query_ref, grad_ref, far_hbm, *rest):
    weight_ref, prob_ref, sum_ref, dot_ref, window, values, sem = rest[-7:]
    block_count, slot_count, head_count, width, scale = sizes
    rank = lax.axis_index("ctx")
    reach = window.shape[0] // BLK
    near = pl.ds((reach - block_count) * BLK, block_count * BLK)

    def fill(rows, source):
        window[rows, :] = source[0]
        values[rows, :] = source[1]

    def fetch(rows, source, first_sem):
        return [
            pltpu.make_async_copy(source.at[i], target.at[rows], sem.at[first_sem + i])
            for i, target in enumerate((window, values))
        ]

    def body(s, block, start):
        def scores(rows):
            score_pass(window[rows, :], values[rows, :], query_ref, grad_ref, s, None, weight_ref,
                       prob_ref, (s, rows), sum_ref, dot_ref, scale * math.log2(math.e))

        over_window(block_count, reach, start, parity == 1, scores)

    @pl.when(lax.rem(rank, 2) == parity)
    def _():
        if parity == 1:
            fill(near, rest[0])
        else:
            fill(block_rows(reach - 1), rest[0])

        @pl.when(need[0] > 0)
        def _():
            copies = fetch(pl.ds(0, far_hbm.shape[1]), far_hbm, 0)
            for copy in copies:
                copy.start()
            for copy in copies:
                copy.wait()

        if parity == 0:
            @pl.when(need[0] > 1)
            def _():
                copies = fetch(near, rest[1], 2)
                for copy in copies:
                    copy.start()
                for copy in copies:
                    copy.wait()

        sum_ref[...] = jnp.zeros_like(sum_ref)
        dot_ref[...] = jnp.zeros_like(dot_ref)
        slots = slots_of(assistant, turn_first, rank * block_count, block_count, slot_count)
        count = 1 if parity == 0 else block_count
        together = all_slots(slots, lambda start: start == -count)

        @pl.when(together)
        def _():
            rows = pl.ds((reach - count) * BLK, count * BLK)
            for s in range(slot_count):
                score_pass(window[rows, :], values[rows, :], query_ref, grad_ref, s, None, weight_ref,
                           prob_ref, (s, rows), sum_ref, dot_ref, scale * math.log2(math.e))

        pl.when(jnp.logical_not(together))(lambda: over_slots(slots, body))


def remote_kernel(sizes, parity, assistant, turn_first, need, query_ref, grad_ref, sum_local, dot_local,
                  weight_near, prob_near, sum_near, dot_near, *rest):
    block_count, slot_count, head_count, width, scale = sizes
    (score_ref, inverse_ref, delta_ref, far_hbm, rest_hbm, *_, near_out, low_ref, key_acc, value_acc, far_low,
     rest_low) = rest[-15 + 4 * parity:]
    rank = lax.axis_index("ctx")
    reach = weight_near.shape[1] // BLK

    def statistics(s):
        inverse = 1.0 / jnp.sum(sum_local[s] + sum_near[s], axis=0, keepdims=True)
        delta = jnp.sum(dot_local[s] + dot_near[s], axis=0, keepdims=True) * inverse
        inverse_ref[s] = jnp.broadcast_to(inverse, inverse_ref.shape[1:])
        delta_ref[s] = jnp.broadcast_to(delta, delta_ref.shape[1:])

    def gradients_of(s, rows, low_first=0):
        grad_pass(weight_near, prob_near, (s, rows), query_ref, grad_ref, s, inverse_ref, delta_ref,
                  low_ref, score_ref, rows, key_acc, value_acc, rows, low_first)

    def body(s, block, start):
        statistics(s)
        over_window(block_count, reach, start, parity == 1, lambda rows: gradients_of(s, rows))

    @pl.when(lax.rem(rank, 2) == parity)
    def _():
        key_acc[...] = jnp.zeros_like(key_acc)
        value_acc[...] = jnp.zeros_like(value_acc)
        slots = slots_of(assistant, turn_first, rank * block_count, block_count, slot_count)
        count = 1 if parity == 0 else block_count
        together = all_slots(slots, lambda start: start == -count)

        @pl.when(together)
        def _():
            rows = pl.ds((reach - count) * BLK, count * BLK)
            for s in range(slot_count):
                statistics(s)
            for s in range(slot_count):
                gradients_of(s, rows, s * count * BLK)

        pl.when(jnp.logical_not(together))(lambda: over_slots(slots, body))

        def round_to(out, first, rows):
            out[0] = (key_acc[first:first + rows, :] * scale).astype(BF16)
            out[1] = value_acc[first:first + rows, :].astype(BF16)

        total = reach * BLK
        round_to(near_out, total - near_out.shape[1], near_out.shape[1])

        @pl.when(need[0] > 0)
        def _():
            round_to(far_low, 0, far_low.shape[1])
            pltpu.sync_copy(far_low, far_hbm)

        if parity == 0:
            @pl.when(need[0] > 1)
            def _():
                round_to(rest_low, far_low.shape[1], rest_low.shape[1])
                pltpu.sync_copy(rest_low, rest_hbm)


def sends_late(rank):
    return (lax.rem(rank, 2) == 1) & (rank > 1)


def finish_kernel(sizes, early, assistant, turn_first, query_ref, grad_ref, weight_ref, prob_ref, score_in,
                  inverse_ref, delta_ref, kv_ref, window, *rest):
    query_hbm, key_acc, value_acc, stage, score_ref, low_ref, query_acc, blank, sem = rest[-9:]
    block_count, slot_count, head_count, width, scale = sizes
    rank = lax.axis_index("ctx")
    base = rank * block_count
    reach = window.shape[0] // BLK
    columns = query_acc.shape[1]

    def blank_copy(i):
        return pltpu.make_async_copy(blank, query_hbm.at[0, pl.ds(i * BLK, BLK)], sem.at[slot_count + i])

    def run():
        slots = slots_of(assistant, turn_first, base, block_count, slot_count)
        more = [live for _, live, _ in slots[1:]]

        def stage_copy(s):
            return pltpu.make_async_copy(stage.at[s], query_hbm.at[0, block_rows(slots[s][0])], sem.at[s])

        blank[...] = jnp.zeros_like(blank)
        for i in range(block_count):
            @pl.when(assistant[0, base + i] != 1)
            def _():
                blank_copy(i).start()
        key_acc[...] = jnp.zeros_like(key_acc)
        value_acc[...] = jnp.zeros_like(value_acc)

        def body(s, block, start):
            def query_part(keys, source, rows, span):
                return nn_dot(keys.T, source[s, rows, span])

            query_acc[...] = jnp.zeros_like(query_acc)

            def remote_part(rows):
                keys = window[rows, :]
                for c in range(0, columns, CHUNK):
                    span = slice(c, c + CHUNK)
                    query_acc[:, span] += query_part(keys, score_in, rows, span)

            over_window(block_count, reach, start, True, remote_part)
            low = jnp.maximum(start, 0)
            for count in range(1, block_count + 1):
                @pl.when(block + 1 - low == count)
                def _():
                    rows = block_rows(low, count)
                    grad_pass(weight_ref, prob_ref, (s, rows), query_ref, grad_ref, s, inverse_ref, delta_ref,
                              low_ref, score_ref, rows, key_acc, value_acc, rows)
                    keys = kv_ref[0, rows, :]
                    for c in range(0, columns, CHUNK):
                        span = slice(c, c + CHUNK)
                        total = query_acc[:, span] + query_part(keys, score_ref, rows, span)
                        for h in range(0, CHUNK, BLK):
                            place = slice((c + h) // BLK * width, ((c + h) // BLK + 1) * width)
                            stage[s, :, place] = (total[:, h:h + BLK] * scale).T.astype(BF16)

            for i in range(slot_count - 1):
                @pl.when((s == i) & more[i])
                def _():
                    stage_copy(i).start()

        over_slots(slots, body)
        key_acc[...] = key_acc[...] * scale
        for i in range(slot_count - 1):
            @pl.when(more[i])
            def _():
                stage_copy(i).wait()

        for i in range(block_count):
            @pl.when(assistant[0, base + i] != 1)
            def _():
                blank_copy(i).wait()

    pl.when(sends_late(rank) if early else jnp.logical_not(sends_late(rank)))(run)


def add_kernel(need, key_in, value_in, outer_ref, far_hbm, rest_hbm, key_acc, value_acc, far, rest):
    pairs = list(enumerate((key_acc, value_acc)))

    def add_last(source):
        for i, acc in pairs:
            acc[acc.shape[0] - source.shape[1]:, :] += source[i].astype(F32)

    add_last(outer_ref)

    @pl.when(need[0] > 0)
    def _():
        pltpu.sync_copy(far_hbm, far)
        add_last(far)

    @pl.when(need[0] > 1)
    def _():
        pltpu.sync_copy(rest_hbm, rest)
        for i, acc in pairs:
            acc[:rest.shape[1], :] += rest[i].astype(F32)


def total_kernel(sizes, parity, assistant, turn_first, key_acc, value_acc, stage, *rest):
    query_hbm, key_hbm, value_hbm, low, sem = rest[-5:]
    block_count, slot_count, head_count, width, scale = sizes
    rank = lax.axis_index("ctx")

    @pl.when(lax.rem(rank, 2) == parity)
    def _():
        slots = slots_of(assistant, turn_first, rank * block_count, block_count, slot_count)
        ends = [
            live & jnp.logical_not(slots[s + 1][1]) if s + 1 < slot_count else live
            for s, (_, live, _) in enumerate(slots)
        ]

        def stage_copy(s):
            rows = block_rows(slots[s][0])
            return pltpu.make_async_copy(stage.at[s], query_hbm.at[0, rows], sem.at[2 + s])

        for s in range(slot_count):
            @pl.when(ends[s])
            def _():
                stage_copy(s).start()

        copies = []
        for i, (acc, out) in enumerate(((key_acc, key_hbm), (value_acc, value_hbm))):
            total = acc[...] if parity == 1 else acc[...] + rest[0][i].astype(F32)
            low[i] = total.astype(BF16)
            copies.append(pltpu.make_async_copy(low.at[i], out.at[0], sem.at[i]))
            copies[i].start()
        for copy in copies:
            copy.wait()
        for s in range(slot_count):
            @pl.when(ends[s])
            def _():
                stage_copy(s).wait()


def call(kernel, inputs, in_specs, outputs, out_specs, scratch, limit, macs, aliases={},
         traffic=2 * MIB):
    return pl.pallas_call(
        kernel,
        out_shape=outputs,
        in_specs=in_specs,
        out_specs=out_specs,
        scratch_shapes=scratch,
        input_output_aliases=aliases,
        compiler_params=pltpu.CompilerParams(vmem_limit_bytes=limit * MIB),
        cost_estimate=pl.CostEstimate(flops=2 * macs, bytes_accessed=traffic, transcendentals=0),
    )(*inputs)


ANY_SPEC = pl.BlockSpec(memory_space=pl.ANY)
SMEM_SPEC = pl.BlockSpec(memory_space=pltpu.SMEM)
VMEM_SPEC = pl.BlockSpec(memory_space=pltpu.VMEM)


def score_shapes(sizes, rows):
    block_count, slot_count, head_count, width, scale = sizes
    columns = head_count * BLK
    return (
        pltpu.VMEM((slot_count, rows, columns), F32),
        pltpu.VMEM((slot_count, rows, columns), F32),
        pltpu.VMEM((slot_count, SUB, columns), F32),
        pltpu.VMEM((slot_count, SUB, columns), F32),
    )


def local_shapes(sizes):
    block_count, slot_count, head_count, width, scale = sizes
    rows = pltpu.VMEM((slot_count, head_count * BLK, width), BF16)
    return (rows, rows) + score_shapes(sizes, block_count * BLK)


def local_sems(sizes):
    return pltpu.SemaphoreType.DMA((sizes[1], 2))


def skip_kernel(*refs):
    pass


def stack_kernel(key_ref, value_ref, *outs):
    *outs, sem = outs
    copies = []
    for out in outs:
        first = key_ref.shape[1] - out.shape[1]
        for i, source in enumerate((key_ref, value_ref)):
            copies.append(
                pltpu.make_async_copy(
                    source.at[0, pl.ds(first, out.shape[1])], out.at[i], sem.at[len(copies)]
                )
            )
    for copy in copies:
        copy.start()
    for copy in copies:
        copy.wait()


def skipped(*shapes):
    return tuple(call(skip_kernel, (), [], shapes, [ANY_SPEC] * len(shapes), [], 4, 1, {}, 1))


def per_device(query_rows, key_rows, value_rows, out_grad, assistant, turn_first):
    token_count = query_rows.shape[1]
    width = key_rows.shape[2]
    head_count = query_rows.shape[2] // width
    block_count = token_count // BLK
    far_rows = block_count // 2 * BLK
    reach_rows = token_count + far_rows
    slot_count = (block_count + 1) // 2
    columns = head_count * BLK
    pair = columns * BLK * width
    sizes = (block_count, slot_count, head_count, width, 1.0 / math.sqrt(width))
    stat_rows = (slot_count, SUB, columns)
    last, own, assistant, turn_first, need = call(
        lambda *refs: pack_kernel(block_count, *refs),
        tuple(hbm(a) for a in (key_rows, value_rows, assistant, turn_first)),
        [ANY_SPEC] * 4,
        (
            pltpu.VMEM((2, far_rows, width), BF16),
            pltpu.VMEM((2, token_count, width), BF16),
            pltpu.SMEM(assistant.shape, jnp.int32),
            pltpu.SMEM(turn_first.shape, jnp.int32),
            pltpu.SMEM((1,), jnp.int32),
        ),
        [VMEM_SPEC] * 2 + [SMEM_SPEC] * 3,
        [pltpu.SemaphoreType.DMA((6,))],
        4,
        BLK,
    )
    marks = (smem(assistant), smem(turn_first))
    flag = smem(need)
    far_shape = jax.ShapeDtypeStruct((2, far_rows, width), BF16)
    whole_shape = jax.ShapeDtypeStruct((2, token_count, width), BF16)
    rest_shape = jax.ShapeDtypeStruct((2, token_count - far_rows, width), BF16)

    def stacked(sources, *shapes):
        return call(stack_kernel, sources, [ANY_SPEC] * 2, shapes, [ANY_SPEC] * len(shapes),
                    [pltpu.SemaphoreType.DMA((2 * len(shapes),))], 4, 1, {}, 1)

    def far_only(*sources):
        far, = stacked(sources, far_shape)
        return (shifted(far, "ctx", 2),) + skipped(whole_shape)

    def far_and_whole(*sources):
        far, whole = stacked(sources, far_shape, whole_shape)
        return shifted(far, "ctx", 2), pair_shift(whole, "ctx", 1, 0)

    far_in, whole_in = lax.switch(
        need[0], [lambda *_: skipped(far_shape, whole_shape), far_only, far_and_whole], key_rows, value_rows
    )
    own, far_in, whole_in = lax.optimization_barrier((own, far_in, whole_in))

    def local(early, state):
        return call(
            lambda *refs: local_kernel(sizes, early, *refs),
            marks + (hbm(query_rows), hbm(out_grad), vmem(own)) + tuple(vmem(a) for a in state),
            [SMEM_SPEC] * 2 + [ANY_SPEC] * 2 + [VMEM_SPEC] * (1 + len(state)),
            local_shapes(sizes),
            [VMEM_SPEC] * 6,
            [local_sems(sizes)],
            8,
            pair,
            {5 + i: i for i in range(len(state))},
            1,
        )

    def near(parity, sources, kept):
        inputs = marks + (flag, vmem(query_slots), vmem(grad_slots), hbm(far_in)) + sources
        return tuple(
            call(
                lambda *refs: near_kernel(sizes, parity, *refs),
                inputs + tuple(vmem(a) for a in kept),
                [SMEM_SPEC] * 3 + [VMEM_SPEC] * 2 + [ANY_SPEC, VMEM_SPEC]
                + [ANY_SPEC] * (len(sources) - 1) + [VMEM_SPEC] * len(kept),
                score_shapes(sizes, reach_rows) + (pltpu.VMEM((reach_rows, width), BF16),),
                [VMEM_SPEC] * 5,
                [pltpu.VMEM((reach_rows, width), BF16), pltpu.SemaphoreType.DMA((4,))],
                8,
                NEAR_HINT[parity] * pair,
                {len(inputs) + i: i for i in range(len(kept))},
                1,
            )
        )

    def remote(parity, near_rows, near_state, kept):
        inputs = marks + (flag,) + tuple(vmem(a) for a in (query_slots, grad_slots, sums, dots))
        held = tuple(vmem(a) for a in kept[:3]) + tuple(hbm(a) for a in kept[3:])
        passed = score_shapes(sizes, reach_rows) if parity == 0 else ()
        aliases = {len(inputs) + 4 + i: i for i in range(len(held))}
        aliases.update({len(inputs) + i: 5 + i for i in range(len(passed))})
        results = call(
            lambda *refs: remote_kernel(sizes, parity, *refs),
            inputs + tuple(vmem(a) for a in near_state) + held,
            [SMEM_SPEC] * 3 + [VMEM_SPEC] * (8 + len(held[:3])) + [ANY_SPEC] * len(held[3:]),
            (
                pltpu.VMEM((slot_count, reach_rows, columns), BF16),
                pltpu.VMEM(stat_rows, F32),
                pltpu.VMEM(stat_rows, F32),
                far_shape,
                rest_shape,
            )
            + passed
            + (pltpu.VMEM((2, near_rows, width), BF16),),
            [VMEM_SPEC] * 3 + [ANY_SPEC] * 2 + [VMEM_SPEC] * (1 + len(passed)),
            [
                pltpu.VMEM((slot_count * token_count, columns), BF16),
                pltpu.VMEM((reach_rows, width), F32),
                pltpu.VMEM((reach_rows, width), F32),
                pltpu.VMEM(far_shape.shape, BF16),
                pltpu.VMEM(rest_shape.shape, BF16),
            ],
            8,
            REMOTE_HINT[parity] * pair,
            aliases,
            1,
        )
        return tuple(results[:5]), tuple(results[5:-1]), results[-1]

    local_state = local(True, ())
    last, own, local_state = lax.optimization_barrier((last, own, local_state))
    outer_in = pair_shift(last, "ctx", 1, 0)
    inner_in = pair_shift(own, "ctx", 1, 1)
    local_state = local(False, local_state)
    query_slots, grad_slots, weights, prob_grad, sums, dots = local_state
    *near_state, window = near(0, (vmem(outer_in), hbm(whole_in)), ())
    remote_state, near_state, outer_grad = remote(0, far_rows, near_state, ())
    outer_back = pair_shift(outer_grad, "ctx", -1, 0)
    *near_state, window = near(1, (vmem(inner_in),), near_state + (window,))
    remote_state, _, inner_grad = remote(1, token_count, near_state, remote_state)
    window = (window,)
    score_grad, inverse, delta, far_grad, rest_grad = remote_state

    def finish(early, state):
        inputs = marks + tuple(
            vmem(a)
            for a in (query_slots, grad_slots, weights, prob_grad, score_grad, inverse, delta, own) + window
        )
        return call(
            lambda *refs: finish_kernel(sizes, early, *refs),
            inputs + tuple(hbm(a) for a in state[:1]) + tuple(vmem(a) for a in state[1:]),
            [SMEM_SPEC] * 2 + [VMEM_SPEC] * 9 + [ANY_SPEC] * len(state[:1]) + [VMEM_SPEC] * len(state[1:]),
            (
                jax.ShapeDtypeStruct(query_rows.shape, BF16),
                pltpu.VMEM((token_count, width), F32),
                pltpu.VMEM((token_count, width), F32),
                pltpu.VMEM((slot_count, BLK, head_count * width), BF16),
            ),
            [ANY_SPEC] + [VMEM_SPEC] * 3,
            [
                pltpu.VMEM((slot_count, token_count, columns), BF16),
                pltpu.VMEM((token_count, columns), BF16),
                pltpu.VMEM((BLK, columns), F32),
                pltpu.VMEM((BLK, head_count * width), BF16),
                pltpu.SemaphoreType.DMA((slot_count + block_count,)),
            ],
            10,
            pair,
            {len(inputs) + i: i for i in range(len(state))},
            1,
        )

    state = finish(True, ())
    inner_grad, state = lax.optimization_barrier((inner_grad, state))
    inner_back = pair_shift(inner_grad, "ctx", -1, 1)
    query_grad, key_acc, value_acc, stage = finish(False, tuple(state))
    far_grad, rest_grad, query_grad = lax.optimization_barrier((far_grad, rest_grad, query_grad))
    far_back, rest_back = lax.switch(
        need[0],
        [
            lambda far, rest: skipped(far_shape, rest_shape),
            lambda far, rest: (shifted(far, "ctx", -2),) + skipped(rest_shape),
            lambda far, rest: (shifted(far, "ctx", -2), pair_shift(rest, "ctx", -1, 0)),
        ],
        far_grad,
        rest_grad,
    )
    key_acc, value_acc = call(
        add_kernel,
        (flag,) + tuple(vmem(a) for a in (key_acc, value_acc, outer_back)) + (hbm(far_back), hbm(rest_back)),
        [SMEM_SPEC] + [VMEM_SPEC] * 3 + [ANY_SPEC] * 2,
        (pltpu.VMEM((token_count, width), F32),) * 2,
        [VMEM_SPEC] * 2,
        [pltpu.VMEM(far_shape.shape, BF16), pltpu.VMEM(rest_shape.shape, BF16)],
        4,
        CROSS_HINT * pair,
        {1: 0, 2: 1},
        1,
    )
    results = (query_grad,)
    for parity, received in ((1, ()), (0, (vmem(inner_back),))):
        inputs = marks + tuple(vmem(a) for a in (key_acc, value_acc, stage)) + received
        results = call(
            lambda *refs: total_kernel(sizes, parity, *refs),
            inputs + tuple(hbm(a) for a in results),
            [SMEM_SPEC] * 2 + [VMEM_SPEC] * (len(inputs) - 2) + [ANY_SPEC] * len(results),
            tuple(jax.ShapeDtypeStruct(a.shape, BF16) for a in (query_rows, key_rows, value_rows)),
            [ANY_SPEC] * 3,
            [pltpu.VMEM((2, token_count, width), BF16), pltpu.SemaphoreType.DMA((2 + slot_count,))],
            8,
            pair,
            {len(inputs) + i: i for i in range(len(results))},
            1,
        )
    return tuple(results)


def solution(mesh):
    return jax.shard_map(
        per_device,
        mesh=mesh,
        in_specs=(
            P("dp", "ctx", "tp"),
            P("dp", "ctx", "tp"),
            P("dp", "ctx", "tp"),
            P("dp", "ctx", "tp"),
            P("dp", None),
            P("dp", None),
        ),
        out_specs=(P("dp", "ctx", "tp"), P("dp", "ctx", "tp"), P("dp", "ctx", "tp")),
        check_vma=False,
    )
```

```python
import math

import jax
import jax.numpy as jnp
from jax import lax
from jax.experimental import pallas as pl
from jax.experimental.pallas import tpu as pltpu
from jax.sharding import PartitionSpec as P

BLK = 128
SUB = 8
CHUNK = 256
F32 = jnp.float32
BF16 = jnp.bfloat16
MIB = 1 << 20
NEAR_HINT = (400, 10)
REMOTE_HINT = (14, 14)
CROSS_HINT = 60


def shifted(block, axis, distance):
    devices = range(lax.axis_size(axis))
    route = [(i - distance, i) for i in devices if i - distance in devices]
    return lax.ppermute(block, axis, route)


def pair_shift(block, axis, distance, parity):
    pairs = [(i - 1, i) for i in range(1, lax.axis_size(axis)) if i % 2 == parity]
    return lax.ppermute(block, axis, pairs if distance == 1 else [pair[::-1] for pair in pairs])


def vmem(array):
    return pltpu.with_memory_space_constraint(array, pltpu.VMEM)


def smem(array):
    return pltpu.with_memory_space_constraint(array, pltpu.SMEM)


def hbm(array):
    return pltpu.with_memory_space_constraint(array, pltpu.HBM)


def nt_dot(left, right):
    return lax.dot_general(left, right, (((1,), (1,)), ((), ())), preferred_element_type=F32)


def nn_dot(left, right):
    return lax.dot_general(left, right, (((1,), (0,)), ((), ())), preferred_element_type=F32)


def fold(tile):
    return jnp.sum(tile.reshape(tile.shape[0] // SUB, SUB, tile.shape[1]), axis=0)


def slots_of(assistant, turn_first, base, block_count, slot_count):
    found = jnp.int32(0)
    blocks = [jnp.int32(0)] * slot_count
    starts = [jnp.int32(0)] * slot_count
    for i in range(block_count):
        mark = assistant[0, base + i]
        start = turn_first[0, base + i] - base
        for s in range(slot_count):
            here = (mark == 1) & (found == s)
            blocks[s] = jnp.where(here, i, blocks[s])
            starts[s] = jnp.where(here, start, starts[s])
        found = found + jnp.where(mark == 1, 1, 0)
    return [(blocks[s], found > s, starts[s]) for s in range(slot_count)]


def score_pass(key_tile, value_tile, query_ref, grad_ref, slot, keep, weight_ref, prob_ref, at, sum_ref,
               dot_ref, scale):
    columns = query_ref.shape[1]
    for c in range(0, columns, CHUNK):
        span = slice(c, c + CHUNK)
        scores = nt_dot(key_tile, query_ref[slot, span, :])
        prob_grad = nt_dot(value_tile, grad_ref[slot, span, :])
        weights = jnp.exp2(scores * scale)
        if keep is not None:
            weights = jnp.where(jnp.concatenate([keep] * (CHUNK // BLK), axis=1), weights, 0.0)
        weight_ref[at + (span,)] = weights
        prob_ref[at + (span,)] = prob_grad
        sum_ref[slot, :, span] += fold(weights)
        dot_ref[slot, :, span] += fold(weights * prob_grad)


def grad_pass(weight_ref, prob_ref, at, query_ref, grad_ref, slot, inverse_ref, delta_ref, low_ref,
              score_ref, score_rows, key_acc, value_acc, acc_rows, low_first=0):
    columns = query_ref.shape[1]
    height = acc_rows.size
    low_rows = slice(low_first, low_first + height)
    for c in range(0, columns, CHUNK):
        span = slice(c, c + CHUNK)
        shape = (height // SUB, SUB, CHUNK)
        attention = weight_ref[at + (span,)].reshape(shape) * inverse_ref[slot, :, span][None]
        lifted = prob_ref[at + (span,)].reshape(shape) - delta_ref[slot, :, span][None]
        score_grad = (attention * lifted).reshape(height, CHUNK)
        low_ref[low_rows, span] = attention.reshape(height, CHUNK).astype(BF16)
        score_ref[slot, score_rows, span] = score_grad.astype(BF16)
    value_acc[acc_rows, :] += nn_dot(low_ref[low_rows], grad_ref[slot])
    key_acc[acc_rows, :] += nn_dot(score_ref[slot, score_rows, :], query_ref[slot])


def block_rows(index, count=1):
    return pl.ds(pl.multiple_of(index * BLK, BLK), count * BLK)


def pick(values, s):
    chosen = values[0]
    for i in range(1, len(values)):
        chosen = jnp.where(s == i, values[i], chosen)
    return chosen


def over_slots(slots, body):
    def step(s, carry):
        block, start = (pick([slot[i] for slot in slots], s) for i in (0, 2))

        @pl.when(pick([jnp.where(slot[1], 1, 0) for slot in slots], s) == 1)
        def _():
            body(s, block, start)

        return carry

    lax.fori_loop(0, len(slots), step, 0)


def packs_late(rank):
    return (lax.rem(rank, 2) == 0) & (rank * 2 >= lax.axis_size("ctx"))


def local_kernel(sizes, assistant, turn_first, query_ref, grad_ref, kv_ref, weight_ref, prob_ref, sum_ref,
                 dot_ref):
    block_count, slot_count, head_count, width, scale = sizes
    base = lax.axis_index("ctx") * block_count
    sum_ref[...] = jnp.zeros_like(sum_ref)
    dot_ref[...] = jnp.zeros_like(dot_ref)
    ahead = lax.broadcasted_iota(jnp.int32, (BLK, BLK), 1) - lax.broadcasted_iota(
        jnp.int32, (BLK, BLK), 0
    )

    def body(s, block, start):
        def step(k, carry):
            rows = block_rows(k)
            score_pass(kv_ref[0, rows, :], kv_ref[1, rows, :], query_ref, grad_ref, s,
                       ahead >= (k - block) * BLK, weight_ref, prob_ref, (s, rows), sum_ref, dot_ref,
                       scale * math.log2(math.e))
            return carry

        lax.fori_loop(jnp.maximum(start, 0), block + 1, step, 0)

    over_slots(slots_of(assistant, turn_first, base, block_count, slot_count), body)


def pack_kernel(sizes, early, key_ref, value_ref, assistant_ref, turn_ref, query_hbm, grad_hbm, *rest):
    block_count, slot_count, head_count, width, scale = sizes
    all_ref, assistant, turn_first, need_ref, query_ref, grad_ref = rest[-9:-3] if early else rest[-8:-2]
    packs = [all_ref, rest[-3]] if early else [all_ref]
    pack_sem, slot_sem = rest[-2:]
    rank = lax.axis_index("ctx")
    token_count = key_ref.shape[1]

    def run():
        marks = [
            pltpu.make_async_copy(assistant_ref, assistant, pack_sem.at[0]),
            pltpu.make_async_copy(turn_ref, turn_first, pack_sem.at[1]),
        ]
        copies = []
        for pack in packs:
            rows = pack.shape[1]
            for i, source in enumerate((key_ref, value_ref)):
                copies.append(
                    pltpu.make_async_copy(
                        source.at[0, pl.ds(token_count - rows, rows)], pack.at[i], pack_sem.at[2 + len(copies)]
                    )
                )
        for copy in marks + copies:
            copy.start()
        for copy in marks:
            copy.wait()
        slots = slots_of(assistant, turn_first, rank * block_count, block_count, slot_count)
        pairs = list(enumerate(((query_hbm, query_ref), (grad_hbm, grad_ref))))
        for s, (block, live, start) in enumerate(slots):
            @pl.when(live)
            def _():
                for i, (source, target) in pairs:
                    for h in range(head_count):
                        pltpu.make_async_copy(
                            source.at[0, block_rows(block), pl.ds(h * width, width)],
                            target.at[s, pl.ds(h * BLK, BLK)],
                            slot_sem.at[s, i],
                        ).start()

        outer = far = jnp.int32(0)
        for i in range(block_count, assistant.shape[1]):
            device = i // block_count
            behind = jnp.where(assistant[0, i] == 1, device * block_count - turn_first[0, i], 0)
            far = jnp.where(behind > block_count, 1, far)
            if device % 2 == 0:
                outer = jnp.maximum(outer, behind)
        need_ref[0] = jnp.where(outer > 1, 2, far)
        for copy in copies:
            copy.wait()
        for s, (block, live, start) in enumerate(slots):
            @pl.when(live)
            def _():
                for i, (source, target) in pairs:
                    pltpu.make_async_copy(target.at[s], target.at[s], slot_sem.at[s, i]).wait()

    pl.when(jnp.logical_not(packs_late(rank)) if early else packs_late(rank))(run)


def over_window(block_count, reach, start, whole, body):
    first = jnp.maximum(start + reach, 0)
    last = reach
    if whole:
        @pl.when(start <= -block_count)
        def _():
            body(pl.ds((reach - block_count) * BLK, block_count * BLK))

        last = jnp.where(start <= -block_count, reach - block_count, reach)

    def step(k, carry):
        body(block_rows(k))
        return carry

    lax.fori_loop(first, last, step, 0)


def all_slots(slots, wanted):
    together = wanted(slots[0][2])
    for _, live, start in slots:
        together = together & live & wanted(start)
    return together


def near_kernel(sizes, parity, assistant, turn_first, need, query_ref, grad_ref, far_hbm, *rest):
    weight_ref, prob_ref, sum_ref, dot_ref, window, values, sem = rest[-7:]
    block_count, slot_count, head_count, width, scale = sizes
    rank = lax.axis_index("ctx")
    reach = window.shape[0] // BLK
    near = pl.ds((reach - block_count) * BLK, block_count * BLK)

    def fill(rows, source):
        window[rows, :] = source[0]
        values[rows, :] = source[1]

    def fetch(rows, source, first_sem):
        return [
            pltpu.make_async_copy(source.at[i], target.at[rows], sem.at[first_sem + i])
            for i, target in enumerate((window, values))
        ]

    def body(s, block, start):
        def scores(rows):
            score_pass(window[rows, :], values[rows, :], query_ref, grad_ref, s, None, weight_ref,
                       prob_ref, (s, rows), sum_ref, dot_ref, scale * math.log2(math.e))

        over_window(block_count, reach, start, parity == 1, scores)

    @pl.when(lax.rem(rank, 2) == parity)
    def _():
        if parity == 1:
            fill(near, rest[0])
        else:
            fill(block_rows(reach - 1), rest[0])

        @pl.when(need[0] > 0)
        def _():
            copies = fetch(pl.ds(0, far_hbm.shape[1]), far_hbm, 0)
            for copy in copies:
                copy.start()
            for copy in copies:
                copy.wait()

        if parity == 0:
            @pl.when(need[0] > 1)
            def _():
                copies = fetch(near, rest[1], 2)
                for copy in copies:
                    copy.start()
                for copy in copies:
                    copy.wait()

        sum_ref[...] = jnp.zeros_like(sum_ref)
        dot_ref[...] = jnp.zeros_like(dot_ref)
        slots = slots_of(assistant, turn_first, rank * block_count, block_count, slot_count)
        count = 1 if parity == 0 else block_count
        together = all_slots(slots, lambda start: start == -count)

        @pl.when(together)
        def _():
            rows = pl.ds((reach - count) * BLK, count * BLK)
            for s in range(slot_count):
                score_pass(window[rows, :], values[rows, :], query_ref, grad_ref, s, None, weight_ref,
                           prob_ref, (s, rows), sum_ref, dot_ref, scale * math.log2(math.e))

        pl.when(jnp.logical_not(together))(lambda: over_slots(slots, body))


def remote_kernel(sizes, parity, assistant, turn_first, need, query_ref, grad_ref, sum_local, dot_local,
                  weight_near, prob_near, sum_near, dot_near, *rest):
    block_count, slot_count, head_count, width, scale = sizes
    (score_ref, inverse_ref, delta_ref, far_hbm, rest_hbm, *_, near_out, low_ref, key_acc, value_acc, far_low,
     rest_low) = rest[-15 + 4 * parity:]
    rank = lax.axis_index("ctx")
    reach = weight_near.shape[1] // BLK

    def statistics(s):
        inverse = 1.0 / jnp.sum(sum_local[s] + sum_near[s], axis=0, keepdims=True)
        delta = jnp.sum(dot_local[s] + dot_near[s], axis=0, keepdims=True) * inverse
        inverse_ref[s] = jnp.broadcast_to(inverse, inverse_ref.shape[1:])
        delta_ref[s] = jnp.broadcast_to(delta, delta_ref.shape[1:])

    def gradients_of(s, rows, low_first=0):
        grad_pass(weight_near, prob_near, (s, rows), query_ref, grad_ref, s, inverse_ref, delta_ref,
                  low_ref, score_ref, rows, key_acc, value_acc, rows, low_first)

    def body(s, block, start):
        statistics(s)
        over_window(block_count, reach, start, parity == 1, lambda rows: gradients_of(s, rows))

    @pl.when(lax.rem(rank, 2) == parity)
    def _():
        key_acc[...] = jnp.zeros_like(key_acc)
        value_acc[...] = jnp.zeros_like(value_acc)
        slots = slots_of(assistant, turn_first, rank * block_count, block_count, slot_count)
        count = 1 if parity == 0 else block_count
        together = all_slots(slots, lambda start: start == -count)

        @pl.when(together)
        def _():
            rows = pl.ds((reach - count) * BLK, count * BLK)
            for s in range(slot_count):
                statistics(s)
            for s in range(slot_count):
                gradients_of(s, rows, s * count * BLK)

        pl.when(jnp.logical_not(together))(lambda: over_slots(slots, body))

        def round_to(out, first, rows):
            out[0] = (key_acc[first:first + rows, :] * scale).astype(BF16)
            out[1] = value_acc[first:first + rows, :].astype(BF16)

        total = reach * BLK
        round_to(near_out, total - near_out.shape[1], near_out.shape[1])

        @pl.when(need[0] > 0)
        def _():
            round_to(far_low, 0, far_low.shape[1])
            pltpu.sync_copy(far_low, far_hbm)

        if parity == 0:
            @pl.when(need[0] > 1)
            def _():
                round_to(rest_low, far_low.shape[1], rest_low.shape[1])
                pltpu.sync_copy(rest_low, rest_hbm)


def sends_late(rank, slots):
    behind = sum(jnp.where(live, jnp.maximum(-start, 0), 0) for _, live, start in slots)
    return (lax.rem(rank, 2) == 1) & (rank > 1) & (behind <= 2)


def finish_kernel(sizes, early, assistant, turn_first, query_ref, grad_ref, weight_ref, prob_ref, score_in,
                  inverse_ref, delta_ref, kv_ref, window, *rest):
    query_hbm, key_acc, value_acc, stage, score_ref, low_ref, query_acc, blank, sem = rest[-9:]
    block_count, slot_count, head_count, width, scale = sizes
    rank = lax.axis_index("ctx")
    base = rank * block_count
    reach = window.shape[0] // BLK
    columns = query_acc.shape[1]

    def blank_copy(i):
        return pltpu.make_async_copy(blank, query_hbm.at[0, pl.ds(i * BLK, BLK)], sem.at[slot_count + i])

    slots = slots_of(assistant, turn_first, base, block_count, slot_count)

    def run():
        more = [live for _, live, _ in slots[1:]]

        def stage_copy(s):
            return pltpu.make_async_copy(stage.at[s], query_hbm.at[0, block_rows(slots[s][0])], sem.at[s])

        blank[...] = jnp.zeros_like(blank)
        for i in range(block_count):
            @pl.when(assistant[0, base + i] != 1)
            def _():
                blank_copy(i).start()
        key_acc[...] = jnp.zeros_like(key_acc)
        value_acc[...] = jnp.zeros_like(value_acc)

        def body(s, block, start):
            def query_part(keys, source, rows, span):
                return nn_dot(keys.T, source[s, rows, span])

            query_acc[...] = jnp.zeros_like(query_acc)

            def remote_part(rows):
                keys = window[rows, :]
                for c in range(0, columns, CHUNK):
                    span = slice(c, c + CHUNK)
                    query_acc[:, span] += query_part(keys, score_in, rows, span)

            over_window(block_count, reach, start, True, remote_part)
            low = jnp.maximum(start, 0)
            for count in range(1, block_count + 1):
                @pl.when(block + 1 - low == count)
                def _():
                    rows = block_rows(low, count)
                    grad_pass(weight_ref, prob_ref, (s, rows), query_ref, grad_ref, s, inverse_ref, delta_ref,
                              low_ref, score_ref, rows, key_acc, value_acc, rows)
                    keys = kv_ref[0, rows, :]
                    for c in range(0, columns, CHUNK):
                        span = slice(c, c + CHUNK)
                        total = query_acc[:, span] + query_part(keys, score_ref, rows, span)
                        for h in range(0, CHUNK, BLK):
                            place = slice((c + h) // BLK * width, ((c + h) // BLK + 1) * width)
                            stage[s, :, place] = (total[:, h:h + BLK] * scale).T.astype(BF16)

            for i in range(slot_count - 1):
                @pl.when((s == i) & more[i])
                def _():
                    stage_copy(i).start()

        over_slots(slots, body)
        key_acc[...] = key_acc[...] * scale
        for i in range(slot_count - 1):
            @pl.when(more[i])
            def _():
                stage_copy(i).wait()

        for i in range(block_count):
            @pl.when(assistant[0, base + i] != 1)
            def _():
                blank_copy(i).wait()

    before = sends_late(rank, slots)
    pl.when(before if early else jnp.logical_not(before))(run)


def add_kernel(need, key_in, value_in, outer_ref, far_hbm, rest_hbm, key_acc, value_acc, far, rest):
    pairs = list(enumerate((key_acc, value_acc)))

    def add_last(source):
        for i, acc in pairs:
            acc[acc.shape[0] - source.shape[1]:, :] += source[i].astype(F32)

    add_last(outer_ref)

    @pl.when(need[0] > 0)
    def _():
        pltpu.sync_copy(far_hbm, far)
        add_last(far)

    @pl.when(need[0] > 1)
    def _():
        pltpu.sync_copy(rest_hbm, rest)
        for i, acc in pairs:
            acc[:rest.shape[1], :] += rest[i].astype(F32)


def total_kernel(sizes, parity, assistant, turn_first, key_acc, value_acc, stage, *rest):
    query_hbm, key_hbm, value_hbm, low, sem = rest[-5:]
    block_count, slot_count, head_count, width, scale = sizes
    rank = lax.axis_index("ctx")

    @pl.when(lax.rem(rank, 2) == parity)
    def _():
        slots = slots_of(assistant, turn_first, rank * block_count, block_count, slot_count)
        ends = [
            live & jnp.logical_not(slots[s + 1][1]) if s + 1 < slot_count else live
            for s, (_, live, _) in enumerate(slots)
        ]

        def stage_copy(s):
            rows = block_rows(slots[s][0])
            return pltpu.make_async_copy(stage.at[s], query_hbm.at[0, rows], sem.at[2 + s])

        for s in range(slot_count):
            @pl.when(ends[s])
            def _():
                stage_copy(s).start()

        copies = []
        for i, (acc, out) in enumerate(((key_acc, key_hbm), (value_acc, value_hbm))):
            total = acc[...] if parity == 1 else acc[...] + rest[0][i].astype(F32)
            low[i] = total.astype(BF16)
            copies.append(pltpu.make_async_copy(low.at[i], out.at[0], sem.at[i]))
            copies[i].start()
        for copy in copies:
            copy.wait()
        for s in range(slot_count):
            @pl.when(ends[s])
            def _():
                stage_copy(s).wait()


def call(kernel, inputs, in_specs, outputs, out_specs, scratch, limit, macs, aliases={},
         traffic=2 * MIB):
    return pl.pallas_call(
        kernel,
        out_shape=outputs,
        in_specs=in_specs,
        out_specs=out_specs,
        scratch_shapes=scratch,
        input_output_aliases=aliases,
        compiler_params=pltpu.CompilerParams(vmem_limit_bytes=limit * MIB),
        cost_estimate=pl.CostEstimate(flops=2 * macs, bytes_accessed=traffic, transcendentals=0),
    )(*inputs)


ANY_SPEC = pl.BlockSpec(memory_space=pl.ANY)
SMEM_SPEC = pl.BlockSpec(memory_space=pltpu.SMEM)
VMEM_SPEC = pl.BlockSpec(memory_space=pltpu.VMEM)


def score_shapes(sizes, rows):
    block_count, slot_count, head_count, width, scale = sizes
    columns = head_count * BLK
    return (
        pltpu.VMEM((slot_count, rows, columns), F32),
        pltpu.VMEM((slot_count, rows, columns), F32),
        pltpu.VMEM((slot_count, SUB, columns), F32),
        pltpu.VMEM((slot_count, SUB, columns), F32),
    )


def skip_kernel(*refs):
    pass


def stack_kernel(key_ref, value_ref, *outs):
    *outs, sem = outs
    copies = []
    for out in outs:
        first = key_ref.shape[1] - out.shape[1]
        for i, source in enumerate((key_ref, value_ref)):
            copies.append(
                pltpu.make_async_copy(
                    source.at[0, pl.ds(first, out.shape[1])], out.at[i], sem.at[len(copies)]
                )
            )
    for copy in copies:
        copy.start()
    for copy in copies:
        copy.wait()


def skipped(*shapes):
    return tuple(call(skip_kernel, (), [], shapes, [ANY_SPEC] * len(shapes), [], 4, 1, {}, 1))


def per_device(query_rows, key_rows, value_rows, out_grad, assistant, turn_first):
    token_count = query_rows.shape[1]
    width = key_rows.shape[2]
    head_count = query_rows.shape[2] // width
    block_count = token_count // BLK
    far_rows = block_count // 2 * BLK
    reach_rows = token_count + far_rows
    slot_count = (block_count + 1) // 2
    columns = head_count * BLK
    pair = columns * BLK * width
    sizes = (block_count, slot_count, head_count, width, 1.0 / math.sqrt(width))
    stat_rows = (slot_count, SUB, columns)
    slot_rows = pltpu.VMEM((slot_count, columns, width), BF16)

    def pack(early, state):
        inputs = tuple(hbm(a) for a in (key_rows, value_rows, assistant, turn_first, query_rows, out_grad))
        last_shape = (pltpu.VMEM((2, far_rows, width), BF16),) if early else ()
        held = tuple(smem(a) if i in (1, 2, 3) else vmem(a) for i, a in enumerate(state))
        specs = [VMEM_SPEC] + [SMEM_SPEC] * 3 + [VMEM_SPEC] * 2
        return call(
            lambda *refs: pack_kernel(sizes, early, *refs),
            inputs + held,
            [ANY_SPEC] * 6 + specs[:len(held)],
            (
                pltpu.VMEM((2, token_count, width), BF16),
                pltpu.SMEM(assistant.shape, jnp.int32),
                pltpu.SMEM(turn_first.shape, jnp.int32),
                pltpu.SMEM((1,), jnp.int32),
                slot_rows,
                slot_rows,
            )
            + last_shape,
            specs + [VMEM_SPEC] * len(last_shape),
            [pltpu.SemaphoreType.DMA((6,)), pltpu.SemaphoreType.DMA((slot_count, 2))],
            4,
            pair,
            {6 + i: i for i in range(len(held))},
            1,
        )

    *state, last = pack(True, ())
    outer_in = pair_shift(last, "ctx", 1, 0)
    own, *marks, need, query_slots, grad_slots = pack(False, state)
    inner_in = pair_shift(own, "ctx", 1, 1)
    marks = tuple(smem(a) for a in marks)
    flag = smem(need)
    far_shape = jax.ShapeDtypeStruct((2, far_rows, width), BF16)
    whole_shape = jax.ShapeDtypeStruct((2, token_count, width), BF16)
    rest_shape = jax.ShapeDtypeStruct((2, token_count - far_rows, width), BF16)

    def stacked(sources, *shapes):
        return call(stack_kernel, sources, [ANY_SPEC] * 2, shapes, [ANY_SPEC] * len(shapes),
                    [pltpu.SemaphoreType.DMA((2 * len(shapes),))], 4, 1, {}, 1)

    def far_only(*sources):
        far, = stacked(sources, far_shape)
        return (shifted(far, "ctx", 2),) + skipped(whole_shape)

    def far_and_whole(*sources):
        far, whole = stacked(sources, far_shape, whole_shape)
        return shifted(far, "ctx", 2), pair_shift(whole, "ctx", 1, 0)

    far_in, whole_in = lax.switch(
        need[0], [lambda *_: skipped(far_shape, whole_shape), far_only, far_and_whole], key_rows, value_rows
    )
    local_own, far_in, whole_in = lax.optimization_barrier((own, far_in, whole_in))
    weights, prob_grad, sums, dots = call(
        lambda *refs: local_kernel(sizes, *refs),
        marks + tuple(vmem(a) for a in (query_slots, grad_slots, local_own)),
        [SMEM_SPEC] * 2 + [VMEM_SPEC] * 3,
        score_shapes(sizes, token_count),
        [VMEM_SPEC] * 4,
        [],
        8,
        pair,
        {},
        1,
    )

    def near(parity, sources, kept):
        inputs = marks + (flag, vmem(query_slots), vmem(grad_slots), hbm(far_in)) + sources
        return tuple(
            call(
                lambda *refs: near_kernel(sizes, parity, *refs),
                inputs + tuple(vmem(a) for a in kept),
                [SMEM_SPEC] * 3 + [VMEM_SPEC] * 2 + [ANY_SPEC, VMEM_SPEC]
                + [ANY_SPEC] * (len(sources) - 1) + [VMEM_SPEC] * len(kept),
                score_shapes(sizes, reach_rows) + (pltpu.VMEM((reach_rows, width), BF16),),
                [VMEM_SPEC] * 5,
                [pltpu.VMEM((reach_rows, width), BF16), pltpu.SemaphoreType.DMA((4,))],
                8,
                NEAR_HINT[parity] * pair,
                {len(inputs) + i: i for i in range(len(kept))},
                1,
            )
        )

    def remote(parity, near_rows, near_state, kept):
        inputs = marks + (flag,) + tuple(vmem(a) for a in (query_slots, grad_slots, sums, dots))
        held = tuple(vmem(a) for a in kept[:3]) + tuple(hbm(a) for a in kept[3:])
        passed = score_shapes(sizes, reach_rows) if parity == 0 else ()
        aliases = {len(inputs) + 4 + i: i for i in range(len(held))}
        aliases.update({len(inputs) + i: 5 + i for i in range(len(passed))})
        results = call(
            lambda *refs: remote_kernel(sizes, parity, *refs),
            inputs + tuple(vmem(a) for a in near_state) + held,
            [SMEM_SPEC] * 3 + [VMEM_SPEC] * (8 + len(held[:3])) + [ANY_SPEC] * len(held[3:]),
            (
                pltpu.VMEM((slot_count, reach_rows, columns), BF16),
                pltpu.VMEM(stat_rows, F32),
                pltpu.VMEM(stat_rows, F32),
                far_shape,
                rest_shape,
            )
            + passed
            + (pltpu.VMEM((2, near_rows, width), BF16),),
            [VMEM_SPEC] * 3 + [ANY_SPEC] * 2 + [VMEM_SPEC] * (1 + len(passed)),
            [
                pltpu.VMEM((slot_count * token_count, columns), BF16),
                pltpu.VMEM((reach_rows, width), F32),
                pltpu.VMEM((reach_rows, width), F32),
                pltpu.VMEM(far_shape.shape, BF16),
                pltpu.VMEM(rest_shape.shape, BF16),
            ],
            8,
            REMOTE_HINT[parity] * pair,
            aliases,
            1,
        )
        return tuple(results[:5]), tuple(results[5:-1]), results[-1]

    *near_state, window = near(0, (vmem(outer_in), hbm(whole_in)), ())
    remote_state, near_state, outer_grad = remote(0, far_rows, near_state, ())
    outer_back = pair_shift(outer_grad, "ctx", -1, 0)
    *near_state, window = near(1, (vmem(inner_in),), near_state + (window,))
    remote_state, _, inner_grad = remote(1, token_count, near_state, remote_state)
    window = (window,)
    score_grad, inverse, delta, far_grad, rest_grad = remote_state

    def finish(early, state):
        inputs = marks + tuple(
            vmem(a)
            for a in (query_slots, grad_slots, weights, prob_grad, score_grad, inverse, delta, own) + window
        )
        return call(
            lambda *refs: finish_kernel(sizes, early, *refs),
            inputs + tuple(hbm(a) for a in state[:1]) + tuple(vmem(a) for a in state[1:]),
            [SMEM_SPEC] * 2 + [VMEM_SPEC] * 9 + [ANY_SPEC] * len(state[:1]) + [VMEM_SPEC] * len(state[1:]),
            (
                jax.ShapeDtypeStruct(query_rows.shape, BF16),
                pltpu.VMEM((token_count, width), F32),
                pltpu.VMEM((token_count, width), F32),
                pltpu.VMEM((slot_count, BLK, head_count * width), BF16),
            ),
            [ANY_SPEC] + [VMEM_SPEC] * 3,
            [
                pltpu.VMEM((slot_count, token_count, columns), BF16),
                pltpu.VMEM((token_count, columns), BF16),
                pltpu.VMEM((BLK, columns), F32),
                pltpu.VMEM((BLK, head_count * width), BF16),
                pltpu.SemaphoreType.DMA((slot_count + block_count,)),
            ],
            10,
            pair,
            {len(inputs) + i: i for i in range(len(state))},
            1,
        )

    state = finish(True, ())
    inner_grad, state = lax.optimization_barrier((inner_grad, state))
    inner_back = pair_shift(inner_grad, "ctx", -1, 1)
    query_grad, key_acc, value_acc, stage = finish(False, tuple(state))
    far_grad, rest_grad, query_grad = lax.optimization_barrier((far_grad, rest_grad, query_grad))
    far_back, rest_back = lax.switch(
        need[0],
        [
            lambda far, rest: skipped(far_shape, rest_shape),
            lambda far, rest: (shifted(far, "ctx", -2),) + skipped(rest_shape),
            lambda far, rest: (shifted(far, "ctx", -2), pair_shift(rest, "ctx", -1, 0)),
        ],
        far_grad,
        rest_grad,
    )
    key_acc, value_acc = call(
        add_kernel,
        (flag,) + tuple(vmem(a) for a in (key_acc, value_acc, outer_back)) + (hbm(far_back), hbm(rest_back)),
        [SMEM_SPEC] + [VMEM_SPEC] * 3 + [ANY_SPEC] * 2,
        (pltpu.VMEM((token_count, width), F32),) * 2,
        [VMEM_SPEC] * 2,
        [pltpu.VMEM(far_shape.shape, BF16), pltpu.VMEM(rest_shape.shape, BF16)],
        4,
        CROSS_HINT * pair,
        {1: 0, 2: 1},
        1,
    )
    results = (query_grad,)
    for parity, received in ((1, ()), (0, (vmem(inner_back),))):
        inputs = marks + tuple(vmem(a) for a in (key_acc, value_acc, stage)) + received
        results = call(
            lambda *refs: total_kernel(sizes, parity, *refs),
            inputs + tuple(hbm(a) for a in results),
            [SMEM_SPEC] * 2 + [VMEM_SPEC] * (len(inputs) - 2) + [ANY_SPEC] * len(results),
            tuple(jax.ShapeDtypeStruct(a.shape, BF16) for a in (query_rows, key_rows, value_rows)),
            [ANY_SPEC] * 3,
            [pltpu.VMEM((2, token_count, width), BF16), pltpu.SemaphoreType.DMA((2 + slot_count,))],
            8,
            pair,
            {len(inputs) + i: i for i in range(len(results))},
            1,
        )
    return tuple(results)


def solution(mesh):
    return jax.shard_map(
        per_device,
        mesh=mesh,
        in_specs=(
            P("dp", "ctx", "tp"),
            P("dp", "ctx", "tp"),
            P("dp", "ctx", "tp"),
            P("dp", "ctx", "tp"),
            P("dp", None),
            P("dp", None),
        ),
        out_specs=(P("dp", "ctx", "tp"), P("dp", "ctx", "tp"), P("dp", "ctx", "tp")),
        check_vma=False,
    )
```

```python
import math

import jax
import jax.numpy as jnp
from jax import lax
from jax.experimental import pallas as pl
from jax.experimental.pallas import tpu as pltpu
from jax.sharding import PartitionSpec as P

BLK = 128
SUB = 8
CHUNK = 256
F32 = jnp.float32
BF16 = jnp.bfloat16
MIB = 1 << 20
NEAR_HINT = (400, 10)
REMOTE_HINT = (14, 14)
CROSS_HINT = 60


def shifted(block, axis, distance):
    devices = range(lax.axis_size(axis))
    route = [(i - distance, i) for i in devices if i - distance in devices]
    return lax.ppermute(block, axis, route)


def pair_shift(block, axis, distance, parity):
    pairs = [(i - 1, i) for i in range(1, lax.axis_size(axis)) if i % 2 == parity]
    return lax.ppermute(block, axis, pairs if distance == 1 else [pair[::-1] for pair in pairs])


def vmem(array):
    return pltpu.with_memory_space_constraint(array, pltpu.VMEM)


def smem(array):
    return pltpu.with_memory_space_constraint(array, pltpu.SMEM)


def hbm(array):
    return pltpu.with_memory_space_constraint(array, pltpu.HBM)


def nt_dot(left, right):
    return lax.dot_general(left, right, (((1,), (1,)), ((), ())), preferred_element_type=F32)


def nn_dot(left, right):
    return lax.dot_general(left, right, (((1,), (0,)), ((), ())), preferred_element_type=F32)


def fold(tile):
    return jnp.sum(tile.reshape(tile.shape[0] // SUB, SUB, tile.shape[1]), axis=0)


def slots_of(assistant, turn_first, base, block_count, slot_count):
    found = jnp.int32(0)
    blocks = [jnp.int32(0)] * slot_count
    starts = [jnp.int32(0)] * slot_count
    for i in range(block_count):
        mark = assistant[0, base + i]
        start = turn_first[0, base + i] - base
        for s in range(slot_count):
            here = (mark == 1) & (found == s)
            blocks[s] = jnp.where(here, i, blocks[s])
            starts[s] = jnp.where(here, start, starts[s])
        found = found + jnp.where(mark == 1, 1, 0)
    return [(blocks[s], found > s, starts[s]) for s in range(slot_count)]


def score_pass(key_tile, value_tile, query_ref, grad_ref, slot, keep, weight_ref, prob_ref, at, sum_ref,
               dot_ref, scale):
    columns = query_ref.shape[1]
    for c in range(0, columns, CHUNK):
        span = slice(c, c + CHUNK)
        scores = nt_dot(key_tile, query_ref[slot, span, :])
        prob_grad = nt_dot(value_tile, grad_ref[slot, span, :])
        weights = jnp.exp2(scores * scale)
        if keep is not None:
            weights = jnp.where(jnp.concatenate([keep] * (CHUNK // BLK), axis=1), weights, 0.0)
        if weight_ref is not None:
            weight_ref[at + (span,)] = weights
            prob_ref[at + (span,)] = prob_grad
        sum_ref[slot, :, span] += fold(weights)
        dot_ref[slot, :, span] += fold(weights * prob_grad)


def grad_pass(weight_ref, prob_ref, at, query_ref, grad_ref, slot, inverse_ref, delta_ref, low_ref,
              score_ref, score_rows, key_acc, value_acc, acc_rows, low_first=0):
    columns = query_ref.shape[1]
    height = acc_rows.size
    low_rows = slice(low_first, low_first + height)
    for c in range(0, columns, CHUNK):
        span = slice(c, c + CHUNK)
        shape = (height // SUB, SUB, CHUNK)
        attention = weight_ref[at + (span,)].reshape(shape) * inverse_ref[slot, :, span][None]
        lifted = prob_ref[at + (span,)].reshape(shape) - delta_ref[slot, :, span][None]
        score_grad = (attention * lifted).reshape(height, CHUNK)
        low_ref[low_rows, span] = attention.reshape(height, CHUNK).astype(BF16)
        score_ref[slot, score_rows, span] = score_grad.astype(BF16)
    value_acc[acc_rows, :] += nn_dot(low_ref[low_rows], grad_ref[slot])
    key_acc[acc_rows, :] += nn_dot(score_ref[slot, score_rows, :], query_ref[slot])


def local_pass(key_tile, value_tile, query_ref, grad_ref, slot, keep, inverse_ref, delta_ref, low_ref, score_ref,
               key_acc, value_acc, rows, scale):
    columns = query_ref.shape[1]
    height = rows.size
    for c in range(0, columns, CHUNK):
        span = slice(c, c + CHUNK)
        weights = jnp.exp2(nt_dot(key_tile, query_ref[slot, span, :]) * scale)
        wide = jnp.concatenate([keep] * (CHUNK // BLK), axis=1)
        last = jnp.where(wide, weights[height - BLK:], 0.0)
        weights = jnp.concatenate([weights[:height - BLK], last], axis=0) if height > BLK else last
        prob_grad = nt_dot(value_tile, grad_ref[slot, span, :])
        shape = (height // SUB, SUB, CHUNK)
        attention = weights.reshape(shape) * inverse_ref[slot, :, span][None]
        lifted = prob_grad.reshape(shape) - delta_ref[slot, :, span][None]
        score_grad = (attention * lifted).reshape(height, CHUNK)
        low_ref[:height, span] = attention.reshape(height, CHUNK).astype(BF16)
        score_ref[slot, rows, span] = score_grad.astype(BF16)
    value_acc[rows, :] += nn_dot(low_ref[:height], grad_ref[slot])
    key_acc[rows, :] += nn_dot(score_ref[slot, rows, :], query_ref[slot])


def block_rows(index, count=1):
    return pl.ds(pl.multiple_of(index * BLK, BLK), count * BLK)


def pick(values, s):
    chosen = values[0]
    for i in range(1, len(values)):
        chosen = jnp.where(s == i, values[i], chosen)
    return chosen


def over_slots(slots, body):
    def step(s, carry):
        block, start = (pick([slot[i] for slot in slots], s) for i in (0, 2))

        @pl.when(pick([jnp.where(slot[1], 1, 0) for slot in slots], s) == 1)
        def _():
            body(s, block, start)

        return carry

    lax.fori_loop(0, len(slots), step, 0)


def packs_late(rank):
    return (lax.rem(rank, 2) == 0) & (rank * 2 >= lax.axis_size("ctx"))


def local_sums(sizes, slots, query_ref, grad_ref, kv_ref, sum_ref, dot_ref):
    sum_ref[...] = jnp.zeros_like(sum_ref)
    dot_ref[...] = jnp.zeros_like(dot_ref)
    ahead = lax.broadcasted_iota(jnp.int32, (BLK, BLK), 1) - lax.broadcasted_iota(
        jnp.int32, (BLK, BLK), 0
    )

    def body(s, block, start):
        def step(k, carry):
            rows = block_rows(k)
            score_pass(kv_ref[0, rows, :], kv_ref[1, rows, :], query_ref, grad_ref, s,
                       ahead >= (k - block) * BLK, None, None, (), sum_ref, dot_ref,
                       sizes[-1] * math.log2(math.e))
            return carry

        lax.fori_loop(jnp.maximum(start, 0), block + 1, step, 0)

    over_slots(slots, body)


def pack_kernel(sizes, early, key_ref, value_ref, assistant_ref, turn_ref, query_hbm, grad_hbm, *rest):
    block_count, slot_count, head_count, width, scale = sizes
    all_ref, assistant, turn_first, need_ref, query_ref, grad_ref, sum_ref, dot_ref = (
        rest[-11:-3] if early else rest[-10:-2]
    )
    packs = [all_ref, rest[-3]] if early else [all_ref]
    pack_sem, slot_sem = rest[-2:]
    rank = lax.axis_index("ctx")
    token_count = key_ref.shape[1]

    def run():
        marks = [
            pltpu.make_async_copy(assistant_ref, assistant, pack_sem.at[0]),
            pltpu.make_async_copy(turn_ref, turn_first, pack_sem.at[1]),
        ]
        copies = []
        for pack in packs:
            rows = pack.shape[1]
            for i, source in enumerate((key_ref, value_ref)):
                copies.append(
                    pltpu.make_async_copy(
                        source.at[0, pl.ds(token_count - rows, rows)], pack.at[i], pack_sem.at[2 + len(copies)]
                    )
                )
        for copy in marks + copies:
            copy.start()
        for copy in marks:
            copy.wait()
        slots = slots_of(assistant, turn_first, rank * block_count, block_count, slot_count)
        pairs = list(enumerate(((query_hbm, query_ref), (grad_hbm, grad_ref))))
        for s, (block, live, start) in enumerate(slots):
            @pl.when(live)
            def _():
                for i, (source, target) in pairs:
                    for h in range(head_count):
                        pltpu.make_async_copy(
                            source.at[0, block_rows(block), pl.ds(h * width, width)],
                            target.at[s, pl.ds(h * BLK, BLK)],
                            slot_sem.at[s, i],
                        ).start()

        outer = far = jnp.int32(0)
        for i in range(block_count, assistant.shape[1]):
            device = i // block_count
            behind = jnp.where(assistant[0, i] == 1, device * block_count - turn_first[0, i], 0)
            far = jnp.where(behind > block_count, 1, far)
            if device % 2 == 0:
                outer = jnp.maximum(outer, behind)
        need_ref[0] = jnp.where(outer > 1, 2, far)
        for copy in copies:
            copy.wait()
        for s, (block, live, start) in enumerate(slots):
            @pl.when(live)
            def _():
                for i, (source, target) in pairs:
                    pltpu.make_async_copy(target.at[s], target.at[s], slot_sem.at[s, i]).wait()

        local_sums(sizes, slots, query_ref, grad_ref, all_ref, sum_ref, dot_ref)

    pl.when(jnp.logical_not(packs_late(rank)) if early else packs_late(rank))(run)


def over_window(block_count, reach, start, whole, body):
    first = jnp.maximum(start + reach, 0)
    last = reach
    if whole:
        @pl.when(start <= -block_count)
        def _():
            body(pl.ds((reach - block_count) * BLK, block_count * BLK))

        last = jnp.where(start <= -block_count, reach - block_count, reach)

    def step(k, carry):
        body(block_rows(k))
        return carry

    lax.fori_loop(first, last, step, 0)


def all_slots(slots, wanted):
    together = wanted(slots[0][2])
    for _, live, start in slots:
        together = together & live & wanted(start)
    return together


def near_kernel(sizes, parity, assistant, turn_first, need, query_ref, grad_ref, far_hbm, *rest):
    weight_ref, prob_ref, sum_ref, dot_ref, window, values, sem = rest[-7:]
    block_count, slot_count, head_count, width, scale = sizes
    rank = lax.axis_index("ctx")
    reach = window.shape[0] // BLK
    near = pl.ds((reach - block_count) * BLK, block_count * BLK)

    def fill(rows, source):
        window[rows, :] = source[0]
        values[rows, :] = source[1]

    def fetch(rows, source, first_sem):
        return [
            pltpu.make_async_copy(source.at[i], target.at[rows], sem.at[first_sem + i])
            for i, target in enumerate((window, values))
        ]

    def body(s, block, start):
        def scores(rows):
            score_pass(window[rows, :], values[rows, :], query_ref, grad_ref, s, None, weight_ref,
                       prob_ref, (s, rows), sum_ref, dot_ref, scale * math.log2(math.e))

        over_window(block_count, reach, start, parity == 1, scores)

    @pl.when(lax.rem(rank, 2) == parity)
    def _():
        if parity == 1:
            fill(near, rest[0])
        else:
            fill(block_rows(reach - 1), rest[0])

        @pl.when(need[0] > 0)
        def _():
            copies = fetch(pl.ds(0, far_hbm.shape[1]), far_hbm, 0)
            for copy in copies:
                copy.start()
            for copy in copies:
                copy.wait()

        if parity == 0:
            @pl.when(need[0] > 1)
            def _():
                copies = fetch(near, rest[1], 2)
                for copy in copies:
                    copy.start()
                for copy in copies:
                    copy.wait()

        sum_ref[...] = jnp.zeros_like(sum_ref)
        dot_ref[...] = jnp.zeros_like(dot_ref)
        slots = slots_of(assistant, turn_first, rank * block_count, block_count, slot_count)
        count = 1 if parity == 0 else block_count
        together = all_slots(slots, lambda start: start == -count)

        @pl.when(together)
        def _():
            rows = pl.ds((reach - count) * BLK, count * BLK)
            for s in range(slot_count):
                score_pass(window[rows, :], values[rows, :], query_ref, grad_ref, s, None, weight_ref,
                           prob_ref, (s, rows), sum_ref, dot_ref, scale * math.log2(math.e))

        pl.when(jnp.logical_not(together))(lambda: over_slots(slots, body))


def remote_kernel(sizes, parity, assistant, turn_first, need, query_ref, grad_ref, sum_local, dot_local,
                  weight_near, prob_near, sum_near, dot_near, *rest):
    block_count, slot_count, head_count, width, scale = sizes
    (score_ref, inverse_ref, delta_ref, far_hbm, rest_hbm, *_, near_out, low_ref, key_acc, value_acc, far_low,
     rest_low) = rest[-15 + 4 * parity:]
    rank = lax.axis_index("ctx")
    reach = weight_near.shape[1] // BLK

    def statistics(s):
        inverse = 1.0 / jnp.sum(sum_local[s] + sum_near[s], axis=0, keepdims=True)
        delta = jnp.sum(dot_local[s] + dot_near[s], axis=0, keepdims=True) * inverse
        inverse_ref[s] = jnp.broadcast_to(inverse, inverse_ref.shape[1:])
        delta_ref[s] = jnp.broadcast_to(delta, delta_ref.shape[1:])

    def gradients_of(s, rows, low_first=0):
        grad_pass(weight_near, prob_near, (s, rows), query_ref, grad_ref, s, inverse_ref, delta_ref,
                  low_ref, score_ref, rows, key_acc, value_acc, rows, low_first)

    def body(s, block, start):
        statistics(s)
        over_window(block_count, reach, start, parity == 1, lambda rows: gradients_of(s, rows))

    @pl.when(lax.rem(rank, 2) == parity)
    def _():
        key_acc[...] = jnp.zeros_like(key_acc)
        value_acc[...] = jnp.zeros_like(value_acc)
        slots = slots_of(assistant, turn_first, rank * block_count, block_count, slot_count)
        count = 1 if parity == 0 else block_count
        together = all_slots(slots, lambda start: start == -count)

        @pl.when(together)
        def _():
            rows = pl.ds((reach - count) * BLK, count * BLK)
            for s in range(slot_count):
                statistics(s)
            for s in range(slot_count):
                gradients_of(s, rows, s * count * BLK)

        pl.when(jnp.logical_not(together))(lambda: over_slots(slots, body))

        def round_to(out, first, rows):
            out[0] = (key_acc[first:first + rows, :] * scale).astype(BF16)
            out[1] = value_acc[first:first + rows, :].astype(BF16)

        total = reach * BLK
        round_to(near_out, total - near_out.shape[1], near_out.shape[1])

        @pl.when(need[0] > 0)
        def _():
            round_to(far_low, 0, far_low.shape[1])
            pltpu.sync_copy(far_low, far_hbm)

        if parity == 0:
            @pl.when(need[0] > 1)
            def _():
                round_to(rest_low, far_low.shape[1], rest_low.shape[1])
                pltpu.sync_copy(rest_low, rest_hbm)


def sends_late(rank, slots):
    behind = sum(jnp.where(live, jnp.maximum(-start, 0), 0) for _, live, start in slots)
    return (lax.rem(rank, 2) == 1) & (rank > 1) & (behind <= 2)


def finish_kernel(sizes, early, assistant, turn_first, query_ref, grad_ref, score_in, inverse_ref, delta_ref,
                  kv_ref, window, *rest):
    query_hbm, key_acc, value_acc, stage, score_ref, low_ref, query_acc, blank, sem = rest[-9:]
    block_count, slot_count, head_count, width, scale = sizes
    rank = lax.axis_index("ctx")
    base = rank * block_count
    reach = window.shape[0] // BLK
    columns = query_acc.shape[1]

    def blank_copy(i):
        return pltpu.make_async_copy(blank, query_hbm.at[0, pl.ds(i * BLK, BLK)], sem.at[slot_count + i])

    slots = slots_of(assistant, turn_first, base, block_count, slot_count)

    def run():
        more = [live for _, live, _ in slots[1:]]

        def stage_copy(s):
            return pltpu.make_async_copy(stage.at[s], query_hbm.at[0, block_rows(slots[s][0])], sem.at[s])

        keep = lax.broadcasted_iota(jnp.int32, (BLK, BLK), 0) <= lax.broadcasted_iota(
            jnp.int32, (BLK, BLK), 1
        )
        blank[...] = jnp.zeros_like(blank)
        for i in range(block_count):
            @pl.when(assistant[0, base + i] != 1)
            def _():
                blank_copy(i).start()
        key_acc[...] = jnp.zeros_like(key_acc)
        value_acc[...] = jnp.zeros_like(value_acc)

        def body(s, block, start):
            def query_part(keys, source, rows, span):
                return nn_dot(keys.T, source[s, rows, span])

            query_acc[...] = jnp.zeros_like(query_acc)

            def remote_part(rows):
                keys = window[rows, :]
                for c in range(0, columns, CHUNK):
                    span = slice(c, c + CHUNK)
                    query_acc[:, span] += query_part(keys, score_in, rows, span)

            over_window(block_count, reach, start, True, remote_part)
            low = jnp.maximum(start, 0)
            for count in range(1, block_count + 1):
                @pl.when(block + 1 - low == count)
                def _():
                    rows = block_rows(low, count)
                    keys = kv_ref[0, rows, :]
                    local_pass(keys, kv_ref[1, rows, :], query_ref, grad_ref, s, keep, inverse_ref, delta_ref,
                               low_ref, score_ref, key_acc, value_acc, rows, scale * math.log2(math.e))
                    for c in range(0, columns, CHUNK):
                        span = slice(c, c + CHUNK)
                        total = query_acc[:, span] + query_part(keys, score_ref, rows, span)
                        for h in range(0, CHUNK, BLK):
                            place = slice((c + h) // BLK * width, ((c + h) // BLK + 1) * width)
                            stage[s, :, place] = (total[:, h:h + BLK] * scale).T.astype(BF16)

            for i in range(slot_count - 1):
                @pl.when((s == i) & more[i])
                def _():
                    stage_copy(i).start()

        over_slots(slots, body)
        key_acc[...] = key_acc[...] * scale
        for i in range(slot_count - 1):
            @pl.when(more[i])
            def _():
                stage_copy(i).wait()

        for i in range(block_count):
            @pl.when(assistant[0, base + i] != 1)
            def _():
                blank_copy(i).wait()

    before = sends_late(rank, slots)
    pl.when(before if early else jnp.logical_not(before))(run)


def add_kernel(need, key_in, value_in, outer_ref, far_hbm, rest_hbm, key_acc, value_acc, far, rest):
    pairs = list(enumerate((key_acc, value_acc)))

    def add_last(source):
        for i, acc in pairs:
            acc[acc.shape[0] - source.shape[1]:, :] += source[i].astype(F32)

    add_last(outer_ref)

    @pl.when(need[0] > 0)
    def _():
        pltpu.sync_copy(far_hbm, far)
        add_last(far)

    @pl.when(need[0] > 1)
    def _():
        pltpu.sync_copy(rest_hbm, rest)
        for i, acc in pairs:
            acc[:rest.shape[1], :] += rest[i].astype(F32)


def total_kernel(sizes, parity, assistant, turn_first, key_acc, value_acc, stage, *rest):
    query_hbm, key_hbm, value_hbm, low, sem = rest[-5:]
    block_count, slot_count, head_count, width, scale = sizes
    rank = lax.axis_index("ctx")

    @pl.when(lax.rem(rank, 2) == parity)
    def _():
        slots = slots_of(assistant, turn_first, rank * block_count, block_count, slot_count)
        ends = [
            live & jnp.logical_not(slots[s + 1][1]) if s + 1 < slot_count else live
            for s, (_, live, _) in enumerate(slots)
        ]

        def stage_copy(s):
            rows = block_rows(slots[s][0])
            return pltpu.make_async_copy(stage.at[s], query_hbm.at[0, rows], sem.at[2 + s])

        for s in range(slot_count):
            @pl.when(ends[s])
            def _():
                stage_copy(s).start()

        copies = []
        for i, (acc, out) in enumerate(((key_acc, key_hbm), (value_acc, value_hbm))):
            total = acc[...] if parity == 1 else acc[...] + rest[0][i].astype(F32)
            low[i] = total.astype(BF16)
            copies.append(pltpu.make_async_copy(low.at[i], out.at[0], sem.at[i]))
            copies[i].start()
        for copy in copies:
            copy.wait()
        for s in range(slot_count):
            @pl.when(ends[s])
            def _():
                stage_copy(s).wait()


def call(kernel, inputs, in_specs, outputs, out_specs, scratch, limit, macs, aliases={},
         traffic=2 * MIB):
    return pl.pallas_call(
        kernel,
        out_shape=outputs,
        in_specs=in_specs,
        out_specs=out_specs,
        scratch_shapes=scratch,
        input_output_aliases=aliases,
        compiler_params=pltpu.CompilerParams(vmem_limit_bytes=limit * MIB),
        cost_estimate=pl.CostEstimate(flops=2 * macs, bytes_accessed=traffic, transcendentals=0),
    )(*inputs)


ANY_SPEC = pl.BlockSpec(memory_space=pl.ANY)
SMEM_SPEC = pl.BlockSpec(memory_space=pltpu.SMEM)
VMEM_SPEC = pl.BlockSpec(memory_space=pltpu.VMEM)


def score_shapes(sizes, rows):
    block_count, slot_count, head_count, width, scale = sizes
    columns = head_count * BLK
    return (
        pltpu.VMEM((slot_count, rows, columns), F32),
        pltpu.VMEM((slot_count, rows, columns), F32),
        pltpu.VMEM((slot_count, SUB, columns), F32),
        pltpu.VMEM((slot_count, SUB, columns), F32),
    )


def skip_kernel(*refs):
    pass


def stack_kernel(key_ref, value_ref, *outs):
    *outs, sem = outs
    copies = []
    for out in outs:
        first = key_ref.shape[1] - out.shape[1]
        for i, source in enumerate((key_ref, value_ref)):
            copies.append(
                pltpu.make_async_copy(
                    source.at[0, pl.ds(first, out.shape[1])], out.at[i], sem.at[len(copies)]
                )
            )
    for copy in copies:
        copy.start()
    for copy in copies:
        copy.wait()


def skipped(*shapes):
    return tuple(call(skip_kernel, (), [], shapes, [ANY_SPEC] * len(shapes), [], 4, 1, {}, 1))


def per_device(query_rows, key_rows, value_rows, out_grad, assistant, turn_first):
    token_count = query_rows.shape[1]
    width = key_rows.shape[2]
    head_count = query_rows.shape[2] // width
    block_count = token_count // BLK
    far_rows = block_count // 2 * BLK
    reach_rows = token_count + far_rows
    slot_count = (block_count + 1) // 2
    columns = head_count * BLK
    pair = columns * BLK * width
    sizes = (block_count, slot_count, head_count, width, 1.0 / math.sqrt(width))
    stat_rows = (slot_count, SUB, columns)
    slot_rows = pltpu.VMEM((slot_count, columns, width), BF16)

    def pack(early, state):
        inputs = tuple(hbm(a) for a in (key_rows, value_rows, assistant, turn_first, query_rows, out_grad))
        last_shape = (pltpu.VMEM((2, far_rows, width), BF16),) if early else ()
        held = tuple(smem(a) if i in (1, 2, 3) else vmem(a) for i, a in enumerate(state))
        specs = [VMEM_SPEC] + [SMEM_SPEC] * 3 + [VMEM_SPEC] * 4
        return call(
            lambda *refs: pack_kernel(sizes, early, *refs),
            inputs + held,
            [ANY_SPEC] * 6 + specs[:len(held)],
            (
                pltpu.VMEM((2, token_count, width), BF16),
                pltpu.SMEM(assistant.shape, jnp.int32),
                pltpu.SMEM(turn_first.shape, jnp.int32),
                pltpu.SMEM((1,), jnp.int32),
                slot_rows,
                slot_rows,
                pltpu.VMEM(stat_rows, F32),
                pltpu.VMEM(stat_rows, F32),
            )
            + last_shape,
            specs + [VMEM_SPEC] * len(last_shape),
            [pltpu.SemaphoreType.DMA((6,)), pltpu.SemaphoreType.DMA((slot_count, 2))],
            8,
            pair,
            {6 + i: i for i in range(len(held))},
            1,
        )

    *state, last = pack(True, ())
    outer_in = pair_shift(last, "ctx", 1, 0)
    own, *marks, need, query_slots, grad_slots, sums, dots = pack(False, state)
    inner_in = pair_shift(own, "ctx", 1, 1)
    marks = tuple(smem(a) for a in marks)
    flag = smem(need)
    far_shape = jax.ShapeDtypeStruct((2, far_rows, width), BF16)
    whole_shape = jax.ShapeDtypeStruct((2, token_count, width), BF16)
    rest_shape = jax.ShapeDtypeStruct((2, token_count - far_rows, width), BF16)

    def stacked(sources, *shapes):
        return call(stack_kernel, sources, [ANY_SPEC] * 2, shapes, [ANY_SPEC] * len(shapes),
                    [pltpu.SemaphoreType.DMA((2 * len(shapes),))], 4, 1, {}, 1)

    def far_only(*sources):
        far, = stacked(sources, far_shape)
        return (shifted(far, "ctx", 2),) + skipped(whole_shape)

    def far_and_whole(*sources):
        far, whole = stacked(sources, far_shape, whole_shape)
        return shifted(far, "ctx", 2), pair_shift(whole, "ctx", 1, 0)

    far_in, whole_in = lax.switch(
        need[0], [lambda *_: skipped(far_shape, whole_shape), far_only, far_and_whole], key_rows, value_rows
    )
    def near(parity, sources, kept):
        inputs = marks + (flag, vmem(query_slots), vmem(grad_slots), hbm(far_in)) + sources
        return tuple(
            call(
                lambda *refs: near_kernel(sizes, parity, *refs),
                inputs + tuple(vmem(a) for a in kept),
                [SMEM_SPEC] * 3 + [VMEM_SPEC] * 2 + [ANY_SPEC, VMEM_SPEC]
                + [ANY_SPEC] * (len(sources) - 1) + [VMEM_SPEC] * len(kept),
                score_shapes(sizes, reach_rows) + (pltpu.VMEM((reach_rows, width), BF16),),
                [VMEM_SPEC] * 5,
                [pltpu.VMEM((reach_rows, width), BF16), pltpu.SemaphoreType.DMA((4,))],
                8,
                NEAR_HINT[parity] * pair,
                {len(inputs) + i: i for i in range(len(kept))},
                1,
            )
        )

    def remote(parity, near_rows, near_state, kept):
        inputs = marks + (flag,) + tuple(vmem(a) for a in (query_slots, grad_slots, sums, dots))
        held = tuple(vmem(a) for a in kept[:3]) + tuple(hbm(a) for a in kept[3:])
        passed = score_shapes(sizes, reach_rows) if parity == 0 else ()
        aliases = {len(inputs) + 4 + i: i for i in range(len(held))}
        aliases.update({len(inputs) + i: 5 + i for i in range(len(passed))})
        results = call(
            lambda *refs: remote_kernel(sizes, parity, *refs),
            inputs + tuple(vmem(a) for a in near_state) + held,
            [SMEM_SPEC] * 3 + [VMEM_SPEC] * (8 + len(held[:3])) + [ANY_SPEC] * len(held[3:]),
            (
                pltpu.VMEM((slot_count, reach_rows, columns), BF16),
                pltpu.VMEM(stat_rows, F32),
                pltpu.VMEM(stat_rows, F32),
                far_shape,
                rest_shape,
            )
            + passed
            + (pltpu.VMEM((2, near_rows, width), BF16),),
            [VMEM_SPEC] * 3 + [ANY_SPEC] * 2 + [VMEM_SPEC] * (1 + len(passed)),
            [
                pltpu.VMEM((slot_count * token_count, columns), BF16),
                pltpu.VMEM((reach_rows, width), F32),
                pltpu.VMEM((reach_rows, width), F32),
                pltpu.VMEM(far_shape.shape, BF16),
                pltpu.VMEM(rest_shape.shape, BF16),
            ],
            8,
            REMOTE_HINT[parity] * pair,
            aliases,
            1,
        )
        return tuple(results[:5]), tuple(results[5:-1]), results[-1]

    *near_state, window = near(0, (vmem(outer_in), hbm(whole_in)), ())
    remote_state, near_state, outer_grad = remote(0, far_rows, near_state, ())
    outer_back = pair_shift(outer_grad, "ctx", -1, 0)
    *near_state, window = near(1, (vmem(inner_in),), near_state + (window,))
    remote_state, _, inner_grad = remote(1, token_count, near_state, remote_state)
    window = (window,)
    score_grad, inverse, delta, far_grad, rest_grad = remote_state

    def finish(early, state):
        inputs = marks + tuple(
            vmem(a)
            for a in (query_slots, grad_slots, score_grad, inverse, delta, own) + window
        )
        return call(
            lambda *refs: finish_kernel(sizes, early, *refs),
            inputs + tuple(hbm(a) for a in state[:1]) + tuple(vmem(a) for a in state[1:]),
            [SMEM_SPEC] * 2 + [VMEM_SPEC] * 7 + [ANY_SPEC] * len(state[:1]) + [VMEM_SPEC] * len(state[1:]),
            (
                jax.ShapeDtypeStruct(query_rows.shape, BF16),
                pltpu.VMEM((token_count, width), F32),
                pltpu.VMEM((token_count, width), F32),
                pltpu.VMEM((slot_count, BLK, head_count * width), BF16),
            ),
            [ANY_SPEC] + [VMEM_SPEC] * 3,
            [
                pltpu.VMEM((slot_count, token_count, columns), BF16),
                pltpu.VMEM((token_count, columns), BF16),
                pltpu.VMEM((BLK, columns), F32),
                pltpu.VMEM((BLK, head_count * width), BF16),
                pltpu.SemaphoreType.DMA((slot_count + block_count,)),
            ],
            10,
            pair,
            {len(inputs) + i: i for i in range(len(state))},
            1,
        )

    state = finish(True, ())
    inner_grad, state = lax.optimization_barrier((inner_grad, state))
    inner_back = pair_shift(inner_grad, "ctx", -1, 1)
    query_grad, key_acc, value_acc, stage = finish(False, tuple(state))
    far_grad, rest_grad, query_grad = lax.optimization_barrier((far_grad, rest_grad, query_grad))
    far_back, rest_back = lax.switch(
        need[0],
        [
            lambda far, rest: skipped(far_shape, rest_shape),
            lambda far, rest: (shifted(far, "ctx", -2),) + skipped(rest_shape),
            lambda far, rest: (shifted(far, "ctx", -2), pair_shift(rest, "ctx", -1, 0)),
        ],
        far_grad,
        rest_grad,
    )
    key_acc, value_acc = call(
        add_kernel,
        (flag,) + tuple(vmem(a) for a in (key_acc, value_acc, outer_back)) + (hbm(far_back), hbm(rest_back)),
        [SMEM_SPEC] + [VMEM_SPEC] * 3 + [ANY_SPEC] * 2,
        (pltpu.VMEM((token_count, width), F32),) * 2,
        [VMEM_SPEC] * 2,
        [pltpu.VMEM(far_shape.shape, BF16), pltpu.VMEM(rest_shape.shape, BF16)],
        4,
        CROSS_HINT * pair,
        {1: 0, 2: 1},
        1,
    )
    results = (query_grad,)
    for parity, received in ((1, ()), (0, (vmem(inner_back),))):
        inputs = marks + tuple(vmem(a) for a in (key_acc, value_acc, stage)) + received
        results = call(
            lambda *refs: total_kernel(sizes, parity, *refs),
            inputs + tuple(hbm(a) for a in results),
            [SMEM_SPEC] * 2 + [VMEM_SPEC] * (len(inputs) - 2) + [ANY_SPEC] * len(results),
            tuple(jax.ShapeDtypeStruct(a.shape, BF16) for a in (query_rows, key_rows, value_rows)),
            [ANY_SPEC] * 3,
            [pltpu.VMEM((2, token_count, width), BF16), pltpu.SemaphoreType.DMA((2 + slot_count,))],
            8,
            pair,
            {len(inputs) + i: i for i in range(len(results))},
            1,
        )
    return tuple(results)


def solution(mesh):
    return jax.shard_map(
        per_device,
        mesh=mesh,
        in_specs=(
            P("dp", "ctx", "tp"),
            P("dp", "ctx", "tp"),
            P("dp", "ctx", "tp"),
            P("dp", "ctx", "tp"),
            P("dp", None),
            P("dp", None),
        ),
        out_specs=(P("dp", "ctx", "tp"), P("dp", "ctx", "tp"), P("dp", "ctx", "tp")),
        check_vma=False,
    )
```

```python
import math

import jax
import jax.numpy as jnp
from jax import lax
from jax.experimental import pallas as pl
from jax.experimental.pallas import tpu as pltpu
from jax.sharding import PartitionSpec as P

BLK = 128
SUB = 8
CHUNK = 256
F32 = jnp.float32
BF16 = jnp.bfloat16
MIB = 1 << 20
NEAR_HINT = (400, 10)
REMOTE_HINT = (14, 14)
CROSS_HINT = 60


def shifted(block, axis, distance):
    devices = range(lax.axis_size(axis))
    route = [(i - distance, i) for i in devices if i - distance in devices]
    return lax.ppermute(block, axis, route)


def pair_shift(block, axis, distance, parity):
    pairs = [(i - 1, i) for i in range(1, lax.axis_size(axis)) if i % 2 == parity]
    return lax.ppermute(block, axis, pairs if distance == 1 else [pair[::-1] for pair in pairs])


def vmem(array):
    return pltpu.with_memory_space_constraint(array, pltpu.VMEM)


def smem(array):
    return pltpu.with_memory_space_constraint(array, pltpu.SMEM)


def hbm(array):
    return pltpu.with_memory_space_constraint(array, pltpu.HBM)


def nt_dot(left, right):
    return lax.dot_general(left, right, (((1,), (1,)), ((), ())), preferred_element_type=F32)


def nn_dot(left, right):
    return lax.dot_general(left, right, (((1,), (0,)), ((), ())), preferred_element_type=F32)


def fold(tile):
    return jnp.sum(tile.reshape(tile.shape[0] // SUB, SUB, tile.shape[1]), axis=0)


def slots_of(assistant, turn_first, base, block_count, slot_count):
    found = jnp.int32(0)
    blocks = [jnp.int32(0)] * slot_count
    starts = [jnp.int32(0)] * slot_count
    for i in range(block_count):
        mark = assistant[0, base + i]
        start = turn_first[0, base + i] - base
        for s in range(slot_count):
            here = (mark == 1) & (found == s)
            blocks[s] = jnp.where(here, i, blocks[s])
            starts[s] = jnp.where(here, start, starts[s])
        found = found + jnp.where(mark == 1, 1, 0)
    return [(blocks[s], found > s, starts[s]) for s in range(slot_count)]


def score_pass(key_tile, value_tile, query_ref, grad_ref, slot, keep, weight_ref, prob_ref, at, sum_ref,
               dot_ref, scale):
    columns = query_ref.shape[1]
    for c in range(0, columns, CHUNK):
        span = slice(c, c + CHUNK)
        scores = nt_dot(key_tile, query_ref[slot, span, :])
        prob_grad = nt_dot(value_tile, grad_ref[slot, span, :])
        weights = jnp.exp2(scores * scale)
        if keep is not None:
            weights = jnp.where(jnp.concatenate([keep] * (CHUNK // BLK), axis=1), weights, 0.0)
        weight_ref[at + (span,)] = weights
        prob_ref[at + (span,)] = prob_grad
        sum_ref[slot, :, span] += fold(weights)
        dot_ref[slot, :, span] += fold(weights * prob_grad)


def grad_pass(weight_ref, prob_ref, at, query_ref, grad_ref, slot, inverse_ref, delta_ref, low_ref,
              score_ref, score_rows, key_acc, value_acc, acc_rows, low_first=0):
    columns = query_ref.shape[1]
    height = acc_rows.size
    low_rows = slice(low_first, low_first + height)
    for c in range(0, columns, CHUNK):
        span = slice(c, c + CHUNK)
        shape = (height // SUB, SUB, CHUNK)
        attention = weight_ref[at + (span,)].reshape(shape) * inverse_ref[slot, :, span][None]
        lifted = prob_ref[at + (span,)].reshape(shape) - delta_ref[slot, :, span][None]
        score_grad = (attention * lifted).reshape(height, CHUNK)
        low_ref[low_rows, span] = attention.reshape(height, CHUNK).astype(BF16)
        score_ref[slot, score_rows, span] = score_grad.astype(BF16)
    value_acc[acc_rows, :] += nn_dot(low_ref[low_rows], grad_ref[slot])
    key_acc[acc_rows, :] += nn_dot(score_ref[slot, score_rows, :], query_ref[slot])


def block_rows(index, count=1):
    return pl.ds(pl.multiple_of(index * BLK, BLK), count * BLK)


def pick(values, s):
    chosen = values[0]
    for i in range(1, len(values)):
        chosen = jnp.where(s == i, values[i], chosen)
    return chosen


def over_slots(slots, body):
    def step(s, carry):
        block, start = (pick([slot[i] for slot in slots], s) for i in (0, 2))

        @pl.when(pick([jnp.where(slot[1], 1, 0) for slot in slots], s) == 1)
        def _():
            body(s, block, start)

        return carry

    lax.fori_loop(0, len(slots), step, 0)


def packs_late(rank):
    return (lax.rem(rank, 2) == 0) & (rank * 2 >= lax.axis_size("ctx"))


def local_kernel(sizes, assistant, turn_first, query_ref, grad_ref, kv_ref, weight_ref, prob_ref, sum_ref,
                 dot_ref):
    block_count, slot_count, head_count, width, scale = sizes
    base = lax.axis_index("ctx") * block_count
    sum_ref[...] = jnp.zeros_like(sum_ref)
    dot_ref[...] = jnp.zeros_like(dot_ref)
    ahead = lax.broadcasted_iota(jnp.int32, (BLK, BLK), 1) - lax.broadcasted_iota(
        jnp.int32, (BLK, BLK), 0
    )

    def body(s, block, start):
        def step(k, carry):
            rows = block_rows(k)
            score_pass(kv_ref[0, rows, :], kv_ref[1, rows, :], query_ref, grad_ref, s,
                       ahead >= (k - block) * BLK, weight_ref, prob_ref, (s, rows), sum_ref, dot_ref,
                       scale * math.log2(math.e))
            return carry

        lax.fori_loop(jnp.maximum(start, 0), block + 1, step, 0)

    over_slots(slots_of(assistant, turn_first, base, block_count, slot_count), body)


def pack_kernel(sizes, early, key_ref, value_ref, assistant_ref, turn_ref, query_hbm, grad_hbm, *rest):
    block_count, slot_count, head_count, width, scale = sizes
    all_ref, assistant, turn_first, need_ref, query_ref, grad_ref = rest[-9:-3] if early else rest[-8:-2]
    packs = [all_ref, rest[-3]] if early else [all_ref]
    pack_sem, slot_sem = rest[-2:]
    rank = lax.axis_index("ctx")
    token_count = key_ref.shape[1]

    def run():
        marks = [
            pltpu.make_async_copy(assistant_ref, assistant, pack_sem.at[0]),
            pltpu.make_async_copy(turn_ref, turn_first, pack_sem.at[1]),
        ]
        copies = []
        for pack in packs:
            rows = pack.shape[1]
            for i, source in enumerate((key_ref, value_ref)):
                copies.append(
                    pltpu.make_async_copy(
                        source.at[0, pl.ds(token_count - rows, rows)], pack.at[i], pack_sem.at[2 + len(copies)]
                    )
                )
        for copy in marks + copies:
            copy.start()
        for copy in marks:
            copy.wait()
        slots = slots_of(assistant, turn_first, rank * block_count, block_count, slot_count)
        pairs = list(enumerate(((query_hbm, query_ref), (grad_hbm, grad_ref))))
        for s, (block, live, start) in enumerate(slots):
            @pl.when(live)
            def _():
                for i, (source, target) in pairs:
                    for h in range(head_count):
                        pltpu.make_async_copy(
                            source.at[0, block_rows(block), pl.ds(h * width, width)],
                            target.at[s, pl.ds(h * BLK, BLK)],
                            slot_sem.at[s, i],
                        ).start()

        outer = far = jnp.int32(0)
        for i in range(block_count, assistant.shape[1]):
            device = i // block_count
            behind = jnp.where(assistant[0, i] == 1, device * block_count - turn_first[0, i], 0)
            far = jnp.where(behind > block_count, 1, far)
            if device % 2 == 0:
                outer = jnp.maximum(outer, behind)
        need_ref[0] = jnp.where(outer > 1, 2, far)
        for copy in copies:
            copy.wait()
        for s, (block, live, start) in enumerate(slots):
            @pl.when(live)
            def _():
                for i, (source, target) in pairs:
                    pltpu.make_async_copy(target.at[s], target.at[s], slot_sem.at[s, i]).wait()

    pl.when(jnp.logical_not(packs_late(rank)) if early else packs_late(rank))(run)


def over_window(block_count, reach, start, whole, body):
    first = jnp.maximum(start + reach, 0)
    last = reach
    if whole:
        @pl.when(start <= -block_count)
        def _():
            body(pl.ds((reach - block_count) * BLK, block_count * BLK))

        last = jnp.where(start <= -block_count, reach - block_count, reach)

    def step(k, carry):
        body(block_rows(k))
        return carry

    lax.fori_loop(first, last, step, 0)


def all_slots(slots, wanted):
    together = wanted(slots[0][2])
    for _, live, start in slots:
        together = together & live & wanted(start)
    return together


def near_kernel(sizes, parity, assistant, turn_first, need, query_ref, grad_ref, own_ref, far_hbm, *rest):
    weight_ref, prob_ref, sum_ref, dot_ref, window, values, sem = rest[-7:]
    block_count, slot_count, head_count, width, scale = sizes
    rank = lax.axis_index("ctx")
    reach = values.shape[0] // BLK
    near = pl.ds((reach - block_count) * BLK, block_count * BLK)

    def fill(rows, source):
        window[rows, :] = source[0]
        values[rows, :] = source[1]

    def fetch(rows, source, first_sem):
        return [
            pltpu.make_async_copy(source.at[i], target.at[rows], sem.at[first_sem + i])
            for i, target in enumerate((window, values))
        ]

    def body(s, block, start):
        def scores(rows):
            score_pass(window[rows, :], values[rows, :], query_ref, grad_ref, s, None, weight_ref,
                       prob_ref, (s, rows), sum_ref, dot_ref, scale * math.log2(math.e))

        over_window(block_count, reach, start, parity == 1, scores)

    @pl.when(lax.rem(rank, 2) == parity)
    def _():
        window[reach * BLK:, :] = own_ref[0]
        if parity == 1:
            fill(near, rest[0])
        else:
            fill(block_rows(reach - 1), rest[0])

        @pl.when(need[0] > 0)
        def _():
            copies = fetch(pl.ds(0, far_hbm.shape[1]), far_hbm, 0)
            for copy in copies:
                copy.start()
            for copy in copies:
                copy.wait()

        if parity == 0:
            @pl.when(need[0] > 1)
            def _():
                copies = fetch(near, rest[1], 2)
                for copy in copies:
                    copy.start()
                for copy in copies:
                    copy.wait()

        sum_ref[...] = jnp.zeros_like(sum_ref)
        dot_ref[...] = jnp.zeros_like(dot_ref)
        slots = slots_of(assistant, turn_first, rank * block_count, block_count, slot_count)
        count = 1 if parity == 0 else block_count
        together = all_slots(slots, lambda start: start == -count)

        @pl.when(together)
        def _():
            rows = pl.ds((reach - count) * BLK, count * BLK)
            for s in range(slot_count):
                score_pass(window[rows, :], values[rows, :], query_ref, grad_ref, s, None, weight_ref,
                           prob_ref, (s, rows), sum_ref, dot_ref, scale * math.log2(math.e))

        pl.when(jnp.logical_not(together))(lambda: over_slots(slots, body))


def remote_kernel(sizes, parity, assistant, turn_first, need, query_ref, grad_ref, sum_local, dot_local,
                  weight_near, prob_near, sum_near, dot_near, *rest):
    block_count, slot_count, head_count, width, scale = sizes
    (score_ref, inverse_ref, delta_ref, far_hbm, rest_hbm, *_, near_out, low_ref, key_acc, value_acc, far_low,
     rest_low) = rest[-15 + 4 * parity:]
    rank = lax.axis_index("ctx")
    reach = weight_near.shape[1] // BLK

    def statistics(s):
        inverse = 1.0 / jnp.sum(sum_local[s] + sum_near[s], axis=0, keepdims=True)
        delta = jnp.sum(dot_local[s] + dot_near[s], axis=0, keepdims=True) * inverse
        inverse_ref[s] = jnp.broadcast_to(inverse, inverse_ref.shape[1:])
        delta_ref[s] = jnp.broadcast_to(delta, delta_ref.shape[1:])

    def gradients_of(s, rows, low_first=0):
        grad_pass(weight_near, prob_near, (s, rows), query_ref, grad_ref, s, inverse_ref, delta_ref,
                  low_ref, score_ref, rows, key_acc, value_acc, rows, low_first)

    def body(s, block, start):
        statistics(s)
        over_window(block_count, reach, start, parity == 1, lambda rows: gradients_of(s, rows))

    @pl.when(lax.rem(rank, 2) == parity)
    def _():
        key_acc[...] = jnp.zeros_like(key_acc)
        value_acc[...] = jnp.zeros_like(value_acc)
        slots = slots_of(assistant, turn_first, rank * block_count, block_count, slot_count)
        count = 1 if parity == 0 else block_count
        together = all_slots(slots, lambda start: start == -count)

        @pl.when(together)
        def _():
            rows = pl.ds((reach - count) * BLK, count * BLK)
            for s in range(slot_count):
                statistics(s)
            for s in range(slot_count):
                gradients_of(s, rows, s * count * BLK)

        pl.when(jnp.logical_not(together))(lambda: over_slots(slots, body))

        def round_to(out, first, rows):
            out[0] = (key_acc[first:first + rows, :] * scale).astype(BF16)
            out[1] = value_acc[first:first + rows, :].astype(BF16)

        total = reach * BLK
        round_to(near_out, total - near_out.shape[1], near_out.shape[1])

        @pl.when(need[0] > 0)
        def _():
            round_to(far_low, 0, far_low.shape[1])
            pltpu.sync_copy(far_low, far_hbm)

        if parity == 0:
            @pl.when(need[0] > 1)
            def _():
                round_to(rest_low, far_low.shape[1], rest_low.shape[1])
                pltpu.sync_copy(rest_low, rest_hbm)


def sends_late(rank, slots):
    behind = sum(jnp.where(live, jnp.maximum(-start, 0), 0) for _, live, start in slots)
    return (lax.rem(rank, 2) == 1) & (rank > 1) & (behind <= 2)


def finish_kernel(sizes, early, assistant, turn_first, query_ref, grad_ref, weight_ref, prob_ref, inverse_ref,
                  delta_ref, window, *rest):
    score_ref, query_hbm, key_acc, value_acc, stage, low_ref, blank, sem = rest[-8:]
    block_count, slot_count, head_count, width, scale = sizes
    rank = lax.axis_index("ctx")
    base = rank * block_count
    reach = window.shape[0] // BLK - block_count
    columns = low_ref.shape[1]

    def blank_copy(i):
        return pltpu.make_async_copy(blank, query_hbm.at[0, pl.ds(i * BLK, BLK)], sem.at[slot_count + i])

    slots = slots_of(assistant, turn_first, base, block_count, slot_count)

    def run():
        more = [live for _, live, _ in slots[1:]]

        def stage_copy(s):
            return pltpu.make_async_copy(stage.at[s], query_hbm.at[0, block_rows(slots[s][0])], sem.at[s])

        blank[...] = jnp.zeros_like(blank)
        for i in range(block_count):
            @pl.when(assistant[0, base + i] != 1)
            def _():
                blank_copy(i).start()
        key_acc[...] = jnp.zeros_like(key_acc)
        value_acc[...] = jnp.zeros_like(value_acc)

        def body(s, block, start):
            low = jnp.maximum(start, 0)
            for count in range(1, block_count + 1):
                @pl.when(block + 1 - low == count)
                def _():
                    rows = block_rows(low, count)
                    grad_pass(weight_ref, prob_ref, (s, rows), query_ref, grad_ref, s, inverse_ref, delta_ref,
                              low_ref, score_ref, block_rows(low + reach, count), key_acc, value_acc, rows)

            for count in range(1, reach + 2):
                @pl.when(block + 1 - start == count)
                def _():
                    rows = block_rows(start + reach, count)
                    keys = window[rows, :].T
                    for c in range(0, columns, CHUNK):
                        total = nn_dot(keys, score_ref[s, rows, c:c + CHUNK])
                        for h in range(0, CHUNK, BLK):
                            place = slice((c + h) // BLK * width, ((c + h) // BLK + 1) * width)
                            stage[s, :, place] = (total[:, h:h + BLK] * scale).T.astype(BF16)

            for i in range(slot_count - 1):
                @pl.when((s == i) & more[i])
                def _():
                    stage_copy(i).start()

        over_slots(slots, body)
        key_acc[...] = key_acc[...] * scale
        for i in range(slot_count - 1):
            @pl.when(more[i])
            def _():
                stage_copy(i).wait()

        for i in range(block_count):
            @pl.when(assistant[0, base + i] != 1)
            def _():
                blank_copy(i).wait()

    before = sends_late(rank, slots)
    pl.when(before if early else jnp.logical_not(before))(run)


def add_kernel(need, key_in, value_in, outer_ref, far_hbm, rest_hbm, key_acc, value_acc, far, rest):
    pairs = list(enumerate((key_acc, value_acc)))

    def add_last(source):
        for i, acc in pairs:
            acc[acc.shape[0] - source.shape[1]:, :] += source[i].astype(F32)

    add_last(outer_ref)

    @pl.when(need[0] > 0)
    def _():
        pltpu.sync_copy(far_hbm, far)
        add_last(far)

    @pl.when(need[0] > 1)
    def _():
        pltpu.sync_copy(rest_hbm, rest)
        for i, acc in pairs:
            acc[:rest.shape[1], :] += rest[i].astype(F32)


def total_kernel(sizes, parity, assistant, turn_first, key_acc, value_acc, stage, *rest):
    query_hbm, key_hbm, value_hbm, low, sem = rest[-5:]
    block_count, slot_count, head_count, width, scale = sizes
    rank = lax.axis_index("ctx")

    @pl.when(lax.rem(rank, 2) == parity)
    def _():
        slots = slots_of(assistant, turn_first, rank * block_count, block_count, slot_count)
        ends = [
            live & jnp.logical_not(slots[s + 1][1]) if s + 1 < slot_count else live
            for s, (_, live, _) in enumerate(slots)
        ]

        def stage_copy(s):
            rows = block_rows(slots[s][0])
            return pltpu.make_async_copy(stage.at[s], query_hbm.at[0, rows], sem.at[2 + s])

        for s in range(slot_count):
            @pl.when(ends[s])
            def _():
                stage_copy(s).start()

        copies = []
        for i, (acc, out) in enumerate(((key_acc, key_hbm), (value_acc, value_hbm))):
            total = acc[...] if parity == 1 else acc[...] + rest[0][i].astype(F32)
            low[i] = total.astype(BF16)
            copies.append(pltpu.make_async_copy(low.at[i], out.at[0], sem.at[i]))
            copies[i].start()
        for copy in copies:
            copy.wait()
        for s in range(slot_count):
            @pl.when(ends[s])
            def _():
                stage_copy(s).wait()


def call(kernel, inputs, in_specs, outputs, out_specs, scratch, limit, macs, aliases={},
         traffic=2 * MIB):
    return pl.pallas_call(
        kernel,
        out_shape=outputs,
        in_specs=in_specs,
        out_specs=out_specs,
        scratch_shapes=scratch,
        input_output_aliases=aliases,
        compiler_params=pltpu.CompilerParams(vmem_limit_bytes=limit * MIB),
        cost_estimate=pl.CostEstimate(flops=2 * macs, bytes_accessed=traffic, transcendentals=0),
    )(*inputs)


ANY_SPEC = pl.BlockSpec(memory_space=pl.ANY)
SMEM_SPEC = pl.BlockSpec(memory_space=pltpu.SMEM)
VMEM_SPEC = pl.BlockSpec(memory_space=pltpu.VMEM)


def score_shapes(sizes, rows):
    block_count, slot_count, head_count, width, scale = sizes
    columns = head_count * BLK
    return (
        pltpu.VMEM((slot_count, rows, columns), F32),
        pltpu.VMEM((slot_count, rows, columns), F32),
        pltpu.VMEM((slot_count, SUB, columns), F32),
        pltpu.VMEM((slot_count, SUB, columns), F32),
    )


def skip_kernel(*refs):
    pass


def stack_kernel(key_ref, value_ref, *outs):
    *outs, sem = outs
    copies = []
    for out in outs:
        first = key_ref.shape[1] - out.shape[1]
        for i, source in enumerate((key_ref, value_ref)):
            copies.append(
                pltpu.make_async_copy(
                    source.at[0, pl.ds(first, out.shape[1])], out.at[i], sem.at[len(copies)]
                )
            )
    for copy in copies:
        copy.start()
    for copy in copies:
        copy.wait()


def skipped(*shapes):
    return tuple(call(skip_kernel, (), [], shapes, [ANY_SPEC] * len(shapes), [], 4, 1, {}, 1))


def per_device(query_rows, key_rows, value_rows, out_grad, assistant, turn_first):
    token_count = query_rows.shape[1]
    width = key_rows.shape[2]
    head_count = query_rows.shape[2] // width
    block_count = token_count // BLK
    far_rows = block_count // 2 * BLK
    reach_rows = token_count + far_rows
    slot_count = (block_count + 1) // 2
    columns = head_count * BLK
    pair = columns * BLK * width
    sizes = (block_count, slot_count, head_count, width, 1.0 / math.sqrt(width))
    stat_rows = (slot_count, SUB, columns)
    slot_rows = pltpu.VMEM((slot_count, columns, width), BF16)

    def pack(early, state):
        inputs = tuple(hbm(a) for a in (key_rows, value_rows, assistant, turn_first, query_rows, out_grad))
        last_shape = (pltpu.VMEM((2, far_rows, width), BF16),) if early else ()
        held = tuple(smem(a) if i in (1, 2, 3) else vmem(a) for i, a in enumerate(state))
        specs = [VMEM_SPEC] + [SMEM_SPEC] * 3 + [VMEM_SPEC] * 2
        return call(
            lambda *refs: pack_kernel(sizes, early, *refs),
            inputs + held,
            [ANY_SPEC] * 6 + specs[:len(held)],
            (
                pltpu.VMEM((2, token_count, width), BF16),
                pltpu.SMEM(assistant.shape, jnp.int32),
                pltpu.SMEM(turn_first.shape, jnp.int32),
                pltpu.SMEM((1,), jnp.int32),
                slot_rows,
                slot_rows,
            )
            + last_shape,
            specs + [VMEM_SPEC] * len(last_shape),
            [pltpu.SemaphoreType.DMA((6,)), pltpu.SemaphoreType.DMA((slot_count, 2))],
            4,
            pair,
            {6 + i: i for i in range(len(held))},
            1,
        )

    *state, last = pack(True, ())
    outer_in = pair_shift(last, "ctx", 1, 0)
    own, *marks, need, query_slots, grad_slots = pack(False, state)
    inner_in = pair_shift(own, "ctx", 1, 1)
    marks = tuple(smem(a) for a in marks)
    flag = smem(need)
    far_shape = jax.ShapeDtypeStruct((2, far_rows, width), BF16)
    whole_shape = jax.ShapeDtypeStruct((2, token_count, width), BF16)
    rest_shape = jax.ShapeDtypeStruct((2, token_count - far_rows, width), BF16)

    def stacked(sources, *shapes):
        return call(stack_kernel, sources, [ANY_SPEC] * 2, shapes, [ANY_SPEC] * len(shapes),
                    [pltpu.SemaphoreType.DMA((2 * len(shapes),))], 4, 1, {}, 1)

    def far_only(*sources):
        far, = stacked(sources, far_shape)
        return (shifted(far, "ctx", 2),) + skipped(whole_shape)

    def far_and_whole(*sources):
        far, whole = stacked(sources, far_shape, whole_shape)
        return shifted(far, "ctx", 2), pair_shift(whole, "ctx", 1, 0)

    far_in, whole_in = lax.switch(
        need[0], [lambda *_: skipped(far_shape, whole_shape), far_only, far_and_whole], key_rows, value_rows
    )
    local_own, far_in, whole_in = lax.optimization_barrier((own, far_in, whole_in))
    weights, prob_grad, sums, dots = call(
        lambda *refs: local_kernel(sizes, *refs),
        marks + tuple(vmem(a) for a in (query_slots, grad_slots, local_own)),
        [SMEM_SPEC] * 2 + [VMEM_SPEC] * 3,
        score_shapes(sizes, token_count),
        [VMEM_SPEC] * 4,
        [],
        8,
        pair,
        {},
        1,
    )

    def near(parity, sources, kept):
        inputs = marks + (flag, vmem(query_slots), vmem(grad_slots), vmem(own), hbm(far_in)) + sources
        return tuple(
            call(
                lambda *refs: near_kernel(sizes, parity, *refs),
                inputs + tuple(vmem(a) for a in kept),
                [SMEM_SPEC] * 3 + [VMEM_SPEC] * 3 + [ANY_SPEC, VMEM_SPEC]
                + [ANY_SPEC] * (len(sources) - 1) + [VMEM_SPEC] * len(kept),
                score_shapes(sizes, reach_rows) + (pltpu.VMEM((reach_rows + token_count, width), BF16),),
                [VMEM_SPEC] * 5,
                [pltpu.VMEM((reach_rows, width), BF16), pltpu.SemaphoreType.DMA((4,))],
                8,
                NEAR_HINT[parity] * pair,
                {len(inputs) + i: i for i in range(len(kept))},
                1,
            )
        )

    def remote(parity, near_rows, near_state, kept):
        inputs = marks + (flag,) + tuple(vmem(a) for a in (query_slots, grad_slots, sums, dots))
        held = tuple(vmem(a) for a in kept[:3]) + tuple(hbm(a) for a in kept[3:])
        passed = score_shapes(sizes, reach_rows) if parity == 0 else ()
        aliases = {len(inputs) + 4 + i: i for i in range(len(held))}
        aliases.update({len(inputs) + i: 5 + i for i in range(len(passed))})
        results = call(
            lambda *refs: remote_kernel(sizes, parity, *refs),
            inputs + tuple(vmem(a) for a in near_state) + held,
            [SMEM_SPEC] * 3 + [VMEM_SPEC] * (8 + len(held[:3])) + [ANY_SPEC] * len(held[3:]),
            (
                pltpu.VMEM((slot_count, reach_rows + token_count, columns), BF16),
                pltpu.VMEM(stat_rows, F32),
                pltpu.VMEM(stat_rows, F32),
                far_shape,
                rest_shape,
            )
            + passed
            + (pltpu.VMEM((2, near_rows, width), BF16),),
            [VMEM_SPEC] * 3 + [ANY_SPEC] * 2 + [VMEM_SPEC] * (1 + len(passed)),
            [
                pltpu.VMEM((slot_count * token_count, columns), BF16),
                pltpu.VMEM((reach_rows, width), F32),
                pltpu.VMEM((reach_rows, width), F32),
                pltpu.VMEM(far_shape.shape, BF16),
                pltpu.VMEM(rest_shape.shape, BF16),
            ],
            8,
            REMOTE_HINT[parity] * pair,
            aliases,
            1,
        )
        return tuple(results[:5]), tuple(results[5:-1]), results[-1]

    *near_state, window = near(0, (vmem(outer_in), hbm(whole_in)), ())
    remote_state, near_state, outer_grad = remote(0, far_rows, near_state, ())
    outer_back = pair_shift(outer_grad, "ctx", -1, 0)
    *near_state, window = near(1, (vmem(inner_in),), near_state + (window,))
    remote_state, _, inner_grad = remote(1, token_count, near_state, remote_state)
    window = (window,)
    score_grad, inverse, delta, far_grad, rest_grad = remote_state

    def finish(early, state):
        inputs = marks + tuple(
            vmem(a) for a in (query_slots, grad_slots, weights, prob_grad, inverse, delta) + window
        )
        held = (vmem(state[0]),) + tuple(hbm(a) for a in state[1:2]) + tuple(vmem(a) for a in state[2:])
        specs = [VMEM_SPEC, ANY_SPEC] + [VMEM_SPEC] * 3
        return call(
            lambda *refs: finish_kernel(sizes, early, *refs),
            inputs + held,
            [SMEM_SPEC] * 2 + [VMEM_SPEC] * 7 + specs[:len(held)],
            (
                pltpu.VMEM(score_grad.shape, BF16),
                jax.ShapeDtypeStruct(query_rows.shape, BF16),
                pltpu.VMEM((token_count, width), F32),
                pltpu.VMEM((token_count, width), F32),
                pltpu.VMEM((slot_count, BLK, head_count * width), BF16),
            ),
            specs,
            [
                pltpu.VMEM((token_count, columns), BF16),
                pltpu.VMEM((BLK, head_count * width), BF16),
                pltpu.SemaphoreType.DMA((slot_count + block_count,)),
            ],
            10,
            pair,
            {len(inputs) + i: i for i in range(len(held))},
            1,
        )

    state = finish(True, (score_grad,))
    inner_grad, state = lax.optimization_barrier((inner_grad, state))
    inner_back = pair_shift(inner_grad, "ctx", -1, 1)
    _, query_grad, key_acc, value_acc, stage = finish(False, tuple(state))
    far_grad, rest_grad, query_grad = lax.optimization_barrier((far_grad, rest_grad, query_grad))
    far_back, rest_back = lax.switch(
        need[0],
        [
            lambda far, rest: skipped(far_shape, rest_shape),
            lambda far, rest: (shifted(far, "ctx", -2),) + skipped(rest_shape),
            lambda far, rest: (shifted(far, "ctx", -2), pair_shift(rest, "ctx", -1, 0)),
        ],
        far_grad,
        rest_grad,
    )
    key_acc, value_acc = call(
        add_kernel,
        (flag,) + tuple(vmem(a) for a in (key_acc, value_acc, outer_back)) + (hbm(far_back), hbm(rest_back)),
        [SMEM_SPEC] + [VMEM_SPEC] * 3 + [ANY_SPEC] * 2,
        (pltpu.VMEM((token_count, width), F32),) * 2,
        [VMEM_SPEC] * 2,
        [pltpu.VMEM(far_shape.shape, BF16), pltpu.VMEM(rest_shape.shape, BF16)],
        4,
        CROSS_HINT * pair,
        {1: 0, 2: 1},
        1,
    )
    results = (query_grad,)
    for parity, received in ((1, ()), (0, (vmem(inner_back),))):
        inputs = marks + tuple(vmem(a) for a in (key_acc, value_acc, stage)) + received
        results = call(
            lambda *refs: total_kernel(sizes, parity, *refs),
            inputs + tuple(hbm(a) for a in results),
            [SMEM_SPEC] * 2 + [VMEM_SPEC] * (len(inputs) - 2) + [ANY_SPEC] * len(results),
            tuple(jax.ShapeDtypeStruct(a.shape, BF16) for a in (query_rows, key_rows, value_rows)),
            [ANY_SPEC] * 3,
            [pltpu.VMEM((2, token_count, width), BF16), pltpu.SemaphoreType.DMA((2 + slot_count,))],
            8,
            pair,
            {len(inputs) + i: i for i in range(len(results))},
            1,
        )
    return tuple(results)


def solution(mesh):
    return jax.shard_map(
        per_device,
        mesh=mesh,
        in_specs=(
            P("dp", "ctx", "tp"),
            P("dp", "ctx", "tp"),
            P("dp", "ctx", "tp"),
            P("dp", "ctx", "tp"),
            P("dp", None),
            P("dp", None),
        ),
        out_specs=(P("dp", "ctx", "tp"), P("dp", "ctx", "tp"), P("dp", "ctx", "tp")),
        check_vma=False,
    )
```

```python
import math

import jax
import jax.numpy as jnp
from jax import lax
from jax.experimental import pallas as pl
from jax.experimental.pallas import tpu as pltpu
from jax.sharding import PartitionSpec as P

BLK = 128
SUB = 8
CHUNK = 256
F32 = jnp.float32
BF16 = jnp.bfloat16
MIB = 1 << 20
NEAR_HINT = (400, 10)
REMOTE_HINT = (14, 14)
CROSS_HINT = 60


def shifted(block, axis, distance):
    devices = range(lax.axis_size(axis))
    route = [(i - distance, i) for i in devices if i - distance in devices]
    return lax.ppermute(block, axis, route)


def pair_shift(block, axis, distance, parity):
    pairs = [(i - 1, i) for i in range(1, lax.axis_size(axis)) if i % 2 == parity]
    return lax.ppermute(block, axis, pairs if distance == 1 else [pair[::-1] for pair in pairs])


def vmem(array):
    return pltpu.with_memory_space_constraint(array, pltpu.VMEM)


def smem(array):
    return pltpu.with_memory_space_constraint(array, pltpu.SMEM)


def hbm(array):
    return pltpu.with_memory_space_constraint(array, pltpu.HBM)


def nt_dot(left, right):
    return lax.dot_general(left, right, (((1,), (1,)), ((), ())), preferred_element_type=F32)


def nn_dot(left, right):
    return lax.dot_general(left, right, (((1,), (0,)), ((), ())), preferred_element_type=F32)


def fold(tile):
    return jnp.sum(tile.reshape(tile.shape[0] // SUB, SUB, tile.shape[1]), axis=0)


def slots_of(assistant, turn_first, base, block_count, slot_count):
    found = jnp.int32(0)
    blocks = [jnp.int32(0)] * slot_count
    starts = [jnp.int32(0)] * slot_count
    for i in range(block_count):
        mark = assistant[0, base + i]
        start = turn_first[0, base + i] - base
        for s in range(slot_count):
            here = (mark == 1) & (found == s)
            blocks[s] = jnp.where(here, i, blocks[s])
            starts[s] = jnp.where(here, start, starts[s])
        found = found + jnp.where(mark == 1, 1, 0)
    return [(blocks[s], found > s, starts[s]) for s in range(slot_count)]


def score_pass(key_tile, value_tile, query_ref, grad_ref, slot, keep, weight_ref, prob_ref, at, sum_ref,
               dot_ref, scale):
    columns = query_ref.shape[1]
    for c in range(0, columns, CHUNK):
        span = slice(c, c + CHUNK)
        scores = nt_dot(key_tile, query_ref[slot, span, :])
        prob_grad = nt_dot(value_tile, grad_ref[slot, span, :])
        weights = jnp.exp2(scores * scale)
        if keep is not None:
            weights = jnp.where(jnp.concatenate([keep] * (CHUNK // BLK), axis=1), weights, 0.0)
        weight_ref[at + (span,)] = weights
        prob_ref[at + (span,)] = prob_grad
        sum_ref[slot, :, span] += fold(weights)
        dot_ref[slot, :, span] += fold(weights * prob_grad)


def grad_pass(weight_ref, prob_ref, at, query_ref, grad_ref, slot, inverse_ref, delta_ref, low_ref,
              score_ref, score_rows, key_acc, value_acc, acc_rows, low_first=0):
    columns = query_ref.shape[1]
    height = acc_rows.size
    low_rows = slice(low_first, low_first + height)
    for c in range(0, columns, CHUNK):
        span = slice(c, c + CHUNK)
        shape = (height // SUB, SUB, CHUNK)
        attention = weight_ref[at + (span,)].reshape(shape) * inverse_ref[slot, :, span][None]
        lifted = prob_ref[at + (span,)].reshape(shape) - delta_ref[slot, :, span][None]
        score_grad = (attention * lifted).reshape(height, CHUNK)
        low_ref[low_rows, span] = attention.reshape(height, CHUNK).astype(BF16)
        score_ref[slot, score_rows, span] = score_grad.astype(BF16)
    value_acc[acc_rows, :] += nn_dot(low_ref[low_rows], grad_ref[slot])
    key_acc[acc_rows, :] += nn_dot(score_ref[slot, score_rows, :], query_ref[slot])


def block_rows(index, count=1):
    return pl.ds(pl.multiple_of(index * BLK, BLK), count * BLK)


def pick(values, s):
    chosen = values[0]
    for i in range(1, len(values)):
        chosen = jnp.where(s == i, values[i], chosen)
    return chosen


def over_slots(slots, body):
    def step(s, carry):
        block, start = (pick([slot[i] for slot in slots], s) for i in (0, 2))

        @pl.when(pick([jnp.where(slot[1], 1, 0) for slot in slots], s) == 1)
        def _():
            body(s, block, start)

        return carry

    lax.fori_loop(0, len(slots), step, 0)


def packs_late(rank):
    return (lax.rem(rank, 2) == 0) & (rank * 2 >= lax.axis_size("ctx"))


def local_kernel(sizes, assistant, turn_first, query_ref, grad_ref, kv_ref, weight_ref, prob_ref, sum_ref,
                 dot_ref):
    block_count, slot_count, head_count, width, scale = sizes
    base = lax.axis_index("ctx") * block_count
    sum_ref[...] = jnp.zeros_like(sum_ref)
    dot_ref[...] = jnp.zeros_like(dot_ref)
    ahead = lax.broadcasted_iota(jnp.int32, (BLK, BLK), 1) - lax.broadcasted_iota(
        jnp.int32, (BLK, BLK), 0
    )

    def body(s, block, start):
        def step(k, carry):
            rows = block_rows(k)
            score_pass(kv_ref[0, rows, :], kv_ref[1, rows, :], query_ref, grad_ref, s,
                       ahead >= (k - block) * BLK, weight_ref, prob_ref, (s, rows), sum_ref, dot_ref,
                       scale * math.log2(math.e))
            return carry

        lax.fori_loop(jnp.maximum(start, 0), block + 1, step, 0)

    over_slots(slots_of(assistant, turn_first, base, block_count, slot_count), body)


def pack_kernel(sizes, early, key_ref, value_ref, assistant_ref, turn_ref, query_hbm, grad_hbm, *rest):
    block_count, slot_count, head_count, width, scale = sizes
    all_ref, assistant, turn_first, need_ref, query_ref, grad_ref = rest[-9:-3] if early else rest[-8:-2]
    packs = [all_ref, rest[-3]] if early else [all_ref]
    pack_sem, slot_sem = rest[-2:]
    rank = lax.axis_index("ctx")
    token_count = key_ref.shape[1]

    def run():
        marks = [
            pltpu.make_async_copy(assistant_ref, assistant, pack_sem.at[0]),
            pltpu.make_async_copy(turn_ref, turn_first, pack_sem.at[1]),
        ]
        copies = []
        for pack in packs:
            rows = pack.shape[1]
            for i, source in enumerate((key_ref, value_ref)):
                copies.append(
                    pltpu.make_async_copy(
                        source.at[0, pl.ds(token_count - rows, rows)], pack.at[i], pack_sem.at[2 + len(copies)]
                    )
                )
        for copy in marks + copies:
            copy.start()
        for copy in marks:
            copy.wait()
        slots = slots_of(assistant, turn_first, rank * block_count, block_count, slot_count)
        pairs = list(enumerate(((query_hbm, query_ref), (grad_hbm, grad_ref))))
        for s, (block, live, start) in enumerate(slots):
            @pl.when(live)
            def _():
                for i, (source, target) in pairs:
                    for h in range(head_count):
                        pltpu.make_async_copy(
                            source.at[0, block_rows(block), pl.ds(h * width, width)],
                            target.at[s, pl.ds(h * BLK, BLK)],
                            slot_sem.at[s, i],
                        ).start()

        outer = far = jnp.int32(0)
        for i in range(block_count, assistant.shape[1]):
            device = i // block_count
            behind = jnp.where(assistant[0, i] == 1, device * block_count - turn_first[0, i], 0)
            far = jnp.where(behind > block_count, 1, far)
            if device % 2 == 0:
                outer = jnp.maximum(outer, behind)
        need_ref[0] = jnp.where(outer > 1, 2, far)
        for copy in copies:
            copy.wait()
        for s, (block, live, start) in enumerate(slots):
            @pl.when(live)
            def _():
                for i, (source, target) in pairs:
                    pltpu.make_async_copy(target.at[s], target.at[s], slot_sem.at[s, i]).wait()

    pl.when(jnp.logical_not(packs_late(rank)) if early else packs_late(rank))(run)


def over_window(block_count, reach, start, whole, body):
    first = jnp.maximum(start + reach, 0)
    last = reach
    if whole:
        @pl.when(start <= -block_count)
        def _():
            body(pl.ds((reach - block_count) * BLK, block_count * BLK))

        last = jnp.where(start <= -block_count, reach - block_count, reach)

    def step(k, carry):
        body(block_rows(k))
        return carry

    lax.fori_loop(first, last, step, 0)


def all_slots(slots, wanted):
    together = wanted(slots[0][2])
    for _, live, start in slots:
        together = together & live & wanted(start)
    return together


def near_kernel(sizes, parity, assistant, turn_first, need, query_ref, grad_ref, far_hbm, *rest):
    weight_ref, prob_ref, sum_ref, dot_ref, window, values, sem = rest[-7:]
    block_count, slot_count, head_count, width, scale = sizes
    rank = lax.axis_index("ctx")
    reach = window.shape[0] // BLK
    near = pl.ds((reach - block_count) * BLK, block_count * BLK)

    def fill(rows, source):
        window[rows, :] = source[0]
        values[rows, :] = source[1]

    def fetch(rows, source, first_sem):
        return [
            pltpu.make_async_copy(source.at[i], target.at[rows], sem.at[first_sem + i])
            for i, target in enumerate((window, values))
        ]

    def body(s, block, start):
        def scores(rows):
            score_pass(window[rows, :], values[rows, :], query_ref, grad_ref, s, None, weight_ref,
                       prob_ref, (s, rows), sum_ref, dot_ref, scale * math.log2(math.e))

        over_window(block_count, reach, start, parity == 1, scores)

    @pl.when(lax.rem(rank, 2) == parity)
    def _():
        if parity == 1:
            fill(near, rest[0])
        else:
            fill(block_rows(reach - 1), rest[0])

        @pl.when(need[0] > 0)
        def _():
            copies = fetch(pl.ds(0, far_hbm.shape[1]), far_hbm, 0)
            for copy in copies:
                copy.start()
            for copy in copies:
                copy.wait()

        if parity == 0:
            @pl.when(need[0] > 1)
            def _():
                copies = fetch(near, rest[1], 2)
                for copy in copies:
                    copy.start()
                for copy in copies:
                    copy.wait()

        sum_ref[...] = jnp.zeros_like(sum_ref)
        dot_ref[...] = jnp.zeros_like(dot_ref)
        slots = slots_of(assistant, turn_first, rank * block_count, block_count, slot_count)
        count = 1 if parity == 0 else block_count
        together = all_slots(slots, lambda start: start == -count)

        @pl.when(together)
        def _():
            rows = pl.ds((reach - count) * BLK, count * BLK)
            for s in range(slot_count):
                score_pass(window[rows, :], values[rows, :], query_ref, grad_ref, s, None, weight_ref,
                           prob_ref, (s, rows), sum_ref, dot_ref, scale * math.log2(math.e))

        pl.when(jnp.logical_not(together))(lambda: over_slots(slots, body))


def remote_kernel(sizes, parity, assistant, turn_first, need, query_ref, grad_ref, sum_local, dot_local,
                  weight_near, prob_near, sum_near, dot_near, *rest):
    block_count, slot_count, head_count, width, scale = sizes
    (score_ref, inverse_ref, delta_ref, far_hbm, rest_hbm, *_, near_out, low_ref, key_acc, value_acc, far_low,
     rest_low) = rest[-15 + 4 * parity:]
    rank = lax.axis_index("ctx")
    reach = weight_near.shape[1] // BLK

    def statistics(s):
        inverse = 1.0 / jnp.sum(sum_local[s] + sum_near[s], axis=0, keepdims=True)
        delta = jnp.sum(dot_local[s] + dot_near[s], axis=0, keepdims=True) * inverse
        inverse_ref[s] = jnp.broadcast_to(inverse, inverse_ref.shape[1:])
        delta_ref[s] = jnp.broadcast_to(delta, delta_ref.shape[1:])

    def gradients_of(s, rows, low_first=0):
        grad_pass(weight_near, prob_near, (s, rows), query_ref, grad_ref, s, inverse_ref, delta_ref,
                  low_ref, score_ref, rows, key_acc, value_acc, rows, low_first)

    def body(s, block, start):
        statistics(s)
        over_window(block_count, reach, start, parity == 1, lambda rows: gradients_of(s, rows))

    @pl.when(lax.rem(rank, 2) == parity)
    def _():
        key_acc[...] = jnp.zeros_like(key_acc)
        value_acc[...] = jnp.zeros_like(value_acc)
        slots = slots_of(assistant, turn_first, rank * block_count, block_count, slot_count)
        count = 1 if parity == 0 else block_count
        together = all_slots(slots, lambda start: start == -count)

        @pl.when(together)
        def _():
            rows = pl.ds((reach - count) * BLK, count * BLK)
            for s in range(slot_count):
                statistics(s)
            for s in range(slot_count):
                gradients_of(s, rows, s * count * BLK)

        pl.when(jnp.logical_not(together))(lambda: over_slots(slots, body))

        def round_to(out, first, rows):
            out[0] = (key_acc[first:first + rows, :] * scale).astype(BF16)
            out[1] = value_acc[first:first + rows, :].astype(BF16)

        total = reach * BLK
        round_to(near_out, total - near_out.shape[1], near_out.shape[1])

        @pl.when(need[0] > 0)
        def _():
            round_to(far_low, 0, far_low.shape[1])
            pltpu.sync_copy(far_low, far_hbm)

        if parity == 0:
            @pl.when(need[0] > 1)
            def _():
                round_to(rest_low, far_low.shape[1], rest_low.shape[1])
                pltpu.sync_copy(rest_low, rest_hbm)


def sends_late(rank, slots):
    behind = sum(jnp.where(live, jnp.maximum(-start, 0), 0) for _, live, start in slots)
    return (lax.rem(rank, 2) == 1) & (rank > 1) & (behind <= 2)


def finish_kernel(sizes, early, assistant, turn_first, query_ref, grad_ref, weight_ref, prob_ref, score_in,
                  inverse_ref, delta_ref, kv_ref, window, *rest):
    query_hbm, key_acc, value_acc, stage, score_ref, low_ref, query_acc, blank, sem = rest[-9:]
    block_count, slot_count, head_count, width, scale = sizes
    rank = lax.axis_index("ctx")
    base = rank * block_count
    reach = window.shape[0] // BLK
    columns = query_acc.shape[1]

    def blank_copy(i):
        return pltpu.make_async_copy(blank, query_hbm.at[0, pl.ds(i * BLK, BLK)], sem.at[slot_count + i])

    slots = slots_of(assistant, turn_first, base, block_count, slot_count)

    def run():
        more = [live for _, live, _ in slots[1:]]

        def stage_copy(s):
            return pltpu.make_async_copy(stage.at[s], query_hbm.at[0, block_rows(slots[s][0])], sem.at[s])

        blank[...] = jnp.zeros_like(blank)
        for i in range(block_count):
            @pl.when(assistant[0, base + i] != 1)
            def _():
                blank_copy(i).start()
        key_acc[...] = jnp.zeros_like(key_acc)
        value_acc[...] = jnp.zeros_like(value_acc)

        def body(s, block, start):
            def query_part(keys, source, rows, span):
                return nn_dot(keys.T, source[s, rows, span])

            def remote_part(rows, first=False):
                keys = window[rows, :]
                for c in range(0, columns, CHUNK):
                    span = slice(c, c + CHUNK)
                    part = query_part(keys, score_in, rows, span)
                    query_acc[:, span] = part if first else query_acc[:, span] + part

            @pl.when(start <= -block_count)
            def _():
                remote_part(pl.ds((reach - block_count) * BLK, block_count * BLK), True)

            @pl.when(start > -block_count)
            def _():
                query_acc[...] = jnp.zeros_like(query_acc)

            def remote_step(k, carry):
                remote_part(block_rows(k))
                return carry

            lax.fori_loop(
                jnp.maximum(start + reach, 0),
                jnp.where(start <= -block_count, reach - block_count, reach),
                remote_step,
                0,
            )
            low = jnp.maximum(start, 0)
            for count in range(1, block_count + 1):
                @pl.when(block + 1 - low == count)
                def _():
                    rows = block_rows(low, count)
                    grad_pass(weight_ref, prob_ref, (s, rows), query_ref, grad_ref, s, inverse_ref, delta_ref,
                              low_ref, score_ref, rows, key_acc, value_acc, rows)
                    keys = kv_ref[0, rows, :]
                    for c in range(0, columns, CHUNK):
                        span = slice(c, c + CHUNK)
                        total = query_acc[:, span] + query_part(keys, score_ref, rows, span)
                        for h in range(0, CHUNK, BLK):
                            place = slice((c + h) // BLK * width, ((c + h) // BLK + 1) * width)
                            stage[s, :, place] = (total[:, h:h + BLK] * scale).T.astype(BF16)

            for i in range(slot_count - 1):
                @pl.when((s == i) & more[i])
                def _():
                    stage_copy(i).start()

        over_slots(slots, body)
        key_acc[...] = key_acc[...] * scale
        for i in range(slot_count - 1):
            @pl.when(more[i])
            def _():
                stage_copy(i).wait()

        for i in range(block_count):
            @pl.when(assistant[0, base + i] != 1)
            def _():
                blank_copy(i).wait()

    before = sends_late(rank, slots)
    pl.when(before if early else jnp.logical_not(before))(run)


def add_kernel(need, key_in, value_in, outer_ref, far_hbm, rest_hbm, key_acc, value_acc, far, rest):
    pairs = list(enumerate((key_acc, value_acc)))

    def add_last(source):
        for i, acc in pairs:
            acc[acc.shape[0] - source.shape[1]:, :] += source[i].astype(F32)

    add_last(outer_ref)

    @pl.when(need[0] > 0)
    def _():
        pltpu.sync_copy(far_hbm, far)
        add_last(far)

    @pl.when(need[0] > 1)
    def _():
        pltpu.sync_copy(rest_hbm, rest)
        for i, acc in pairs:
            acc[:rest.shape[1], :] += rest[i].astype(F32)


def total_kernel(sizes, parity, assistant, turn_first, key_acc, value_acc, stage, *rest):
    query_hbm, key_hbm, value_hbm, low, sem = rest[-5:]
    block_count, slot_count, head_count, width, scale = sizes
    rank = lax.axis_index("ctx")

    @pl.when(lax.rem(rank, 2) == parity)
    def _():
        slots = slots_of(assistant, turn_first, rank * block_count, block_count, slot_count)
        ends = [
            live & jnp.logical_not(slots[s + 1][1]) if s + 1 < slot_count else live
            for s, (_, live, _) in enumerate(slots)
        ]

        def stage_copy(s):
            rows = block_rows(slots[s][0])
            return pltpu.make_async_copy(stage.at[s], query_hbm.at[0, rows], sem.at[2 + s])

        for s in range(slot_count):
            @pl.when(ends[s])
            def _():
                stage_copy(s).start()

        copies = []
        for i, (acc, out) in enumerate(((key_acc, key_hbm), (value_acc, value_hbm))):
            total = acc[...] if parity == 1 else acc[...] + rest[0][i].astype(F32)
            low[i] = total.astype(BF16)
            copies.append(pltpu.make_async_copy(low.at[i], out.at[0], sem.at[i]))
            copies[i].start()
        for copy in copies:
            copy.wait()
        for s in range(slot_count):
            @pl.when(ends[s])
            def _():
                stage_copy(s).wait()


def call(kernel, inputs, in_specs, outputs, out_specs, scratch, limit, macs, aliases={},
         traffic=2 * MIB):
    return pl.pallas_call(
        kernel,
        out_shape=outputs,
        in_specs=in_specs,
        out_specs=out_specs,
        scratch_shapes=scratch,
        input_output_aliases=aliases,
        compiler_params=pltpu.CompilerParams(vmem_limit_bytes=limit * MIB),
        cost_estimate=pl.CostEstimate(flops=2 * macs, bytes_accessed=traffic, transcendentals=0),
    )(*inputs)


ANY_SPEC = pl.BlockSpec(memory_space=pl.ANY)
SMEM_SPEC = pl.BlockSpec(memory_space=pltpu.SMEM)
VMEM_SPEC = pl.BlockSpec(memory_space=pltpu.VMEM)


def score_shapes(sizes, rows):
    block_count, slot_count, head_count, width, scale = sizes
    columns = head_count * BLK
    return (
        pltpu.VMEM((slot_count, rows, columns), F32),
        pltpu.VMEM((slot_count, rows, columns), F32),
        pltpu.VMEM((slot_count, SUB, columns), F32),
        pltpu.VMEM((slot_count, SUB, columns), F32),
    )


def skip_kernel(*refs):
    pass


def stack_kernel(key_ref, value_ref, *outs):
    *outs, sem = outs
    copies = []
    for out in outs:
        first = key_ref.shape[1] - out.shape[1]
        for i, source in enumerate((key_ref, value_ref)):
            copies.append(
                pltpu.make_async_copy(
                    source.at[0, pl.ds(first, out.shape[1])], out.at[i], sem.at[len(copies)]
                )
            )
    for copy in copies:
        copy.start()
    for copy in copies:
        copy.wait()


def skipped(*shapes):
    return tuple(call(skip_kernel, (), [], shapes, [ANY_SPEC] * len(shapes), [], 4, 1, {}, 1))


def per_device(query_rows, key_rows, value_rows, out_grad, assistant, turn_first):
    token_count = query_rows.shape[1]
    width = key_rows.shape[2]
    head_count = query_rows.shape[2] // width
    block_count = token_count // BLK
    far_rows = block_count // 2 * BLK
    reach_rows = token_count + far_rows
    slot_count = (block_count + 1) // 2
    columns = head_count * BLK
    pair = columns * BLK * width
    sizes = (block_count, slot_count, head_count, width, 1.0 / math.sqrt(width))
    stat_rows = (slot_count, SUB, columns)
    slot_rows = pltpu.VMEM((slot_count, columns, width), BF16)

    def pack(early, state):
        inputs = tuple(hbm(a) for a in (key_rows, value_rows, assistant, turn_first, query_rows, out_grad))
        last_shape = (pltpu.VMEM((2, far_rows, width), BF16),) if early else ()
        held = tuple(smem(a) if i in (1, 2, 3) else vmem(a) for i, a in enumerate(state))
        specs = [VMEM_SPEC] + [SMEM_SPEC] * 3 + [VMEM_SPEC] * 2
        return call(
            lambda *refs: pack_kernel(sizes, early, *refs),
            inputs + held,
            [ANY_SPEC] * 6 + specs[:len(held)],
            (
                pltpu.VMEM((2, token_count, width), BF16),
                pltpu.SMEM(assistant.shape, jnp.int32),
                pltpu.SMEM(turn_first.shape, jnp.int32),
                pltpu.SMEM((1,), jnp.int32),
                slot_rows,
                slot_rows,
            )
            + last_shape,
            specs + [VMEM_SPEC] * len(last_shape),
            [pltpu.SemaphoreType.DMA((6,)), pltpu.SemaphoreType.DMA((slot_count, 2))],
            4,
            pair,
            {6 + i: i for i in range(len(held))},
            1,
        )

    *state, last = pack(True, ())
    outer_in = pair_shift(last, "ctx", 1, 0)
    own, *marks, need, query_slots, grad_slots = pack(False, state)
    inner_in = pair_shift(own, "ctx", 1, 1)
    marks = tuple(smem(a) for a in marks)
    flag = smem(need)
    far_shape = jax.ShapeDtypeStruct((2, far_rows, width), BF16)
    whole_shape = jax.ShapeDtypeStruct((2, token_count, width), BF16)
    rest_shape = jax.ShapeDtypeStruct((2, token_count - far_rows, width), BF16)

    def stacked(sources, *shapes):
        return call(stack_kernel, sources, [ANY_SPEC] * 2, shapes, [ANY_SPEC] * len(shapes),
                    [pltpu.SemaphoreType.DMA((2 * len(shapes),))], 4, 1, {}, 1)

    def far_only(*sources):
        far, = stacked(sources, far_shape)
        return (shifted(far, "ctx", 2),) + skipped(whole_shape)

    def far_and_whole(*sources):
        far, whole = stacked(sources, far_shape, whole_shape)
        return shifted(far, "ctx", 2), pair_shift(whole, "ctx", 1, 0)

    far_in, whole_in = lax.switch(
        need[0], [lambda *_: skipped(far_shape, whole_shape), far_only, far_and_whole], key_rows, value_rows
    )
    local_own, far_in, whole_in = lax.optimization_barrier((own, far_in, whole_in))
    weights, prob_grad, sums, dots = call(
        lambda *refs: local_kernel(sizes, *refs),
        marks + tuple(vmem(a) for a in (query_slots, grad_slots, local_own)),
        [SMEM_SPEC] * 2 + [VMEM_SPEC] * 3,
        score_shapes(sizes, token_count),
        [VMEM_SPEC] * 4,
        [],
        8,
        pair,
        {},
        1,
    )

    def near(parity, sources, kept):
        inputs = marks + (flag, vmem(query_slots), vmem(grad_slots), hbm(far_in)) + sources
        return tuple(
            call(
                lambda *refs: near_kernel(sizes, parity, *refs),
                inputs + tuple(vmem(a) for a in kept),
                [SMEM_SPEC] * 3 + [VMEM_SPEC] * 2 + [ANY_SPEC, VMEM_SPEC]
                + [ANY_SPEC] * (len(sources) - 1) + [VMEM_SPEC] * len(kept),
                score_shapes(sizes, reach_rows) + (pltpu.VMEM((reach_rows, width), BF16),),
                [VMEM_SPEC] * 5,
                [pltpu.VMEM((reach_rows, width), BF16), pltpu.SemaphoreType.DMA((4,))],
                8,
                NEAR_HINT[parity] * pair,
                {len(inputs) + i: i for i in range(len(kept))},
                1,
            )
        )

    def remote(parity, near_rows, near_state, kept):
        inputs = marks + (flag,) + tuple(vmem(a) for a in (query_slots, grad_slots, sums, dots))
        held = tuple(vmem(a) for a in kept[:3]) + tuple(hbm(a) for a in kept[3:])
        passed = score_shapes(sizes, reach_rows) if parity == 0 else ()
        aliases = {len(inputs) + 4 + i: i for i in range(len(held))}
        aliases.update({len(inputs) + i: 5 + i for i in range(len(passed))})
        results = call(
            lambda *refs: remote_kernel(sizes, parity, *refs),
            inputs + tuple(vmem(a) for a in near_state) + held,
            [SMEM_SPEC] * 3 + [VMEM_SPEC] * (8 + len(held[:3])) + [ANY_SPEC] * len(held[3:]),
            (
                pltpu.VMEM((slot_count, reach_rows, columns), BF16),
                pltpu.VMEM(stat_rows, F32),
                pltpu.VMEM(stat_rows, F32),
                far_shape,
                rest_shape,
            )
            + passed
            + (pltpu.VMEM((2, near_rows, width), BF16),),
            [VMEM_SPEC] * 3 + [ANY_SPEC] * 2 + [VMEM_SPEC] * (1 + len(passed)),
            [
                pltpu.VMEM((slot_count * token_count, columns), BF16),
                pltpu.VMEM((reach_rows, width), F32),
                pltpu.VMEM((reach_rows, width), F32),
                pltpu.VMEM(far_shape.shape, BF16),
                pltpu.VMEM(rest_shape.shape, BF16),
            ],
            8,
            REMOTE_HINT[parity] * pair,
            aliases,
            1,
        )
        return tuple(results[:5]), tuple(results[5:-1]), results[-1]

    *near_state, window = near(0, (vmem(outer_in), hbm(whole_in)), ())
    remote_state, near_state, outer_grad = remote(0, far_rows, near_state, ())
    outer_back = pair_shift(outer_grad, "ctx", -1, 0)
    *near_state, window = near(1, (vmem(inner_in),), near_state + (window,))
    remote_state, _, inner_grad = remote(1, token_count, near_state, remote_state)
    window = (window,)
    score_grad, inverse, delta, far_grad, rest_grad = remote_state

    def finish(early, state):
        inputs = marks + tuple(
            vmem(a)
            for a in (query_slots, grad_slots, weights, prob_grad, score_grad, inverse, delta, own) + window
        )
        return call(
            lambda *refs: finish_kernel(sizes, early, *refs),
            inputs + tuple(hbm(a) for a in state[:1]) + tuple(vmem(a) for a in state[1:]),
            [SMEM_SPEC] * 2 + [VMEM_SPEC] * 9 + [ANY_SPEC] * len(state[:1]) + [VMEM_SPEC] * len(state[1:]),
            (
                jax.ShapeDtypeStruct(query_rows.shape, BF16),
                pltpu.VMEM((token_count, width), F32),
                pltpu.VMEM((token_count, width), F32),
                pltpu.VMEM((slot_count, BLK, head_count * width), BF16),
            ),
            [ANY_SPEC] + [VMEM_SPEC] * 3,
            [
                pltpu.VMEM((slot_count, token_count, columns), BF16),
                pltpu.VMEM((token_count, columns), BF16),
                pltpu.VMEM((BLK, columns), F32),
                pltpu.VMEM((BLK, head_count * width), BF16),
                pltpu.SemaphoreType.DMA((slot_count + block_count,)),
            ],
            10,
            pair,
            {len(inputs) + i: i for i in range(len(state))},
            1,
        )

    state = finish(True, ())
    inner_grad, state = lax.optimization_barrier((inner_grad, state))
    inner_back = pair_shift(inner_grad, "ctx", -1, 1)
    query_grad, key_acc, value_acc, stage = finish(False, tuple(state))
    far_grad, rest_grad, query_grad = lax.optimization_barrier((far_grad, rest_grad, query_grad))
    far_back, rest_back = lax.switch(
        need[0],
        [
            lambda far, rest: skipped(far_shape, rest_shape),
            lambda far, rest: (shifted(far, "ctx", -2),) + skipped(rest_shape),
            lambda far, rest: (shifted(far, "ctx", -2), pair_shift(rest, "ctx", -1, 0)),
        ],
        far_grad,
        rest_grad,
    )
    key_acc, value_acc = call(
        add_kernel,
        (flag,) + tuple(vmem(a) for a in (key_acc, value_acc, outer_back)) + (hbm(far_back), hbm(rest_back)),
        [SMEM_SPEC] + [VMEM_SPEC] * 3 + [ANY_SPEC] * 2,
        (pltpu.VMEM((token_count, width), F32),) * 2,
        [VMEM_SPEC] * 2,
        [pltpu.VMEM(far_shape.shape, BF16), pltpu.VMEM(rest_shape.shape, BF16)],
        4,
        CROSS_HINT * pair,
        {1: 0, 2: 1},
        1,
    )
    results = (query_grad,)
    for parity, received in ((1, ()), (0, (vmem(inner_back),))):
        inputs = marks + tuple(vmem(a) for a in (key_acc, value_acc, stage)) + received
        results = call(
            lambda *refs: total_kernel(sizes, parity, *refs),
            inputs + tuple(hbm(a) for a in results),
            [SMEM_SPEC] * 2 + [VMEM_SPEC] * (len(inputs) - 2) + [ANY_SPEC] * len(results),
            tuple(jax.ShapeDtypeStruct(a.shape, BF16) for a in (query_rows, key_rows, value_rows)),
            [ANY_SPEC] * 3,
            [pltpu.VMEM((2, token_count, width), BF16), pltpu.SemaphoreType.DMA((2 + slot_count,))],
            8,
            pair,
            {len(inputs) + i: i for i in range(len(results))},
            1,
        )
    return tuple(results)


def solution(mesh):
    return jax.shard_map(
        per_device,
        mesh=mesh,
        in_specs=(
            P("dp", "ctx", "tp"),
            P("dp", "ctx", "tp"),
            P("dp", "ctx", "tp"),
            P("dp", "ctx", "tp"),
            P("dp", None),
            P("dp", None),
        ),
        out_specs=(P("dp", "ctx", "tp"), P("dp", "ctx", "tp"), P("dp", "ctx", "tp")),
        check_vma=False,
    )
```

```python
import math

import jax
import jax.numpy as jnp
from jax import lax
from jax.experimental import pallas as pl
from jax.experimental.pallas import tpu as pltpu
from jax.sharding import PartitionSpec as P

BLK = 128
SUB = 8
CHUNK = 512
F32 = jnp.float32
BF16 = jnp.bfloat16
MIB = 1 << 20
NEAR_HINT = (400, 10)
REMOTE_HINT = (14, 14)
CROSS_HINT = 60


def shifted(block, axis, distance):
    devices = range(lax.axis_size(axis))
    route = [(i - distance, i) for i in devices if i - distance in devices]
    return lax.ppermute(block, axis, route)


def pair_shift(block, axis, distance, parity):
    pairs = [(i - 1, i) for i in range(1, lax.axis_size(axis)) if i % 2 == parity]
    return lax.ppermute(block, axis, pairs if distance == 1 else [pair[::-1] for pair in pairs])


def vmem(array):
    return pltpu.with_memory_space_constraint(array, pltpu.VMEM)


def smem(array):
    return pltpu.with_memory_space_constraint(array, pltpu.SMEM)


def hbm(array):
    return pltpu.with_memory_space_constraint(array, pltpu.HBM)


def nt_dot(left, right):
    return lax.dot_general(left, right, (((1,), (1,)), ((), ())), preferred_element_type=F32)


def nn_dot(left, right):
    return lax.dot_general(left, right, (((1,), (0,)), ((), ())), preferred_element_type=F32)


def fold(tile):
    return jnp.sum(tile.reshape(tile.shape[0] // SUB, SUB, tile.shape[1]), axis=0)


def slots_of(assistant, turn_first, base, block_count, slot_count):
    found = jnp.int32(0)
    blocks = [jnp.int32(0)] * slot_count
    starts = [jnp.int32(0)] * slot_count
    for i in range(block_count):
        mark = assistant[0, base + i]
        start = turn_first[0, base + i] - base
        for s in range(slot_count):
            here = (mark == 1) & (found == s)
            blocks[s] = jnp.where(here, i, blocks[s])
            starts[s] = jnp.where(here, start, starts[s])
        found = found + jnp.where(mark == 1, 1, 0)
    return [(blocks[s], found > s, starts[s]) for s in range(slot_count)]


def score_pass(key_tile, value_tile, query_ref, grad_ref, slot, keep, weight_ref, prob_ref, at, sum_ref,
               dot_ref, scale):
    columns = query_ref.shape[1]
    for c in range(0, columns, CHUNK):
        span = slice(c, c + CHUNK)
        scores = nt_dot(key_tile, query_ref[slot, span, :])
        prob_grad = nt_dot(value_tile, grad_ref[slot, span, :])
        weights = jnp.exp2(scores * scale)
        if keep is not None:
            weights = jnp.where(jnp.concatenate([keep] * (CHUNK // BLK), axis=1), weights, 0.0)
        weight_ref[at + (span,)] = weights
        prob_ref[at + (span,)] = prob_grad
        sum_ref[slot, :, span] += fold(weights)
        dot_ref[slot, :, span] += fold(weights * prob_grad)


def grad_pass(weight_ref, prob_ref, at, query_ref, grad_ref, slot, inverse_ref, delta_ref, low_ref,
              score_ref, score_rows, key_acc, value_acc, acc_rows, low_first=0):
    columns = query_ref.shape[1]
    height = acc_rows.size
    low_rows = slice(low_first, low_first + height)
    for c in range(0, columns, CHUNK):
        span = slice(c, c + CHUNK)
        shape = (height // SUB, SUB, CHUNK)
        attention = weight_ref[at + (span,)].reshape(shape) * inverse_ref[slot, :, span][None]
        lifted = prob_ref[at + (span,)].reshape(shape) - delta_ref[slot, :, span][None]
        score_grad = (attention * lifted).reshape(height, CHUNK)
        low_ref[low_rows, span] = attention.reshape(height, CHUNK).astype(BF16)
        score_ref[slot, score_rows, span] = score_grad.astype(BF16)
    value_acc[acc_rows, :] += nn_dot(low_ref[low_rows], grad_ref[slot])
    key_acc[acc_rows, :] += nn_dot(score_ref[slot, score_rows, :], query_ref[slot])


def block_rows(index, count=1):
    return pl.ds(pl.multiple_of(index * BLK, BLK), count * BLK)


def pick(values, s):
    chosen = values[0]
    for i in range(1, len(values)):
        chosen = jnp.where(s == i, values[i], chosen)
    return chosen


def over_slots(slots, body):
    def step(s, carry):
        block, start = (pick([slot[i] for slot in slots], s) for i in (0, 2))

        @pl.when(pick([jnp.where(slot[1], 1, 0) for slot in slots], s) == 1)
        def _():
            body(s, block, start)

        return carry

    lax.fori_loop(0, len(slots), step, 0)


def packs_late(rank):
    return (lax.rem(rank, 2) == 0) & (rank * 2 >= lax.axis_size("ctx"))


def local_kernel(sizes, assistant, turn_first, query_ref, grad_ref, kv_ref, weight_ref, prob_ref, sum_ref,
                 dot_ref):
    block_count, slot_count, head_count, width, scale = sizes
    base = lax.axis_index("ctx") * block_count
    sum_ref[...] = jnp.zeros_like(sum_ref)
    dot_ref[...] = jnp.zeros_like(dot_ref)
    ahead = lax.broadcasted_iota(jnp.int32, (BLK, BLK), 1) - lax.broadcasted_iota(
        jnp.int32, (BLK, BLK), 0
    )

    def body(s, block, start):
        def step(k, carry):
            rows = block_rows(k)
            score_pass(kv_ref[0, rows, :], kv_ref[1, rows, :], query_ref, grad_ref, s,
                       ahead >= (k - block) * BLK, weight_ref, prob_ref, (s, rows), sum_ref, dot_ref,
                       scale * math.log2(math.e))
            return carry

        lax.fori_loop(jnp.maximum(start, 0), block + 1, step, 0)

    over_slots(slots_of(assistant, turn_first, base, block_count, slot_count), body)


def pack_kernel(sizes, early, key_ref, value_ref, assistant_ref, turn_ref, query_hbm, grad_hbm, *rest):
    block_count, slot_count, head_count, width, scale = sizes
    all_ref, assistant, turn_first, need_ref, query_ref, grad_ref = rest[-9:-3] if early else rest[-8:-2]
    packs = [all_ref, rest[-3]] if early else [all_ref]
    pack_sem, slot_sem = rest[-2:]
    rank = lax.axis_index("ctx")
    token_count = key_ref.shape[1]

    def run():
        marks = [
            pltpu.make_async_copy(assistant_ref, assistant, pack_sem.at[0]),
            pltpu.make_async_copy(turn_ref, turn_first, pack_sem.at[1]),
        ]
        copies = []
        for pack in packs:
            rows = pack.shape[1]
            for i, source in enumerate((key_ref, value_ref)):
                copies.append(
                    pltpu.make_async_copy(
                        source.at[0, pl.ds(token_count - rows, rows)], pack.at[i], pack_sem.at[2 + len(copies)]
                    )
                )
        for copy in marks + copies:
            copy.start()
        for copy in marks:
            copy.wait()
        slots = slots_of(assistant, turn_first, rank * block_count, block_count, slot_count)
        pairs = list(enumerate(((query_hbm, query_ref), (grad_hbm, grad_ref))))
        for s, (block, live, start) in enumerate(slots):
            @pl.when(live)
            def _():
                for i, (source, target) in pairs:
                    for h in range(head_count):
                        pltpu.make_async_copy(
                            source.at[0, block_rows(block), pl.ds(h * width, width)],
                            target.at[s, pl.ds(h * BLK, BLK)],
                            slot_sem.at[s, i],
                        ).start()

        outer = far = jnp.int32(0)
        for i in range(block_count, assistant.shape[1]):
            device = i // block_count
            behind = jnp.where(assistant[0, i] == 1, device * block_count - turn_first[0, i], 0)
            far = jnp.where(behind > block_count, 1, far)
            if device % 2 == 0:
                outer = jnp.maximum(outer, behind)
        need_ref[0] = jnp.where(outer > 1, 2, far)
        for copy in copies:
            copy.wait()
        for s, (block, live, start) in enumerate(slots):
            @pl.when(live)
            def _():
                for i, (source, target) in pairs:
                    pltpu.make_async_copy(target.at[s], target.at[s], slot_sem.at[s, i]).wait()

    pl.when(jnp.logical_not(packs_late(rank)) if early else packs_late(rank))(run)


def over_window(block_count, reach, start, whole, body):
    first = jnp.maximum(start + reach, 0)
    last = reach
    if whole:
        @pl.when(start <= -block_count)
        def _():
            body(pl.ds((reach - block_count) * BLK, block_count * BLK))

        last = jnp.where(start <= -block_count, reach - block_count, reach)

    def step(k, carry):
        body(block_rows(k))
        return carry

    lax.fori_loop(first, last, step, 0)


def all_slots(slots, wanted):
    together = wanted(slots[0][2])
    for _, live, start in slots:
        together = together & live & wanted(start)
    return together


def near_kernel(sizes, parity, assistant, turn_first, need, query_ref, grad_ref, far_hbm, *rest):
    weight_ref, prob_ref, sum_ref, dot_ref, window, values, sem = rest[-7:]
    block_count, slot_count, head_count, width, scale = sizes
    rank = lax.axis_index("ctx")
    reach = window.shape[0] // BLK
    near = pl.ds((reach - block_count) * BLK, block_count * BLK)

    def fill(rows, source):
        window[rows, :] = source[0]
        values[rows, :] = source[1]

    def fetch(rows, source, first_sem):
        return [
            pltpu.make_async_copy(source.at[i], target.at[rows], sem.at[first_sem + i])
            for i, target in enumerate((window, values))
        ]

    def body(s, block, start):
        def scores(rows):
            score_pass(window[rows, :], values[rows, :], query_ref, grad_ref, s, None, weight_ref,
                       prob_ref, (s, rows), sum_ref, dot_ref, scale * math.log2(math.e))

        over_window(block_count, reach, start, parity == 1, scores)

    @pl.when(lax.rem(rank, 2) == parity)
    def _():
        if parity == 1:
            fill(near, rest[0])
        else:
            fill(block_rows(reach - 1), rest[0])

        @pl.when(need[0] > 0)
        def _():
            copies = fetch(pl.ds(0, far_hbm.shape[1]), far_hbm, 0)
            for copy in copies:
                copy.start()
            for copy in copies:
                copy.wait()

        if parity == 0:
            @pl.when(need[0] > 1)
            def _():
                copies = fetch(near, rest[1], 2)
                for copy in copies:
                    copy.start()
                for copy in copies:
                    copy.wait()

        sum_ref[...] = jnp.zeros_like(sum_ref)
        dot_ref[...] = jnp.zeros_like(dot_ref)
        slots = slots_of(assistant, turn_first, rank * block_count, block_count, slot_count)
        count = 1 if parity == 0 else block_count
        together = all_slots(slots, lambda start: start == -count)

        @pl.when(together)
        def _():
            rows = pl.ds((reach - count) * BLK, count * BLK)
            for s in range(slot_count):
                score_pass(window[rows, :], values[rows, :], query_ref, grad_ref, s, None, weight_ref,
                           prob_ref, (s, rows), sum_ref, dot_ref, scale * math.log2(math.e))

        pl.when(jnp.logical_not(together))(lambda: over_slots(slots, body))


def remote_kernel(sizes, parity, assistant, turn_first, need, query_ref, grad_ref, sum_local, dot_local,
                  weight_near, prob_near, sum_near, dot_near, *rest):
    block_count, slot_count, head_count, width, scale = sizes
    (score_ref, inverse_ref, delta_ref, far_hbm, rest_hbm, *_, near_out, low_ref, key_acc, value_acc, far_low,
     rest_low) = rest[-15 + 4 * parity:]
    rank = lax.axis_index("ctx")
    reach = weight_near.shape[1] // BLK

    def statistics(s):
        inverse = 1.0 / jnp.sum(sum_local[s] + sum_near[s], axis=0, keepdims=True)
        delta = jnp.sum(dot_local[s] + dot_near[s], axis=0, keepdims=True) * inverse
        inverse_ref[s] = jnp.broadcast_to(inverse, inverse_ref.shape[1:])
        delta_ref[s] = jnp.broadcast_to(delta, delta_ref.shape[1:])

    def gradients_of(s, rows, low_first=0):
        grad_pass(weight_near, prob_near, (s, rows), query_ref, grad_ref, s, inverse_ref, delta_ref,
                  low_ref, score_ref, rows, key_acc, value_acc, rows, low_first)

    def body(s, block, start):
        statistics(s)
        over_window(block_count, reach, start, parity == 1, lambda rows: gradients_of(s, rows))

    @pl.when(lax.rem(rank, 2) == parity)
    def _():
        key_acc[...] = jnp.zeros_like(key_acc)
        value_acc[...] = jnp.zeros_like(value_acc)
        slots = slots_of(assistant, turn_first, rank * block_count, block_count, slot_count)
        count = 1 if parity == 0 else block_count
        together = all_slots(slots, lambda start: start == -count)

        @pl.when(together)
        def _():
            rows = pl.ds((reach - count) * BLK, count * BLK)
            for s in range(slot_count):
                statistics(s)
            for s in range(slot_count):
                gradients_of(s, rows, s * count * BLK)

        pl.when(jnp.logical_not(together))(lambda: over_slots(slots, body))

        def round_to(out, first, rows):
            out[0] = (key_acc[first:first + rows, :] * scale).astype(BF16)
            out[1] = value_acc[first:first + rows, :].astype(BF16)

        total = reach * BLK
        round_to(near_out, total - near_out.shape[1], near_out.shape[1])

        @pl.when(need[0] > 0)
        def _():
            round_to(far_low, 0, far_low.shape[1])
            pltpu.sync_copy(far_low, far_hbm)

        if parity == 0:
            @pl.when(need[0] > 1)
            def _():
                round_to(rest_low, far_low.shape[1], rest_low.shape[1])
                pltpu.sync_copy(rest_low, rest_hbm)


def sends_late(rank, slots):
    behind = sum(jnp.where(live, jnp.maximum(-start, 0), 0) for _, live, start in slots)
    return (lax.rem(rank, 2) == 1) & (rank > 1) & (behind <= 2)


def finish_kernel(sizes, early, assistant, turn_first, query_ref, grad_ref, weight_ref, prob_ref, score_in,
                  inverse_ref, delta_ref, kv_ref, window, *rest):
    query_hbm, key_acc, value_acc, stage, score_ref, low_ref, query_acc, blank, sem = rest[-9:]
    block_count, slot_count, head_count, width, scale = sizes
    rank = lax.axis_index("ctx")
    base = rank * block_count
    reach = window.shape[0] // BLK
    columns = query_acc.shape[1]

    def blank_copy(i):
        return pltpu.make_async_copy(blank, query_hbm.at[0, pl.ds(i * BLK, BLK)], sem.at[slot_count + i])

    slots = slots_of(assistant, turn_first, base, block_count, slot_count)

    def run():
        more = [live for _, live, _ in slots[1:]]

        def stage_copy(s):
            return pltpu.make_async_copy(stage.at[s], query_hbm.at[0, block_rows(slots[s][0])], sem.at[s])

        blank[...] = jnp.zeros_like(blank)
        for i in range(block_count):
            @pl.when(assistant[0, base + i] != 1)
            def _():
                blank_copy(i).start()
        key_acc[...] = jnp.zeros_like(key_acc)
        value_acc[...] = jnp.zeros_like(value_acc)

        def body(s, block, start):
            def query_part(keys, source, rows, span):
                return nn_dot(keys.T, source[s, rows, span])

            def remote_part(rows, first=False):
                keys = window[rows, :]
                for c in range(0, columns, CHUNK):
                    span = slice(c, c + CHUNK)
                    part = query_part(keys, score_in, rows, span)
                    query_acc[:, span] = part if first else query_acc[:, span] + part

            @pl.when(start <= -block_count)
            def _():
                remote_part(pl.ds((reach - block_count) * BLK, block_count * BLK), True)

            @pl.when(start > -block_count)
            def _():
                query_acc[...] = jnp.zeros_like(query_acc)

            def remote_step(k, carry):
                remote_part(block_rows(k))
                return carry

            lax.fori_loop(
                jnp.maximum(start + reach, 0),
                jnp.where(start <= -block_count, reach - block_count, reach),
                remote_step,
                0,
            )
            low = jnp.maximum(start, 0)
            for count in range(1, block_count + 1):
                @pl.when(block + 1 - low == count)
                def _():
                    rows = block_rows(low, count)
                    grad_pass(weight_ref, prob_ref, (s, rows), query_ref, grad_ref, s, inverse_ref, delta_ref,
                              low_ref, score_ref, rows, key_acc, value_acc, rows)
                    keys = kv_ref[0, rows, :]
                    for c in range(0, columns, CHUNK):
                        span = slice(c, c + CHUNK)
                        total = query_acc[:, span] + query_part(keys, score_ref, rows, span)
                        for h in range(0, CHUNK, BLK):
                            place = slice((c + h) // BLK * width, ((c + h) // BLK + 1) * width)
                            stage[s, :, place] = (total[:, h:h + BLK] * scale).T.astype(BF16)

            for i in range(slot_count - 1):
                @pl.when((s == i) & more[i])
                def _():
                    stage_copy(i).start()

        over_slots(slots, body)
        key_acc[...] = key_acc[...] * scale
        for i in range(slot_count - 1):
            @pl.when(more[i])
            def _():
                stage_copy(i).wait()

        for i in range(block_count):
            @pl.when(assistant[0, base + i] != 1)
            def _():
                blank_copy(i).wait()

    before = sends_late(rank, slots)
    pl.when(before if early else jnp.logical_not(before))(run)


def add_kernel(need, key_in, value_in, outer_ref, far_hbm, rest_hbm, key_acc, value_acc, far, rest):
    pairs = list(enumerate((key_acc, value_acc)))

    def add_last(source):
        for i, acc in pairs:
            acc[acc.shape[0] - source.shape[1]:, :] += source[i].astype(F32)

    add_last(outer_ref)

    @pl.when(need[0] > 0)
    def _():
        pltpu.sync_copy(far_hbm, far)
        add_last(far)

    @pl.when(need[0] > 1)
    def _():
        pltpu.sync_copy(rest_hbm, rest)
        for i, acc in pairs:
            acc[:rest.shape[1], :] += rest[i].astype(F32)


def total_kernel(sizes, parity, assistant, turn_first, key_acc, value_acc, stage, *rest):
    query_hbm, key_hbm, value_hbm, low, sem = rest[-5:]
    block_count, slot_count, head_count, width, scale = sizes
    rank = lax.axis_index("ctx")

    @pl.when(lax.rem(rank, 2) == parity)
    def _():
        slots = slots_of(assistant, turn_first, rank * block_count, block_count, slot_count)
        ends = [
            live & jnp.logical_not(slots[s + 1][1]) if s + 1 < slot_count else live
            for s, (_, live, _) in enumerate(slots)
        ]

        def stage_copy(s):
            rows = block_rows(slots[s][0])
            return pltpu.make_async_copy(stage.at[s], query_hbm.at[0, rows], sem.at[2 + s])

        for s in range(slot_count):
            @pl.when(ends[s])
            def _():
                stage_copy(s).start()

        copies = []
        for i, (acc, out) in enumerate(((key_acc, key_hbm), (value_acc, value_hbm))):
            total = acc[...] if parity == 1 else acc[...] + rest[0][i].astype(F32)
            low[i] = total.astype(BF16)
            copies.append(pltpu.make_async_copy(low.at[i], out.at[0], sem.at[i]))
            copies[i].start()
        for copy in copies:
            copy.wait()
        for s in range(slot_count):
            @pl.when(ends[s])
            def _():
                stage_copy(s).wait()


def call(kernel, inputs, in_specs, outputs, out_specs, scratch, limit, macs, aliases={},
         traffic=2 * MIB):
    return pl.pallas_call(
        kernel,
        out_shape=outputs,
        in_specs=in_specs,
        out_specs=out_specs,
        scratch_shapes=scratch,
        input_output_aliases=aliases,
        compiler_params=pltpu.CompilerParams(vmem_limit_bytes=limit * MIB),
        cost_estimate=pl.CostEstimate(flops=2 * macs, bytes_accessed=traffic, transcendentals=0),
    )(*inputs)


ANY_SPEC = pl.BlockSpec(memory_space=pl.ANY)
SMEM_SPEC = pl.BlockSpec(memory_space=pltpu.SMEM)
VMEM_SPEC = pl.BlockSpec(memory_space=pltpu.VMEM)


def score_shapes(sizes, rows):
    block_count, slot_count, head_count, width, scale = sizes
    columns = head_count * BLK
    return (
        pltpu.VMEM((slot_count, rows, columns), F32),
        pltpu.VMEM((slot_count, rows, columns), F32),
        pltpu.VMEM((slot_count, SUB, columns), F32),
        pltpu.VMEM((slot_count, SUB, columns), F32),
    )


def skip_kernel(*refs):
    pass


def stack_kernel(key_ref, value_ref, *outs):
    *outs, sem = outs
    copies = []
    for out in outs:
        first = key_ref.shape[1] - out.shape[1]
        for i, source in enumerate((key_ref, value_ref)):
            copies.append(
                pltpu.make_async_copy(
                    source.at[0, pl.ds(first, out.shape[1])], out.at[i], sem.at[len(copies)]
                )
            )
    for copy in copies:
        copy.start()
    for copy in copies:
        copy.wait()


def skipped(*shapes):
    return tuple(call(skip_kernel, (), [], shapes, [ANY_SPEC] * len(shapes), [], 4, 1, {}, 1))


def per_device(query_rows, key_rows, value_rows, out_grad, assistant, turn_first):
    token_count = query_rows.shape[1]
    width = key_rows.shape[2]
    head_count = query_rows.shape[2] // width
    block_count = token_count // BLK
    far_rows = block_count // 2 * BLK
    reach_rows = token_count + far_rows
    slot_count = (block_count + 1) // 2
    columns = head_count * BLK
    pair = columns * BLK * width
    sizes = (block_count, slot_count, head_count, width, 1.0 / math.sqrt(width))
    stat_rows = (slot_count, SUB, columns)
    slot_rows = pltpu.VMEM((slot_count, columns, width), BF16)

    def pack(early, state):
        inputs = tuple(hbm(a) for a in (key_rows, value_rows, assistant, turn_first, query_rows, out_grad))
        last_shape = (pltpu.VMEM((2, far_rows, width), BF16),) if early else ()
        held = tuple(smem(a) if i in (1, 2, 3) else vmem(a) for i, a in enumerate(state))
        specs = [VMEM_SPEC] + [SMEM_SPEC] * 3 + [VMEM_SPEC] * 2
        return call(
            lambda *refs: pack_kernel(sizes, early, *refs),
            inputs + held,
            [ANY_SPEC] * 6 + specs[:len(held)],
            (
                pltpu.VMEM((2, token_count, width), BF16),
                pltpu.SMEM(assistant.shape, jnp.int32),
                pltpu.SMEM(turn_first.shape, jnp.int32),
                pltpu.SMEM((1,), jnp.int32),
                slot_rows,
                slot_rows,
            )
            + last_shape,
            specs + [VMEM_SPEC] * len(last_shape),
            [pltpu.SemaphoreType.DMA((6,)), pltpu.SemaphoreType.DMA((slot_count, 2))],
            4,
            pair,
            {6 + i: i for i in range(len(held))},
            1,
        )

    *state, last = pack(True, ())
    outer_in = pair_shift(last, "ctx", 1, 0)
    own, *marks, need, query_slots, grad_slots = pack(False, state)
    inner_in = pair_shift(own, "ctx", 1, 1)
    marks = tuple(smem(a) for a in marks)
    flag = smem(need)
    far_shape = jax.ShapeDtypeStruct((2, far_rows, width), BF16)
    whole_shape = jax.ShapeDtypeStruct((2, token_count, width), BF16)
    rest_shape = jax.ShapeDtypeStruct((2, token_count - far_rows, width), BF16)

    def stacked(sources, *shapes):
        return call(stack_kernel, sources, [ANY_SPEC] * 2, shapes, [ANY_SPEC] * len(shapes),
                    [pltpu.SemaphoreType.DMA((2 * len(shapes),))], 4, 1, {}, 1)

    def far_only(*sources):
        far, = stacked(sources, far_shape)
        return (shifted(far, "ctx", 2),) + skipped(whole_shape)

    def far_and_whole(*sources):
        far, whole = stacked(sources, far_shape, whole_shape)
        return shifted(far, "ctx", 2), pair_shift(whole, "ctx", 1, 0)

    far_in, whole_in = lax.switch(
        need[0], [lambda *_: skipped(far_shape, whole_shape), far_only, far_and_whole], key_rows, value_rows
    )
    local_own, far_in, whole_in = lax.optimization_barrier((own, far_in, whole_in))
    weights, prob_grad, sums, dots = call(
        lambda *refs: local_kernel(sizes, *refs),
        marks + tuple(vmem(a) for a in (query_slots, grad_slots, local_own)),
        [SMEM_SPEC] * 2 + [VMEM_SPEC] * 3,
        score_shapes(sizes, token_count),
        [VMEM_SPEC] * 4,
        [],
        8,
        pair,
        {},
        1,
    )

    def near(parity, sources, kept):
        inputs = marks + (flag, vmem(query_slots), vmem(grad_slots), hbm(far_in)) + sources
        return tuple(
            call(
                lambda *refs: near_kernel(sizes, parity, *refs),
                inputs + tuple(vmem(a) for a in kept),
                [SMEM_SPEC] * 3 + [VMEM_SPEC] * 2 + [ANY_SPEC, VMEM_SPEC]
                + [ANY_SPEC] * (len(sources) - 1) + [VMEM_SPEC] * len(kept),
                score_shapes(sizes, reach_rows) + (pltpu.VMEM((reach_rows, width), BF16),),
                [VMEM_SPEC] * 5,
                [pltpu.VMEM((reach_rows, width), BF16), pltpu.SemaphoreType.DMA((4,))],
                8,
                NEAR_HINT[parity] * pair,
                {len(inputs) + i: i for i in range(len(kept))},
                1,
            )
        )

    def remote(parity, near_rows, near_state, kept):
        inputs = marks + (flag,) + tuple(vmem(a) for a in (query_slots, grad_slots, sums, dots))
        held = tuple(vmem(a) for a in kept[:3]) + tuple(hbm(a) for a in kept[3:])
        passed = score_shapes(sizes, reach_rows) if parity == 0 else ()
        aliases = {len(inputs) + 4 + i: i for i in range(len(held))}
        aliases.update({len(inputs) + i: 5 + i for i in range(len(passed))})
        results = call(
            lambda *refs: remote_kernel(sizes, parity, *refs),
            inputs + tuple(vmem(a) for a in near_state) + held,
            [SMEM_SPEC] * 3 + [VMEM_SPEC] * (8 + len(held[:3])) + [ANY_SPEC] * len(held[3:]),
            (
                pltpu.VMEM((slot_count, reach_rows, columns), BF16),
                pltpu.VMEM(stat_rows, F32),
                pltpu.VMEM(stat_rows, F32),
                far_shape,
                rest_shape,
            )
            + passed
            + (pltpu.VMEM((2, near_rows, width), BF16),),
            [VMEM_SPEC] * 3 + [ANY_SPEC] * 2 + [VMEM_SPEC] * (1 + len(passed)),
            [
                pltpu.VMEM((slot_count * token_count, columns), BF16),
                pltpu.VMEM((reach_rows, width), F32),
                pltpu.VMEM((reach_rows, width), F32),
                pltpu.VMEM(far_shape.shape, BF16),
                pltpu.VMEM(rest_shape.shape, BF16),
            ],
            8,
            REMOTE_HINT[parity] * pair,
            aliases,
            1,
        )
        return tuple(results[:5]), tuple(results[5:-1]), results[-1]

    *near_state, window = near(0, (vmem(outer_in), hbm(whole_in)), ())
    remote_state, near_state, outer_grad = remote(0, far_rows, near_state, ())
    outer_back = pair_shift(outer_grad, "ctx", -1, 0)
    *near_state, window = near(1, (vmem(inner_in),), near_state + (window,))
    remote_state, _, inner_grad = remote(1, token_count, near_state, remote_state)
    window = (window,)
    score_grad, inverse, delta, far_grad, rest_grad = remote_state

    def finish(early, state):
        inputs = marks + tuple(
            vmem(a)
            for a in (query_slots, grad_slots, weights, prob_grad, score_grad, inverse, delta, own) + window
        )
        return call(
            lambda *refs: finish_kernel(sizes, early, *refs),
            inputs + tuple(hbm(a) for a in state[:1]) + tuple(vmem(a) for a in state[1:]),
            [SMEM_SPEC] * 2 + [VMEM_SPEC] * 9 + [ANY_SPEC] * len(state[:1]) + [VMEM_SPEC] * len(state[1:]),
            (
                jax.ShapeDtypeStruct(query_rows.shape, BF16),
                pltpu.VMEM((token_count, width), F32),
                pltpu.VMEM((token_count, width), F32),
                pltpu.VMEM((slot_count, BLK, head_count * width), BF16),
            ),
            [ANY_SPEC] + [VMEM_SPEC] * 3,
            [
                pltpu.VMEM((slot_count, token_count, columns), BF16),
                pltpu.VMEM((token_count, columns), BF16),
                pltpu.VMEM((BLK, columns), F32),
                pltpu.VMEM((BLK, head_count * width), BF16),
                pltpu.SemaphoreType.DMA((slot_count + block_count,)),
            ],
            10,
            pair,
            {len(inputs) + i: i for i in range(len(state))},
            1,
        )

    state = finish(True, ())
    inner_grad, state = lax.optimization_barrier((inner_grad, state))
    inner_back = pair_shift(inner_grad, "ctx", -1, 1)
    query_grad, key_acc, value_acc, stage = finish(False, tuple(state))
    far_grad, rest_grad, query_grad = lax.optimization_barrier((far_grad, rest_grad, query_grad))
    far_back, rest_back = lax.switch(
        need[0],
        [
            lambda far, rest: skipped(far_shape, rest_shape),
            lambda far, rest: (shifted(far, "ctx", -2),) + skipped(rest_shape),
            lambda far, rest: (shifted(far, "ctx", -2), pair_shift(rest, "ctx", -1, 0)),
        ],
        far_grad,
        rest_grad,
    )
    key_acc, value_acc = call(
        add_kernel,
        (flag,) + tuple(vmem(a) for a in (key_acc, value_acc, outer_back)) + (hbm(far_back), hbm(rest_back)),
        [SMEM_SPEC] + [VMEM_SPEC] * 3 + [ANY_SPEC] * 2,
        (pltpu.VMEM((token_count, width), F32),) * 2,
        [VMEM_SPEC] * 2,
        [pltpu.VMEM(far_shape.shape, BF16), pltpu.VMEM(rest_shape.shape, BF16)],
        4,
        CROSS_HINT * pair,
        {1: 0, 2: 1},
        1,
    )
    results = (query_grad,)
    for parity, received in ((1, ()), (0, (vmem(inner_back),))):
        inputs = marks + tuple(vmem(a) for a in (key_acc, value_acc, stage)) + received
        results = call(
            lambda *refs: total_kernel(sizes, parity, *refs),
            inputs + tuple(hbm(a) for a in results),
            [SMEM_SPEC] * 2 + [VMEM_SPEC] * (len(inputs) - 2) + [ANY_SPEC] * len(results),
            tuple(jax.ShapeDtypeStruct(a.shape, BF16) for a in (query_rows, key_rows, value_rows)),
            [ANY_SPEC] * 3,
            [pltpu.VMEM((2, token_count, width), BF16), pltpu.SemaphoreType.DMA((2 + slot_count,))],
            8,
            pair,
            {len(inputs) + i: i for i in range(len(results))},
            1,
        )
    return tuple(results)


def solution(mesh):
    return jax.shard_map(
        per_device,
        mesh=mesh,
        in_specs=(
            P("dp", "ctx", "tp"),
            P("dp", "ctx", "tp"),
            P("dp", "ctx", "tp"),
            P("dp", "ctx", "tp"),
            P("dp", None),
            P("dp", None),
        ),
        out_specs=(P("dp", "ctx", "tp"), P("dp", "ctx", "tp"), P("dp", "ctx", "tp")),
        check_vma=False,
    )
```

```python
import math

import jax
import jax.numpy as jnp
from jax import lax
from jax.experimental import pallas as pl
from jax.experimental.pallas import tpu as pltpu
from jax.sharding import PartitionSpec as P

BLK = 128
SUB = 8
CHUNK = 256
F32 = jnp.float32
BF16 = jnp.bfloat16
MIB = 1 << 20
NEAR_HINT = (400, 10)
REMOTE_HINT = (14, 14)
CROSS_HINT = 60


def shifted(block, axis, distance):
    devices = range(lax.axis_size(axis))
    route = [(i - distance, i) for i in devices if i - distance in devices]
    return lax.ppermute(block, axis, route)


def pair_shift(block, axis, distance, parity):
    pairs = [(i - 1, i) for i in range(1, lax.axis_size(axis)) if i % 2 == parity]
    return lax.ppermute(block, axis, pairs if distance == 1 else [pair[::-1] for pair in pairs])


def vmem(array):
    return pltpu.with_memory_space_constraint(array, pltpu.VMEM)


def smem(array):
    return pltpu.with_memory_space_constraint(array, pltpu.SMEM)


def hbm(array):
    return pltpu.with_memory_space_constraint(array, pltpu.HBM)


def nt_dot(left, right):
    return lax.dot_general(left, right, (((1,), (1,)), ((), ())), preferred_element_type=F32)


def nn_dot(left, right):
    return lax.dot_general(left, right, (((1,), (0,)), ((), ())), preferred_element_type=F32)


def fold(tile):
    return jnp.sum(tile.reshape(tile.shape[0] // SUB, SUB, tile.shape[1]), axis=0)


def slots_of(assistant, turn_first, base, block_count, slot_count):
    found = jnp.int32(0)
    blocks = [jnp.int32(0)] * slot_count
    starts = [jnp.int32(0)] * slot_count
    for i in range(block_count):
        mark = assistant[0, base + i]
        start = turn_first[0, base + i] - base
        for s in range(slot_count):
            here = (mark == 1) & (found == s)
            blocks[s] = jnp.where(here, i, blocks[s])
            starts[s] = jnp.where(here, start, starts[s])
        found = found + jnp.where(mark == 1, 1, 0)
    return [(blocks[s], found > s, starts[s]) for s in range(slot_count)]


def score_pass(key_tile, value_tile, query_ref, grad_ref, slot, keep, weight_ref, prob_ref, at, sum_ref,
               dot_ref, scale):
    columns = query_ref.shape[1]
    for c in range(0, columns, CHUNK):
        span = slice(c, c + CHUNK)
        scores = nt_dot(key_tile, query_ref[slot, span, :])
        prob_grad = nt_dot(value_tile, grad_ref[slot, span, :])
        weights = jnp.exp2(scores * scale)
        if keep is not None:
            weights = jnp.where(jnp.concatenate([keep] * (CHUNK // BLK), axis=1), weights, 0.0)
        weight_ref[at + (span,)] = weights
        prob_ref[at + (span,)] = prob_grad
        sum_ref[slot, :, span] += fold(weights)
        dot_ref[slot, :, span] += fold(weights * prob_grad)


def grad_pass(weight_ref, prob_ref, at, query_ref, grad_ref, slot, inverse_ref, delta_ref, low_ref,
              score_ref, score_rows, key_acc, value_acc, acc_rows, low_first=0):
    columns = query_ref.shape[1]
    height = acc_rows.size
    low_rows = slice(low_first, low_first + height)
    for c in range(0, columns, CHUNK):
        span = slice(c, c + CHUNK)
        shape = (height // SUB, SUB, CHUNK)
        attention = weight_ref[at + (span,)].reshape(shape) * inverse_ref[slot, :, span][None]
        lifted = prob_ref[at + (span,)].reshape(shape) - delta_ref[slot, :, span][None]
        score_grad = (attention * lifted).reshape(height, CHUNK)
        low_ref[low_rows, span] = attention.reshape(height, CHUNK).astype(BF16)
        score_ref[slot, score_rows, span] = score_grad.astype(BF16)
    value_acc[acc_rows, :] += nn_dot(low_ref[low_rows], grad_ref[slot])
    key_acc[acc_rows, :] += nn_dot(score_ref[slot, score_rows, :], query_ref[slot])


def block_rows(index, count=1):
    return pl.ds(pl.multiple_of(index * BLK, BLK), count * BLK)


def pick(values, s):
    chosen = values[0]
    for i in range(1, len(values)):
        chosen = jnp.where(s == i, values[i], chosen)
    return chosen


def over_slots(slots, body):
    def step(s, carry):
        block, start = (pick([slot[i] for slot in slots], s) for i in (0, 2))

        @pl.when(pick([jnp.where(slot[1], 1, 0) for slot in slots], s) == 1)
        def _():
            body(s, block, start)

        return carry

    lax.fori_loop(0, len(slots), step, 0)


def packs_late(rank):
    return (lax.rem(rank, 2) == 0) & (rank * 2 >= lax.axis_size("ctx"))


def local_kernel(sizes, assistant, turn_first, query_ref, grad_ref, kv_ref, weight_ref, prob_ref, sum_ref,
                 dot_ref):
    block_count, slot_count, head_count, width, scale = sizes
    base = lax.axis_index("ctx") * block_count
    sum_ref[...] = jnp.zeros_like(sum_ref)
    dot_ref[...] = jnp.zeros_like(dot_ref)
    ahead = lax.broadcasted_iota(jnp.int32, (BLK, BLK), 1) - lax.broadcasted_iota(
        jnp.int32, (BLK, BLK), 0
    )

    def body(s, block, start):
        def step(k, carry):
            rows = block_rows(k)
            score_pass(kv_ref[0, rows, :], kv_ref[1, rows, :], query_ref, grad_ref, s,
                       ahead >= (k - block) * BLK, weight_ref, prob_ref, (s, rows), sum_ref, dot_ref,
                       scale * math.log2(math.e))
            return carry

        lax.fori_loop(jnp.maximum(start, 0), block + 1, step, 0)

    over_slots(slots_of(assistant, turn_first, base, block_count, slot_count), body)


def pack_kernel(sizes, early, key_ref, value_ref, assistant_ref, turn_ref, query_hbm, grad_hbm, *rest):
    block_count, slot_count, head_count, width, scale = sizes
    all_ref, assistant, turn_first, need_ref, query_ref, grad_ref = rest[-9:-3] if early else rest[-8:-2]
    packs = [all_ref, rest[-3]] if early else [all_ref]
    pack_sem, slot_sem = rest[-2:]
    rank = lax.axis_index("ctx")
    token_count = key_ref.shape[1]

    def run():
        marks = [
            pltpu.make_async_copy(assistant_ref, assistant, pack_sem.at[0]),
            pltpu.make_async_copy(turn_ref, turn_first, pack_sem.at[1]),
        ]
        copies = []
        for pack in packs:
            rows = pack.shape[1]
            for i, source in enumerate((key_ref, value_ref)):
                copies.append(
                    pltpu.make_async_copy(
                        source.at[0, pl.ds(token_count - rows, rows)], pack.at[i], pack_sem.at[2 + len(copies)]
                    )
                )
        for copy in marks + copies:
            copy.start()
        for copy in marks:
            copy.wait()
        slots = slots_of(assistant, turn_first, rank * block_count, block_count, slot_count)
        pairs = list(enumerate(((query_hbm, query_ref), (grad_hbm, grad_ref))))
        for s, (block, live, start) in enumerate(slots):
            @pl.when(live)
            def _():
                for i, (source, target) in pairs:
                    for h in range(head_count):
                        pltpu.make_async_copy(
                            source.at[0, block_rows(block), pl.ds(h * width, width)],
                            target.at[s, pl.ds(h * BLK, BLK)],
                            slot_sem.at[s, i],
                        ).start()

        outer = far = jnp.int32(0)
        for i in range(block_count, assistant.shape[1]):
            device = i // block_count
            behind = jnp.where(assistant[0, i] == 1, device * block_count - turn_first[0, i], 0)
            far = jnp.where(behind > block_count, 1, far)
            if device % 2 == 0:
                outer = jnp.maximum(outer, behind)
        need_ref[0] = jnp.where(outer > 1, 2, far)
        for copy in copies:
            copy.wait()
        for s, (block, live, start) in enumerate(slots):
            @pl.when(live)
            def _():
                for i, (source, target) in pairs:
                    pltpu.make_async_copy(target.at[s], target.at[s], slot_sem.at[s, i]).wait()

    pl.when(jnp.logical_not(packs_late(rank)) if early else packs_late(rank))(run)


def over_window(block_count, reach, start, whole, body):
    first = jnp.maximum(start + reach, 0)
    last = reach
    if whole:
        @pl.when(start <= -block_count)
        def _():
            body(pl.ds((reach - block_count) * BLK, block_count * BLK))

        last = jnp.where(start <= -block_count, reach - block_count, reach)

    def step(k, carry):
        body(block_rows(k))
        return carry

    lax.fori_loop(first, last, step, 0)


def all_slots(slots, wanted):
    together = wanted(slots[0][2])
    for _, live, start in slots:
        together = together & live & wanted(start)
    return together


def near_kernel(sizes, parity, assistant, turn_first, need, query_ref, grad_ref, far_hbm, *rest):
    weight_ref, prob_ref, sum_ref, dot_ref, window, values, sem = rest[-7:]
    block_count, slot_count, head_count, width, scale = sizes
    rank = lax.axis_index("ctx")
    reach = window.shape[0] // BLK
    near = pl.ds((reach - block_count) * BLK, block_count * BLK)

    def fill(rows, source):
        window[rows, :] = source[0]
        values[rows, :] = source[1]

    def fetch(rows, source, first_sem):
        return [
            pltpu.make_async_copy(source.at[i], target.at[rows], sem.at[first_sem + i])
            for i, target in enumerate((window, values))
        ]

    def body(s, block, start):
        def scores(rows):
            score_pass(window[rows, :], values[rows, :], query_ref, grad_ref, s, None, weight_ref,
                       prob_ref, (s, rows), sum_ref, dot_ref, scale * math.log2(math.e))

        over_window(block_count, reach, start, parity == 1, scores)

    @pl.when(lax.rem(rank, 2) == parity)
    def _():
        if parity == 1:
            fill(near, rest[0])
        else:
            fill(block_rows(reach - 1), rest[0])

        @pl.when(need[0] > 0)
        def _():
            copies = fetch(pl.ds(0, far_hbm.shape[1]), far_hbm, 0)
            for copy in copies:
                copy.start()
            for copy in copies:
                copy.wait()

        if parity == 0:
            @pl.when(need[0] > 1)
            def _():
                copies = fetch(near, rest[1], 2)
                for copy in copies:
                    copy.start()
                for copy in copies:
                    copy.wait()

        sum_ref[...] = jnp.zeros_like(sum_ref)
        dot_ref[...] = jnp.zeros_like(dot_ref)
        slots = slots_of(assistant, turn_first, rank * block_count, block_count, slot_count)
        count = 1 if parity == 0 else block_count
        together = all_slots(slots, lambda start: start == -count)

        @pl.when(together)
        def _():
            rows = pl.ds((reach - count) * BLK, count * BLK)
            for s in range(slot_count):
                score_pass(window[rows, :], values[rows, :], query_ref, grad_ref, s, None, weight_ref,
                           prob_ref, (s, rows), sum_ref, dot_ref, scale * math.log2(math.e))

        pl.when(jnp.logical_not(together))(lambda: over_slots(slots, body))


def remote_kernel(sizes, parity, assistant, turn_first, need, query_ref, grad_ref, sum_local, dot_local,
                  weight_near, prob_near, sum_near, dot_near, *rest):
    block_count, slot_count, head_count, width, scale = sizes
    (score_ref, inverse_ref, delta_ref, far_hbm, rest_hbm, *_, near_out, low_ref, key_acc, value_acc, far_low,
     rest_low) = rest[-15 + 4 * parity:]
    rank = lax.axis_index("ctx")
    reach = weight_near.shape[1] // BLK

    def statistics(s):
        inverse = 1.0 / jnp.sum(sum_local[s] + sum_near[s], axis=0, keepdims=True)
        delta = jnp.sum(dot_local[s] + dot_near[s], axis=0, keepdims=True) * inverse
        inverse_ref[s] = jnp.broadcast_to(inverse, inverse_ref.shape[1:])
        delta_ref[s] = jnp.broadcast_to(delta, delta_ref.shape[1:])

    def gradients_of(s, rows, low_first=0):
        grad_pass(weight_near, prob_near, (s, rows), query_ref, grad_ref, s, inverse_ref, delta_ref,
                  low_ref, score_ref, rows, key_acc, value_acc, rows, low_first)

    def body(s, block, start):
        statistics(s)
        over_window(block_count, reach, start, parity == 1, lambda rows: gradients_of(s, rows))

    @pl.when(lax.rem(rank, 2) == parity)
    def _():
        key_acc[...] = jnp.zeros_like(key_acc)
        value_acc[...] = jnp.zeros_like(value_acc)
        slots = slots_of(assistant, turn_first, rank * block_count, block_count, slot_count)
        count = 1 if parity == 0 else block_count
        together = all_slots(slots, lambda start: start == -count)

        @pl.when(together)
        def _():
            rows = pl.ds((reach - count) * BLK, count * BLK)
            for s in range(slot_count):
                statistics(s)
            for s in range(slot_count):
                gradients_of(s, rows, s * count * BLK)

        pl.when(jnp.logical_not(together))(lambda: over_slots(slots, body))

        def round_to(out, first, rows):
            out[0] = (key_acc[first:first + rows, :] * scale).astype(BF16)
            out[1] = value_acc[first:first + rows, :].astype(BF16)

        total = reach * BLK
        round_to(near_out, total - near_out.shape[1], near_out.shape[1])

        @pl.when(need[0] > 0)
        def _():
            round_to(far_low, 0, far_low.shape[1])
            pltpu.sync_copy(far_low, far_hbm)

        if parity == 0:
            @pl.when(need[0] > 1)
            def _():
                round_to(rest_low, far_low.shape[1], rest_low.shape[1])
                pltpu.sync_copy(rest_low, rest_hbm)


def sends_late(rank, slots):
    behind = sum(jnp.where(live, jnp.maximum(-start, 0), 0) for _, live, start in slots)
    return (lax.rem(rank, 2) == 1) & (rank > 1) & (behind <= 3)


def finish_kernel(sizes, early, assistant, turn_first, query_ref, grad_ref, weight_ref, prob_ref, score_in,
                  inverse_ref, delta_ref, kv_ref, window, *rest):
    query_hbm, key_acc, value_acc, stage, score_ref, low_ref, query_acc, blank, sem = rest[-9:]
    block_count, slot_count, head_count, width, scale = sizes
    rank = lax.axis_index("ctx")
    base = rank * block_count
    reach = window.shape[0] // BLK
    columns = query_acc.shape[1]

    def blank_copy(i):
        return pltpu.make_async_copy(blank, query_hbm.at[0, pl.ds(i * BLK, BLK)], sem.at[slot_count + i])

    slots = slots_of(assistant, turn_first, base, block_count, slot_count)

    def run():
        more = [live for _, live, _ in slots[1:]]

        def stage_copy(s):
            return pltpu.make_async_copy(stage.at[s], query_hbm.at[0, block_rows(slots[s][0])], sem.at[s])

        blank[...] = jnp.zeros_like(blank)
        for i in range(block_count):
            @pl.when(assistant[0, base + i] != 1)
            def _():
                blank_copy(i).start()
        key_acc[...] = jnp.zeros_like(key_acc)
        value_acc[...] = jnp.zeros_like(value_acc)

        def body(s, block, start):
            def query_part(keys, source, rows, span):
                return nn_dot(keys.T, source[s, rows, span])

            def remote_part(rows, first=False):
                keys = window[rows, :]
                for c in range(0, columns, CHUNK):
                    span = slice(c, c + CHUNK)
                    part = query_part(keys, score_in, rows, span)
                    query_acc[:, span] = part if first else query_acc[:, span] + part

            @pl.when(start <= -block_count)
            def _():
                remote_part(pl.ds((reach - block_count) * BLK, block_count * BLK), True)

            @pl.when(start > -block_count)
            def _():
                query_acc[...] = jnp.zeros_like(query_acc)

            def remote_step(k, carry):
                remote_part(block_rows(k))
                return carry

            lax.fori_loop(
                jnp.maximum(start + reach, 0),
                jnp.where(start <= -block_count, reach - block_count, reach),
                remote_step,
                0,
            )
            low = jnp.maximum(start, 0)
            for count in range(1, block_count + 1):
                @pl.when(block + 1 - low == count)
                def _():
                    rows = block_rows(low, count)
                    grad_pass(weight_ref, prob_ref, (s, rows), query_ref, grad_ref, s, inverse_ref, delta_ref,
                              low_ref, score_ref, rows, key_acc, value_acc, rows)
                    keys = kv_ref[0, rows, :]
                    for c in range(0, columns, CHUNK):
                        span = slice(c, c + CHUNK)
                        total = query_acc[:, span] + query_part(keys, score_ref, rows, span)
                        for h in range(0, CHUNK, BLK):
                            place = slice((c + h) // BLK * width, ((c + h) // BLK + 1) * width)
                            stage[s, :, place] = (total[:, h:h + BLK] * scale).T.astype(BF16)

            for i in range(slot_count - 1):
                @pl.when((s == i) & more[i])
                def _():
                    stage_copy(i).start()

        over_slots(slots, body)
        key_acc[...] = key_acc[...] * scale
        for i in range(slot_count - 1):
            @pl.when(more[i])
            def _():
                stage_copy(i).wait()

        for i in range(block_count):
            @pl.when(assistant[0, base + i] != 1)
            def _():
                blank_copy(i).wait()

    before = sends_late(rank, slots)
    pl.when(before if early else jnp.logical_not(before))(run)


def add_kernel(need, key_in, value_in, outer_ref, far_hbm, rest_hbm, key_acc, value_acc, far, rest):
    pairs = list(enumerate((key_acc, value_acc)))

    def add_last(source):
        for i, acc in pairs:
            acc[acc.shape[0] - source.shape[1]:, :] += source[i].astype(F32)

    add_last(outer_ref)

    @pl.when(need[0] > 0)
    def _():
        pltpu.sync_copy(far_hbm, far)
        add_last(far)

    @pl.when(need[0] > 1)
    def _():
        pltpu.sync_copy(rest_hbm, rest)
        for i, acc in pairs:
            acc[:rest.shape[1], :] += rest[i].astype(F32)


def total_kernel(sizes, parity, assistant, turn_first, key_acc, value_acc, stage, *rest):
    query_hbm, key_hbm, value_hbm, low, sem = rest[-5:]
    block_count, slot_count, head_count, width, scale = sizes
    rank = lax.axis_index("ctx")

    @pl.when(lax.rem(rank, 2) == parity)
    def _():
        slots = slots_of(assistant, turn_first, rank * block_count, block_count, slot_count)
        ends = [
            live & jnp.logical_not(slots[s + 1][1]) if s + 1 < slot_count else live
            for s, (_, live, _) in enumerate(slots)
        ]

        def stage_copy(s):
            rows = block_rows(slots[s][0])
            return pltpu.make_async_copy(stage.at[s], query_hbm.at[0, rows], sem.at[2 + s])

        for s in range(slot_count):
            @pl.when(ends[s])
            def _():
                stage_copy(s).start()

        copies = []
        for i, (acc, out) in enumerate(((key_acc, key_hbm), (value_acc, value_hbm))):
            total = acc[...] if parity == 1 else acc[...] + rest[0][i].astype(F32)
            low[i] = total.astype(BF16)
            copies.append(pltpu.make_async_copy(low.at[i], out.at[0], sem.at[i]))
            copies[i].start()
        for copy in copies:
            copy.wait()
        for s in range(slot_count):
            @pl.when(ends[s])
            def _():
                stage_copy(s).wait()


def call(kernel, inputs, in_specs, outputs, out_specs, scratch, limit, macs, aliases={},
         traffic=2 * MIB):
    return pl.pallas_call(
        kernel,
        out_shape=outputs,
        in_specs=in_specs,
        out_specs=out_specs,
        scratch_shapes=scratch,
        input_output_aliases=aliases,
        compiler_params=pltpu.CompilerParams(vmem_limit_bytes=limit * MIB),
        cost_estimate=pl.CostEstimate(flops=2 * macs, bytes_accessed=traffic, transcendentals=0),
    )(*inputs)


ANY_SPEC = pl.BlockSpec(memory_space=pl.ANY)
SMEM_SPEC = pl.BlockSpec(memory_space=pltpu.SMEM)
VMEM_SPEC = pl.BlockSpec(memory_space=pltpu.VMEM)


def score_shapes(sizes, rows):
    block_count, slot_count, head_count, width, scale = sizes
    columns = head_count * BLK
    return (
        pltpu.VMEM((slot_count, rows, columns), F32),
        pltpu.VMEM((slot_count, rows, columns), F32),
        pltpu.VMEM((slot_count, SUB, columns), F32),
        pltpu.VMEM((slot_count, SUB, columns), F32),
    )


def skip_kernel(*refs):
    pass


def stack_kernel(key_ref, value_ref, *outs):
    *outs, sem = outs
    copies = []
    for out in outs:
        first = key_ref.shape[1] - out.shape[1]
        for i, source in enumerate((key_ref, value_ref)):
            copies.append(
                pltpu.make_async_copy(
                    source.at[0, pl.ds(first, out.shape[1])], out.at[i], sem.at[len(copies)]
                )
            )
    for copy in copies:
        copy.start()
    for copy in copies:
        copy.wait()


def skipped(*shapes):
    return tuple(call(skip_kernel, (), [], shapes, [ANY_SPEC] * len(shapes), [], 4, 1, {}, 1))


def per_device(query_rows, key_rows, value_rows, out_grad, assistant, turn_first):
    token_count = query_rows.shape[1]
    width = key_rows.shape[2]
    head_count = query_rows.shape[2] // width
    block_count = token_count // BLK
    far_rows = block_count // 2 * BLK
    reach_rows = token_count + far_rows
    slot_count = (block_count + 1) // 2
    columns = head_count * BLK
    pair = columns * BLK * width
    sizes = (block_count, slot_count, head_count, width, 1.0 / math.sqrt(width))
    stat_rows = (slot_count, SUB, columns)
    slot_rows = pltpu.VMEM((slot_count, columns, width), BF16)

    def pack(early, state):
        inputs = tuple(hbm(a) for a in (key_rows, value_rows, assistant, turn_first, query_rows, out_grad))
        last_shape = (pltpu.VMEM((2, far_rows, width), BF16),) if early else ()
        held = tuple(smem(a) if i in (1, 2, 3) else vmem(a) for i, a in enumerate(state))
        specs = [VMEM_SPEC] + [SMEM_SPEC] * 3 + [VMEM_SPEC] * 2
        return call(
            lambda *refs: pack_kernel(sizes, early, *refs),
            inputs + held,
            [ANY_SPEC] * 6 + specs[:len(held)],
            (
                pltpu.VMEM((2, token_count, width), BF16),
                pltpu.SMEM(assistant.shape, jnp.int32),
                pltpu.SMEM(turn_first.shape, jnp.int32),
                pltpu.SMEM((1,), jnp.int32),
                slot_rows,
                slot_rows,
            )
            + last_shape,
            specs + [VMEM_SPEC] * len(last_shape),
            [pltpu.SemaphoreType.DMA((6,)), pltpu.SemaphoreType.DMA((slot_count, 2))],
            4,
            pair,
            {6 + i: i for i in range(len(held))},
            1,
        )

    *state, last = pack(True, ())
    outer_in = pair_shift(last, "ctx", 1, 0)
    own, *marks, need, query_slots, grad_slots = pack(False, state)
    inner_in = pair_shift(own, "ctx", 1, 1)
    marks = tuple(smem(a) for a in marks)
    flag = smem(need)
    far_shape = jax.ShapeDtypeStruct((2, far_rows, width), BF16)
    whole_shape = jax.ShapeDtypeStruct((2, token_count, width), BF16)
    rest_shape = jax.ShapeDtypeStruct((2, token_count - far_rows, width), BF16)

    def stacked(sources, *shapes):
        return call(stack_kernel, sources, [ANY_SPEC] * 2, shapes, [ANY_SPEC] * len(shapes),
                    [pltpu.SemaphoreType.DMA((2 * len(shapes),))], 4, 1, {}, 1)

    def far_only(*sources):
        far, = stacked(sources, far_shape)
        return (shifted(far, "ctx", 2),) + skipped(whole_shape)

    def far_and_whole(*sources):
        far, whole = stacked(sources, far_shape, whole_shape)
        return shifted(far, "ctx", 2), pair_shift(whole, "ctx", 1, 0)

    far_in, whole_in = lax.switch(
        need[0], [lambda *_: skipped(far_shape, whole_shape), far_only, far_and_whole], key_rows, value_rows
    )
    local_own, far_in, whole_in = lax.optimization_barrier((own, far_in, whole_in))
    weights, prob_grad, sums, dots = call(
        lambda *refs: local_kernel(sizes, *refs),
        marks + tuple(vmem(a) for a in (query_slots, grad_slots, local_own)),
        [SMEM_SPEC] * 2 + [VMEM_SPEC] * 3,
        score_shapes(sizes, token_count),
        [VMEM_SPEC] * 4,
        [],
        8,
        pair,
        {},
        1,
    )

    def near(parity, sources, kept):
        inputs = marks + (flag, vmem(query_slots), vmem(grad_slots), hbm(far_in)) + sources
        return tuple(
            call(
                lambda *refs: near_kernel(sizes, parity, *refs),
                inputs + tuple(vmem(a) for a in kept),
                [SMEM_SPEC] * 3 + [VMEM_SPEC] * 2 + [ANY_SPEC, VMEM_SPEC]
                + [ANY_SPEC] * (len(sources) - 1) + [VMEM_SPEC] * len(kept),
                score_shapes(sizes, reach_rows) + (pltpu.VMEM((reach_rows, width), BF16),),
                [VMEM_SPEC] * 5,
                [pltpu.VMEM((reach_rows, width), BF16), pltpu.SemaphoreType.DMA((4,))],
                8,
                NEAR_HINT[parity] * pair,
                {len(inputs) + i: i for i in range(len(kept))},
                1,
            )
        )

    def remote(parity, near_rows, near_state, kept):
        inputs = marks + (flag,) + tuple(vmem(a) for a in (query_slots, grad_slots, sums, dots))
        held = tuple(vmem(a) for a in kept[:3]) + tuple(hbm(a) for a in kept[3:])
        passed = score_shapes(sizes, reach_rows) if parity == 0 else ()
        aliases = {len(inputs) + 4 + i: i for i in range(len(held))}
        aliases.update({len(inputs) + i: 5 + i for i in range(len(passed))})
        results = call(
            lambda *refs: remote_kernel(sizes, parity, *refs),
            inputs + tuple(vmem(a) for a in near_state) + held,
            [SMEM_SPEC] * 3 + [VMEM_SPEC] * (8 + len(held[:3])) + [ANY_SPEC] * len(held[3:]),
            (
                pltpu.VMEM((slot_count, reach_rows, columns), BF16),
                pltpu.VMEM(stat_rows, F32),
                pltpu.VMEM(stat_rows, F32),
                far_shape,
                rest_shape,
            )
            + passed
            + (pltpu.VMEM((2, near_rows, width), BF16),),
            [VMEM_SPEC] * 3 + [ANY_SPEC] * 2 + [VMEM_SPEC] * (1 + len(passed)),
            [
                pltpu.VMEM((slot_count * token_count, columns), BF16),
                pltpu.VMEM((reach_rows, width), F32),
                pltpu.VMEM((reach_rows, width), F32),
                pltpu.VMEM(far_shape.shape, BF16),
                pltpu.VMEM(rest_shape.shape, BF16),
            ],
            8,
            REMOTE_HINT[parity] * pair,
            aliases,
            1,
        )
        return tuple(results[:5]), tuple(results[5:-1]), results[-1]

    *near_state, window = near(0, (vmem(outer_in), hbm(whole_in)), ())
    remote_state, near_state, outer_grad = remote(0, far_rows, near_state, ())
    outer_back = pair_shift(outer_grad, "ctx", -1, 0)
    *near_state, window = near(1, (vmem(inner_in),), near_state + (window,))
    remote_state, _, inner_grad = remote(1, token_count, near_state, remote_state)
    window = (window,)
    score_grad, inverse, delta, far_grad, rest_grad = remote_state

    def finish(early, state):
        inputs = marks + tuple(
            vmem(a)
            for a in (query_slots, grad_slots, weights, prob_grad, score_grad, inverse, delta, own) + window
        )
        return call(
            lambda *refs: finish_kernel(sizes, early, *refs),
            inputs + tuple(hbm(a) for a in state[:1]) + tuple(vmem(a) for a in state[1:]),
            [SMEM_SPEC] * 2 + [VMEM_SPEC] * 9 + [ANY_SPEC] * len(state[:1]) + [VMEM_SPEC] * len(state[1:]),
            (
                jax.ShapeDtypeStruct(query_rows.shape, BF16),
                pltpu.VMEM((token_count, width), F32),
                pltpu.VMEM((token_count, width), F32),
                pltpu.VMEM((slot_count, BLK, head_count * width), BF16),
            ),
            [ANY_SPEC] + [VMEM_SPEC] * 3,
            [
                pltpu.VMEM((slot_count, token_count, columns), BF16),
                pltpu.VMEM((token_count, columns), BF16),
                pltpu.VMEM((BLK, columns), F32),
                pltpu.VMEM((BLK, head_count * width), BF16),
                pltpu.SemaphoreType.DMA((slot_count + block_count,)),
            ],
            10,
            pair,
            {len(inputs) + i: i for i in range(len(state))},
            1,
        )

    state = finish(True, ())
    inner_grad, state = lax.optimization_barrier((inner_grad, state))
    inner_back = pair_shift(inner_grad, "ctx", -1, 1)
    query_grad, key_acc, value_acc, stage = finish(False, tuple(state))
    far_grad, rest_grad, query_grad = lax.optimization_barrier((far_grad, rest_grad, query_grad))
    far_back, rest_back = lax.switch(
        need[0],
        [
            lambda far, rest: skipped(far_shape, rest_shape),
            lambda far, rest: (shifted(far, "ctx", -2),) + skipped(rest_shape),
            lambda far, rest: (shifted(far, "ctx", -2), pair_shift(rest, "ctx", -1, 0)),
        ],
        far_grad,
        rest_grad,
    )
    key_acc, value_acc = call(
        add_kernel,
        (flag,) + tuple(vmem(a) for a in (key_acc, value_acc, outer_back)) + (hbm(far_back), hbm(rest_back)),
        [SMEM_SPEC] + [VMEM_SPEC] * 3 + [ANY_SPEC] * 2,
        (pltpu.VMEM((token_count, width), F32),) * 2,
        [VMEM_SPEC] * 2,
        [pltpu.VMEM(far_shape.shape, BF16), pltpu.VMEM(rest_shape.shape, BF16)],
        4,
        CROSS_HINT * pair,
        {1: 0, 2: 1},
        1,
    )
    results = (query_grad,)
    for parity, received in ((1, ()), (0, (vmem(inner_back),))):
        inputs = marks + tuple(vmem(a) for a in (key_acc, value_acc, stage)) + received
        results = call(
            lambda *refs: total_kernel(sizes, parity, *refs),
            inputs + tuple(hbm(a) for a in results),
            [SMEM_SPEC] * 2 + [VMEM_SPEC] * (len(inputs) - 2) + [ANY_SPEC] * len(results),
            tuple(jax.ShapeDtypeStruct(a.shape, BF16) for a in (query_rows, key_rows, value_rows)),
            [ANY_SPEC] * 3,
            [pltpu.VMEM((2, token_count, width), BF16), pltpu.SemaphoreType.DMA((2 + slot_count,))],
            8,
            pair,
            {len(inputs) + i: i for i in range(len(results))},
            1,
        )
    return tuple(results)


def solution(mesh):
    return jax.shard_map(
        per_device,
        mesh=mesh,
        in_specs=(
            P("dp", "ctx", "tp"),
            P("dp", "ctx", "tp"),
            P("dp", "ctx", "tp"),
            P("dp", "ctx", "tp"),
            P("dp", None),
            P("dp", None),
        ),
        out_specs=(P("dp", "ctx", "tp"), P("dp", "ctx", "tp"), P("dp", "ctx", "tp")),
        check_vma=False,
    )
```

```python
import math

import jax
import jax.numpy as jnp
from jax import lax
from jax.experimental import pallas as pl
from jax.experimental.pallas import tpu as pltpu
from jax.sharding import PartitionSpec as P

BLK = 128
SUB = 8
CHUNK = 256
F32 = jnp.float32
BF16 = jnp.bfloat16
MIB = 1 << 20
NEAR_HINT = (400, 10)
REMOTE_HINT = (14, 14)
CROSS_HINT = 60


def shifted(block, axis, distance):
    devices = range(lax.axis_size(axis))
    route = [(i - distance, i) for i in devices if i - distance in devices]
    return lax.ppermute(block, axis, route)


def pair_shift(block, axis, distance, parity):
    pairs = [(i - 1, i) for i in range(1, lax.axis_size(axis)) if i % 2 == parity]
    return lax.ppermute(block, axis, pairs if distance == 1 else [pair[::-1] for pair in pairs])


def vmem(array):
    return pltpu.with_memory_space_constraint(array, pltpu.VMEM)


def smem(array):
    return pltpu.with_memory_space_constraint(array, pltpu.SMEM)


def hbm(array):
    return pltpu.with_memory_space_constraint(array, pltpu.HBM)


def nt_dot(left, right):
    return lax.dot_general(left, right, (((1,), (1,)), ((), ())), preferred_element_type=F32)


def nn_dot(left, right):
    return lax.dot_general(left, right, (((1,), (0,)), ((), ())), preferred_element_type=F32)


def fold(tile):
    return jnp.sum(tile.reshape(tile.shape[0] // SUB, SUB, tile.shape[1]), axis=0)


def slots_of(assistant, turn_first, base, block_count, slot_count):
    found = jnp.int32(0)
    blocks = [jnp.int32(0)] * slot_count
    starts = [jnp.int32(0)] * slot_count
    for i in range(block_count):
        mark = assistant[0, base + i]
        start = turn_first[0, base + i] - base
        for s in range(slot_count):
            here = (mark == 1) & (found == s)
            blocks[s] = jnp.where(here, i, blocks[s])
            starts[s] = jnp.where(here, start, starts[s])
        found = found + jnp.where(mark == 1, 1, 0)
    return [(blocks[s], found > s, starts[s]) for s in range(slot_count)]


def score_pass(key_tile, value_tile, query_ref, grad_ref, slot, keep, weight_ref, prob_ref, at, sum_ref,
               dot_ref, scale):
    columns = query_ref.shape[1]
    for c in range(0, columns, CHUNK):
        span = slice(c, c + CHUNK)
        scores = nt_dot(key_tile, query_ref[slot, span, :])
        prob_grad = nt_dot(value_tile, grad_ref[slot, span, :])
        weights = jnp.exp2(scores * scale)
        if keep is not None:
            weights = jnp.where(jnp.concatenate([keep] * (CHUNK // BLK), axis=1), weights, 0.0)
        weight_ref[at + (span,)] = weights
        prob_ref[at + (span,)] = prob_grad
        sum_ref[slot, :, span] += fold(weights)
        dot_ref[slot, :, span] += fold(weights * prob_grad)


def grad_pass(weight_ref, prob_ref, at, query_ref, grad_ref, slot, inverse_ref, delta_ref, low_ref,
              score_ref, score_rows, key_acc, value_acc, acc_rows, low_first=0):
    columns = query_ref.shape[1]
    height = acc_rows.size
    low_rows = slice(low_first, low_first + height)
    for c in range(0, columns, CHUNK):
        span = slice(c, c + CHUNK)
        shape = (height // SUB, SUB, CHUNK)
        attention = weight_ref[at + (span,)].reshape(shape) * inverse_ref[slot, :, span][None]
        lifted = prob_ref[at + (span,)].reshape(shape) - delta_ref[slot, :, span][None]
        score_grad = (attention * lifted).reshape(height, CHUNK)
        low_ref[low_rows, span] = attention.reshape(height, CHUNK).astype(BF16)
        score_ref[slot, score_rows, span] = score_grad.astype(BF16)
    value_acc[acc_rows, :] += nn_dot(low_ref[low_rows], grad_ref[slot])
    key_acc[acc_rows, :] += nn_dot(score_ref[slot, score_rows, :], query_ref[slot])


def block_rows(index, count=1):
    return pl.ds(pl.multiple_of(index * BLK, BLK), count * BLK)


def pick(values, s):
    chosen = values[0]
    for i in range(1, len(values)):
        chosen = jnp.where(s == i, values[i], chosen)
    return chosen


def over_slots(slots, body):
    def step(s, carry):
        block, start = (pick([slot[i] for slot in slots], s) for i in (0, 2))

        @pl.when(pick([jnp.where(slot[1], 1, 0) for slot in slots], s) == 1)
        def _():
            body(s, block, start)

        return carry

    lax.fori_loop(0, len(slots), step, 0)


def packs_late(rank):
    return (lax.rem(rank, 2) == 0) & (rank * 2 >= lax.axis_size("ctx"))


def local_kernel(sizes, assistant, turn_first, query_ref, grad_ref, kv_ref, weight_ref, prob_ref, sum_ref,
                 dot_ref):
    block_count, slot_count, head_count, width, scale = sizes
    base = lax.axis_index("ctx") * block_count
    sum_ref[...] = jnp.zeros_like(sum_ref)
    dot_ref[...] = jnp.zeros_like(dot_ref)
    ahead = lax.broadcasted_iota(jnp.int32, (BLK, BLK), 1) - lax.broadcasted_iota(
        jnp.int32, (BLK, BLK), 0
    )

    slots = slots_of(assistant, turn_first, base, block_count, slot_count)
    together = all_slots(slots, lambda start: True)

    def scores(s, rows, keep):
        score_pass(kv_ref[0, rows, :], kv_ref[1, rows, :], query_ref, grad_ref, s, keep, weight_ref, prob_ref,
                   (s, rows), sum_ref, dot_ref, scale * math.log2(math.e))

    @pl.when(together)
    def _():
        for s, (block, live, start) in enumerate(slots):
            scores(s, block_rows(block), ahead >= 0)

    def body(s, block, start):
        def step(k, carry):
            scores(s, block_rows(k), ahead >= (k - block) * BLK)
            return carry

        lax.fori_loop(jnp.maximum(start, 0), jnp.where(together, block, block + 1), step, 0)

    over_slots(slots, body)


def pack_kernel(sizes, early, key_ref, value_ref, assistant_ref, turn_ref, query_hbm, grad_hbm, *rest):
    block_count, slot_count, head_count, width, scale = sizes
    all_ref, assistant, turn_first, need_ref, query_ref, grad_ref = rest[-9:-3] if early else rest[-8:-2]
    packs = [all_ref, rest[-3]] if early else [all_ref]
    pack_sem, slot_sem = rest[-2:]
    rank = lax.axis_index("ctx")
    token_count = key_ref.shape[1]

    def run():
        marks = [
            pltpu.make_async_copy(assistant_ref, assistant, pack_sem.at[0]),
            pltpu.make_async_copy(turn_ref, turn_first, pack_sem.at[1]),
        ]
        copies = []
        for pack in packs:
            rows = pack.shape[1]
            for i, source in enumerate((key_ref, value_ref)):
                copies.append(
                    pltpu.make_async_copy(
                        source.at[0, pl.ds(token_count - rows, rows)], pack.at[i], pack_sem.at[2 + len(copies)]
                    )
                )
        for copy in marks + copies:
            copy.start()
        for copy in marks:
            copy.wait()
        slots = slots_of(assistant, turn_first, rank * block_count, block_count, slot_count)
        pairs = list(enumerate(((query_hbm, query_ref), (grad_hbm, grad_ref))))
        for s, (block, live, start) in enumerate(slots):
            @pl.when(live)
            def _():
                for i, (source, target) in pairs:
                    for h in range(head_count):
                        pltpu.make_async_copy(
                            source.at[0, block_rows(block), pl.ds(h * width, width)],
                            target.at[s, pl.ds(h * BLK, BLK)],
                            slot_sem.at[s, i],
                        ).start()

        outer = far = jnp.int32(0)
        for i in range(block_count, assistant.shape[1]):
            device = i // block_count
            behind = jnp.where(assistant[0, i] == 1, device * block_count - turn_first[0, i], 0)
            far = jnp.where(behind > block_count, 1, far)
            if device % 2 == 0:
                outer = jnp.maximum(outer, behind)
        need_ref[0] = jnp.where(outer > 1, 2, far)
        for copy in copies:
            copy.wait()
        for s, (block, live, start) in enumerate(slots):
            @pl.when(live)
            def _():
                for i, (source, target) in pairs:
                    pltpu.make_async_copy(target.at[s], target.at[s], slot_sem.at[s, i]).wait()

    pl.when(jnp.logical_not(packs_late(rank)) if early else packs_late(rank))(run)


def over_window(block_count, reach, start, whole, body):
    first = jnp.maximum(start + reach, 0)
    last = reach
    if whole:
        @pl.when(start <= -block_count)
        def _():
            body(pl.ds((reach - block_count) * BLK, block_count * BLK))

        last = jnp.where(start <= -block_count, reach - block_count, reach)

    def step(k, carry):
        body(block_rows(k))
        return carry

    lax.fori_loop(first, last, step, 0)


def all_slots(slots, wanted):
    together = wanted(slots[0][2])
    for _, live, start in slots:
        together = together & live & wanted(start)
    return together


def near_kernel(sizes, parity, assistant, turn_first, need, query_ref, grad_ref, far_hbm, *rest):
    weight_ref, prob_ref, sum_ref, dot_ref, window, values, sem = rest[-7:]
    block_count, slot_count, head_count, width, scale = sizes
    rank = lax.axis_index("ctx")
    reach = window.shape[0] // BLK
    near = pl.ds((reach - block_count) * BLK, block_count * BLK)

    def fill(rows, source):
        window[rows, :] = source[0]
        values[rows, :] = source[1]

    def fetch(rows, source, first_sem):
        return [
            pltpu.make_async_copy(source.at[i], target.at[rows], sem.at[first_sem + i])
            for i, target in enumerate((window, values))
        ]

    def body(s, block, start):
        def scores(rows):
            score_pass(window[rows, :], values[rows, :], query_ref, grad_ref, s, None, weight_ref,
                       prob_ref, (s, rows), sum_ref, dot_ref, scale * math.log2(math.e))

        over_window(block_count, reach, start, parity == 1, scores)

    @pl.when(lax.rem(rank, 2) == parity)
    def _():
        if parity == 1:
            fill(near, rest[0])
        else:
            fill(block_rows(reach - 1), rest[0])

        @pl.when(need[0] > 0)
        def _():
            copies = fetch(pl.ds(0, far_hbm.shape[1]), far_hbm, 0)
            for copy in copies:
                copy.start()
            for copy in copies:
                copy.wait()

        if parity == 0:
            @pl.when(need[0] > 1)
            def _():
                copies = fetch(near, rest[1], 2)
                for copy in copies:
                    copy.start()
                for copy in copies:
                    copy.wait()

        sum_ref[...] = jnp.zeros_like(sum_ref)
        dot_ref[...] = jnp.zeros_like(dot_ref)
        slots = slots_of(assistant, turn_first, rank * block_count, block_count, slot_count)
        count = 1 if parity == 0 else block_count
        together = all_slots(slots, lambda start: start == -count)

        @pl.when(together)
        def _():
            rows = pl.ds((reach - count) * BLK, count * BLK)
            for s in range(slot_count):
                score_pass(window[rows, :], values[rows, :], query_ref, grad_ref, s, None, weight_ref,
                           prob_ref, (s, rows), sum_ref, dot_ref, scale * math.log2(math.e))

        pl.when(jnp.logical_not(together))(lambda: over_slots(slots, body))


def remote_kernel(sizes, parity, assistant, turn_first, need, query_ref, grad_ref, sum_local, dot_local,
                  weight_near, prob_near, sum_near, dot_near, *rest):
    block_count, slot_count, head_count, width, scale = sizes
    (score_ref, inverse_ref, delta_ref, far_hbm, rest_hbm, *_, near_out, low_ref, key_acc, value_acc, far_low,
     rest_low) = rest[-15 + 4 * parity:]
    rank = lax.axis_index("ctx")
    reach = weight_near.shape[1] // BLK

    def statistics(s):
        inverse = 1.0 / jnp.sum(sum_local[s] + sum_near[s], axis=0, keepdims=True)
        delta = jnp.sum(dot_local[s] + dot_near[s], axis=0, keepdims=True) * inverse
        inverse_ref[s] = jnp.broadcast_to(inverse, inverse_ref.shape[1:])
        delta_ref[s] = jnp.broadcast_to(delta, delta_ref.shape[1:])

    def gradients_of(s, rows, low_first=0):
        grad_pass(weight_near, prob_near, (s, rows), query_ref, grad_ref, s, inverse_ref, delta_ref,
                  low_ref, score_ref, rows, key_acc, value_acc, rows, low_first)

    def body(s, block, start):
        statistics(s)
        over_window(block_count, reach, start, parity == 1, lambda rows: gradients_of(s, rows))

    @pl.when(lax.rem(rank, 2) == parity)
    def _():
        key_acc[...] = jnp.zeros_like(key_acc)
        value_acc[...] = jnp.zeros_like(value_acc)
        slots = slots_of(assistant, turn_first, rank * block_count, block_count, slot_count)
        count = 1 if parity == 0 else block_count
        together = all_slots(slots, lambda start: start == -count)

        @pl.when(together)
        def _():
            rows = pl.ds((reach - count) * BLK, count * BLK)
            for s in range(slot_count):
                statistics(s)
            for s in range(slot_count):
                gradients_of(s, rows, s * count * BLK)

        pl.when(jnp.logical_not(together))(lambda: over_slots(slots, body))

        def round_to(out, first, rows):
            out[0] = (key_acc[first:first + rows, :] * scale).astype(BF16)
            out[1] = value_acc[first:first + rows, :].astype(BF16)

        total = reach * BLK
        round_to(near_out, total - near_out.shape[1], near_out.shape[1])

        @pl.when(need[0] > 0)
        def _():
            round_to(far_low, 0, far_low.shape[1])
            pltpu.sync_copy(far_low, far_hbm)

        if parity == 0:
            @pl.when(need[0] > 1)
            def _():
                round_to(rest_low, far_low.shape[1], rest_low.shape[1])
                pltpu.sync_copy(rest_low, rest_hbm)


def sends_late(rank, slots):
    behind = sum(jnp.where(live, jnp.maximum(-start, 0), 0) for _, live, start in slots)
    return (lax.rem(rank, 2) == 1) & (rank > 1) & (behind <= 3)


def finish_kernel(sizes, early, assistant, turn_first, query_ref, grad_ref, weight_ref, prob_ref, score_in,
                  inverse_ref, delta_ref, kv_ref, window, *rest):
    query_hbm, key_acc, value_acc, stage, score_ref, low_ref, query_acc, blank, sem = rest[-9:]
    block_count, slot_count, head_count, width, scale = sizes
    rank = lax.axis_index("ctx")
    base = rank * block_count
    reach = window.shape[0] // BLK
    columns = query_acc.shape[1]

    def blank_copy(i):
        return pltpu.make_async_copy(blank, query_hbm.at[0, pl.ds(i * BLK, BLK)], sem.at[slot_count + i])

    slots = slots_of(assistant, turn_first, base, block_count, slot_count)

    def run():
        more = [live for _, live, _ in slots[1:]]

        def stage_copy(s):
            return pltpu.make_async_copy(stage.at[s], query_hbm.at[0, block_rows(slots[s][0])], sem.at[s])

        blank[...] = jnp.zeros_like(blank)
        for i in range(block_count):
            @pl.when(assistant[0, base + i] != 1)
            def _():
                blank_copy(i).start()
        key_acc[...] = jnp.zeros_like(key_acc)
        value_acc[...] = jnp.zeros_like(value_acc)

        def body(s, block, start):
            def query_part(keys, source, rows, span):
                return nn_dot(keys.T, source[s, rows, span])

            def remote_part(rows, first=False):
                keys = window[rows, :]
                for c in range(0, columns, CHUNK):
                    span = slice(c, c + CHUNK)
                    part = query_part(keys, score_in, rows, span)
                    query_acc[:, span] = part if first else query_acc[:, span] + part

            @pl.when(start <= -block_count)
            def _():
                remote_part(pl.ds((reach - block_count) * BLK, block_count * BLK), True)

            @pl.when(start > -block_count)
            def _():
                query_acc[...] = jnp.zeros_like(query_acc)

            def remote_step(k, carry):
                remote_part(block_rows(k))
                return carry

            lax.fori_loop(
                jnp.maximum(start + reach, 0),
                jnp.where(start <= -block_count, reach - block_count, reach),
                remote_step,
                0,
            )
            low = jnp.maximum(start, 0)
            for count in range(1, block_count + 1):
                @pl.when(block + 1 - low == count)
                def _():
                    rows = block_rows(low, count)
                    grad_pass(weight_ref, prob_ref, (s, rows), query_ref, grad_ref, s, inverse_ref, delta_ref,
                              low_ref, score_ref, rows, key_acc, value_acc, rows)
                    keys = kv_ref[0, rows, :]
                    for c in range(0, columns, CHUNK):
                        span = slice(c, c + CHUNK)
                        total = query_acc[:, span] + query_part(keys, score_ref, rows, span)
                        for h in range(0, CHUNK, BLK):
                            place = slice((c + h) // BLK * width, ((c + h) // BLK + 1) * width)
                            stage[s, :, place] = (total[:, h:h + BLK] * scale).T.astype(BF16)

            for i in range(slot_count - 1):
                @pl.when((s == i) & more[i])
                def _():
                    stage_copy(i).start()

        over_slots(slots, body)
        key_acc[...] = key_acc[...] * scale
        for i in range(slot_count - 1):
            @pl.when(more[i])
            def _():
                stage_copy(i).wait()

        for i in range(block_count):
            @pl.when(assistant[0, base + i] != 1)
            def _():
                blank_copy(i).wait()

    before = sends_late(rank, slots)
    pl.when(before if early else jnp.logical_not(before))(run)


def add_kernel(need, key_in, value_in, outer_ref, far_hbm, rest_hbm, key_acc, value_acc, far, rest):
    pairs = list(enumerate((key_acc, value_acc)))

    def add_last(source):
        for i, acc in pairs:
            acc[acc.shape[0] - source.shape[1]:, :] += source[i].astype(F32)

    add_last(outer_ref)

    @pl.when(need[0] > 0)
    def _():
        pltpu.sync_copy(far_hbm, far)
        add_last(far)

    @pl.when(need[0] > 1)
    def _():
        pltpu.sync_copy(rest_hbm, rest)
        for i, acc in pairs:
            acc[:rest.shape[1], :] += rest[i].astype(F32)


def total_kernel(sizes, parity, assistant, turn_first, key_acc, value_acc, stage, *rest):
    query_hbm, key_hbm, value_hbm, low, sem = rest[-5:]
    block_count, slot_count, head_count, width, scale = sizes
    rank = lax.axis_index("ctx")

    @pl.when(lax.rem(rank, 2) == parity)
    def _():
        slots = slots_of(assistant, turn_first, rank * block_count, block_count, slot_count)
        ends = [
            live & jnp.logical_not(slots[s + 1][1]) if s + 1 < slot_count else live
            for s, (_, live, _) in enumerate(slots)
        ]

        def stage_copy(s):
            rows = block_rows(slots[s][0])
            return pltpu.make_async_copy(stage.at[s], query_hbm.at[0, rows], sem.at[2 + s])

        for s in range(slot_count):
            @pl.when(ends[s])
            def _():
                stage_copy(s).start()

        copies = []
        for i, (acc, out) in enumerate(((key_acc, key_hbm), (value_acc, value_hbm))):
            total = acc[...] if parity == 1 else acc[...] + rest[0][i].astype(F32)
            low[i] = total.astype(BF16)
            copies.append(pltpu.make_async_copy(low.at[i], out.at[0], sem.at[i]))
            copies[i].start()
        for copy in copies:
            copy.wait()
        for s in range(slot_count):
            @pl.when(ends[s])
            def _():
                stage_copy(s).wait()


def call(kernel, inputs, in_specs, outputs, out_specs, scratch, limit, macs, aliases={},
         traffic=2 * MIB):
    return pl.pallas_call(
        kernel,
        out_shape=outputs,
        in_specs=in_specs,
        out_specs=out_specs,
        scratch_shapes=scratch,
        input_output_aliases=aliases,
        compiler_params=pltpu.CompilerParams(vmem_limit_bytes=limit * MIB),
        cost_estimate=pl.CostEstimate(flops=2 * macs, bytes_accessed=traffic, transcendentals=0),
    )(*inputs)


ANY_SPEC = pl.BlockSpec(memory_space=pl.ANY)
SMEM_SPEC = pl.BlockSpec(memory_space=pltpu.SMEM)
VMEM_SPEC = pl.BlockSpec(memory_space=pltpu.VMEM)


def score_shapes(sizes, rows):
    block_count, slot_count, head_count, width, scale = sizes
    columns = head_count * BLK
    return (
        pltpu.VMEM((slot_count, rows, columns), F32),
        pltpu.VMEM((slot_count, rows, columns), F32),
        pltpu.VMEM((slot_count, SUB, columns), F32),
        pltpu.VMEM((slot_count, SUB, columns), F32),
    )


def skip_kernel(*refs):
    pass


def stack_kernel(key_ref, value_ref, *outs):
    *outs, sem = outs
    copies = []
    for out in outs:
        first = key_ref.shape[1] - out.shape[1]
        for i, source in enumerate((key_ref, value_ref)):
            copies.append(
                pltpu.make_async_copy(
                    source.at[0, pl.ds(first, out.shape[1])], out.at[i], sem.at[len(copies)]
                )
            )
    for copy in copies:
        copy.start()
    for copy in copies:
        copy.wait()


def skipped(*shapes):
    return tuple(call(skip_kernel, (), [], shapes, [ANY_SPEC] * len(shapes), [], 4, 1, {}, 1))


def per_device(query_rows, key_rows, value_rows, out_grad, assistant, turn_first):
    token_count = query_rows.shape[1]
    width = key_rows.shape[2]
    head_count = query_rows.shape[2] // width
    block_count = token_count // BLK
    far_rows = block_count // 2 * BLK
    reach_rows = token_count + far_rows
    slot_count = (block_count + 1) // 2
    columns = head_count * BLK
    pair = columns * BLK * width
    sizes = (block_count, slot_count, head_count, width, 1.0 / math.sqrt(width))
    stat_rows = (slot_count, SUB, columns)
    slot_rows = pltpu.VMEM((slot_count, columns, width), BF16)

    def pack(early, state):
        inputs = tuple(hbm(a) for a in (key_rows, value_rows, assistant, turn_first, query_rows, out_grad))
        last_shape = (pltpu.VMEM((2, far_rows, width), BF16),) if early else ()
        held = tuple(smem(a) if i in (1, 2, 3) else vmem(a) for i, a in enumerate(state))
        specs = [VMEM_SPEC] + [SMEM_SPEC] * 3 + [VMEM_SPEC] * 2
        return call(
            lambda *refs: pack_kernel(sizes, early, *refs),
            inputs + held,
            [ANY_SPEC] * 6 + specs[:len(held)],
            (
                pltpu.VMEM((2, token_count, width), BF16),
                pltpu.SMEM(assistant.shape, jnp.int32),
                pltpu.SMEM(turn_first.shape, jnp.int32),
                pltpu.SMEM((1,), jnp.int32),
                slot_rows,
                slot_rows,
            )
            + last_shape,
            specs + [VMEM_SPEC] * len(last_shape),
            [pltpu.SemaphoreType.DMA((6,)), pltpu.SemaphoreType.DMA((slot_count, 2))],
            4,
            pair,
            {6 + i: i for i in range(len(held))},
            1,
        )

    *state, last = pack(True, ())
    outer_in = pair_shift(last, "ctx", 1, 0)
    own, *marks, need, query_slots, grad_slots = pack(False, state)
    inner_in = pair_shift(own, "ctx", 1, 1)
    marks = tuple(smem(a) for a in marks)
    flag = smem(need)
    far_shape = jax.ShapeDtypeStruct((2, far_rows, width), BF16)
    whole_shape = jax.ShapeDtypeStruct((2, token_count, width), BF16)
    rest_shape = jax.ShapeDtypeStruct((2, token_count - far_rows, width), BF16)

    def stacked(sources, *shapes):
        return call(stack_kernel, sources, [ANY_SPEC] * 2, shapes, [ANY_SPEC] * len(shapes),
                    [pltpu.SemaphoreType.DMA((2 * len(shapes),))], 4, 1, {}, 1)

    def far_only(*sources):
        far, = stacked(sources, far_shape)
        return (shifted(far, "ctx", 2),) + skipped(whole_shape)

    def far_and_whole(*sources):
        far, whole = stacked(sources, far_shape, whole_shape)
        return shifted(far, "ctx", 2), pair_shift(whole, "ctx", 1, 0)

    far_in, whole_in = lax.switch(
        need[0], [lambda *_: skipped(far_shape, whole_shape), far_only, far_and_whole], key_rows, value_rows
    )
    local_own, far_in, whole_in = lax.optimization_barrier((own, far_in, whole_in))
    weights, prob_grad, sums, dots = call(
        lambda *refs: local_kernel(sizes, *refs),
        marks + tuple(vmem(a) for a in (query_slots, grad_slots, local_own)),
        [SMEM_SPEC] * 2 + [VMEM_SPEC] * 3,
        score_shapes(sizes, token_count),
        [VMEM_SPEC] * 4,
        [],
        8,
        pair,
        {},
        1,
    )

    def near(parity, sources, kept):
        inputs = marks + (flag, vmem(query_slots), vmem(grad_slots), hbm(far_in)) + sources
        return tuple(
            call(
                lambda *refs: near_kernel(sizes, parity, *refs),
                inputs + tuple(vmem(a) for a in kept),
                [SMEM_SPEC] * 3 + [VMEM_SPEC] * 2 + [ANY_SPEC, VMEM_SPEC]
                + [ANY_SPEC] * (len(sources) - 1) + [VMEM_SPEC] * len(kept),
                score_shapes(sizes, reach_rows) + (pltpu.VMEM((reach_rows, width), BF16),),
                [VMEM_SPEC] * 5,
                [pltpu.VMEM((reach_rows, width), BF16), pltpu.SemaphoreType.DMA((4,))],
                8,
                NEAR_HINT[parity] * pair,
                {len(inputs) + i: i for i in range(len(kept))},
                1,
            )
        )

    def remote(parity, near_rows, near_state, kept):
        inputs = marks + (flag,) + tuple(vmem(a) for a in (query_slots, grad_slots, sums, dots))
        held = tuple(vmem(a) for a in kept[:3]) + tuple(hbm(a) for a in kept[3:])
        passed = score_shapes(sizes, reach_rows) if parity == 0 else ()
        aliases = {len(inputs) + 4 + i: i for i in range(len(held))}
        aliases.update({len(inputs) + i: 5 + i for i in range(len(passed))})
        results = call(
            lambda *refs: remote_kernel(sizes, parity, *refs),
            inputs + tuple(vmem(a) for a in near_state) + held,
            [SMEM_SPEC] * 3 + [VMEM_SPEC] * (8 + len(held[:3])) + [ANY_SPEC] * len(held[3:]),
            (
                pltpu.VMEM((slot_count, reach_rows, columns), BF16),
                pltpu.VMEM(stat_rows, F32),
                pltpu.VMEM(stat_rows, F32),
                far_shape,
                rest_shape,
            )
            + passed
            + (pltpu.VMEM((2, near_rows, width), BF16),),
            [VMEM_SPEC] * 3 + [ANY_SPEC] * 2 + [VMEM_SPEC] * (1 + len(passed)),
            [
                pltpu.VMEM((slot_count * token_count, columns), BF16),
                pltpu.VMEM((reach_rows, width), F32),
                pltpu.VMEM((reach_rows, width), F32),
                pltpu.VMEM(far_shape.shape, BF16),
                pltpu.VMEM(rest_shape.shape, BF16),
            ],
            8,
            REMOTE_HINT[parity] * pair,
            aliases,
            1,
        )
        return tuple(results[:5]), tuple(results[5:-1]), results[-1]

    *near_state, window = near(0, (vmem(outer_in), hbm(whole_in)), ())
    remote_state, near_state, outer_grad = remote(0, far_rows, near_state, ())
    outer_back = pair_shift(outer_grad, "ctx", -1, 0)
    *near_state, window = near(1, (vmem(inner_in),), near_state + (window,))
    remote_state, _, inner_grad = remote(1, token_count, near_state, remote_state)
    window = (window,)
    score_grad, inverse, delta, far_grad, rest_grad = remote_state

    def finish(early, state):
        inputs = marks + tuple(
            vmem(a)
            for a in (query_slots, grad_slots, weights, prob_grad, score_grad, inverse, delta, own) + window
        )
        return call(
            lambda *refs: finish_kernel(sizes, early, *refs),
            inputs + tuple(hbm(a) for a in state[:1]) + tuple(vmem(a) for a in state[1:]),
            [SMEM_SPEC] * 2 + [VMEM_SPEC] * 9 + [ANY_SPEC] * len(state[:1]) + [VMEM_SPEC] * len(state[1:]),
            (
                jax.ShapeDtypeStruct(query_rows.shape, BF16),
                pltpu.VMEM((token_count, width), F32),
                pltpu.VMEM((token_count, width), F32),
                pltpu.VMEM((slot_count, BLK, head_count * width), BF16),
            ),
            [ANY_SPEC] + [VMEM_SPEC] * 3,
            [
                pltpu.VMEM((slot_count, token_count, columns), BF16),
                pltpu.VMEM((token_count, columns), BF16),
                pltpu.VMEM((BLK, columns), F32),
                pltpu.VMEM((BLK, head_count * width), BF16),
                pltpu.SemaphoreType.DMA((slot_count + block_count,)),
            ],
            10,
            pair,
            {len(inputs) + i: i for i in range(len(state))},
            1,
        )

    state = finish(True, ())
    inner_grad, state = lax.optimization_barrier((inner_grad, state))
    inner_back = pair_shift(inner_grad, "ctx", -1, 1)
    query_grad, key_acc, value_acc, stage = finish(False, tuple(state))
    far_grad, rest_grad, query_grad = lax.optimization_barrier((far_grad, rest_grad, query_grad))
    far_back, rest_back = lax.switch(
        need[0],
        [
            lambda far, rest: skipped(far_shape, rest_shape),
            lambda far, rest: (shifted(far, "ctx", -2),) + skipped(rest_shape),
            lambda far, rest: (shifted(far, "ctx", -2), pair_shift(rest, "ctx", -1, 0)),
        ],
        far_grad,
        rest_grad,
    )
    key_acc, value_acc = call(
        add_kernel,
        (flag,) + tuple(vmem(a) for a in (key_acc, value_acc, outer_back)) + (hbm(far_back), hbm(rest_back)),
        [SMEM_SPEC] + [VMEM_SPEC] * 3 + [ANY_SPEC] * 2,
        (pltpu.VMEM((token_count, width), F32),) * 2,
        [VMEM_SPEC] * 2,
        [pltpu.VMEM(far_shape.shape, BF16), pltpu.VMEM(rest_shape.shape, BF16)],
        4,
        CROSS_HINT * pair,
        {1: 0, 2: 1},
        1,
    )
    results = (query_grad,)
    for parity, received in ((1, ()), (0, (vmem(inner_back),))):
        inputs = marks + tuple(vmem(a) for a in (key_acc, value_acc, stage)) + received
        results = call(
            lambda *refs: total_kernel(sizes, parity, *refs),
            inputs + tuple(hbm(a) for a in results),
            [SMEM_SPEC] * 2 + [VMEM_SPEC] * (len(inputs) - 2) + [ANY_SPEC] * len(results),
            tuple(jax.ShapeDtypeStruct(a.shape, BF16) for a in (query_rows, key_rows, value_rows)),
            [ANY_SPEC] * 3,
            [pltpu.VMEM((2, token_count, width), BF16), pltpu.SemaphoreType.DMA((2 + slot_count,))],
            8,
            pair,
            {len(inputs) + i: i for i in range(len(results))},
            1,
        )
    return tuple(results)


def solution(mesh):
    return jax.shard_map(
        per_device,
        mesh=mesh,
        in_specs=(
            P("dp", "ctx", "tp"),
            P("dp", "ctx", "tp"),
            P("dp", "ctx", "tp"),
            P("dp", "ctx", "tp"),
            P("dp", None),
            P("dp", None),
        ),
        out_specs=(P("dp", "ctx", "tp"), P("dp", "ctx", "tp"), P("dp", "ctx", "tp")),
        check_vma=False,
    )
```
